32 devices in a mesh: sx: 4 (over y, x), sy: 8 (over z, core).
Axes of the slice: x: 2, y: 2, z: 4, core: 2. Of those that a mesh axis runs over, the one named last changes fastest.
Arguments:
- traces: bfloat16 [4, 8, 4, 6, 16, 768], P('sx', 'sy'), may hold values from -6 to 6
- viscosity: float32 [4, 8, 4], P('sx', 'sy'), may hold values from 0.1 to 10
- partner: int32 [4, 8, 4, 4], P('sx', 'sy'), may hold values from 0 to 3, as said below
- corner_owner: int32 [4, 8, 4, 8], P('sx', 'sy'), may hold values from 0 to 63
- self_block: bfloat16 [768, 768], replicated, may hold values from -0.21875 to 0.21875
- opposite_block: bfloat16 [768, 768], replicated, may hold values from -0.21875 to 0.21875
- cross_block: bfloat16 [768, 768], replicated, may hold values from -0.21875 to 0.21875
- corner_map: bfloat16 [24, 6, 768], replicated, may hold values from -0.09375 to 0.09375
Outputs:
- applied: float32 [4, 8, 4, 6, 16, 768], P('sx', 'sy')
- coarse: float32 [48, 256], P(None, ('sx', 'sy'))
The draws below stay inside these ranges and needn't reach their ends.
Inputs may be any that keep to these rules, and one draw needn't show every extreme that they name: Face partners match: if the +x partner of (i, j, k) is slot p of (i+1, j), then the -x partner of (i+1, j, p) is slot k, likewise for y; each column of one device is a permutation of the 4 slots.
All inputs are finite; a program needn't handle non-finite values.
Results may differ from the reference program's by a relative error of at most 0.0042.
Values may be sent and summed in bfloat16 or wider, within the bound.
No kernel may reach another device: no remote copies, remote signals or barrier semaphores. Data moves between devices by JAX's collectives and lax.ppermute only.
A program may use at most 64 MiB of HBM per device.

```python
import math
import jax
import jax.numpy as jnp
from jax import lax

FACE = 768
RHS = 16
SUB_DEV = 4
CORNERS = 8
COMPS = 3
SUB_X = 4
SUB_Y = 8
NC_ROW = 64


def draw_partner(key, part):
    key = jax.random.fold_in(key, 7)
    key_x, key_y = jax.random.split(key)
    slots = jnp.arange(SUB_DEV, dtype=jnp.int32)

    def one_perm(sub_key):
        scores = jax.random.randint(sub_key, (SUB_X, SUB_Y, SUB_DEV), 0, 1 << 20, dtype=jnp.int32)
        scores = scores * SUB_DEV + slots
        return jnp.argsort(scores, axis=-1).astype(jnp.int32)
    perm_x = one_perm(key_x)
    perm_y = one_perm(key_y)
    inverse_x = jnp.argsort(perm_x, axis=-1).astype(jnp.int32)
    inverse_y = jnp.argsort(perm_y, axis=-1).astype(jnp.int32)
    back_x = jnp.roll(inverse_x, 1, axis=0)
    back_y = jnp.roll(inverse_y, 1, axis=1)
    return jnp.stack([perm_x, back_x, perm_y, back_y], axis=-1).astype(jnp.int32)


def touch_ends(result, own_key, low, top_value):
    index_at = [jax.random.randint(jax.random.fold_in(own_key, axis), (), 0, length) for axis, length in enumerate(result.shape)]
    widest = result.shape.index(max(result.shape))
    beside = index_at[:widest] + [(index_at[widest] + 1) % result.shape[widest]] + index_at[widest + 1:]
    return result.at[tuple(index_at)].set(low).at[tuple(beside)].set(top_value)


def level_of(stream_key, extent, cuts, smallest, high):
    loudness, own = 1.0, jax.random.fold_in(stream_key, 6)
    for dim, shards_of in cuts:
        draws = jnp.exp(jax.random.uniform(jax.random.fold_in(own, dim), (shards_of,), jnp.float32, smallest / len(cuts), high / len(cuts)))
        loudness = loudness * jnp.repeat(draws, extent[dim] // shards_of).reshape([-1 if axis == dim else 1 for axis in range(len(extent))])
    return loudness


def bell_draw(key, dims, spread, reach, shards=(), kind=jnp.bfloat16):
    loudness = level_of(key, dims, shards, -0.22, 0.18) if shards else 1.0
    drawn = jax.random.normal(key, dims, jnp.float32) * spread * loudness
    return jnp.minimum(jnp.maximum(drawn, -reach), reach).astype(kind)


def setup_inputs(seed: int = 0) -> dict:
    seeds = jax.random.split(jax.random.key(seed), 9)
    return {
        "traces": bell_draw(seeds[0], (SUB_X, SUB_Y, SUB_DEV, 6, RHS, FACE), 1.0, 6.0, ((0, 4), (1, 8))),
        "viscosity": jnp.clip(jnp.exp(math.log(10.0) - 4.6051702 * jax.random.uniform(seeds[1], (SUB_X, SUB_Y, SUB_DEV), jnp.float32) ** level_of(seeds[1], (SUB_X, SUB_Y, SUB_DEV), ((0, 4), (1, 8)), -0.2, 0.2)), 0.1, 10.0),
        "partner": draw_partner(jax.random.fold_in(seeds[8], 71), 0),
        "corner_owner": touch_ends(jax.random.randint(seeds[3], (SUB_X, SUB_Y, SUB_DEV, CORNERS), 0, NC_ROW), jax.random.fold_in(seeds[3], 1), 0, NC_ROW - 1).astype(jnp.int32),
        "self_block": bell_draw(seeds[4], (FACE, FACE), FACE ** -0.5, 0.21875),
        "opposite_block": bell_draw(seeds[5], (FACE, FACE), FACE ** -0.5, 0.21875),
        "cross_block": bell_draw(seeds[6], (FACE, FACE), FACE ** -0.5, 0.21875),
        "corner_map": bell_draw(seeds[7], (CORNERS * COMPS, 6, FACE), (6 * FACE) ** -0.5, 0.09375),
    }


FLIP = (1, 0, 3, 2, 5, 4)


def facing(data, partner):
    zero_row = jnp.zeros_like(data[:1, :, :, 0])
    zero_col = jnp.zeros_like(data[:, :1, :, 0])
    zero_sub = jnp.zeros_like(data[:, :, :1, 0])
    up_x = jnp.concatenate([data[1:, :, :, 1], zero_row], 0)
    down_x = jnp.concatenate([zero_row, data[:-1, :, :, 0]], 0)
    up_y = jnp.concatenate([data[:, 1:, :, 3], zero_col], 1)
    down_y = jnp.concatenate([zero_col, data[:, :-1, :, 2]], 1)
    up_z = jnp.concatenate([data[:, :, 1:, 5], zero_sub], 2)
    down_z = jnp.concatenate([zero_sub, data[:, :, :-1, 4]], 2)

    def select(values, column):
        index = partner[:, :, :, column][:, :, :, None, None].astype(jnp.int32)
        return jnp.take_along_axis(values, index, axis=2)

    faces = [select(up_x, 0), select(down_x, 1), select(up_y, 2), select(down_y, 3), up_z, down_z]
    return jnp.stack(faces, axis=3)


def reference(traces, viscosity, partner, corner_owner, self_block, opposite_block, cross_block, corner_map):
    flip = jnp.array(FLIP, dtype=jnp.int32)
    jumps = (traces.astype(jnp.float32) - facing(traces, partner).astype(jnp.float32)).astype(jnp.bfloat16)
    width = self_block.shape[0]

    def row_work(inputs):
        jump_row, visc_row = inputs
        shape = jump_row.shape
        flat = jump_row.reshape(-1, width)
        with_self = jnp.dot(flat, self_block, preferred_element_type=jnp.float32).reshape(shape)
        with_opp = jnp.dot(flat, opposite_block, preferred_element_type=jnp.float32).reshape(shape)
        with_cross = jnp.dot(flat, cross_block, preferred_element_type=jnp.float32).reshape(shape)
        adjacent = jnp.sum(with_cross, axis=2, keepdims=True) - with_cross - jnp.take(with_cross, flip, axis=2)
        total = with_self + jnp.take(with_opp, flip, axis=2) + adjacent
        return (visc_row[:, :, None, None, None] * total).astype(jnp.bfloat16)

    local = lax.map(row_work, (jumps, viscosity))
    applied = local.astype(jnp.float32) - facing(local, partner).astype(jnp.float32)
    partials = jnp.einsum("xyzfqi,kfi->xyzqk", local.astype(jnp.float32), corner_map.astype(jnp.float32))
    rows = partials.shape[0]
    per_row = partials.reshape(rows, -1, RHS, CORNERS, COMPS)
    per_row = jnp.transpose(per_row, (0, 1, 3, 2, 4)).reshape(rows, -1, RHS * COMPS)
    owners = corner_owner.reshape(rows, -1).astype(jnp.int32)

    def assemble(inputs):
        values, ids = inputs
        return jnp.zeros((NC_ROW, RHS * COMPS), jnp.float32).at[ids].add(values)

    coarse = lax.map(assemble, (per_row, owners))
    coarse = jnp.transpose(coarse, (2, 0, 1)).reshape(RHS * COMPS, rows * NC_ROW)
    return applied, coarse
```

```python
import jax
import jax.numpy as jnp
from jax import lax
from jax.experimental import pallas as pl
from jax.experimental.pallas import tpu as pltpu
from jax.sharding import PartitionSpec as P

CORNERS = 8
COMPS = 3
COARSE_DEV = 8
LANES = 128

VMEM = pl.BlockSpec(memory_space=pltpu.VMEM)
SMEM = pl.BlockSpec(memory_space=pltpu.SMEM)
ANY = pl.BlockSpec(memory_space=pl.ANY)


def in_vmem(shape, dtype):
    return pltpu.VMEM(shape, dtype)


def signs(axis):
    return lax.rem(lax.axis_index(axis), 2)


def swap(value, axis, offset, wrap):
    count = lax.axis_size(axis)
    pairs = []
    for source in range(count):
        target = source + (offset if source % 2 == 0 else -offset)
        if wrap or 0 <= target < count:
            pairs.append((source, target % count))
    return lax.ppermute(value, axis, pairs)


def traded_faces():
    odd_x, odd_y = signs("sx"), signs("sy")
    return odd_x, 1 - odd_x, 2 + odd_y, 3 - odd_y


def send_kernel(traces, xa, xb, ya, yb, sems):
    copies = []
    for index, (face, out) in enumerate(zip(traded_faces(), (xa, xb, ya, yb))):
        copies.append(pltpu.make_async_copy(traces.at[:, face], out, sems.at[index]))
        copies[-1].start()
    for copy in copies:
        copy.wait()


def high_low(value):
    high = value.astype(jnp.bfloat16).astype(jnp.float32)
    return high, value - high


def coarse_rows(partials, owners, rows):
    subs = owners.shape[0]
    width = partials.shape[1]
    rhs = width // subs
    entries = jnp.zeros((2 * CORNERS, subs * LANES), jnp.float32)
    source = lax.broadcasted_iota(jnp.int32, (width, subs * LANES), 0)
    target = lax.broadcasted_iota(jnp.int32, (width, subs * LANES), 1)
    spread = (source // rhs) * LANES + (source % rhs) * COMPS
    for comp in range(COMPS):
        part = partials[comp * CORNERS : (comp + 1) * CORNERS]
        stacked = jnp.concatenate(high_low(part), axis=0).astype(jnp.bfloat16)
        place = (target == spread + comp).astype(jnp.float32).astype(jnp.bfloat16)
        entries += jnp.dot(stacked, place, preferred_element_type=jnp.float32)
    entries = entries[:CORNERS] + entries[CORNERS:]
    total = jnp.zeros((rows, LANES), jnp.float32)
    numbers = lax.broadcasted_iota(jnp.int32, (rows, CORNERS), 0)
    for sub in range(subs):
        onehot = (numbers == owners[sub : sub + 1, :]).astype(jnp.float32).astype(jnp.bfloat16)
        for term in high_low(entries[:, sub * LANES : (sub + 1) * LANES]):
            total += jnp.dot(
                onehot, term.astype(jnp.bfloat16), preferred_element_type=jnp.float32
            )
    return total


def local_kernel(
    count, reach,
    partner, viscosity, owners, traces, rxa, rxb, rya, ryb, self_block, opposite_block,
    cross_block, corner_map,
    local, xa, xb, ya, yb, msg_a, msg_b, kept,
    jumps, dense,
):
    subs, _, rhs, face_size = traces.shape
    faces = traded_faces()
    for face, received in zip(faces, (rxa, rxb, rya, ryb)):
        for sub in range(subs):
            other = received[partner[sub, face]].astype(jnp.float32)
            own = traces[sub, face].astype(jnp.float32)
            jumps[face, sub] = (own - other).astype(jnp.bfloat16)
    for sub in range(subs):
        up = traces[sub, 4].astype(jnp.float32)
        down = traces[sub, 5].astype(jnp.float32)
        if sub + 1 < subs:
            up = up - traces[sub + 1, 5].astype(jnp.float32)
        if sub > 0:
            down = down - traces[sub - 1, 4].astype(jnp.float32)
        jumps[4, sub] = up.astype(jnp.bfloat16)
        jumps[5, sub] = down.astype(jnp.bfloat16)

    rows = subs * rhs
    pairs = []
    for pair in range(3):
        both = jumps[2 * pair : 2 * pair + 2].reshape(2 * rows, face_size).astype(jnp.float32)
        pairs.append(both[:rows] + both[rows:])
    beside = jnp.concatenate(
        [pairs[1] + pairs[2], pairs[0] + pairs[2], pairs[0] + pairs[1]], axis=0
    ).astype(jnp.bfloat16)
    with_cross = jnp.dot(beside, cross_block[...], preferred_element_type=jnp.float32)
    flat = jumps[...].reshape(6 * rows, face_size)
    with_self = jnp.dot(flat, self_block[...], preferred_element_type=jnp.float32)
    with_opp = jnp.dot(flat, opposite_block[...], preferred_element_type=jnp.float32)
    for face in range(6):
        opp, pair = face ^ 1, face // 2
        total = (
            with_self[face * rows : (face + 1) * rows]
            + with_opp[opp * rows : (opp + 1) * rows]
            + with_cross[pair * rows : (pair + 1) * rows]
        )
        for sub in range(subs):
            scaled = viscosity[sub] * total[sub * rhs : (sub + 1) * rhs]
            local[face, sub] = scaled.astype(jnp.bfloat16)
    for face, out in zip(faces, (xa, xb, ya, yb)):
        out[0:subs] = local[face]
    blank = jnp.zeros((rhs, face_size), jnp.bfloat16)
    ya[subs] = blank
    yb[subs] = blank

    partials = jnp.zeros((COMPS * CORNERS, rows), jnp.float32)
    for face in range(6):
        partials += lax.dot_general(
            corner_map[face],
            local[face].reshape(rows, face_size),
            (((1,), (1,)), ((), ())),
            preferred_element_type=jnp.float32,
        )
    dense[...] = coarse_rows(partials, owners[...], dense.shape[0])
    me = lax.axis_index("sy")
    step = (2 * reach + 1)
    sign = 1 - 2 * signs("sy")

    def block(offset):
        index = lax.rem(me + offset + 2 * count, count)
        return dense[pl.ds(pl.multiple_of(index * COARSE_DEV, COARSE_DEV), COARSE_DEV), :]

    for rest in range(-reach, reach + 1):
        kept[rest + reach] = block(rest)
        for out, way in ((msg_a, sign), (msg_b, -sign)):
            offset = rest + step * way
            inside = (offset > -count // 2) & (offset <= count // 2)
            out[rest + reach] = jnp.where(inside, block(offset), 0.0)


def coarse_kernel(kept, got_a, got_b, ya_in, yb_in, own, ya, yb):
    del ya_in, yb_in
    odd = signs("sy")
    subs = ya.shape[0] - 1
    own[...] = kept[1] + got_a[1] + got_b[1]
    for out, index in ((ya, 2 - 2 * odd), (yb, 2 * odd)):
        total = kept[index] + got_a[index] + got_b[index]
        out[subs, :, 0:LANES] = jnp.concatenate(high_low(total), axis=0).astype(jnp.bfloat16)


def apply_kernel(partner, local, rxa, rxb, rya, ryb, own, applied, coarse, held, sems):
    subs, _, rhs, _ = held.shape
    me, count = lax.axis_index("sy"), lax.axis_size("sy")
    inner = ((me > 0) & (me < count - 1)).astype(jnp.float32)
    copies = []
    faces = traded_faces()
    for sub in range(subs):
        for face, received in zip(faces, (rxa, rxb, rya, ryb)):
            other = received[partner[sub, face]].astype(jnp.float32)
            if received is ryb:
                other = other * inner
            held[sub, face] = local[face, sub].astype(jnp.float32) - other
        up = local[4, sub].astype(jnp.float32)
        down = local[5, sub].astype(jnp.float32)
        if sub + 1 < subs:
            up = up - local[5, sub + 1].astype(jnp.float32)
        if sub > 0:
            down = down - local[4, sub - 1].astype(jnp.float32)
        held[sub, 4] = up
        held[sub, 5] = down
        copies.append(pltpu.make_async_copy(held.at[sub], applied.at[sub], sems.at[sub]))
        copies[-1].start()
    total = own[...]
    for received in (rya, ryb):
        both = received[subs, :, 0:LANES].astype(jnp.float32)
        total = total + both[:COARSE_DEV] + both[COARSE_DEV:]
    coarse[...] = total[:, : rhs * COMPS]
    for copy in copies:
        copy.wait()


def params(mib):
    return pltpu.CompilerParams(vmem_limit_bytes=mib * 1024 * 1024)


def body(
    traces, viscosity, partner, corner_owner, self_block, opposite_block, cross_block, corner_map
):
    values = traces[0, 0]
    subs, _, rhs, face_size = values.shape
    count = lax.axis_size("sy")
    face_shape = (subs, rhs, face_size)
    long_shape = (subs + 1, rhs, face_size)
    coarse_total = COARSE_DEV * count

    sent = pl.pallas_call(
        send_kernel,
        in_specs=[ANY],
        out_specs=[VMEM] * 4,
        out_shape=[in_vmem(face_shape, jnp.bfloat16)] * 4,
        scratch_shapes=[pltpu.SemaphoreType.DMA((4,))],
        compiler_params=params(8),
    )(values)
    rya = swap(sent[2], "sy", 1, False)
    ryb = swap(sent[3], "sy", -1, False)
    rxa = swap(sent[0], "sx", 1, False)
    rxb = swap(sent[1], "sx", -1, False)

    steps = []
    step = 1
    while step * 3 - 1 < count:
        step *= 3
        steps.append(step)
    steps.reverse()
    reach = (steps[0] - 1) // 2
    chunks = (2 * reach + 1, COARSE_DEV, LANES)

    map_faces = corner_map.reshape(CORNERS, COMPS, 6, face_size).transpose(2, 1, 0, 3)
    map_faces = map_faces.reshape(6, CORNERS * COMPS, face_size)
    local, xa, xb, ya, yb, msg_a, msg_b, kept = pl.pallas_call(
        lambda *refs: local_kernel(count, reach, *refs),
        in_specs=[SMEM, SMEM] + [VMEM] * 10,
        out_specs=[VMEM] * 8,
        out_shape=[
            in_vmem((6,) + face_shape, jnp.bfloat16),
            in_vmem(face_shape, jnp.bfloat16),
            in_vmem(face_shape, jnp.bfloat16),
            in_vmem(long_shape, jnp.bfloat16),
            in_vmem(long_shape, jnp.bfloat16),
            in_vmem(chunks, jnp.float32),
            in_vmem(chunks, jnp.float32),
            in_vmem(chunks, jnp.float32),
        ],
        scratch_shapes=[
            pltpu.VMEM((6,) + face_shape, jnp.bfloat16),
            pltpu.VMEM((coarse_total, LANES), jnp.float32),
        ],
        compiler_params=params(24),
        cost_estimate=pl.CostEstimate(
            flops=2_000_000_000, bytes_accessed=6_000_000, transcendentals=0
        ),
    )(
        partner[0, 0], viscosity[0, 0], corner_owner[0, 0], values, rxa, rxb, rya, ryb,
        self_block, opposite_block, cross_block, map_faces,
    )

    got_a = swap(msg_a, "sy", steps[0], True)
    got_b = swap(msg_b, "sy", -steps[0], True)
    sign = 1 - 2 * signs("sy")
    for step in steps[1:]:
        total = kept + got_a + got_b
        inner = (step - 1) // 2
        at = lambda way: lax.dynamic_slice_in_dim(total, reach - inner + step * way, 2 * inner + 1)
        kept, reach = at(0), inner
        got_a = swap(at(sign), "sy", step, True)
        got_b = swap(at(-sign), "sy", -step, True)
    rxa = swap(xa, "sx", 1, False)
    rxb = swap(xb, "sx", -1, False)
    own, ya, yb = pl.pallas_call(
        coarse_kernel,
        in_specs=[VMEM] * 5,
        out_specs=[VMEM] * 3,
        out_shape=[
            in_vmem((COARSE_DEV, LANES), jnp.float32),
            in_vmem(long_shape, jnp.bfloat16),
            in_vmem(long_shape, jnp.bfloat16),
        ],
        input_output_aliases={3: 1, 4: 2},
        compiler_params=params(8),
    )(kept, got_a, got_b, ya, yb)
    rya = swap(ya, "sy", 1, True)
    ryb = swap(yb, "sy", -1, True)

    applied, coarse = pl.pallas_call(
        apply_kernel,
        in_specs=[SMEM] + [VMEM] * 6,
        out_specs=[ANY, VMEM],
        out_shape=[
            jax.ShapeDtypeStruct(values.shape, jnp.float32),
            jax.ShapeDtypeStruct((COARSE_DEV, rhs * COMPS), jnp.float32),
        ],
        scratch_shapes=[
            pltpu.VMEM(values.shape, jnp.float32),
            pltpu.SemaphoreType.DMA((subs,)),
        ],
        compiler_params=params(12),
    )(partner[0, 0], local, rxa, rxb, rya, ryb, own)
    return applied[None, None], coarse.T


def solution(mesh):
    return jax.shard_map(
        body,
        mesh=mesh,
        in_specs=(
            P("sx", "sy", None, None, None, None),
            P("sx", "sy", None),
            P("sx", "sy", None, None),
            P("sx", "sy", None, None),
            P(),
            P(),
            P(),
            P(),
        ),
        out_specs=(P("sx", "sy", None, None, None, None), P(None, ("sx", "sy"))),
        check_vma=False,
    )
```

```python
import jax
import jax.numpy as jnp
from jax import lax
from jax.experimental import pallas as pl
from jax.experimental.pallas import tpu as pltpu
from jax.sharding import PartitionSpec as P

CORNERS = 8
COMPS = 3
COARSE_DEV = 8
LANES = 128

VMEM = pl.BlockSpec(memory_space=pltpu.VMEM)
SMEM = pl.BlockSpec(memory_space=pltpu.SMEM)
HBM = pl.BlockSpec(memory_space=pltpu.HBM)
ANY = pl.BlockSpec(memory_space=pl.ANY)


def in_vmem(shape, dtype):
    return pltpu.VMEM(shape, dtype)


def signs(axis):
    return lax.rem(lax.axis_index(axis), 2)


def swap(value, axis, offset):
    count = lax.axis_size(axis)
    return lax.ppermute(
        value,
        axis,
        [(i, (i + (offset if i % 2 == 0 else -offset)) % count) for i in range(count)],
    )


def inner(axis):
    me = lax.axis_index(axis)
    return ((me > 0) & (me < lax.axis_size(axis) - 1)).astype(jnp.float32)


def traded_faces():
    odd_x, odd_y = signs("sx"), signs("sy")
    return odd_x, 1 - odd_x, 2 + odd_y, 3 - odd_y


def send_kernel(traces, xa, xb, ya, yb, sems):
    copies = []
    for index, (face, out) in enumerate(zip(traded_faces(), (xa, xb, ya, yb))):
        copies.append(pltpu.make_async_copy(traces.at[:, face], out, sems.at[index]))
        copies[-1].start()
    for copy in copies:
        copy.wait()


def fetch_kernel(
    after, traces, self_block, opposite_block, cross_block, corner_map,
    traces_out, self_out, opposite_out, cross_out, map_out, map_in, sems,
):
    del after
    copies = [pltpu.make_async_copy(corner_map, map_in, sems.at[0])]
    for source, target in ((self_block, self_out), (opposite_block, opposite_out), (cross_block, cross_out)):
        for part in range(3):
            rows = pl.ds(part * 256, 256)
            copies.append(
                pltpu.make_async_copy(source.at[rows], target.at[rows], sems.at[len(copies)])
            )
    copies.append(pltpu.make_async_copy(traces, traces_out, sems.at[len(copies)]))
    for copy in copies:
        copy.start()
    copies[0].wait()
    size = CORNERS * COMPS
    row = lax.broadcasted_iota(jnp.int32, (size, size), 0)
    col = lax.broadcasted_iota(jnp.int32, (size, size), 1)
    order = (col == (row % CORNERS) * COMPS + row // CORNERS).astype(jnp.float32)
    order = order.astype(jnp.bfloat16)
    for face in range(6):
        moved = jnp.dot(order, map_in[face], preferred_element_type=jnp.float32)
        map_out[face] = moved.astype(jnp.bfloat16)
    for copy in copies[1:]:
        copy.wait()


def high_low(value):
    high = value.astype(jnp.bfloat16).astype(jnp.float32)
    return high, value - high


def coarse_rows(partials, owners, rows):
    subs = owners.shape[0]
    width = partials.shape[1]
    rhs = width // subs
    entries = jnp.zeros((2 * CORNERS, subs * LANES), jnp.float32)
    source = lax.broadcasted_iota(jnp.int32, (width, subs * LANES), 0)
    target = lax.broadcasted_iota(jnp.int32, (width, subs * LANES), 1)
    spread = (source // rhs) * LANES + (source % rhs) * COMPS
    for comp in range(COMPS):
        part = partials[comp * CORNERS : (comp + 1) * CORNERS]
        stacked = jnp.concatenate(high_low(part), axis=0).astype(jnp.bfloat16)
        place = (target == spread + comp).astype(jnp.float32).astype(jnp.bfloat16)
        entries += jnp.dot(stacked, place, preferred_element_type=jnp.float32)
    entries = entries[:CORNERS] + entries[CORNERS:]
    total = jnp.zeros((rows, LANES), jnp.float32)
    numbers = lax.broadcasted_iota(jnp.int32, (rows, CORNERS), 0)
    for sub in range(subs):
        onehot = (numbers == owners[sub : sub + 1, :]).astype(jnp.float32).astype(jnp.bfloat16)
        for term in high_low(entries[:, sub * LANES : (sub + 1) * LANES]):
            total += jnp.dot(
                onehot, term.astype(jnp.bfloat16), preferred_element_type=jnp.float32
            )
    return total


def local_kernel(
    count, reach,
    partner, viscosity, owners, traces, rxa, rxb, rya, ryb, self_block, opposite_block,
    cross_block, corner_map,
    local, xa, xb, ya, yb, msg_a, msg_b, kept,
    jumps, dense,
):
    subs, _, rhs, face_size = traces.shape
    faces = traded_faces()
    for face, received in zip(faces, (rxa, rxb, rya, ryb)):
        for sub in range(subs):
            other = received[partner[sub, face]].astype(jnp.float32)
            if received is rxb:
                other = other * inner("sx")
            if received is ryb:
                other = other * inner("sy")
            own = traces[sub, face].astype(jnp.float32)
            jumps[face, sub] = (own - other).astype(jnp.bfloat16)
    for sub in range(subs):
        up = traces[sub, 4].astype(jnp.float32)
        down = traces[sub, 5].astype(jnp.float32)
        if sub + 1 < subs:
            up = up - traces[sub + 1, 5].astype(jnp.float32)
        if sub > 0:
            down = down - traces[sub - 1, 4].astype(jnp.float32)
        jumps[4, sub] = up.astype(jnp.bfloat16)
        jumps[5, sub] = down.astype(jnp.bfloat16)

    rows = subs * rhs
    pairs = []
    for pair in range(3):
        both = jumps[2 * pair : 2 * pair + 2].reshape(2 * rows, face_size).astype(jnp.float32)
        pairs.append(both[:rows] + both[rows:])
    beside = jnp.concatenate(
        [pairs[1] + pairs[2], pairs[0] + pairs[2], pairs[0] + pairs[1]], axis=0
    ).astype(jnp.bfloat16)
    with_cross = jnp.dot(beside, cross_block[...], preferred_element_type=jnp.float32)
    flat = jumps[...].reshape(6 * rows, face_size)
    with_self = jnp.dot(flat, self_block[...], preferred_element_type=jnp.float32)
    with_opp = jnp.dot(flat, opposite_block[...], preferred_element_type=jnp.float32)
    for face in range(6):
        opp, pair = face ^ 1, face // 2
        total = (
            with_self[face * rows : (face + 1) * rows]
            + with_opp[opp * rows : (opp + 1) * rows]
            + with_cross[pair * rows : (pair + 1) * rows]
        )
        for sub in range(subs):
            scaled = viscosity[sub] * total[sub * rhs : (sub + 1) * rhs]
            local[face, sub] = scaled.astype(jnp.bfloat16)
    for face, out in zip(faces, (xa, xb, ya, yb)):
        out[0:subs] = local[face]
    blank = jnp.zeros((rhs, face_size), jnp.bfloat16)
    ya[subs] = blank
    yb[subs] = blank

    partials = jnp.zeros((COMPS * CORNERS, rows), jnp.float32)
    for face in range(6):
        partials += lax.dot_general(
            corner_map[face],
            local[face].reshape(rows, face_size),
            (((1,), (1,)), ((), ())),
            preferred_element_type=jnp.float32,
        )
    dense[...] = coarse_rows(partials, owners[...], dense.shape[0])
    me = lax.axis_index("sy")
    step = (2 * reach + 1)
    sign = 1 - 2 * signs("sy")

    def block(offset):
        index = lax.rem(me + offset + 2 * count, count)
        return dense[pl.ds(pl.multiple_of(index * COARSE_DEV, COARSE_DEV), COARSE_DEV), :]

    for rest in range(-reach, reach + 1):
        kept[rest + reach] = block(rest)
        for out, way in ((msg_a, sign), (msg_b, -sign)):
            offset = rest + step * way
            inside = (offset > -count // 2) & (offset <= count // 2)
            out[rest + reach] = jnp.where(inside, block(offset), 0.0)


def coarse_kernel(kept, got_a, got_b, ya_in, yb_in, own, ya, yb):
    del ya_in, yb_in
    odd = signs("sy")
    subs = ya.shape[0] - 1
    own[...] = kept[1] + got_a[1] + got_b[1]
    for out, index in ((ya, 2 - 2 * odd), (yb, 2 * odd)):
        total = kept[index] + got_a[index] + got_b[index]
        out[subs, :, 0:LANES] = jnp.concatenate(high_low(total), axis=0).astype(jnp.bfloat16)


def apply_kernel(partner, local, rxa, rxb, rya, ryb, own, applied, coarse, held, sems):
    subs, _, rhs, _ = held.shape
    copies = []
    faces = traded_faces()
    for sub in range(subs):
        for face, received in zip(faces, (rxa, rxb, rya, ryb)):
            other = received[partner[sub, face]].astype(jnp.float32)
            if received is rxb:
                other = other * inner("sx")
            if received is ryb:
                other = other * inner("sy")
            held[sub, face] = local[face, sub].astype(jnp.float32) - other
        up = local[4, sub].astype(jnp.float32)
        down = local[5, sub].astype(jnp.float32)
        if sub + 1 < subs:
            up = up - local[5, sub + 1].astype(jnp.float32)
        if sub > 0:
            down = down - local[4, sub - 1].astype(jnp.float32)
        held[sub, 4] = up
        held[sub, 5] = down
        copies.append(pltpu.make_async_copy(held.at[sub], applied.at[sub], sems.at[sub]))
        copies[-1].start()
    total = own[...]
    for received in (rya, ryb):
        both = received[subs, :, 0:LANES].astype(jnp.float32)
        total = total + both[:COARSE_DEV] + both[COARSE_DEV:]
    coarse[...] = total[:, : rhs * COMPS]
    for copy in copies:
        copy.wait()


def params(mib):
    return pltpu.CompilerParams(vmem_limit_bytes=mib * 1024 * 1024)


def body(
    traces, viscosity, partner, corner_owner, self_block, opposite_block, cross_block, corner_map
):
    values = traces[0, 0]
    subs, _, rhs, face_size = values.shape
    count = lax.axis_size("sy")
    face_shape = (subs, rhs, face_size)
    long_shape = (subs + 1, rhs, face_size)
    coarse_total = COARSE_DEV * count

    sent = pl.pallas_call(
        send_kernel,
        in_specs=[HBM],
        out_specs=[VMEM] * 4,
        out_shape=[in_vmem(face_shape, jnp.bfloat16)] * 4,
        scratch_shapes=[pltpu.SemaphoreType.DMA((4,))],
        compiler_params=params(8),
    )(pltpu.with_memory_space_constraint(values, pltpu.HBM))
    rya = swap(sent[2], "sy", 1)
    ryb = swap(sent[3], "sy", -1)
    rxa = swap(sent[0], "sx", 1)
    rxb = swap(sent[1], "sx", -1)

    steps = []
    step = 1
    while step * 3 - 1 < count:
        step *= 3
        steps.append(step)
    steps.reverse()
    reach = (steps[0] - 1) // 2
    chunks = (2 * reach + 1, COARSE_DEV, LANES)

    map_shape = (6, CORNERS * COMPS, face_size)
    block_shape = (face_size, face_size)
    fetched = pl.pallas_call(
        fetch_kernel,
        in_specs=[HBM] * 6,
        out_specs=[VMEM] * 5,
        out_shape=[in_vmem(values.shape, jnp.bfloat16)]
        + [in_vmem(block_shape, jnp.bfloat16)] * 3
        + [in_vmem(map_shape, jnp.bfloat16)],
        scratch_shapes=[pltpu.VMEM(map_shape, jnp.bfloat16), pltpu.SemaphoreType.DMA((11,))],
        compiler_params=params(8),
        cost_estimate=pl.CostEstimate(flops=0, bytes_accessed=9_000_000, transcendentals=0),
    )(
        sent[0],
        *(
            pltpu.with_memory_space_constraint(value, pltpu.HBM)
            for value in (
                values, self_block, opposite_block, cross_block,
                jnp.transpose(corner_map, (1, 0, 2)),
            )
        ),
    )
    local, xa, xb, ya, yb, msg_a, msg_b, kept = pl.pallas_call(
        lambda *refs: local_kernel(count, reach, *refs),
        in_specs=[SMEM, SMEM] + [VMEM] * 10,
        out_specs=[VMEM] * 8,
        out_shape=[
            in_vmem((6,) + face_shape, jnp.bfloat16),
            in_vmem(face_shape, jnp.bfloat16),
            in_vmem(face_shape, jnp.bfloat16),
            in_vmem(long_shape, jnp.bfloat16),
            in_vmem(long_shape, jnp.bfloat16),
            in_vmem(chunks, jnp.float32),
            in_vmem(chunks, jnp.float32),
            in_vmem(chunks, jnp.float32),
        ],
        scratch_shapes=[
            pltpu.VMEM((6,) + face_shape, jnp.bfloat16),
            pltpu.VMEM((coarse_total, LANES), jnp.float32),
        ],
        compiler_params=params(24),
        cost_estimate=pl.CostEstimate(
            flops=2_000_000_000, bytes_accessed=6_000_000, transcendentals=0
        ),
    )(
        partner[0, 0], viscosity[0, 0], corner_owner[0, 0], fetched[0], rxa, rxb, rya, ryb,
        *fetched[1:],
    )

    got_a = swap(msg_a, "sy", steps[0])
    got_b = swap(msg_b, "sy", -steps[0])
    sign = 1 - 2 * signs("sy")
    for step in steps[1:]:
        total = kept + got_a + got_b
        inner = (step - 1) // 2
        at = lambda way: lax.dynamic_slice_in_dim(total, reach - inner + step * way, 2 * inner + 1)
        kept, reach = at(0), inner
        got_a = swap(at(sign), "sy", step)
        got_b = swap(at(-sign), "sy", -step)
    rxa = swap(xa, "sx", 1)
    rxb = swap(xb, "sx", -1)
    own, ya, yb = pl.pallas_call(
        coarse_kernel,
        in_specs=[VMEM] * 5,
        out_specs=[VMEM] * 3,
        out_shape=[
            in_vmem((COARSE_DEV, LANES), jnp.float32),
            in_vmem(long_shape, jnp.bfloat16),
            in_vmem(long_shape, jnp.bfloat16),
        ],
        input_output_aliases={3: 1, 4: 2},
        compiler_params=params(8),
    )(kept, got_a, got_b, ya, yb)
    rya = swap(ya, "sy", 1)
    ryb = swap(yb, "sy", -1)

    applied, coarse = pl.pallas_call(
        apply_kernel,
        in_specs=[SMEM] + [VMEM] * 6,
        out_specs=[ANY, VMEM],
        out_shape=[
            jax.ShapeDtypeStruct(values.shape, jnp.float32),
            jax.ShapeDtypeStruct((COARSE_DEV, rhs * COMPS), jnp.float32),
        ],
        scratch_shapes=[
            pltpu.VMEM(values.shape, jnp.float32),
            pltpu.SemaphoreType.DMA((subs,)),
        ],
        compiler_params=params(12),
    )(partner[0, 0], local, rxa, rxb, rya, ryb, own)
    return applied[None, None], coarse.T


def solution(mesh):
    return jax.shard_map(
        body,
        mesh=mesh,
        in_specs=(
            P("sx", "sy", None, None, None, None),
            P("sx", "sy", None),
            P("sx", "sy", None, None),
            P("sx", "sy", None, None),
            P(),
            P(),
            P(),
            P(),
        ),
        out_specs=(P("sx", "sy", None, None, None, None), P(None, ("sx", "sy"))),
        check_vma=False,
    )
```

```python
import jax
import jax.numpy as jnp
from jax import lax
from jax.experimental import pallas as pl
from jax.experimental.pallas import tpu as pltpu
from jax.sharding import PartitionSpec as P

CORNERS = 8
COMPS = 3
COARSE_DEV = 8
LANES = 128

VMEM = pl.BlockSpec(memory_space=pltpu.VMEM)
SMEM = pl.BlockSpec(memory_space=pltpu.SMEM)
HBM = pl.BlockSpec(memory_space=pltpu.HBM)
ANY = pl.BlockSpec(memory_space=pl.ANY)


def in_vmem(shape, dtype):
    return pltpu.VMEM(shape, dtype)


def in_hbm(value):
    return pltpu.with_memory_space_constraint(value, pltpu.HBM)


def params(mib):
    return pltpu.CompilerParams(vmem_limit_bytes=mib * 1024 * 1024)


LONG = pl.CostEstimate(flops=10**12, bytes_accessed=0, transcendentals=0)


def odd(axis):
    return lax.rem(lax.axis_index(axis), 2)


def swap(value, axis, offset):
    count = lax.axis_size(axis)
    pairs = []
    for source in range(count):
        target = source + (offset if source % 2 == 0 else -offset)
        pairs.append((source, target if 0 <= target < count else source))
    return lax.ppermute(value, axis, pairs)


def cross_swap(value, axis, bits):
    return lax.ppermute(value, axis, [(i, i ^ bits) for i in range(lax.axis_size(axis))])


def inner(axis):
    me = lax.axis_index(axis)
    return ((me > 0) & (me < lax.axis_size(axis) - 1)).astype(jnp.float32)


def x_faces():
    return odd("sx"), 1 - odd("sx")


def y_faces():
    return 2 + odd("sy"), 3 - odd("sy")


def start_all(copies):
    for copy in copies:
        copy.start()
    for copy in copies:
        copy.wait()


def send_kernel(faces, *refs):
    traces, first, second, sems = refs[-4:]
    start_all(
        [
            pltpu.make_async_copy(traces.at[:, face], out, sems.at[index])
            for index, (face, out) in enumerate(zip(faces(), (first, second)))
        ]
    )


def fetch_kernel(
    after, traces, self_block, opposite_block, cross_block, corner_map,
    traces_out, self_out, opposite_out, cross_out, map_out, map_in, sems,
):
    del after
    copies = [pltpu.make_async_copy(corner_map, map_in, sems.at[0])]
    for source, target in (
        (self_block, self_out), (opposite_block, opposite_out), (cross_block, cross_out)
    ):
        for part in range(3):
            size = source.shape[0] // 3
            rows = pl.ds(part * size, size)
            copies.append(
                pltpu.make_async_copy(source.at[rows], target.at[rows], sems.at[len(copies)])
            )
    copies.append(pltpu.make_async_copy(traces, traces_out, sems.at[len(copies)]))
    for copy in copies:
        copy.start()
    copies[0].wait()
    size = CORNERS * COMPS
    row = lax.broadcasted_iota(jnp.int32, (size, size), 0)
    col = lax.broadcasted_iota(jnp.int32, (size, size), 1)
    order = (col == (row % CORNERS) * COMPS + row // CORNERS).astype(jnp.float32)
    order = order.astype(jnp.bfloat16)
    for face in range(6):
        moved = jnp.dot(order, map_in[face], preferred_element_type=jnp.float32)
        map_out[face] = moved.astype(jnp.bfloat16)
    for copy in copies[1:]:
        copy.wait()


def product(left, right):
    return jnp.dot(left, right, preferred_element_type=jnp.float32)


def trade_jumps(jumps, traces, partner, axis, faces, received):
    for trade, (face, got) in enumerate(zip(faces, received)):
        for sub in range(traces.shape[0]):
            other = got[partner[sub, face]].astype(jnp.float32)
            if trade == 1:
                other = other * inner(axis)
            own = traces[sub, face].astype(jnp.float32)
            jumps[trade, sub] = (own - other).astype(jnp.bfloat16)


def flat_face(jumps, index):
    _, subs, rhs, size = jumps.shape
    return jumps[index].reshape(subs * rhs, size)


def pair_sum(jumps, first):
    up = flat_face(jumps, first).astype(jnp.float32)
    return (up + flat_face(jumps, first + 1).astype(jnp.float32)).astype(jnp.bfloat16)


def side_kernel(
    partner, traces, rya, ryb, self_block, opposite_block, cross_block, base, base_x, jumps
):
    subs, _, rhs, size = traces.shape
    rows = subs * rhs
    for sub in range(subs):
        up = traces[sub, 4].astype(jnp.float32)
        down = traces[sub, 5].astype(jnp.float32)
        if sub + 1 < subs:
            up = up - traces[sub + 1, 5].astype(jnp.float32)
        if sub > 0:
            down = down - traces[sub - 1, 4].astype(jnp.float32)
        jumps[2, sub] = up.astype(jnp.bfloat16)
        jumps[3, sub] = down.astype(jnp.bfloat16)
    trade_jumps(jumps, traces, partner, "sy", y_faces(), (rya, ryb))
    pairs = jnp.concatenate([pair_sum(jumps, 0), pair_sum(jumps, 2)], axis=0)
    with_cross = product(pairs, cross_block[...])
    base_x[...] = with_cross[:rows] + with_cross[rows:]
    flat = jumps[...].reshape(4 * rows, size)
    with_self = product(flat, self_block[...])
    with_opp = product(flat, opposite_block[...])
    for index in range(4):
        opp, beside = index ^ 1, 1 - index // 2
        base[index] = (
            with_self[index * rows : (index + 1) * rows]
            + with_opp[opp * rows : (opp + 1) * rows]
            + with_cross[beside * rows : (beside + 1) * rows]
        )


def x_kernel(
    partner, viscosity, traces, rxa, rxb, self_block, opposite_block, base_x, xa, xb, pair_x, jumps
):
    subs, _, rhs, size = traces.shape
    rows = subs * rhs
    trade_jumps(jumps, traces, partner, "sx", x_faces(), (rxa, rxb))
    flat = jumps[...].reshape(2 * rows, size)
    with_self = product(flat, self_block[...])
    with_opp = product(flat, opposite_block[...])
    pair_x[...] = pair_sum(jumps, 0)
    for index, out in enumerate((xa, xb)):
        for sub in range(subs):
            here = slice(sub * rhs, (sub + 1) * rhs)
            own = slice(index * rows + sub * rhs, index * rows + (sub + 1) * rhs)
            opp = slice((1 - index) * rows + sub * rhs, (1 - index) * rows + (sub + 1) * rhs)
            total = with_self[own] + with_opp[opp] + base_x[here]
            out[sub] = (viscosity[sub] * total).astype(jnp.bfloat16)


def high_low(value):
    high = value.astype(jnp.bfloat16).astype(jnp.float32)
    return high, value - high


def coarse_rows(partials, owners, rows):
    subs = owners.shape[0]
    width = partials.shape[1]
    rhs = width // subs
    entries = jnp.zeros((2 * CORNERS, subs * LANES), jnp.float32)
    source = lax.broadcasted_iota(jnp.int32, (width, subs * LANES), 0)
    target = lax.broadcasted_iota(jnp.int32, (width, subs * LANES), 1)
    spread = (source // rhs) * LANES + (source % rhs) * COMPS
    for comp in range(COMPS):
        part = partials[comp * CORNERS : (comp + 1) * CORNERS]
        stacked = jnp.concatenate(high_low(part), axis=0).astype(jnp.bfloat16)
        place = (target == spread + comp).astype(jnp.float32).astype(jnp.bfloat16)
        entries += product(stacked, place)
    entries = entries[:CORNERS] + entries[CORNERS:]
    total = jnp.zeros((rows, LANES), jnp.float32)
    numbers = lax.broadcasted_iota(jnp.int32, (rows, CORNERS), 0)
    for sub in range(subs):
        onehot = (numbers == owners[sub : sub + 1, :]).astype(jnp.float32).astype(jnp.bfloat16)
        for term in high_low(entries[:, sub * LANES : (sub + 1) * LANES]):
            total += product(onehot, term.astype(jnp.bfloat16))
    return total


def rest_kernel(
    count,
    viscosity, owners, base, pair_x, cross_block, xa, xb, corner_map,
    ya, yb, local_z, kept,
    dense,
):
    subs, rhs, size = xa.shape
    rows = subs * rhs
    from_x = product(pair_x[...], cross_block[...])
    places = [ya, yb, local_z.at[0], local_z.at[1]]
    for index, out in enumerate(places):
        for sub in range(subs):
            here = slice(sub * rhs, (sub + 1) * rhs)
            total = base[index, here] + from_x[here]
            out[sub] = (viscosity[sub] * total).astype(jnp.bfloat16)

    partials = jnp.zeros((COMPS * CORNERS, rows), jnp.float32)
    faces = (*x_faces(), *y_faces(), 4, 5)
    for face, local in zip(faces, (xa, xb, *places)):
        partials += lax.dot_general(
            corner_map[face],
            local[0:subs].reshape(rows, size),
            (((1,), (1,)), ((), ())),
            preferred_element_type=jnp.float32,
        )
    dense[...] = coarse_rows(partials, owners[...], dense.shape[0])
    me = lax.axis_index("sy")

    def block(bits):
        start = pl.multiple_of((me ^ bits) * COARSE_DEV, COARSE_DEV)
        return dense[pl.ds(start, COARSE_DEV), :]

    per_row = size // LANES
    for index in range(count // 2):
        kept[index] = block(2 * index)
        lanes = slice(index % per_row * LANES, (index % per_row + 1) * LANES)
        both = jnp.concatenate(high_low(block(2 * index + 1)), axis=0)
        ya[subs + index // per_row, :, lanes] = both.astype(jnp.bfloat16)
    for index in range(count // 2, (ya.shape[0] - subs) * per_row):
        lanes = slice(index % per_row * LANES, (index % per_row + 1) * LANES)
        ya[subs + index // per_row, :, lanes] = jnp.zeros((rhs, LANES), jnp.bfloat16)


def coarse_kernel(subs, kept, got, *outs):
    per_row = got.shape[2] // LANES
    for index in range(kept.shape[0]):
        lanes = slice(index % per_row * LANES, (index % per_row + 1) * LANES)
        both = got[subs + index // per_row, :, lanes].astype(jnp.float32)
        total = kept[index] + both[:COARSE_DEV] + both[COARSE_DEV:]
        outs[index % 4][index // 4] = total


def apply_z_kernel(local_z, applied, held, sems):
    subs = local_z.shape[1]
    copies = []
    for sub in range(subs):
        up = local_z[0, sub].astype(jnp.float32)
        down = local_z[1, sub].astype(jnp.float32)
        if sub + 1 < subs:
            up = up - local_z[1, sub + 1].astype(jnp.float32)
        if sub > 0:
            down = down - local_z[0, sub - 1].astype(jnp.float32)
        held[sub, 0] = up
        held[sub, 1] = down
        copies.append(
            pltpu.make_async_copy(held.at[sub], applied.at[sub, pl.ds(4, 2)], sems.at[sub])
        )
        copies[-1].start()
    for copy in copies:
        copy.wait()


def apply_face(partner, face, axis, local, got, held, applied, sems):
    copies = []
    for trade in range(2):
        for sub in range(held.shape[1]):
            other = got[trade][partner[sub, face[trade]]].astype(jnp.float32)
            if trade == 1:
                other = other * inner(axis)
            held[trade, sub] = local[trade][sub].astype(jnp.float32) - other
            copies.append(
                pltpu.make_async_copy(
                    held.at[trade, sub], applied.at[sub, face[trade]], sems.at[trade, sub]
                )
            )
            copies[-1].start()
    return copies


def apply_y_kernel(partner, applied_in, ya, yb, rya, ryb, applied, held, sems):
    del applied_in
    for copy in apply_face(partner, y_faces(), "sy", (ya, yb), (rya, ryb), held, applied, sems):
        copy.wait()


def apply_x_kernel(partner, applied_in, xa, xb, rxa, rxb, *refs):
    *terms, applied, coarse, held, sems = refs
    del applied_in
    copies = apply_face(partner, x_faces(), "sx", (xa, xb), (rxa, rxb), held, applied, sems)
    total = terms[0][0]
    for term in terms[1:]:
        total = total + term[0]
    coarse[...] = total[:, : coarse.shape[1]]
    for copy in copies:
        copy.wait()


def body(
    traces, viscosity, partner, corner_owner, self_block, opposite_block, cross_block, corner_map
):
    values = in_hbm(traces[0, 0])
    slots, visc, owners = partner[0, 0], viscosity[0, 0], corner_owner[0, 0]
    subs, _, rhs, size = values.shape
    count = lax.axis_size("sy")
    rows = subs * rhs
    face_shape = (subs, rhs, size)
    block_shape = (size, size)
    map_shape = (6, CORNERS * COMPS, size)
    bf16, f32 = jnp.bfloat16, jnp.float32

    def send(faces, after):
        return pl.pallas_call(
            lambda *refs: send_kernel(faces, *refs),
            in_specs=[ANY] * len(after) + [HBM],
            out_specs=[VMEM] * 2,
            out_shape=[in_vmem(face_shape, bf16)] * 2,
            scratch_shapes=[pltpu.SemaphoreType.DMA((2,))],
            compiler_params=params(4),
        )(*after, values)

    xa, xb = send(x_faces, ())
    rxa = swap(xa, "sx", 1)
    rxb = swap(xb, "sx", -1)
    ya, yb = send(y_faces, (xa,))
    rya = swap(ya, "sy", 1)
    ryb = swap(yb, "sy", -1)
    held_traces, self_v, opposite_v, cross_v, map_v = pl.pallas_call(
        fetch_kernel,
        in_specs=[ANY] + [HBM] * 5,
        out_specs=[VMEM] * 5,
        out_shape=[in_vmem(values.shape, bf16)]
        + [in_vmem(block_shape, bf16)] * 3
        + [in_vmem(map_shape, bf16)],
        scratch_shapes=[pltpu.VMEM(map_shape, bf16), pltpu.SemaphoreType.DMA((11,))],
        compiler_params=params(8),
        cost_estimate=LONG,
    )(
        ya,
        values,
        *map(in_hbm, (self_block, opposite_block, cross_block)),
        in_hbm(jnp.transpose(corner_map, (1, 0, 2))),
    )
    base, base_x = pl.pallas_call(
        side_kernel,
        in_specs=[SMEM] + [VMEM] * 6,
        out_specs=[VMEM] * 2,
        out_shape=[in_vmem((4, rows, size), f32), in_vmem((rows, size), f32)],
        scratch_shapes=[pltpu.VMEM((4,) + face_shape, bf16)],
        compiler_params=params(16),
    )(slots, held_traces, rya, ryb, self_v, opposite_v, cross_v)
    xa, xb, pair_x = pl.pallas_call(
        x_kernel,
        in_specs=[SMEM] * 2 + [VMEM] * 6,
        out_specs=[VMEM] * 3,
        out_shape=[in_vmem(face_shape, bf16)] * 2 + [in_vmem((rows, size), bf16)],
        scratch_shapes=[pltpu.VMEM((2,) + face_shape, bf16)],
        compiler_params=params(12),
    )(slots, visc, held_traces, rxa, rxb, self_v, opposite_v, base_x)
    rxa = swap(xa, "sx", 1)
    rxb = swap(xb, "sx", -1)

    half = count // 2
    per_row = size // LANES
    long_shape = (subs + -(-half // per_row), rhs, size)
    ya, yb, local_z, kept = pl.pallas_call(
        lambda *refs: rest_kernel(count, *refs),
        in_specs=[SMEM] + [VMEM] * 7,
        out_specs=[VMEM] * 4,
        out_shape=[
            in_vmem(long_shape, bf16),
            in_vmem(face_shape, bf16),
            in_vmem((2,) + face_shape, bf16),
            in_vmem((half, COARSE_DEV, LANES), f32),
        ],
        scratch_shapes=[pltpu.VMEM((COARSE_DEV * count, LANES), f32)],
        compiler_params=params(12),
    )(visc, owners, base, pair_x, cross_v, xa, xb, map_v)
    rya = swap(ya, "sy", 1)
    ryb = swap(yb, "sy", -1)
    applied = pl.pallas_call(
        apply_z_kernel,
        in_specs=[VMEM],
        out_specs=HBM,
        out_shape=jax.ShapeDtypeStruct(values.shape, f32),
        scratch_shapes=[
            pltpu.VMEM((subs, 2, rhs, size), f32),
            pltpu.SemaphoreType.DMA((subs,)),
        ],
        compiler_params=params(8),
        cost_estimate=LONG,
    )(local_z)
    parts = pl.pallas_call(
        lambda after, *refs: coarse_kernel(subs, *refs),
        in_specs=[HBM] + [VMEM] * 2,
        out_specs=[VMEM] * 4,
        out_shape=[in_vmem((half // 4, COARSE_DEV, LANES), f32)] * 4,
        compiler_params=params(4),
    )(in_hbm(applied), kept, rya)
    terms = [parts[0]] + [cross_swap(parts[k], "sy", 2 * k) for k in range(1, 4)]
    base_bits = 8
    while base_bits < count:
        total = sum(terms[1:], terms[0])
        width = min(4, count // base_bits)
        terms = [total[0::width]] + [
            cross_swap(total[k::width], "sy", base_bits * k) for k in range(1, width)
        ]
        base_bits *= width
    out_shape = jax.ShapeDtypeStruct(values.shape, f32)
    scratch = [pltpu.VMEM((2,) + face_shape, f32), pltpu.SemaphoreType.DMA((2, subs))]
    applied = pl.pallas_call(
        apply_y_kernel,
        in_specs=[SMEM, HBM] + [VMEM] * 4,
        out_specs=HBM,
        out_shape=out_shape,
        input_output_aliases={1: 0},
        scratch_shapes=scratch,
        compiler_params=params(8),
        cost_estimate=LONG,
    )(slots, applied, ya, yb, rya, ryb)
    applied, coarse = pl.pallas_call(
        apply_x_kernel,
        in_specs=[SMEM, HBM] + [VMEM] * (4 + len(terms)),
        out_specs=[HBM, VMEM],
        out_shape=[out_shape, jax.ShapeDtypeStruct((COARSE_DEV, rhs * COMPS), f32)],
        input_output_aliases={1: 0},
        scratch_shapes=scratch,
        compiler_params=params(8),
    )(slots, applied, xa, xb, rxa, rxb, *terms)
    return applied[None, None], coarse.T


def solution(mesh):
    return jax.shard_map(
        body,
        mesh=mesh,
        in_specs=(
            P("sx", "sy", None, None, None, None),
            P("sx", "sy", None),
            P("sx", "sy", None, None),
            P("sx", "sy", None, None),
            P(),
            P(),
            P(),
            P(),
        ),
        out_specs=(P("sx", "sy", None, None, None, None), P(None, ("sx", "sy"))),
        check_vma=False,
    )
```

```python
import jax
import jax.numpy as jnp
from jax import lax
from jax.experimental import pallas as pl
from jax.experimental.pallas import tpu as pltpu
from jax.sharding import PartitionSpec as P

CORNERS = 8
COMPS = 3
COARSE_DEV = 8
LANES = 128

VMEM = pl.BlockSpec(memory_space=pltpu.VMEM)
SMEM = pl.BlockSpec(memory_space=pltpu.SMEM)
HBM = pl.BlockSpec(memory_space=pltpu.HBM)
ANY = pl.BlockSpec(memory_space=pl.ANY)


def in_vmem(shape, dtype):
    return pltpu.VMEM(shape, dtype)


def in_hbm(value):
    return pltpu.with_memory_space_constraint(value, pltpu.HBM)


def params(mib):
    return pltpu.CompilerParams(vmem_limit_bytes=mib * 1024 * 1024)


LONG = pl.CostEstimate(flops=20 * 10**9, bytes_accessed=0, transcendentals=0)


def odd(axis):
    return lax.rem(lax.axis_index(axis), 2)


def swap(value, axis, offset):
    count = lax.axis_size(axis)
    pairs = [(i, (i + (offset if i % 2 == 0 else -offset)) % count) for i in range(count)]
    return lax.ppermute(value, axis, pairs)


def cross_swap(value, axis, bits):
    return lax.ppermute(value, axis, [(i, i ^ bits) for i in range(lax.axis_size(axis))])


def inner(axis):
    me = lax.axis_index(axis)
    return ((me > 0) & (me < lax.axis_size(axis) - 1)).astype(jnp.float32)


def x_faces():
    return odd("sx"), 1 - odd("sx")


def y_faces():
    return 2 + odd("sy"), 3 - odd("sy")


def send_kernel(traces, xa, ya, yb, sems):
    faces = (x_faces()[0], *y_faces())
    copies = [
        pltpu.make_async_copy(traces.at[:, face], out, sems.at[index])
        for index, (face, out) in enumerate(zip(faces, (xa, ya, yb)))
    ]
    for copy in copies:
        copy.start()
    for copy in copies:
        copy.wait()


def fetch_kernel(
    after, traces, self_block, opposite_block, cross_block, corner_map,
    xb, traces_out, self_out, opposite_out, cross_out, map_out, map_in, sems,
):
    del after
    copies = [pltpu.make_async_copy(corner_map, map_in, sems.at[0])]
    for source, target in (
        (self_block, self_out), (opposite_block, opposite_out), (cross_block, cross_out)
    ):
        for part in range(3):
            size = source.shape[0] // 3
            rows = pl.ds(part * size, size)
            copies.append(
                pltpu.make_async_copy(source.at[rows], target.at[rows], sems.at[len(copies)])
            )
    copies.append(pltpu.make_async_copy(traces, traces_out, sems.at[len(copies)]))
    copies.append(pltpu.make_async_copy(traces.at[:, x_faces()[1]], xb, sems.at[len(copies)]))
    for copy in copies:
        copy.start()
    copies[0].wait()
    size = CORNERS * COMPS
    row = lax.broadcasted_iota(jnp.int32, (size, size), 0)
    col = lax.broadcasted_iota(jnp.int32, (size, size), 1)
    order = (col == (row % CORNERS) * COMPS + row // CORNERS).astype(jnp.float32)
    order = order.astype(jnp.bfloat16)
    for face in range(6):
        moved = jnp.dot(order, map_in[face], preferred_element_type=jnp.float32)
        map_out[face] = moved.astype(jnp.bfloat16)
    for copy in copies[1:]:
        copy.wait()


def product(left, right):
    return jnp.dot(left, right, preferred_element_type=jnp.float32)


def trade_jumps(jumps, traces, partner, axis, faces, received):
    for trade, (face, got) in enumerate(zip(faces, received)):
        for sub in range(traces.shape[0]):
            other = got[partner[sub, face]].astype(jnp.float32)
            if trade == 1:
                other = other * inner(axis)
            own = traces[sub, face].astype(jnp.float32)
            jumps[trade, sub] = (own - other).astype(jnp.bfloat16)


def flat_face(jumps, index):
    _, subs, rhs, size = jumps.shape
    return jumps[index].reshape(subs * rhs, size)


def pair_sum(jumps, first):
    up = flat_face(jumps, first).astype(jnp.float32)
    return (up + flat_face(jumps, first + 1).astype(jnp.float32)).astype(jnp.bfloat16)


def side_kernel(
    partner, traces, rya, ryb, self_block, opposite_block, cross_block, base, base_x, jumps
):
    subs, _, rhs, size = traces.shape
    rows = subs * rhs
    for sub in range(subs):
        up = traces[sub, 4].astype(jnp.float32)
        down = traces[sub, 5].astype(jnp.float32)
        if sub + 1 < subs:
            up = up - traces[sub + 1, 5].astype(jnp.float32)
        if sub > 0:
            down = down - traces[sub - 1, 4].astype(jnp.float32)
        jumps[2, sub] = up.astype(jnp.bfloat16)
        jumps[3, sub] = down.astype(jnp.bfloat16)
    trade_jumps(jumps, traces, partner, "sy", y_faces(), (rya, ryb))
    pairs = jnp.concatenate([pair_sum(jumps, 0), pair_sum(jumps, 2)], axis=0)
    with_cross = product(pairs, cross_block[...])
    base_x[...] = with_cross[:rows] + with_cross[rows:]
    flat = jumps[...].reshape(4 * rows, size)
    with_self = product(flat, self_block[...])
    with_opp = product(flat, opposite_block[...])
    for index in range(4):
        opp, beside = index ^ 1, 1 - index // 2
        base[index] = (
            with_self[index * rows : (index + 1) * rows]
            + with_opp[opp * rows : (opp + 1) * rows]
            + with_cross[beside * rows : (beside + 1) * rows]
        )


def x_kernel(
    partner, viscosity, traces, rxa, rxb, self_block, opposite_block, base_x, xa, xb, pair_x, jumps
):
    subs, _, rhs, size = traces.shape
    rows = subs * rhs
    trade_jumps(jumps, traces, partner, "sx", x_faces(), (rxa, rxb))
    flat = jumps[...].reshape(2 * rows, size)
    with_self = product(flat, self_block[...])
    with_opp = product(flat, opposite_block[...])
    pair_x[...] = pair_sum(jumps, 0)
    for index, out in enumerate((xa, xb)):
        for sub in range(subs):
            here = slice(sub * rhs, (sub + 1) * rhs)
            own = slice(index * rows + sub * rhs, index * rows + (sub + 1) * rhs)
            opp = slice((1 - index) * rows + sub * rhs, (1 - index) * rows + (sub + 1) * rhs)
            total = with_self[own] + with_opp[opp] + base_x[here]
            out[sub] = (viscosity[sub] * total).astype(jnp.bfloat16)


def high_low(value):
    high = value.astype(jnp.bfloat16).astype(jnp.float32)
    return high, value - high


def coarse_rows(partials, owners, rows):
    subs = owners.shape[0]
    width = partials.shape[1]
    rhs = width // subs
    entries = jnp.zeros((2 * CORNERS, subs * LANES), jnp.float32)
    source = lax.broadcasted_iota(jnp.int32, (width, subs * LANES), 0)
    target = lax.broadcasted_iota(jnp.int32, (width, subs * LANES), 1)
    spread = (source // rhs) * LANES + (source % rhs) * COMPS
    for comp in range(COMPS):
        part = partials[comp * CORNERS : (comp + 1) * CORNERS]
        stacked = jnp.concatenate(high_low(part), axis=0).astype(jnp.bfloat16)
        place = (target == spread + comp).astype(jnp.float32).astype(jnp.bfloat16)
        entries += product(stacked, place)
    entries = entries[:CORNERS] + entries[CORNERS:]
    total = jnp.zeros((rows, LANES), jnp.float32)
    numbers = lax.broadcasted_iota(jnp.int32, (rows, CORNERS), 0)
    for sub in range(subs):
        onehot = (numbers == owners[sub : sub + 1, :]).astype(jnp.float32).astype(jnp.bfloat16)
        for term in high_low(entries[:, sub * LANES : (sub + 1) * LANES]):
            total += product(onehot, term.astype(jnp.bfloat16))
    return total


def rest_kernel(
    count,
    viscosity, owners, base, pair_x, cross_block, xa, xb, corner_map,
    xb_out, ya, yb, local_z, kept,
    dense,
):
    subs, rhs, size = xa.shape
    rows = subs * rhs
    xb_out[...] = xb[...]
    from_x = product(pair_x[...], cross_block[...])
    places = [ya, yb, local_z.at[0], local_z.at[1]]
    for index, out in enumerate(places):
        for sub in range(subs):
            here = slice(sub * rhs, (sub + 1) * rhs)
            total = base[index, here] + from_x[here]
            out[sub] = (viscosity[sub] * total).astype(jnp.bfloat16)

    partials = jnp.zeros((COMPS * CORNERS, rows), jnp.float32)
    faces = (*x_faces(), *y_faces(), 4, 5)
    for face, local in zip(faces, (xa, xb, *places)):
        partials += lax.dot_general(
            corner_map[face],
            local[0:subs].reshape(rows, size),
            (((1,), (1,)), ((), ())),
            preferred_element_type=jnp.float32,
        )
    dense[...] = coarse_rows(partials, owners[...], dense.shape[0])
    me = lax.axis_index("sy")

    def block(bits):
        start = pl.multiple_of((me ^ bits) * COARSE_DEV, COARSE_DEV)
        return dense[pl.ds(start, COARSE_DEV), :]

    per_row = size // LANES
    for index in range(count // 2):
        kept[index] = block(2 * index)
        lanes = slice(index % per_row * LANES, (index % per_row + 1) * LANES)
        both = jnp.concatenate(high_low(block(2 * index + 1)), axis=0)
        ya[subs + index // per_row, :, lanes] = both.astype(jnp.bfloat16)
    for index in range(count // 2, (ya.shape[0] - subs) * per_row):
        lanes = slice(index % per_row * LANES, (index % per_row + 1) * LANES)
        ya[subs + index // per_row, :, lanes] = jnp.zeros((rhs, LANES), jnp.bfloat16)


def coarse_kernel(subs, kept, got, *outs):
    per_row = got.shape[2] // LANES
    for index in range(kept.shape[0]):
        lanes = slice(index % per_row * LANES, (index % per_row + 1) * LANES)
        both = got[subs + index // per_row, :, lanes].astype(jnp.float32)
        total = kept[index] + both[:COARSE_DEV] + both[COARSE_DEV:]
        outs[index % 4][index // 4] = total


def apply_z_kernel(local_z, applied, held, sems):
    subs = local_z.shape[1]
    copies = []
    for sub in range(subs):
        up = local_z[0, sub].astype(jnp.float32)
        down = local_z[1, sub].astype(jnp.float32)
        if sub + 1 < subs:
            up = up - local_z[1, sub + 1].astype(jnp.float32)
        if sub > 0:
            down = down - local_z[0, sub - 1].astype(jnp.float32)
        held[sub, 0] = up
        held[sub, 1] = down
        copies.append(
            pltpu.make_async_copy(held.at[sub], applied.at[sub, pl.ds(4, 2)], sems.at[sub])
        )
        copies[-1].start()
    for copy in copies:
        copy.wait()


def apply_face(partner, face, axis, local, got, held, applied, sems):
    copies = []
    for trade in range(2):
        for sub in range(held.shape[1]):
            other = got[trade][partner[sub, face[trade]]].astype(jnp.float32)
            if trade == 1:
                other = other * inner(axis)
            held[trade, sub] = local[trade][sub].astype(jnp.float32) - other
            copies.append(
                pltpu.make_async_copy(
                    held.at[trade, sub], applied.at[sub, face[trade]], sems.at[trade, sub]
                )
            )
            copies[-1].start()
    return copies


def apply_y_kernel(partner, applied_in, ya, yb, rya, ryb, applied, held, sems):
    del applied_in
    for copy in apply_face(partner, y_faces(), "sy", (ya, yb), (rya, ryb), held, applied, sems):
        copy.wait()


def apply_x_kernel(partner, applied_in, xa, xb, rxa, rxb, *refs):
    *terms, applied, coarse, held, sems = refs
    del applied_in
    copies = apply_face(partner, x_faces(), "sx", (xa, xb), (rxa, rxb), held, applied, sems)
    total = terms[0][0]
    for term in terms[1:]:
        total = total + term[0]
    coarse[...] = total[:, : coarse.shape[1]]
    for copy in copies:
        copy.wait()


def body(
    traces, viscosity, partner, corner_owner, self_block, opposite_block, cross_block, corner_map
):
    values = in_hbm(traces[0, 0])
    slots, visc, owners = partner[0, 0], viscosity[0, 0], corner_owner[0, 0]
    subs, _, rhs, size = values.shape
    count = lax.axis_size("sy")
    rows = subs * rhs
    face_shape = (subs, rhs, size)
    block_shape = (size, size)
    map_shape = (6, CORNERS * COMPS, size)
    bf16, f32 = jnp.bfloat16, jnp.float32

    xa, ya, yb = pl.pallas_call(
        send_kernel,
        in_specs=[HBM],
        out_specs=[VMEM] * 3,
        out_shape=[in_vmem(face_shape, bf16)] * 3,
        scratch_shapes=[pltpu.SemaphoreType.DMA((3,))],
        compiler_params=params(8),
    )(values)
    rxa = swap(xa, "sx", 1)
    rya = swap(ya, "sy", 1)
    ryb = swap(yb, "sy", -1)
    xb, held_traces, self_v, opposite_v, cross_v, map_v = pl.pallas_call(
        fetch_kernel,
        in_specs=[ANY] + [HBM] * 5,
        out_specs=[VMEM] * 6,
        out_shape=[in_vmem(face_shape, bf16), in_vmem(values.shape, bf16)]
        + [in_vmem(block_shape, bf16)] * 3
        + [in_vmem(map_shape, bf16)],
        scratch_shapes=[pltpu.VMEM(map_shape, bf16), pltpu.SemaphoreType.DMA((12,))],
        compiler_params=params(8),
        cost_estimate=LONG,
    )(
        ya,
        values,
        *map(in_hbm, (self_block, opposite_block, cross_block)),
        in_hbm(jnp.transpose(corner_map, (1, 0, 2))),
    )
    rxb = swap(xb, "sx", -1)
    base, base_x = pl.pallas_call(
        side_kernel,
        in_specs=[SMEM] + [VMEM] * 6,
        out_specs=[VMEM] * 2,
        out_shape=[in_vmem((4, rows, size), f32), in_vmem((rows, size), f32)],
        scratch_shapes=[pltpu.VMEM((4,) + face_shape, bf16)],
        compiler_params=params(16),
    )(slots, held_traces, rya, ryb, self_v, opposite_v, cross_v)
    xa, xb, pair_x = pl.pallas_call(
        x_kernel,
        in_specs=[SMEM] * 2 + [VMEM] * 6,
        out_specs=[VMEM] * 3,
        out_shape=[in_vmem(face_shape, bf16)] * 2 + [in_vmem((rows, size), bf16)],
        scratch_shapes=[pltpu.VMEM((2,) + face_shape, bf16)],
        compiler_params=params(12),
    )(slots, visc, held_traces, rxa, rxb, self_v, opposite_v, base_x)
    rxa = swap(xa, "sx", 1)

    half = count // 2
    per_row = size // LANES
    long_shape = (subs + -(-half // per_row), rhs, size)
    xb, ya, yb, local_z, kept = pl.pallas_call(
        lambda *refs: rest_kernel(count, *refs),
        in_specs=[SMEM] + [VMEM] * 7,
        out_specs=[VMEM] * 5,
        out_shape=[
            in_vmem(face_shape, bf16),
            in_vmem(long_shape, bf16),
            in_vmem(face_shape, bf16),
            in_vmem((2,) + face_shape, bf16),
            in_vmem((half, COARSE_DEV, LANES), f32),
        ],
        scratch_shapes=[pltpu.VMEM((COARSE_DEV * count, LANES), f32)],
        compiler_params=params(12),
    )(visc, owners, base, pair_x, cross_v, xa, xb, map_v)
    rya = swap(ya, "sy", 1)
    ryb = swap(yb, "sy", -1)
    rxb = swap(xb, "sx", -1)
    applied = pl.pallas_call(
        apply_z_kernel,
        in_specs=[VMEM],
        out_specs=HBM,
        out_shape=jax.ShapeDtypeStruct(values.shape, f32),
        scratch_shapes=[
            pltpu.VMEM((subs, 2, rhs, size), f32),
            pltpu.SemaphoreType.DMA((subs,)),
        ],
        compiler_params=params(8),
        cost_estimate=LONG,
    )(local_z)
    parts = pl.pallas_call(
        lambda after, *refs: coarse_kernel(subs, *refs),
        in_specs=[HBM] + [VMEM] * 2,
        out_specs=[VMEM] * 4,
        out_shape=[in_vmem((half // 4, COARSE_DEV, LANES), f32)] * 4,
        compiler_params=params(4),
    )(in_hbm(applied), kept, rya)
    terms = [parts[0]] + [cross_swap(parts[k], "sy", 2 * k) for k in range(1, 4)]
    base_bits = 8
    while base_bits < count:
        total = sum(terms[1:], terms[0])
        width = min(4, count // base_bits)
        terms = [total[0::width]] + [
            cross_swap(total[k::width], "sy", base_bits * k) for k in range(1, width)
        ]
        base_bits *= width
    out_shape = jax.ShapeDtypeStruct(values.shape, f32)
    scratch = [pltpu.VMEM((2,) + face_shape, f32), pltpu.SemaphoreType.DMA((2, subs))]
    applied = pl.pallas_call(
        apply_y_kernel,
        in_specs=[SMEM, HBM] + [VMEM] * 4,
        out_specs=HBM,
        out_shape=out_shape,
        input_output_aliases={1: 0},
        scratch_shapes=scratch,
        compiler_params=params(8),
        cost_estimate=LONG,
    )(slots, applied, ya, yb, rya, ryb)
    applied, coarse = pl.pallas_call(
        apply_x_kernel,
        in_specs=[SMEM, HBM] + [VMEM] * (4 + len(terms)),
        out_specs=[HBM, VMEM],
        out_shape=[out_shape, jax.ShapeDtypeStruct((COARSE_DEV, rhs * COMPS), f32)],
        input_output_aliases={1: 0},
        scratch_shapes=scratch,
        compiler_params=params(8),
    )(slots, applied, xa, xb, rxa, rxb, *terms)
    return applied[None, None], coarse.T


def solution(mesh):
    return jax.shard_map(
        body,
        mesh=mesh,
        in_specs=(
            P("sx", "sy", None, None, None, None),
            P("sx", "sy", None),
            P("sx", "sy", None, None),
            P("sx", "sy", None, None),
            P(),
            P(),
            P(),
            P(),
        ),
        out_specs=(P("sx", "sy", None, None, None, None), P(None, ("sx", "sy"))),
        check_vma=False,
    )
```

```python
import jax
import jax.numpy as jnp
from jax import lax
from jax.experimental import pallas as pl
from jax.experimental.pallas import tpu as pltpu
from jax.sharding import PartitionSpec as P

CORNERS = 8
COMPS = 3
COARSE_DEV = 8
LANES = 128

VMEM = pl.BlockSpec(memory_space=pltpu.VMEM)
SMEM = pl.BlockSpec(memory_space=pltpu.SMEM)
HBM = pl.BlockSpec(memory_space=pltpu.HBM)
ANY = pl.BlockSpec(memory_space=pl.ANY)


def in_vmem(shape, dtype):
    return pltpu.VMEM(shape, dtype)


def in_hbm(value):
    return pltpu.with_memory_space_constraint(value, pltpu.HBM)


def params(mib):
    return pltpu.CompilerParams(vmem_limit_bytes=mib * 1024 * 1024)


LONG = pl.CostEstimate(flops=20 * 10**9, bytes_accessed=0, transcendentals=0)


def odd(axis):
    return lax.rem(lax.axis_index(axis), 2)


def first_swap(value, axis):
    return lax.ppermute(value, axis, [(i, i ^ 1) for i in range(lax.axis_size(axis))])


def second_swap(value, axis):
    rows, cols = lax.axis_size("sx"), lax.axis_size("sy")
    pairs = []
    for i in range(rows):
        for j in range(cols):
            if axis == "sx":
                k = i - 1 if i % 2 == 0 else i + 1
                target = (k, j) if 0 <= k < rows else (i, j ^ 1)
            else:
                k = j - 1 if j % 2 == 0 else j + 1
                target = (i, k) if 0 <= k < cols else (i ^ 2, j)
            pairs.append((i * cols + j, target[0] * cols + target[1]))
    return lax.ppermute(value, ("sx", "sy"), pairs)


def cross_swap(value, axis, bits):
    return lax.ppermute(value, axis, [(i, i ^ bits) for i in range(lax.axis_size(axis))])


def inner(axis):
    me = lax.axis_index(axis)
    return ((me > 0) & (me < lax.axis_size(axis) - 1)).astype(jnp.float32)


def x_faces():
    return odd("sx"), 1 - odd("sx")


def y_faces():
    return 2 + odd("sy"), 3 - odd("sy")


def send_kernel(traces, xa, xb, ya, yb, sems):
    faces = (*x_faces(), *y_faces())
    copies = [
        pltpu.make_async_copy(traces.at[:, face], out, sems.at[index])
        for index, (face, out) in enumerate(zip(faces, (xa, xb, ya, yb)))
    ]
    for copy in copies:
        copy.start()
    for copy in copies:
        copy.wait()


def fetch_kernel(
    ya, yb, traces, self_block, opposite_block, cross_block, corner_map,
    traces_out, self_out, opposite_out, cross_out, map_out, map_in, sems,
):
    del ya, yb
    copies = [pltpu.make_async_copy(corner_map, map_in, sems.at[0])]
    for source, target in (
        (self_block, self_out), (opposite_block, opposite_out), (cross_block, cross_out)
    ):
        for part in range(3):
            size = source.shape[0] // 3
            rows = pl.ds(part * size, size)
            copies.append(
                pltpu.make_async_copy(source.at[rows], target.at[rows], sems.at[len(copies)])
            )
    copies.append(pltpu.make_async_copy(traces, traces_out, sems.at[len(copies)]))
    for copy in copies:
        copy.start()
    copies[0].wait()
    size = CORNERS * COMPS
    row = lax.broadcasted_iota(jnp.int32, (size, size), 0)
    col = lax.broadcasted_iota(jnp.int32, (size, size), 1)
    order = (col == (row % CORNERS) * COMPS + row // CORNERS).astype(jnp.float32)
    order = order.astype(jnp.bfloat16)
    for face in range(6):
        moved = jnp.dot(order, map_in[face], preferred_element_type=jnp.float32)
        map_out[face] = moved.astype(jnp.bfloat16)
    for copy in copies[1:]:
        copy.wait()


def product(left, right):
    return jnp.dot(left, right, preferred_element_type=jnp.float32)


def trade_jumps(jumps, traces, partner, axis, faces, received):
    for trade, (face, got) in enumerate(zip(faces, received)):
        for sub in range(traces.shape[0]):
            other = got[partner[sub, face]].astype(jnp.float32)
            if trade == 1:
                other = other * inner(axis)
            own = traces[sub, face].astype(jnp.float32)
            jumps[trade, sub] = (own - other).astype(jnp.bfloat16)


def flat_face(jumps, index):
    _, subs, rhs, size = jumps.shape
    return jumps[index].reshape(subs * rhs, size)


def pair_sum(jumps, first):
    up = flat_face(jumps, first).astype(jnp.float32)
    return (up + flat_face(jumps, first + 1).astype(jnp.float32)).astype(jnp.bfloat16)


def side_kernel(
    partner, traces, rya, ryb, self_block, opposite_block, cross_block, base, base_x, jumps
):
    subs, _, rhs, size = traces.shape
    rows = subs * rhs
    for sub in range(subs):
        up = traces[sub, 4].astype(jnp.float32)
        down = traces[sub, 5].astype(jnp.float32)
        if sub + 1 < subs:
            up = up - traces[sub + 1, 5].astype(jnp.float32)
        if sub > 0:
            down = down - traces[sub - 1, 4].astype(jnp.float32)
        jumps[2, sub] = up.astype(jnp.bfloat16)
        jumps[3, sub] = down.astype(jnp.bfloat16)
    trade_jumps(jumps, traces, partner, "sy", y_faces(), (rya, ryb))
    pairs = jnp.concatenate([pair_sum(jumps, 0), pair_sum(jumps, 2)], axis=0)
    with_cross = product(pairs, cross_block[...])
    base_x[...] = with_cross[:rows] + with_cross[rows:]
    flat = jumps[...].reshape(4 * rows, size)
    with_self = product(flat, self_block[...])
    with_opp = product(flat, opposite_block[...])
    for index in range(4):
        opp, beside = index ^ 1, 1 - index // 2
        base[index] = (
            with_self[index * rows : (index + 1) * rows]
            + with_opp[opp * rows : (opp + 1) * rows]
            + with_cross[beside * rows : (beside + 1) * rows]
        )


def x_kernel(
    partner, viscosity, traces, rxa, rxb, self_block, opposite_block, base_x,
    xa, xb, to_xa, to_xb, pair_x, jumps,
):
    subs, _, rhs, size = traces.shape
    rows = subs * rhs
    trade_jumps(jumps, traces, partner, "sx", x_faces(), (rxa, rxb))
    flat = jumps[...].reshape(2 * rows, size)
    with_self = product(flat, self_block[...])
    with_opp = product(flat, opposite_block[...])
    pair_x[...] = pair_sum(jumps, 0)
    for index, (face, out, to) in enumerate(zip(x_faces(), (xa, xb), (to_xa, to_xb))):
        for sub in range(subs):
            here = slice(sub * rhs, (sub + 1) * rhs)
            own = slice(index * rows + sub * rhs, index * rows + (sub + 1) * rhs)
            opp = slice((1 - index) * rows + sub * rhs, (1 - index) * rows + (sub + 1) * rhs)
            total = with_self[own] + with_opp[opp] + base_x[here]
            value = (viscosity[sub] * total).astype(jnp.bfloat16)
            out[sub] = value
            to[partner[sub, face]] = value


def high_low(value):
    high = value.astype(jnp.bfloat16).astype(jnp.float32)
    return high, value - high


def coarse_rows(partials, owners, rows):
    subs = owners.shape[0]
    width = partials.shape[1]
    rhs = width // subs
    entries = jnp.zeros((2 * CORNERS, subs * LANES), jnp.float32)
    source = lax.broadcasted_iota(jnp.int32, (width, subs * LANES), 0)
    target = lax.broadcasted_iota(jnp.int32, (width, subs * LANES), 1)
    spread = (source // rhs) * LANES + (source % rhs) * COMPS
    for comp in range(COMPS):
        part = partials[comp * CORNERS : (comp + 1) * CORNERS]
        stacked = jnp.concatenate(high_low(part), axis=0).astype(jnp.bfloat16)
        place = (target == spread + comp).astype(jnp.float32).astype(jnp.bfloat16)
        entries += product(stacked, place)
    entries = entries[:CORNERS] + entries[CORNERS:]
    total = jnp.zeros((rows, LANES), jnp.float32)
    numbers = lax.broadcasted_iota(jnp.int32, (rows, CORNERS), 0)
    for sub in range(subs):
        onehot = (numbers == owners[sub : sub + 1, :]).astype(jnp.float32).astype(jnp.bfloat16)
        for term in high_low(entries[:, sub * LANES : (sub + 1) * LANES]):
            total += product(onehot, term.astype(jnp.bfloat16))
    return total


def rest_kernel(
    count,
    partner, viscosity, owners, base, pair_x, cross_block, to_xa, to_xb, corner_map,
    ya, yb, to_ya, to_yb, local_z, kept,
    dense,
):
    subs, rhs, size = to_xa.shape
    rows = subs * rhs
    from_x = product(pair_x[...], cross_block[...])
    places = [ya, yb, local_z.at[0], local_z.at[1]]
    for index, out in enumerate(places):
        for sub in range(subs):
            here = slice(sub * rhs, (sub + 1) * rhs)
            total = base[index, here] + from_x[here]
            value = (viscosity[sub] * total).astype(jnp.bfloat16)
            out[sub] = value
            if index < 2:
                (to_ya, to_yb)[index][partner[sub, y_faces()[index]]] = value

    partials = jnp.zeros((COMPS * CORNERS, rows), jnp.float32)
    faces = (*x_faces(), *y_faces(), 4, 5)
    for index, (face, local) in enumerate(zip(faces, (to_xa, to_xb, *places))):
        order = [partner[sub, face] if index < 2 else sub for sub in range(subs)]
        partials += lax.dot_general(
            corner_map[face],
            jnp.concatenate([local[slot] for slot in order], axis=0),
            (((1,), (1,)), ((), ())),
            preferred_element_type=jnp.float32,
        )
    dense[...] = coarse_rows(partials, owners[...], dense.shape[0])
    me = lax.axis_index("sy")

    def block(bits):
        start = pl.multiple_of((me ^ bits) * COARSE_DEV, COARSE_DEV)
        return dense[pl.ds(start, COARSE_DEV), :]

    per_row = size // LANES
    for index in range(count // 2):
        kept[index] = block(2 * index)
        lanes = slice(index % per_row * LANES, (index % per_row + 1) * LANES)
        both = jnp.concatenate(high_low(block(2 * index + 1)), axis=0)
        to_ya[subs + index // per_row, :, lanes] = both.astype(jnp.bfloat16)
    for index in range(count // 2, (to_ya.shape[0] - subs) * per_row):
        lanes = slice(index % per_row * LANES, (index % per_row + 1) * LANES)
        to_ya[subs + index // per_row, :, lanes] = jnp.zeros((rhs, LANES), jnp.bfloat16)


def coarse_kernel(subs, kept, got, *outs):
    per_row = got.shape[2] // LANES
    for index in range(kept.shape[0]):
        lanes = slice(index % per_row * LANES, (index % per_row + 1) * LANES)
        both = got[subs + index // per_row, :, lanes].astype(jnp.float32)
        total = kept[index] + both[:COARSE_DEV] + both[COARSE_DEV:]
        outs[index % 4][index // 4] = total


def apply_z_kernel(to_yb, local_z, applied, held, sems):
    del to_yb
    subs = local_z.shape[1]
    copies = []
    for sub in range(subs):
        up = local_z[0, sub].astype(jnp.float32)
        down = local_z[1, sub].astype(jnp.float32)
        if sub + 1 < subs:
            up = up - local_z[1, sub + 1].astype(jnp.float32)
        if sub > 0:
            down = down - local_z[0, sub - 1].astype(jnp.float32)
        held[sub, 0] = up
        held[sub, 1] = down
        copies.append(
            pltpu.make_async_copy(held.at[sub], applied.at[sub, pl.ds(4, 2)], sems.at[sub])
        )
        copies[-1].start()
    for copy in copies:
        copy.wait()


def apply_faces(faces, axis, local, got, held, applied, sems):
    copies = []
    for trade in range(2):
        for sub in range(held.shape[1]):
            other = got[trade][sub].astype(jnp.float32)
            if trade == 1:
                other = other * inner(axis)
            held[trade, sub] = local[trade][sub].astype(jnp.float32) - other
            copies.append(
                pltpu.make_async_copy(
                    held.at[trade, sub], applied.at[sub, faces[trade]], sems.at[trade, sub]
                )
            )
            copies[-1].start()
    return copies


def apply_y_kernel(applied_in, ya, yb, rya, ryb, applied, held, sems):
    del applied_in
    for copy in apply_faces(y_faces(), "sy", (ya, yb), (rya, ryb), held, applied, sems):
        copy.wait()


def apply_x_kernel(applied_in, xa, xb, rxa, rxb, *refs):
    *terms, applied, coarse, held, sems, sums, sum_sem = refs
    del applied_in
    total = terms[0][0]
    for term in terms[1:]:
        total = total + term[0]
    sums[...] = total[:, : sums.shape[1]]
    copies = [pltpu.make_async_copy(sums, coarse, sum_sem)]
    copies[0].start()
    copies += apply_faces(x_faces(), "sx", (xa, xb), (rxa, rxb), held, applied, sems)
    for copy in copies:
        copy.wait()


def body(
    traces, viscosity, partner, corner_owner, self_block, opposite_block, cross_block, corner_map
):
    values = in_hbm(traces[0, 0])
    slots, visc, owners = partner[0, 0], viscosity[0, 0], corner_owner[0, 0]
    subs, _, rhs, size = values.shape
    count = lax.axis_size("sy")
    rows = subs * rhs
    face_shape = (subs, rhs, size)
    block_shape = (size, size)
    map_shape = (6, CORNERS * COMPS, size)
    bf16, f32 = jnp.bfloat16, jnp.float32

    xa, xb, ya, yb = pl.pallas_call(
        send_kernel,
        in_specs=[HBM],
        out_specs=[VMEM] * 4,
        out_shape=[in_vmem(face_shape, bf16)] * 4,
        scratch_shapes=[pltpu.SemaphoreType.DMA((4,))],
        compiler_params=params(8),
    )(values)
    rxa = first_swap(xa, "sx")
    rxb = second_swap(xb, "sx")
    rya = first_swap(ya, "sy")
    ryb = second_swap(yb, "sy")
    held_traces, self_v, opposite_v, cross_v, map_v = pl.pallas_call(
        fetch_kernel,
        in_specs=[VMEM] * 2 + [HBM] * 5,
        out_specs=[VMEM] * 5,
        out_shape=[in_vmem(values.shape, bf16)]
        + [in_vmem(block_shape, bf16)] * 3
        + [in_vmem(map_shape, bf16)],
        scratch_shapes=[pltpu.VMEM(map_shape, bf16), pltpu.SemaphoreType.DMA((11,))],
        compiler_params=params(8),
        cost_estimate=LONG,
    )(
        ya,
        yb,
        values,
        *map(in_hbm, (self_block, opposite_block, cross_block)),
        in_hbm(jnp.transpose(corner_map, (1, 0, 2))),
    )
    base, base_x = pl.pallas_call(
        side_kernel,
        in_specs=[SMEM] + [VMEM] * 6,
        out_specs=[VMEM] * 2,
        out_shape=[in_vmem((4, rows, size), f32), in_vmem((rows, size), f32)],
        scratch_shapes=[pltpu.VMEM((4,) + face_shape, bf16)],
        compiler_params=params(16),
    )(slots, held_traces, rya, ryb, self_v, opposite_v, cross_v)
    xa, xb, to_xa, to_xb, pair_x = pl.pallas_call(
        x_kernel,
        in_specs=[SMEM] * 2 + [VMEM] * 6,
        out_specs=[VMEM] * 5,
        out_shape=[in_vmem(face_shape, bf16)] * 4 + [in_vmem((rows, size), bf16)],
        scratch_shapes=[pltpu.VMEM((2,) + face_shape, bf16)],
        compiler_params=params(12),
    )(slots, visc, held_traces, rxa, rxb, self_v, opposite_v, base_x)
    rxb = second_swap(to_xb, "sx")
    rxa = first_swap(to_xa, "sx")

    half = count // 2
    per_row = size // LANES
    long_shape = (subs + -(-half // per_row), rhs, size)
    ya, yb, to_ya, to_yb, local_z, kept = pl.pallas_call(
        lambda *refs: rest_kernel(count, *refs),
        in_specs=[SMEM] * 2 + [VMEM] * 7,
        out_specs=[VMEM] * 6,
        out_shape=[
            in_vmem(face_shape, bf16),
            in_vmem(face_shape, bf16),
            in_vmem(long_shape, bf16),
            in_vmem(face_shape, bf16),
            in_vmem((2,) + face_shape, bf16),
            in_vmem((half, COARSE_DEV, LANES), f32),
        ],
        scratch_shapes=[pltpu.VMEM((COARSE_DEV * count, LANES), f32)],
        compiler_params=params(12),
    )(slots, visc, owners, base, pair_x, cross_v, to_xa, to_xb, map_v)
    rya = first_swap(to_ya, "sy")
    ryb = second_swap(to_yb, "sy")
    applied = pl.pallas_call(
        apply_z_kernel,
        in_specs=[VMEM] * 2,
        out_specs=HBM,
        out_shape=jax.ShapeDtypeStruct(values.shape, f32),
        scratch_shapes=[
            pltpu.VMEM((subs, 2, rhs, size), f32),
            pltpu.SemaphoreType.DMA((subs,)),
        ],
        compiler_params=params(8),
        cost_estimate=LONG,
    )(to_yb, local_z)
    parts = pl.pallas_call(
        lambda after, *refs: coarse_kernel(subs, *refs),
        in_specs=[HBM] + [VMEM] * 2,
        out_specs=[VMEM] * 4,
        out_shape=[in_vmem((half // 4, COARSE_DEV, LANES), f32)] * 4,
        compiler_params=params(4),
    )(in_hbm(applied), kept, rya)
    terms = [parts[0]] + [cross_swap(parts[k], "sy", 2 * k) for k in range(1, 4)]
    base_bits = 8
    while base_bits < count:
        total = sum(terms[1:], terms[0])
        width = min(4, count // base_bits)
        terms = [total[0::width]] + [
            cross_swap(total[k::width], "sy", base_bits * k) for k in range(1, width)
        ]
        base_bits *= width
    out_shape = jax.ShapeDtypeStruct(values.shape, f32)
    scratch = [pltpu.VMEM((2,) + face_shape, f32), pltpu.SemaphoreType.DMA((2, subs))]
    applied = pl.pallas_call(
        apply_y_kernel,
        in_specs=[HBM] + [VMEM] * 4,
        out_specs=HBM,
        out_shape=out_shape,
        input_output_aliases={0: 0},
        scratch_shapes=scratch,
        compiler_params=params(8),
        cost_estimate=LONG,
    )(applied, ya, yb, rya, ryb)
    applied, coarse = pl.pallas_call(
        apply_x_kernel,
        in_specs=[HBM] + [VMEM] * (4 + len(terms)),
        out_specs=[HBM, HBM],
        out_shape=[out_shape, jax.ShapeDtypeStruct((COARSE_DEV, rhs * COMPS), f32)],
        input_output_aliases={0: 0},
        scratch_shapes=scratch
        + [pltpu.VMEM((COARSE_DEV, rhs * COMPS), f32), pltpu.SemaphoreType.DMA],
        compiler_params=params(8),
    )(applied, xa, xb, rxa, rxb, *terms)
    return applied[None, None], coarse.T


def solution(mesh):
    return jax.shard_map(
        body,
        mesh=mesh,
        in_specs=(
            P("sx", "sy", None, None, None, None),
            P("sx", "sy", None),
            P("sx", "sy", None, None),
            P("sx", "sy", None, None),
            P(),
            P(),
            P(),
            P(),
        ),
        out_specs=(P("sx", "sy", None, None, None, None), P(None, ("sx", "sy"))),
        check_vma=False,
    )
```

```python
import jax
import jax.numpy as jnp
from jax import lax
from jax.experimental import pallas as pl
from jax.experimental.pallas import tpu as pltpu
from jax.sharding import PartitionSpec as P

CORNERS = 8
COMPS = 3
COARSE_DEV = 8
LANES = 128

VMEM = pl.BlockSpec(memory_space=pltpu.VMEM)
SMEM = pl.BlockSpec(memory_space=pltpu.SMEM)
HBM = pl.BlockSpec(memory_space=pltpu.HBM)
ANY = pl.BlockSpec(memory_space=pl.ANY)


def in_vmem(shape, dtype):
    return pltpu.VMEM(shape, dtype)


def in_hbm(value):
    return pltpu.with_memory_space_constraint(value, pltpu.HBM)


def params(mib):
    return pltpu.CompilerParams(vmem_limit_bytes=mib * 1024 * 1024)


LONG = pl.CostEstimate(flops=20 * 10**9, bytes_accessed=0, transcendentals=0)


def odd(axis):
    return lax.rem(lax.axis_index(axis), 2)


def first_swap(value, axis):
    return lax.ppermute(value, axis, [(i, i ^ 1) for i in range(lax.axis_size(axis))])


def second_swap(value, axis):
    rows, cols = lax.axis_size("sx"), lax.axis_size("sy")
    pairs = []
    for i in range(rows):
        for j in range(cols):
            if axis == "sx":
                k = i - 1 if i % 2 == 0 else i + 1
                target = (k, j) if 0 <= k < rows else (i, j ^ 1)
            else:
                k = j - 1 if j % 2 == 0 else j + 1
                target = (i, k) if 0 <= k < cols else (i ^ 2, j)
            pairs.append((i * cols + j, target[0] * cols + target[1]))
    return lax.ppermute(value, ("sx", "sy"), pairs)


def inner(axis):
    me = lax.axis_index(axis)
    return ((me > 0) & (me < lax.axis_size(axis) - 1)).astype(jnp.float32)


def x_faces():
    return odd("sx"), 1 - odd("sx")


def y_faces():
    return 2 + odd("sy"), 3 - odd("sy")


def send_kernel(traces, xa, xb, ya, yb, sems):
    faces = (*x_faces(), *y_faces())
    copies = [
        pltpu.make_async_copy(traces.at[:, face], out, sems.at[index])
        for index, (face, out) in enumerate(zip(faces, (xa, xb, ya, yb)))
    ]
    for copy in copies:
        copy.start()
    for copy in copies:
        copy.wait()


def product(left, right):
    return jnp.dot(left, right, preferred_element_type=jnp.float32)


def trade_jumps(jumps, traces, partner, axis, faces, received):
    for trade, (face, got) in enumerate(zip(faces, received)):
        for sub in range(traces.shape[0]):
            other = got[partner[sub, face]].astype(jnp.float32)
            if trade == 1:
                other = other * inner(axis)
            own = traces[sub, face].astype(jnp.float32)
            jumps[trade, sub] = (own - other).astype(jnp.bfloat16)


def flat_face(jumps, index):
    _, subs, rhs, size = jumps.shape
    return jumps[index].reshape(subs * rhs, size)


def pair_sum(jumps, first):
    up = flat_face(jumps, first).astype(jnp.float32)
    return (up + flat_face(jumps, first + 1).astype(jnp.float32)).astype(jnp.bfloat16)


def fetch_kernel(
    ya, yb, traces, self_block, opposite_block, cross_block, corner_map,
    traces_out, self_out, opposite_out, cross_out, map_out, base_z, cross_z,
    map_in, jumps, sems,
):
    del ya, yb
    subs, _, rhs, size = traces.shape
    rows = subs * rhs
    copies = [
        pltpu.make_async_copy(traces, traces_out, sems.at[0]),
        pltpu.make_async_copy(corner_map, map_in, sems.at[1]),
    ]
    for source, target in (
        (self_block, self_out), (opposite_block, opposite_out), (cross_block, cross_out)
    ):
        for part in range(3):
            third = pl.ds(part * (size // 3), size // 3)
            copies.append(
                pltpu.make_async_copy(source.at[third], target.at[third], sems.at[len(copies)])
            )
    for copy in copies:
        copy.start()

    copies[0].wait()
    for sub in range(subs):
        up = traces_out[sub, 4].astype(jnp.float32)
        down = traces_out[sub, 5].astype(jnp.float32)
        if sub + 1 < subs:
            up = up - traces_out[sub + 1, 5].astype(jnp.float32)
        if sub > 0:
            down = down - traces_out[sub - 1, 4].astype(jnp.float32)
        jumps[0, sub] = up.astype(jnp.bfloat16)
        jumps[1, sub] = down.astype(jnp.bfloat16)
    copies[1].wait()
    width = CORNERS * COMPS
    row = lax.broadcasted_iota(jnp.int32, (width, width), 0)
    col = lax.broadcasted_iota(jnp.int32, (width, width), 1)
    order = (col == (row % CORNERS) * COMPS + row // CORNERS).astype(jnp.float32)
    order = order.astype(jnp.bfloat16)
    for face in range(6):
        map_out[face] = product(order, map_in[face]).astype(jnp.bfloat16)
    flat = jumps[...].reshape(2 * rows, size)
    for copy in copies[2:5]:
        copy.wait()
    with_self = product(flat, self_out[...])
    for copy in copies[5:8]:
        copy.wait()
    with_opp = product(flat, opposite_out[...])
    base_z[0] = with_self[:rows] + with_opp[rows:]
    base_z[1] = with_self[rows:] + with_opp[:rows]
    for copy in copies[8:]:
        copy.wait()
    cross_z[...] = product(pair_sum(jumps, 0), cross_out[...])


def y_kernel(
    partner, traces, rya, ryb, self_block, opposite_block, cross_block, cross_z,
    base_y, cross_y, base_x, jumps,
):
    subs, _, rhs, size = traces.shape
    rows = subs * rhs
    trade_jumps(jumps, traces, partner, "sy", y_faces(), (rya, ryb))
    from_y = product(pair_sum(jumps, 0), cross_block[...])
    cross_y[...] = from_y
    base_x[...] = from_y + cross_z[...]
    flat = jumps[...].reshape(2 * rows, size)
    with_self = product(flat, self_block[...])
    with_opp = product(flat, opposite_block[...])
    base_y[0] = with_self[:rows] + with_opp[rows:] + cross_z[...]
    base_y[1] = with_self[rows:] + with_opp[:rows] + cross_z[...]


def x_kernel(
    partner, viscosity, traces, rxa, rxb, self_block, opposite_block, base_x,
    xa, xb, to_xa, to_xb, pair_x, jumps,
):
    subs, _, rhs, size = traces.shape
    rows = subs * rhs
    trade_jumps(jumps, traces, partner, "sx", x_faces(), (rxa, rxb))
    flat = jumps[...].reshape(2 * rows, size)
    with_self = product(flat, self_block[...])
    with_opp = product(flat, opposite_block[...])
    pair_x[...] = pair_sum(jumps, 0)
    for index, (face, out, to) in enumerate(zip(x_faces(), (xa, xb), (to_xa, to_xb))):
        for sub in range(subs):
            here = slice(sub * rhs, (sub + 1) * rhs)
            own = slice(index * rows + sub * rhs, index * rows + (sub + 1) * rhs)
            opp = slice((1 - index) * rows + sub * rhs, (1 - index) * rows + (sub + 1) * rhs)
            total = with_self[own] + with_opp[opp] + base_x[here]
            value = (viscosity[sub] * total).astype(jnp.bfloat16)
            out[sub] = value
            to[partner[sub, face]] = value


def high_low(value):
    high = value.astype(jnp.bfloat16).astype(jnp.float32)
    return high, value - high


def coarse_rows(partials, owners, rows):
    subs = owners.shape[0]
    width = partials.shape[1]
    rhs = width // subs
    entries = jnp.zeros((2 * CORNERS, subs * LANES), jnp.float32)
    source = lax.broadcasted_iota(jnp.int32, (width, subs * LANES), 0)
    target = lax.broadcasted_iota(jnp.int32, (width, subs * LANES), 1)
    spread = (source // rhs) * LANES + (source % rhs) * COMPS
    for comp in range(COMPS):
        part = partials[comp * CORNERS : (comp + 1) * CORNERS]
        stacked = jnp.concatenate(high_low(part), axis=0).astype(jnp.bfloat16)
        place = (target == spread + comp).astype(jnp.float32).astype(jnp.bfloat16)
        entries += product(stacked, place)
    entries = entries[:CORNERS] + entries[CORNERS:]
    total = jnp.zeros((rows, LANES), jnp.float32)
    numbers = lax.broadcasted_iota(jnp.int32, (rows, CORNERS), 0)
    for sub in range(subs):
        onehot = (numbers == owners[sub : sub + 1, :]).astype(jnp.float32).astype(jnp.bfloat16)
        for term in high_low(entries[:, sub * LANES : (sub + 1) * LANES]):
            total += product(onehot, term.astype(jnp.bfloat16))
    return total


def rest_kernel(
    partner, viscosity, owners, base_y, base_z, cross_y, pair_x, cross_block, to_xa, to_xb,
    corner_map, ya, yb, to_ya, to_yb, local_z, dense,
):
    subs, rhs, size = to_xa.shape
    rows = subs * rhs
    from_x = product(pair_x[...], cross_block[...])
    from_xy = from_x + cross_y[...]
    places = [ya, yb, local_z.at[0], local_z.at[1]]
    for index, out in enumerate(places):
        base, cross = (base_y[index], from_x) if index < 2 else (base_z[index - 2], from_xy)
        for sub in range(subs):
            here = slice(sub * rhs, (sub + 1) * rhs)
            value = (viscosity[sub] * (base[here] + cross[here])).astype(jnp.bfloat16)
            out[sub] = value
            if index < 2:
                (to_ya, to_yb)[index][partner[sub, y_faces()[index]]] = value

    partials = jnp.zeros((COMPS * CORNERS, rows), jnp.float32)
    faces = (*x_faces(), *y_faces(), 4, 5)
    for index, (face, local) in enumerate(zip(faces, (to_xa, to_xb, *places))):
        order = [partner[sub, face] if index < 2 else sub for sub in range(subs)]
        partials += lax.dot_general(
            corner_map[face],
            jnp.concatenate([local[slot] for slot in order], axis=0),
            (((1,), (1,)), ((), ())),
            preferred_element_type=jnp.float32,
        )
    total = coarse_rows(partials, owners[...], dense.shape[0] * COARSE_DEV)
    dense[...] = total.reshape(dense.shape)


def apply_z_kernel(to_yb, local_z, applied, held, sems):
    del to_yb
    subs = local_z.shape[1]
    copies = []
    for sub in range(subs):
        up = local_z[0, sub].astype(jnp.float32)
        down = local_z[1, sub].astype(jnp.float32)
        if sub + 1 < subs:
            up = up - local_z[1, sub + 1].astype(jnp.float32)
        if sub > 0:
            down = down - local_z[0, sub - 1].astype(jnp.float32)
        held[sub, 0] = up
        held[sub, 1] = down
        copies.append(
            pltpu.make_async_copy(held.at[sub], applied.at[sub, pl.ds(4, 2)], sems.at[sub])
        )
        copies[-1].start()
    for copy in copies:
        copy.wait()


def apply_faces(faces, axis, local, got, held, applied, sems):
    copies = []
    for trade in range(2):
        for sub in range(held.shape[1]):
            other = got[trade][sub].astype(jnp.float32)
            if trade == 1:
                other = other * inner(axis)
            held[trade, sub] = local[trade][sub].astype(jnp.float32) - other
            copies.append(
                pltpu.make_async_copy(
                    held.at[trade, sub], applied.at[sub, faces[trade]], sems.at[trade, sub]
                )
            )
            copies[-1].start()
    return copies


def apply_y_kernel(applied_in, ya, yb, rya, ryb, applied, held, sems):
    del applied_in
    for copy in apply_faces(y_faces(), "sy", (ya, yb), (rya, ryb), held, applied, sems):
        copy.wait()


def apply_x_kernel(
    applied_in, xa, xb, rxa, rxb, parts, applied, coarse, held, sems, sums, sum_sem
):
    del applied_in
    total = parts[0]
    for source in range(1, parts.shape[0]):
        total = total + parts[source]
    sums[...] = total[:, : sums.shape[1]]
    copies = [pltpu.make_async_copy(sums, coarse, sum_sem)]
    copies[0].start()
    copies += apply_faces(x_faces(), "sx", (xa, xb), (rxa, rxb), held, applied, sems)
    for copy in copies:
        copy.wait()


def body(
    traces, viscosity, partner, corner_owner, self_block, opposite_block, cross_block, corner_map
):
    values = in_hbm(traces[0, 0])
    slots, visc, owners = partner[0, 0], viscosity[0, 0], corner_owner[0, 0]
    subs, _, rhs, size = values.shape
    count = lax.axis_size("sy")
    rows = subs * rhs
    face_shape = (subs, rhs, size)
    block_shape = (size, size)
    map_shape = (6, CORNERS * COMPS, size)
    bf16, f32 = jnp.bfloat16, jnp.float32

    xa, xb, ya, yb = pl.pallas_call(
        send_kernel,
        in_specs=[HBM],
        out_specs=[VMEM] * 4,
        out_shape=[in_vmem(face_shape, bf16)] * 4,
        scratch_shapes=[pltpu.SemaphoreType.DMA((4,))],
        compiler_params=params(8),
    )(values)
    rxa = first_swap(xa, "sx")
    rxb = second_swap(xb, "sx")
    rya = first_swap(ya, "sy")
    ryb = second_swap(yb, "sy")
    held_traces, self_v, opposite_v, cross_v, map_v, base_z, cross_z = pl.pallas_call(
        fetch_kernel,
        in_specs=[VMEM] * 2 + [HBM] * 5,
        out_specs=[VMEM] * 7,
        out_shape=[in_vmem(values.shape, bf16)]
        + [in_vmem(block_shape, bf16)] * 3
        + [in_vmem(map_shape, bf16), in_vmem((2, rows, size), f32), in_vmem((rows, size), f32)],
        scratch_shapes=[
            pltpu.VMEM(map_shape, bf16),
            pltpu.VMEM((2,) + face_shape, bf16),
            pltpu.SemaphoreType.DMA((11,)),
        ],
        compiler_params=params(12),
        cost_estimate=LONG,
    )(
        ya,
        yb,
        values,
        *map(in_hbm, (self_block, opposite_block, cross_block)),
        in_hbm(jnp.transpose(corner_map, (1, 0, 2))),
    )
    base_y, cross_y, base_x = pl.pallas_call(
        y_kernel,
        in_specs=[SMEM] + [VMEM] * 7,
        out_specs=[VMEM] * 3,
        out_shape=[in_vmem((2, rows, size), f32)] + [in_vmem((rows, size), f32)] * 2,
        scratch_shapes=[pltpu.VMEM((2,) + face_shape, bf16)],
        compiler_params=params(12),
    )(slots, held_traces, rya, ryb, self_v, opposite_v, cross_v, cross_z)
    xa, xb, to_xa, to_xb, pair_x = pl.pallas_call(
        x_kernel,
        in_specs=[SMEM] * 2 + [VMEM] * 6,
        out_specs=[VMEM] * 5,
        out_shape=[in_vmem(face_shape, bf16)] * 4 + [in_vmem((rows, size), bf16)],
        scratch_shapes=[pltpu.VMEM((2,) + face_shape, bf16)],
        compiler_params=params(12),
    )(slots, visc, held_traces, rxa, rxb, self_v, opposite_v, base_x)
    rxb = second_swap(to_xb, "sx")
    rxa = first_swap(to_xa, "sx")

    ya, yb, to_ya, to_yb, local_z, dense = pl.pallas_call(
        rest_kernel,
        in_specs=[SMEM] * 2 + [VMEM] * 9,
        out_specs=[VMEM] * 6,
        out_shape=[in_vmem(face_shape, bf16)] * 4
        + [in_vmem((2,) + face_shape, bf16), in_vmem((count, COARSE_DEV, LANES), f32)],
        compiler_params=params(12),
    )(slots, visc, owners, base_y, base_z, cross_y, pair_x, cross_v, to_xa, to_xb, map_v)
    parts = lax.all_to_all(dense, "sy", 0, 0, tiled=True)
    rya = first_swap(to_ya, "sy")
    ryb = second_swap(to_yb, "sy")
    applied = pl.pallas_call(
        apply_z_kernel,
        in_specs=[VMEM] * 2,
        out_specs=HBM,
        out_shape=jax.ShapeDtypeStruct(values.shape, f32),
        scratch_shapes=[
            pltpu.VMEM((subs, 2, rhs, size), f32),
            pltpu.SemaphoreType.DMA((subs,)),
        ],
        compiler_params=params(8),
        cost_estimate=LONG,
    )(to_yb, local_z)
    out_shape = jax.ShapeDtypeStruct(values.shape, f32)
    scratch = [pltpu.VMEM((2,) + face_shape, f32), pltpu.SemaphoreType.DMA((2, subs))]
    applied = pl.pallas_call(
        apply_y_kernel,
        in_specs=[HBM] + [VMEM] * 4,
        out_specs=HBM,
        out_shape=out_shape,
        input_output_aliases={0: 0},
        scratch_shapes=scratch,
        compiler_params=params(8),
        cost_estimate=LONG,
    )(applied, ya, yb, rya, ryb)
    applied, coarse = pl.pallas_call(
        apply_x_kernel,
        in_specs=[HBM] + [VMEM] * 5,
        out_specs=[HBM, HBM],
        out_shape=[out_shape, jax.ShapeDtypeStruct((COARSE_DEV, rhs * COMPS), f32)],
        input_output_aliases={0: 0},
        scratch_shapes=scratch
        + [pltpu.VMEM((COARSE_DEV, rhs * COMPS), f32), pltpu.SemaphoreType.DMA],
        compiler_params=params(8),
    )(applied, xa, xb, rxa, rxb, parts)
    return applied[None, None], coarse.T


def solution(mesh):
    return jax.shard_map(
        body,
        mesh=mesh,
        in_specs=(
            P("sx", "sy", None, None, None, None),
            P("sx", "sy", None),
            P("sx", "sy", None, None),
            P("sx", "sy", None, None),
            P(),
            P(),
            P(),
            P(),
        ),
        out_specs=(P("sx", "sy", None, None, None, None), P(None, ("sx", "sy"))),
        check_vma=False,
    )
```

```python
import jax
import jax.numpy as jnp
from jax import lax
from jax.experimental import pallas as pl
from jax.experimental.pallas import tpu as pltpu
from jax.sharding import PartitionSpec as P

CORNERS = 8
COMPS = 3
COARSE_DEV = 8
LANES = 128

VMEM = pl.BlockSpec(memory_space=pltpu.VMEM)
SMEM = pl.BlockSpec(memory_space=pltpu.SMEM)
HBM = pl.BlockSpec(memory_space=pltpu.HBM)
ANY = pl.BlockSpec(memory_space=pl.ANY)


def in_vmem(shape, dtype):
    return pltpu.VMEM(shape, dtype)


def in_hbm(value):
    return pltpu.with_memory_space_constraint(value, pltpu.HBM)


def params(mib):
    return pltpu.CompilerParams(vmem_limit_bytes=mib * 1024 * 1024)


LONG = pl.CostEstimate(flops=20 * 10**9, bytes_accessed=0, transcendentals=0)


def odd(axis):
    return lax.rem(lax.axis_index(axis), 2)


def first_swap(value, axis):
    return lax.ppermute(value, axis, [(i, i ^ 1) for i in range(lax.axis_size(axis))])


def second_swap(value, axis):
    rows, cols = lax.axis_size("sx"), lax.axis_size("sy")
    pairs = []
    for i in range(rows):
        for j in range(cols):
            if axis == "sx":
                k = i - 1 if i % 2 == 0 else i + 1
                target = (k, j) if 0 <= k < rows else (i, j ^ 1)
            else:
                k = j - 1 if j % 2 == 0 else j + 1
                target = (i, k) if 0 <= k < cols else (i ^ 2, j)
            pairs.append((i * cols + j, target[0] * cols + target[1]))
    return lax.ppermute(value, ("sx", "sy"), pairs)


def inner(axis):
    me = lax.axis_index(axis)
    return ((me > 0) & (me < lax.axis_size(axis) - 1)).astype(jnp.float32)


def x_faces():
    return odd("sx"), 1 - odd("sx")


def y_faces():
    return 2 + odd("sy"), 3 - odd("sy")


def send_kernel(traces, xa, xb, ya, yb, sems):
    faces = (*x_faces(), *y_faces())
    copies = [
        pltpu.make_async_copy(traces.at[:, face], out, sems.at[index])
        for index, (face, out) in enumerate(zip(faces, (xa, xb, ya, yb)))
    ]
    for copy in copies:
        copy.start()
    for copy in copies:
        copy.wait()


def product(left, right):
    return jnp.dot(left, right, preferred_element_type=jnp.float32)


def trade_jumps(jumps, traces, partner, axis, faces, received):
    for trade, (face, got) in enumerate(zip(faces, received)):
        for sub in range(traces.shape[0]):
            other = got[partner[sub, face]].astype(jnp.float32)
            if trade == 1:
                other = other * inner(axis)
            own = traces[sub, face].astype(jnp.float32)
            jumps[trade, sub] = (own - other).astype(jnp.bfloat16)


def flat_face(jumps, index):
    _, subs, rhs, size = jumps.shape
    return jumps[index].reshape(subs * rhs, size)


def pair_sum(jumps, first):
    up = flat_face(jumps, first).astype(jnp.float32)
    return (up + flat_face(jumps, first + 1).astype(jnp.float32)).astype(jnp.bfloat16)


def fetch_kernel(
    ya, yb, traces, self_block, opposite_block, cross_block, corner_map,
    traces_out, self_out, opposite_out, cross_out, map_out, base_z, cross_z,
    map_in, jumps, sems,
):
    del ya, yb
    subs, _, rhs, size = traces.shape
    rows = subs * rhs
    copies = [
        pltpu.make_async_copy(traces, traces_out, sems.at[0]),
        pltpu.make_async_copy(corner_map, map_in, sems.at[1]),
    ]
    for source, target in (
        (self_block, self_out), (opposite_block, opposite_out), (cross_block, cross_out)
    ):
        for part in range(3):
            third = pl.ds(part * (size // 3), size // 3)
            copies.append(
                pltpu.make_async_copy(source.at[third], target.at[third], sems.at[len(copies)])
            )
    for copy in copies:
        copy.start()

    copies[0].wait()
    for sub in range(subs):
        up = traces_out[sub, 4].astype(jnp.float32)
        down = traces_out[sub, 5].astype(jnp.float32)
        if sub + 1 < subs:
            up = up - traces_out[sub + 1, 5].astype(jnp.float32)
        if sub > 0:
            down = down - traces_out[sub - 1, 4].astype(jnp.float32)
        jumps[0, sub] = up.astype(jnp.bfloat16)
        jumps[1, sub] = down.astype(jnp.bfloat16)
    copies[1].wait()
    width = CORNERS * COMPS
    row = lax.broadcasted_iota(jnp.int32, (width, width), 0)
    col = lax.broadcasted_iota(jnp.int32, (width, width), 1)
    order = (col == (row % CORNERS) * COMPS + row // CORNERS).astype(jnp.float32)
    order = order.astype(jnp.bfloat16)
    for face in range(6):
        map_out[face] = product(order, map_in[face]).astype(jnp.bfloat16)
    flat = jumps[...].reshape(2 * rows, size)
    for copy in copies[2:5]:
        copy.wait()
    with_self = product(flat, self_out[...])
    for copy in copies[5:8]:
        copy.wait()
    with_opp = product(flat, opposite_out[...])
    base_z[0] = with_self[:rows] + with_opp[rows:]
    base_z[1] = with_self[rows:] + with_opp[:rows]
    for copy in copies[8:]:
        copy.wait()
    cross_z[...] = product(pair_sum(jumps, 0), cross_out[...])


def y_kernel(
    partner, traces, rya, ryb, self_block, opposite_block, cross_block, cross_z,
    base_y, cross_y, base_x, jumps,
):
    subs, _, rhs, size = traces.shape
    rows = subs * rhs
    trade_jumps(jumps, traces, partner, "sy", y_faces(), (rya, ryb))
    from_y = product(pair_sum(jumps, 0), cross_block[...])
    cross_y[...] = from_y
    base_x[...] = from_y + cross_z[...]
    flat = jumps[...].reshape(2 * rows, size)
    with_self = product(flat, self_block[...])
    with_opp = product(flat, opposite_block[...])
    base_y[0] = with_self[:rows] + with_opp[rows:] + cross_z[...]
    base_y[1] = with_self[rows:] + with_opp[:rows] + cross_z[...]


def x_kernel(
    partner, viscosity, traces, rxa, rxb, self_block, opposite_block, base_x,
    xa, xb, to_xa, to_xb, pair_x, jumps,
):
    subs, _, rhs, size = traces.shape
    rows = subs * rhs
    trade_jumps(jumps, traces, partner, "sx", x_faces(), (rxa, rxb))
    flat = jumps[...].reshape(2 * rows, size)
    with_self = product(flat, self_block[...])
    with_opp = product(flat, opposite_block[...])
    pair_x[...] = pair_sum(jumps, 0)
    for index, (face, out, to) in enumerate(zip(x_faces(), (xa, xb), (to_xa, to_xb))):
        for sub in range(subs):
            here = slice(sub * rhs, (sub + 1) * rhs)
            own = slice(index * rows + sub * rhs, index * rows + (sub + 1) * rhs)
            opp = slice((1 - index) * rows + sub * rhs, (1 - index) * rows + (sub + 1) * rhs)
            total = with_self[own] + with_opp[opp] + base_x[here]
            value = (viscosity[sub] * total).astype(jnp.bfloat16)
            out[sub] = value
            to[partner[sub, face]] = value


def high_low(value):
    high = value.astype(jnp.bfloat16).astype(jnp.float32)
    return high, value - high


def coarse_rows(partials, owners, rows):
    subs = owners.shape[0]
    width = partials.shape[1]
    rhs = width // subs
    entries = jnp.zeros((2 * CORNERS, subs * LANES), jnp.float32)
    source = lax.broadcasted_iota(jnp.int32, (width, subs * LANES), 0)
    target = lax.broadcasted_iota(jnp.int32, (width, subs * LANES), 1)
    spread = (source // rhs) * LANES + (source % rhs) * COMPS
    for comp in range(COMPS):
        part = partials[comp * CORNERS : (comp + 1) * CORNERS]
        stacked = jnp.concatenate(high_low(part), axis=0).astype(jnp.bfloat16)
        place = (target == spread + comp).astype(jnp.float32).astype(jnp.bfloat16)
        entries += product(stacked, place)
    entries = entries[:CORNERS] + entries[CORNERS:]
    total = jnp.zeros((rows, LANES), jnp.float32)
    numbers = lax.broadcasted_iota(jnp.int32, (rows, CORNERS), 0)
    for sub in range(subs):
        onehot = (numbers == owners[sub : sub + 1, :]).astype(jnp.float32).astype(jnp.bfloat16)
        for term in high_low(entries[:, sub * LANES : (sub + 1) * LANES]):
            total += product(onehot, term.astype(jnp.bfloat16))
    return total


def rest_kernel(
    partner, viscosity, owners, base_y, base_z, cross_y, pair_x, cross_block, to_xa, to_xb,
    corner_map, ya, yb, to_ya, to_yb, local_z, dense,
):
    subs, rhs, size = to_xa.shape
    rows = subs * rhs
    from_x = product(pair_x[...], cross_block[...])
    from_xy = from_x + cross_y[...]
    places = [ya, yb, local_z.at[0], local_z.at[1]]
    for index, out in enumerate(places):
        base, cross = (base_y[index], from_x) if index < 2 else (base_z[index - 2], from_xy)
        for sub in range(subs):
            here = slice(sub * rhs, (sub + 1) * rhs)
            value = (viscosity[sub] * (base[here] + cross[here])).astype(jnp.bfloat16)
            out[sub] = value
            if index < 2:
                (to_ya, to_yb)[index][partner[sub, y_faces()[index]]] = value

    partials = jnp.zeros((COMPS * CORNERS, rows), jnp.float32)
    faces = (*x_faces(), *y_faces(), 4, 5)
    for index, (face, local) in enumerate(zip(faces, (to_xa, to_xb, *places))):
        order = [partner[sub, face] if index < 2 else sub for sub in range(subs)]
        partials += lax.dot_general(
            corner_map[face],
            jnp.concatenate([local[slot] for slot in order], axis=0),
            (((1,), (1,)), ((), ())),
            preferred_element_type=jnp.float32,
        )
    total = coarse_rows(partials, owners[...], dense.shape[0] * COARSE_DEV)
    dense[...] = total.reshape(dense.shape)


def apply_z_kernel(to_ya, to_yb, local_z, applied, held, sems):
    del to_ya, to_yb
    subs = local_z.shape[1]
    copies = []
    for sub in range(subs):
        up = local_z[0, sub].astype(jnp.float32)
        down = local_z[1, sub].astype(jnp.float32)
        if sub + 1 < subs:
            up = up - local_z[1, sub + 1].astype(jnp.float32)
        if sub > 0:
            down = down - local_z[0, sub - 1].astype(jnp.float32)
        held[sub, 0] = up
        held[sub, 1] = down
        copies.append(
            pltpu.make_async_copy(held.at[sub], applied.at[sub, pl.ds(4, 2)], sems.at[sub])
        )
        copies[-1].start()
    for copy in copies:
        copy.wait()


def apply_faces(faces, axis, local, got, held, applied, sems):
    copies = []
    for trade in range(2):
        for sub in range(held.shape[1]):
            other = got[trade][sub].astype(jnp.float32)
            if trade == 1:
                other = other * inner(axis)
            held[trade, sub] = local[trade][sub].astype(jnp.float32) - other
            copies.append(
                pltpu.make_async_copy(
                    held.at[trade, sub], applied.at[sub, faces[trade]], sems.at[trade, sub]
                )
            )
            copies[-1].start()
    return copies


def apply_y_kernel(applied_in, ya, yb, rya, ryb, applied, held, sems):
    del applied_in
    for copy in apply_faces(y_faces(), "sy", (ya, yb), (rya, ryb), held, applied, sems):
        copy.wait()


def apply_x_kernel(
    applied_in, xa, xb, rxa, rxb, parts, applied, coarse, held, sems, mine, sums, sum_sems
):
    del applied_in
    count = mine.shape[0]
    fetch = []
    for source in range(count):
        block = source * count + lax.axis_index("sy")
        fetch.append(pltpu.make_async_copy(parts.at[block], mine.at[source], sum_sems.at[source]))
        fetch[-1].start()
    copies = apply_faces(x_faces(), "sx", (xa, xb), (rxa, rxb), held, applied, sems)
    for copy in fetch:
        copy.wait()
    total = mine[0]
    for source in range(1, count):
        total = total + mine[source]
    sums[...] = total[:, : sums.shape[1]]
    copies.append(pltpu.make_async_copy(sums, coarse, sum_sems.at[count]))
    copies[-1].start()
    for copy in copies:
        copy.wait()


def body(
    traces, viscosity, partner, corner_owner, self_block, opposite_block, cross_block, corner_map
):
    values = in_hbm(traces[0, 0])
    slots, visc, owners = partner[0, 0], viscosity[0, 0], corner_owner[0, 0]
    subs, _, rhs, size = values.shape
    count = lax.axis_size("sy")
    rows = subs * rhs
    face_shape = (subs, rhs, size)
    block_shape = (size, size)
    map_shape = (6, CORNERS * COMPS, size)
    bf16, f32 = jnp.bfloat16, jnp.float32

    xa, xb, ya, yb = pl.pallas_call(
        send_kernel,
        in_specs=[HBM],
        out_specs=[VMEM] * 4,
        out_shape=[in_vmem(face_shape, bf16)] * 4,
        scratch_shapes=[pltpu.SemaphoreType.DMA((4,))],
        compiler_params=params(8),
    )(values)
    rxa = first_swap(xa, "sx")
    rxb = second_swap(xb, "sx")
    rya = first_swap(ya, "sy")
    ryb = second_swap(yb, "sy")
    held_traces, self_v, opposite_v, cross_v, map_v, base_z, cross_z = pl.pallas_call(
        fetch_kernel,
        in_specs=[VMEM] * 2 + [HBM] * 5,
        out_specs=[VMEM] * 7,
        out_shape=[in_vmem(values.shape, bf16)]
        + [in_vmem(block_shape, bf16)] * 3
        + [in_vmem(map_shape, bf16), in_vmem((2, rows, size), f32), in_vmem((rows, size), f32)],
        scratch_shapes=[
            pltpu.VMEM(map_shape, bf16),
            pltpu.VMEM((2,) + face_shape, bf16),
            pltpu.SemaphoreType.DMA((11,)),
        ],
        compiler_params=params(12),
        cost_estimate=LONG,
    )(
        ya,
        yb,
        values,
        *map(in_hbm, (self_block, opposite_block, cross_block)),
        in_hbm(jnp.transpose(corner_map, (1, 0, 2))),
    )
    base_y, cross_y, base_x = pl.pallas_call(
        y_kernel,
        in_specs=[SMEM] + [VMEM] * 7,
        out_specs=[VMEM] * 3,
        out_shape=[in_vmem((2, rows, size), f32)] + [in_vmem((rows, size), f32)] * 2,
        scratch_shapes=[pltpu.VMEM((2,) + face_shape, bf16)],
        compiler_params=params(12),
    )(slots, held_traces, rya, ryb, self_v, opposite_v, cross_v, cross_z)
    xa, xb, to_xa, to_xb, pair_x = pl.pallas_call(
        x_kernel,
        in_specs=[SMEM] * 2 + [VMEM] * 6,
        out_specs=[VMEM] * 5,
        out_shape=[in_vmem(face_shape, bf16)] * 4 + [in_vmem((rows, size), bf16)],
        scratch_shapes=[pltpu.VMEM((2,) + face_shape, bf16)],
        compiler_params=params(12),
    )(slots, visc, held_traces, rxa, rxb, self_v, opposite_v, base_x)
    rxb = second_swap(to_xb, "sx")
    rxa = first_swap(to_xa, "sx")

    ya, yb, to_ya, to_yb, local_z, dense = pl.pallas_call(
        rest_kernel,
        in_specs=[SMEM] * 2 + [VMEM] * 9,
        out_specs=[VMEM] * 6,
        out_shape=[in_vmem(face_shape, bf16)] * 4
        + [in_vmem((2,) + face_shape, bf16), in_vmem((count, COARSE_DEV, LANES), f32)],
        compiler_params=params(12),
    )(slots, visc, owners, base_y, base_z, cross_y, pair_x, cross_v, to_xa, to_xb, map_v)
    parts = lax.all_gather(dense, "sy", axis=0, tiled=True)
    rya = first_swap(to_ya, "sy")
    ryb = second_swap(to_yb, "sy")
    applied = pl.pallas_call(
        apply_z_kernel,
        in_specs=[VMEM] * 3,
        out_specs=HBM,
        out_shape=jax.ShapeDtypeStruct(values.shape, f32),
        scratch_shapes=[
            pltpu.VMEM((subs, 2, rhs, size), f32),
            pltpu.SemaphoreType.DMA((subs,)),
        ],
        compiler_params=params(8),
        cost_estimate=LONG,
    )(to_ya, to_yb, local_z)
    out_shape = jax.ShapeDtypeStruct(values.shape, f32)
    scratch = [pltpu.VMEM((2,) + face_shape, f32), pltpu.SemaphoreType.DMA((2, subs))]
    applied = pl.pallas_call(
        apply_y_kernel,
        in_specs=[HBM] + [VMEM] * 4,
        out_specs=HBM,
        out_shape=out_shape,
        input_output_aliases={0: 0},
        scratch_shapes=scratch,
        compiler_params=params(8),
    )(applied, ya, yb, rya, ryb)
    applied, coarse = pl.pallas_call(
        apply_x_kernel,
        in_specs=[HBM] + [VMEM] * 4 + [HBM],
        out_specs=[HBM, HBM],
        out_shape=[out_shape, jax.ShapeDtypeStruct((COARSE_DEV, rhs * COMPS), f32)],
        input_output_aliases={0: 0},
        scratch_shapes=scratch
        + [
            pltpu.VMEM((count, COARSE_DEV, LANES), f32),
            pltpu.VMEM((COARSE_DEV, rhs * COMPS), f32),
            pltpu.SemaphoreType.DMA((count + 1,)),
        ],
        compiler_params=params(8),
    )(applied, xa, xb, rxa, rxb, in_hbm(parts))
    return applied[None, None], coarse.T


def solution(mesh):
    return jax.shard_map(
        body,
        mesh=mesh,
        in_specs=(
            P("sx", "sy", None, None, None, None),
            P("sx", "sy", None),
            P("sx", "sy", None, None),
            P("sx", "sy", None, None),
            P(),
            P(),
            P(),
            P(),
        ),
        out_specs=(P("sx", "sy", None, None, None, None), P(None, ("sx", "sy"))),
        check_vma=False,
    )
```

```python
import jax
import jax.numpy as jnp
from jax import lax
from jax.experimental import pallas as pl
from jax.experimental.pallas import tpu as pltpu
from jax.sharding import PartitionSpec as P

CORNERS = 8
COMPS = 3
COARSE_DEV = 8
LANES = 128

VMEM = pl.BlockSpec(memory_space=pltpu.VMEM)
SMEM = pl.BlockSpec(memory_space=pltpu.SMEM)
HBM = pl.BlockSpec(memory_space=pltpu.HBM)
ANY = pl.BlockSpec(memory_space=pl.ANY)


def in_vmem(shape, dtype):
    return pltpu.VMEM(shape, dtype)


def in_hbm(value):
    return pltpu.with_memory_space_constraint(value, pltpu.HBM)


def params(mib):
    return pltpu.CompilerParams(vmem_limit_bytes=mib * 1024 * 1024)


LONG = pl.CostEstimate(flops=20 * 10**9, bytes_accessed=0, transcendentals=0)


def odd(axis):
    return lax.rem(lax.axis_index(axis), 2)


def first_swap(value, axis):
    return lax.ppermute(value, axis, [(i, i ^ 1) for i in range(lax.axis_size(axis))])


def second_swap(value, axis):
    rows, cols = lax.axis_size("sx"), lax.axis_size("sy")
    pairs = []
    for i in range(rows):
        for j in range(cols):
            if axis == "sx":
                k = i - 1 if i % 2 == 0 else i + 1
                target = (k, j) if 0 <= k < rows else (i, j ^ 1)
            else:
                k = j - 1 if j % 2 == 0 else j + 1
                target = (i, k) if 0 <= k < cols else (i ^ 2, j)
            pairs.append((i * cols + j, target[0] * cols + target[1]))
    return lax.ppermute(value, ("sx", "sy"), pairs)


def cross_swap(value, axis, bits):
    return lax.ppermute(value, axis, [(i, i ^ bits) for i in range(lax.axis_size(axis))])


def inner(axis):
    me = lax.axis_index(axis)
    return ((me > 0) & (me < lax.axis_size(axis) - 1)).astype(jnp.float32)


def x_faces():
    return odd("sx"), 1 - odd("sx")


def y_faces():
    return 2 + odd("sy"), 3 - odd("sy")


def send_kernel(traces, xa, xb, ya, yb, sems):
    faces = (*x_faces(), *y_faces())
    copies = [
        pltpu.make_async_copy(traces.at[:, face], out, sems.at[index])
        for index, (face, out) in enumerate(zip(faces, (xa, xb, ya, yb)))
    ]
    for copy in copies:
        copy.start()
    for copy in copies:
        copy.wait()


def product(left, right):
    return jnp.dot(left, right, preferred_element_type=jnp.float32)


def trade_jumps(jumps, traces, partner, axis, faces, received):
    for trade, (face, got) in enumerate(zip(faces, received)):
        for sub in range(traces.shape[0]):
            other = got[partner[sub, face]].astype(jnp.float32)
            if trade == 1:
                other = other * inner(axis)
            own = traces[sub, face].astype(jnp.float32)
            jumps[trade, sub] = (own - other).astype(jnp.bfloat16)


def flat_face(jumps, index):
    _, subs, rhs, size = jumps.shape
    return jumps[index].reshape(subs * rhs, size)


def pair_sum(jumps, first):
    up = flat_face(jumps, first).astype(jnp.float32)
    return (up + flat_face(jumps, first + 1).astype(jnp.float32)).astype(jnp.bfloat16)


def fetch_kernel(
    ya, yb, traces, self_block, opposite_block, cross_block, corner_map,
    traces_out, self_out, opposite_out, cross_out, map_out, base_z, cross_z,
    map_in, jumps, sems,
):
    del ya, yb
    subs, _, rhs, size = traces.shape
    rows = subs * rhs
    copies = [
        pltpu.make_async_copy(traces, traces_out, sems.at[0]),
        pltpu.make_async_copy(corner_map, map_in, sems.at[1]),
    ]
    for source, target in (
        (self_block, self_out), (opposite_block, opposite_out), (cross_block, cross_out)
    ):
        for part in range(3):
            third = pl.ds(part * (size // 3), size // 3)
            copies.append(
                pltpu.make_async_copy(source.at[third], target.at[third], sems.at[len(copies)])
            )
    for copy in copies:
        copy.start()

    copies[0].wait()
    for sub in range(subs):
        up = traces_out[sub, 4].astype(jnp.float32)
        down = traces_out[sub, 5].astype(jnp.float32)
        if sub + 1 < subs:
            up = up - traces_out[sub + 1, 5].astype(jnp.float32)
        if sub > 0:
            down = down - traces_out[sub - 1, 4].astype(jnp.float32)
        jumps[0, sub] = up.astype(jnp.bfloat16)
        jumps[1, sub] = down.astype(jnp.bfloat16)
    copies[1].wait()
    width = CORNERS * COMPS
    row = lax.broadcasted_iota(jnp.int32, (width, width), 0)
    col = lax.broadcasted_iota(jnp.int32, (width, width), 1)
    order = (col == (row % CORNERS) * COMPS + row // CORNERS).astype(jnp.float32)
    order = order.astype(jnp.bfloat16)
    for face in range(6):
        map_out[face] = product(order, map_in[face]).astype(jnp.bfloat16)
    flat = jumps[...].reshape(2 * rows, size)
    for copy in copies[2:5]:
        copy.wait()
    with_self = product(flat, self_out[...])
    for copy in copies[5:8]:
        copy.wait()
    with_opp = product(flat, opposite_out[...])
    base_z[0] = with_self[:rows] + with_opp[rows:]
    base_z[1] = with_self[rows:] + with_opp[:rows]
    for copy in copies[8:]:
        copy.wait()
    cross_z[...] = product(pair_sum(jumps, 0), cross_out[...])


def y_kernel(
    partner, traces, rya, ryb, self_block, opposite_block, cross_block, cross_z,
    base_y, cross_y, base_x, jumps,
):
    subs, _, rhs, size = traces.shape
    rows = subs * rhs
    trade_jumps(jumps, traces, partner, "sy", y_faces(), (rya, ryb))
    from_y = product(pair_sum(jumps, 0), cross_block[...])
    cross_y[...] = from_y
    base_x[...] = from_y + cross_z[...]
    flat = jumps[...].reshape(2 * rows, size)
    with_self = product(flat, self_block[...])
    with_opp = product(flat, opposite_block[...])
    base_y[0] = with_self[:rows] + with_opp[rows:] + cross_z[...]
    base_y[1] = with_self[rows:] + with_opp[:rows] + cross_z[...]


def x_kernel(
    partner, viscosity, traces, rxa, rxb, self_block, opposite_block, base_x,
    xa, xb, to_xa, to_xb, pair_x, jumps,
):
    subs, _, rhs, size = traces.shape
    rows = subs * rhs
    trade_jumps(jumps, traces, partner, "sx", x_faces(), (rxa, rxb))
    flat = jumps[...].reshape(2 * rows, size)
    with_self = product(flat, self_block[...])
    with_opp = product(flat, opposite_block[...])
    pair_x[...] = pair_sum(jumps, 0)
    for index, (face, out, to) in enumerate(zip(x_faces(), (xa, xb), (to_xa, to_xb))):
        for sub in range(subs):
            here = slice(sub * rhs, (sub + 1) * rhs)
            own = slice(index * rows + sub * rhs, index * rows + (sub + 1) * rhs)
            opp = slice((1 - index) * rows + sub * rhs, (1 - index) * rows + (sub + 1) * rhs)
            total = with_self[own] + with_opp[opp] + base_x[here]
            value = (viscosity[sub] * total).astype(jnp.bfloat16)
            out[sub] = value
            to[partner[sub, face]] = value


def high_low(value):
    high = value.astype(jnp.bfloat16).astype(jnp.float32)
    return high, value - high


def coarse_rows(partials, owners, rows):
    subs = owners.shape[0]
    width = partials.shape[1]
    rhs = width // subs
    entries = jnp.zeros((2 * CORNERS, subs * LANES), jnp.float32)
    source = lax.broadcasted_iota(jnp.int32, (width, subs * LANES), 0)
    target = lax.broadcasted_iota(jnp.int32, (width, subs * LANES), 1)
    spread = (source // rhs) * LANES + (source % rhs) * COMPS
    for comp in range(COMPS):
        part = partials[comp * CORNERS : (comp + 1) * CORNERS]
        stacked = jnp.concatenate(high_low(part), axis=0).astype(jnp.bfloat16)
        place = (target == spread + comp).astype(jnp.float32).astype(jnp.bfloat16)
        entries += product(stacked, place)
    entries = entries[:CORNERS] + entries[CORNERS:]
    total = jnp.zeros((rows, LANES), jnp.float32)
    numbers = lax.broadcasted_iota(jnp.int32, (rows, CORNERS), 0)
    for sub in range(subs):
        onehot = (numbers == owners[sub : sub + 1, :]).astype(jnp.float32).astype(jnp.bfloat16)
        for term in high_low(entries[:, sub * LANES : (sub + 1) * LANES]):
            total += product(onehot, term.astype(jnp.bfloat16))
    return total


def rest_kernel(
    partner, viscosity, owners, base_y, base_z, cross_y, pair_x, cross_block, to_xa, to_xb,
    corner_map, ya, yb, to_ya, to_yb, local_z, kept, dense,
):
    subs, rhs, size = to_xa.shape
    rows = subs * rhs
    from_x = product(pair_x[...], cross_block[...])
    from_xy = from_x + cross_y[...]
    places = [ya, yb, local_z.at[0], local_z.at[1]]
    for index, out in enumerate(places):
        base, cross = (base_y[index], from_x) if index < 2 else (base_z[index - 2], from_xy)
        for sub in range(subs):
            here = slice(sub * rhs, (sub + 1) * rhs)
            value = (viscosity[sub] * (base[here] + cross[here])).astype(jnp.bfloat16)
            out[sub] = value
            if index < 2:
                (to_ya, to_yb)[index][partner[sub, y_faces()[index]]] = value

    partials = jnp.zeros((COMPS * CORNERS, rows), jnp.float32)
    faces = (*x_faces(), *y_faces(), 4, 5)
    for index, (face, local) in enumerate(zip(faces, (to_xa, to_xb, *places))):
        order = [partner[sub, face] if index < 2 else sub for sub in range(subs)]
        partials += lax.dot_general(
            corner_map[face],
            jnp.concatenate([local[slot] for slot in order], axis=0),
            (((1,), (1,)), ((), ())),
            preferred_element_type=jnp.float32,
        )
    dense[...] = coarse_rows(partials, owners[...], dense.shape[0])
    me = lax.axis_index("sy")

    def block(bits):
        start = pl.multiple_of((me ^ bits) * COARSE_DEV, COARSE_DEV)
        return dense[pl.ds(start, COARSE_DEV), :]

    half, per_row = kept.shape[0], size // LANES
    for index in range((to_ya.shape[0] - subs) * per_row):
        lanes = slice(index % per_row * LANES, (index % per_row + 1) * LANES)
        both = jnp.zeros((2 * COARSE_DEV, LANES), jnp.float32)
        if index < half:
            kept[index] = block(2 * index)
            both = jnp.concatenate(high_low(block(2 * index + 1)), axis=0)
        to_ya[subs + index // per_row, :, lanes] = both.astype(jnp.bfloat16)


def first_add_kernel(subs, after, kept, got, keep, give):
    del after
    half, per_row = kept.shape[0], got.shape[2] // LANES
    for index in range(half):
        lanes = slice(index % per_row * LANES, (index % per_row + 1) * LANES)
        both = got[subs + index // per_row, :, lanes].astype(jnp.float32)
        total = kept[index] + both[:COARSE_DEV] + both[COARSE_DEV:]
        out = keep if index < half // 2 else give
        out[index % (half // 2)] = total


def next_add_kernel(after, kept, got, keep, give):
    del after
    half = kept.shape[0]
    total = kept[...] + got[...]
    keep[...] = total[: half // 2]
    give[...] = total[half // 2 :]


def last_add_kernel(kept, got, coarse, total, sem):
    total[...] = (kept[0] + got[0])[:, : total.shape[1]]
    copy = pltpu.make_async_copy(total, coarse, sem)
    copy.start()
    copy.wait()


def apply_z_kernel(to_yb, local_z, applied, held, sems):
    del to_yb
    subs = local_z.shape[1]
    copies = []
    for sub in range(subs):
        up = local_z[0, sub].astype(jnp.float32)
        down = local_z[1, sub].astype(jnp.float32)
        if sub + 1 < subs:
            up = up - local_z[1, sub + 1].astype(jnp.float32)
        if sub > 0:
            down = down - local_z[0, sub - 1].astype(jnp.float32)
        held[sub, 0] = up
        held[sub, 1] = down
        copies.append(
            pltpu.make_async_copy(held.at[sub], applied.at[sub, pl.ds(4, 2)], sems.at[sub])
        )
        copies[-1].start()
    for copy in copies:
        copy.wait()


def apply_faces(faces, axis, local, got, held, applied, sems):
    copies = []
    for trade in range(2):
        for sub in range(held.shape[1]):
            other = got[trade][sub].astype(jnp.float32)
            if trade == 1:
                other = other * inner(axis)
            held[trade, sub] = local[trade][sub].astype(jnp.float32) - other
            copies.append(
                pltpu.make_async_copy(
                    held.at[trade, sub], applied.at[sub, faces[trade]], sems.at[trade, sub]
                )
            )
            copies[-1].start()
    return copies


def apply_kernel(faces, axis, applied_in, first, second, *refs):
    got_first, got_second, applied, held, sems = refs[-5:]
    del applied_in
    local, got = (first, second), (got_first, got_second)
    for copy in apply_faces(faces(), axis, local, got, held, applied, sems):
        copy.wait()


def body(
    traces, viscosity, partner, corner_owner, self_block, opposite_block, cross_block, corner_map
):
    values = in_hbm(traces[0, 0])
    slots, visc, owners = partner[0, 0], viscosity[0, 0], corner_owner[0, 0]
    subs, _, rhs, size = values.shape
    count = lax.axis_size("sy")
    rows = subs * rhs
    face_shape = (subs, rhs, size)
    block_shape = (size, size)
    map_shape = (6, CORNERS * COMPS, size)
    bf16, f32 = jnp.bfloat16, jnp.float32

    xa, xb, ya, yb = pl.pallas_call(
        send_kernel,
        in_specs=[HBM],
        out_specs=[VMEM] * 4,
        out_shape=[in_vmem(face_shape, bf16)] * 4,
        scratch_shapes=[pltpu.SemaphoreType.DMA((4,))],
        compiler_params=params(8),
    )(values)
    rxa = first_swap(xa, "sx")
    rxb = second_swap(xb, "sx")
    rya = first_swap(ya, "sy")
    ryb = second_swap(yb, "sy")
    held_traces, self_v, opposite_v, cross_v, map_v, base_z, cross_z = pl.pallas_call(
        fetch_kernel,
        in_specs=[VMEM] * 2 + [HBM] * 5,
        out_specs=[VMEM] * 7,
        out_shape=[in_vmem(values.shape, bf16)]
        + [in_vmem(block_shape, bf16)] * 3
        + [in_vmem(map_shape, bf16), in_vmem((2, rows, size), f32), in_vmem((rows, size), f32)],
        scratch_shapes=[
            pltpu.VMEM(map_shape, bf16),
            pltpu.VMEM((2,) + face_shape, bf16),
            pltpu.SemaphoreType.DMA((11,)),
        ],
        compiler_params=params(12),
        cost_estimate=LONG,
    )(
        ya,
        yb,
        values,
        *map(in_hbm, (self_block, opposite_block, cross_block)),
        in_hbm(jnp.transpose(corner_map, (1, 0, 2))),
    )
    base_y, cross_y, base_x = pl.pallas_call(
        y_kernel,
        in_specs=[SMEM] + [VMEM] * 7,
        out_specs=[VMEM] * 3,
        out_shape=[in_vmem((2, rows, size), f32)] + [in_vmem((rows, size), f32)] * 2,
        scratch_shapes=[pltpu.VMEM((2,) + face_shape, bf16)],
        compiler_params=params(12),
    )(slots, held_traces, rya, ryb, self_v, opposite_v, cross_v, cross_z)
    xa, xb, to_xa, to_xb, pair_x = pl.pallas_call(
        x_kernel,
        in_specs=[SMEM] * 2 + [VMEM] * 6,
        out_specs=[VMEM] * 5,
        out_shape=[in_vmem(face_shape, bf16)] * 4 + [in_vmem((rows, size), bf16)],
        scratch_shapes=[pltpu.VMEM((2,) + face_shape, bf16)],
        compiler_params=params(12),
    )(slots, visc, held_traces, rxa, rxb, self_v, opposite_v, base_x)
    rxb = second_swap(to_xb, "sx")
    rxa = first_swap(to_xa, "sx")

    half, per_row = count // 2, size // LANES
    long_shape = (subs + -(-half // per_row), rhs, size)

    def blocks(number):
        return in_vmem((number, COARSE_DEV, LANES), f32)

    ya, yb, to_ya, to_yb, local_z, kept = pl.pallas_call(
        rest_kernel,
        in_specs=[SMEM] * 2 + [VMEM] * 9,
        out_specs=[VMEM] * 6,
        out_shape=[in_vmem(face_shape, bf16)] * 2
        + [in_vmem(long_shape, bf16), in_vmem(face_shape, bf16)]
        + [in_vmem((2,) + face_shape, bf16), blocks(half)],
        scratch_shapes=[pltpu.VMEM((COARSE_DEV * count, LANES), f32)],
        compiler_params=params(12),
    )(slots, visc, owners, base_y, base_z, cross_y, pair_x, cross_v, to_xa, to_xb, map_v)
    rya = first_swap(to_ya, "sy")
    ryb = second_swap(to_yb, "sy")
    applied = pl.pallas_call(
        apply_z_kernel,
        in_specs=[VMEM] * 2,
        out_specs=HBM,
        out_shape=jax.ShapeDtypeStruct(values.shape, f32),
        scratch_shapes=[
            pltpu.VMEM((subs, 2, rhs, size), f32),
            pltpu.SemaphoreType.DMA((subs,)),
        ],
        compiler_params=params(8),
        cost_estimate=LONG,
    )(to_yb, local_z)

    def apply(faces, axis, applied, *args):
        return pl.pallas_call(
            lambda *refs: apply_kernel(faces, axis, *refs),
            in_specs=[HBM] + [VMEM] * len(args),
            out_specs=HBM,
            out_shape=jax.ShapeDtypeStruct(values.shape, f32),
            input_output_aliases={0: 0},
            scratch_shapes=[pltpu.VMEM((2,) + face_shape, f32), pltpu.SemaphoreType.DMA((2, subs))],
            compiler_params=params(8),
            cost_estimate=LONG,
        )(applied, *args)

    half //= 2
    kept, give = pl.pallas_call(
        lambda *refs: first_add_kernel(subs, *refs),
        in_specs=[HBM] + [VMEM] * 2,
        out_specs=[VMEM] * 2,
        out_shape=[blocks(half)] * 2,
        compiler_params=params(4),
    )(in_hbm(applied), kept, rya)
    got = cross_swap(give, "sy", 2 * half)
    applied = apply(y_faces, "sy", applied, ya, yb, rya, ryb)
    while half > 1:
        half //= 2
        kept, give = pl.pallas_call(
            next_add_kernel,
            in_specs=[HBM] + [VMEM] * 2,
            out_specs=[VMEM] * 2,
            out_shape=[blocks(half)] * 2,
            compiler_params=params(4),
        )(in_hbm(applied), kept, got)
        got = cross_swap(give, "sy", 2 * half)
    applied = apply(x_faces, "sx", applied, xa, xb, rxa, rxb)
    coarse = pl.pallas_call(
        last_add_kernel,
        in_specs=[VMEM] * 2,
        out_specs=HBM,
        out_shape=jax.ShapeDtypeStruct((COARSE_DEV, rhs * COMPS), f32),
        scratch_shapes=[pltpu.VMEM((COARSE_DEV, rhs * COMPS), f32), pltpu.SemaphoreType.DMA],
        compiler_params=params(4),
    )(kept, got)
    return applied[None, None], coarse.T


def solution(mesh):
    return jax.shard_map(
        body,
        mesh=mesh,
        in_specs=(
            P("sx", "sy", None, None, None, None),
            P("sx", "sy", None),
            P("sx", "sy", None, None),
            P("sx", "sy", None, None),
            P(),
            P(),
            P(),
            P(),
        ),
        out_specs=(P("sx", "sy", None, None, None, None), P(None, ("sx", "sy"))),
        check_vma=False,
    )
```

```python
import jax
import jax.numpy as jnp
from jax import lax
from jax.experimental import pallas as pl
from jax.experimental.pallas import tpu as pltpu
from jax.sharding import PartitionSpec as P

CORNERS = 8
COMPS = 3
COARSE_DEV = 8
LANES = 128

VMEM = pl.BlockSpec(memory_space=pltpu.VMEM)
SMEM = pl.BlockSpec(memory_space=pltpu.SMEM)
HBM = pl.BlockSpec(memory_space=pltpu.HBM)
ANY = pl.BlockSpec(memory_space=pl.ANY)


def in_vmem(shape, dtype):
    return pltpu.VMEM(shape, dtype)


def in_hbm(value):
    return pltpu.with_memory_space_constraint(value, pltpu.HBM)


def params(mib):
    return pltpu.CompilerParams(vmem_limit_bytes=mib * 1024 * 1024)


LONG = pl.CostEstimate(flops=20 * 10**9, bytes_accessed=0, transcendentals=0)


def odd(axis):
    return lax.rem(lax.axis_index(axis), 2)


def first_swap(value, axis):
    return lax.ppermute(value, axis, [(i, i ^ 1) for i in range(lax.axis_size(axis))])


def second_swap(value, axis):
    rows, cols = lax.axis_size("sx"), lax.axis_size("sy")
    pairs = []
    for i in range(rows):
        for j in range(cols):
            if axis == "sx":
                k = i - 1 if i % 2 == 0 else i + 1
                target = (k, j) if 0 <= k < rows else (i, j ^ 1)
            else:
                k = j - 1 if j % 2 == 0 else j + 1
                target = (i, k) if 0 <= k < cols else (i ^ 2, j)
            pairs.append((i * cols + j, target[0] * cols + target[1]))
    return lax.ppermute(value, ("sx", "sy"), pairs)


def inner(axis):
    me = lax.axis_index(axis)
    return ((me > 0) & (me < lax.axis_size(axis) - 1)).astype(jnp.float32)


def x_faces():
    return odd("sx"), 1 - odd("sx")


def y_faces():
    return 2 + odd("sy"), 3 - odd("sy")


def send_kernel(traces, xa, xb, ya, yb, sems):
    faces = (*x_faces(), *y_faces())
    copies = [
        pltpu.make_async_copy(traces.at[:, face], out, sems.at[index])
        for index, (face, out) in enumerate(zip(faces, (xa, xb, ya, yb)))
    ]
    for copy in copies:
        copy.start()
    for copy in copies:
        copy.wait()


def product(left, right):
    return jnp.dot(left, right, preferred_element_type=jnp.float32)


def trade_jumps(jumps, traces, partner, axis, faces, received):
    for trade, (face, got) in enumerate(zip(faces, received)):
        for sub in range(traces.shape[0]):
            other = got[partner[sub, face]].astype(jnp.float32)
            if trade == 1:
                other = other * inner(axis)
            own = traces[sub, face].astype(jnp.float32)
            jumps[trade, sub] = (own - other).astype(jnp.bfloat16)


def flat_face(jumps, index):
    _, subs, rhs, size = jumps.shape
    return jumps[index].reshape(subs * rhs, size)


def pair_sum(jumps, first):
    up = flat_face(jumps, first).astype(jnp.float32)
    return (up + flat_face(jumps, first + 1).astype(jnp.float32)).astype(jnp.bfloat16)


def fetch_kernel(
    xa, xb, ya, traces, self_block, opposite_block, cross_block, corner_map,
    traces_out, self_out, opposite_out, cross_out, map_out, base_z, cross_z,
    map_in, jumps, sems,
):
    del xa, xb, ya
    subs, _, rhs, size = traces.shape
    rows = subs * rhs
    copies = [
        pltpu.make_async_copy(traces, traces_out, sems.at[0]),
        pltpu.make_async_copy(corner_map, map_in, sems.at[1]),
    ]
    for source, target in (
        (self_block, self_out), (opposite_block, opposite_out), (cross_block, cross_out)
    ):
        for part in range(3):
            third = pl.ds(part * (size // 3), size // 3)
            copies.append(
                pltpu.make_async_copy(source.at[third], target.at[third], sems.at[len(copies)])
            )
    for copy in copies:
        copy.start()

    copies[0].wait()
    for sub in range(subs):
        up = traces_out[sub, 4].astype(jnp.float32)
        down = traces_out[sub, 5].astype(jnp.float32)
        if sub + 1 < subs:
            up = up - traces_out[sub + 1, 5].astype(jnp.float32)
        if sub > 0:
            down = down - traces_out[sub - 1, 4].astype(jnp.float32)
        jumps[0, sub] = up.astype(jnp.bfloat16)
        jumps[1, sub] = down.astype(jnp.bfloat16)
    copies[1].wait()
    width = CORNERS * COMPS
    row = lax.broadcasted_iota(jnp.int32, (width, width), 0)
    col = lax.broadcasted_iota(jnp.int32, (width, width), 1)
    order = (col == (row % CORNERS) * COMPS + row // CORNERS).astype(jnp.float32)
    order = order.astype(jnp.bfloat16)
    for face in range(6):
        map_out[face] = product(order, map_in[face]).astype(jnp.bfloat16)
    flat = jumps[...].reshape(2 * rows, size)
    for copy in copies[2:5]:
        copy.wait()
    with_self = product(flat, self_out[...])
    for copy in copies[5:8]:
        copy.wait()
    with_opp = product(flat, opposite_out[...])
    base_z[0] = with_self[:rows] + with_opp[rows:]
    base_z[1] = with_self[rows:] + with_opp[:rows]
    for copy in copies[8:]:
        copy.wait()
    cross_z[...] = product(pair_sum(jumps, 0), cross_out[...])


def y_kernel(
    partner, traces, rya, ryb, self_block, opposite_block, cross_block, cross_z,
    base_y, cross_y, base_x, jumps,
):
    subs, _, rhs, size = traces.shape
    rows = subs * rhs
    trade_jumps(jumps, traces, partner, "sy", y_faces(), (rya, ryb))
    from_y = product(pair_sum(jumps, 0), cross_block[...])
    cross_y[...] = from_y
    base_x[...] = from_y + cross_z[...]
    flat = jumps[...].reshape(2 * rows, size)
    with_self = product(flat, self_block[...])
    with_opp = product(flat, opposite_block[...])
    base_y[0] = with_self[:rows] + with_opp[rows:] + cross_z[...]
    base_y[1] = with_self[rows:] + with_opp[:rows] + cross_z[...]


def x_kernel(
    partner, viscosity, traces, rxa, rxb, self_block, opposite_block, base_x,
    xa, xb, to_xa, to_xb, pair_x, jumps,
):
    subs, _, rhs, size = traces.shape
    rows = subs * rhs
    trade_jumps(jumps, traces, partner, "sx", x_faces(), (rxa, rxb))
    flat = jumps[...].reshape(2 * rows, size)
    with_self = product(flat, self_block[...])
    with_opp = product(flat, opposite_block[...])
    pair_x[...] = pair_sum(jumps, 0)
    for index, (face, out, to) in enumerate(zip(x_faces(), (xa, xb), (to_xa, to_xb))):
        for sub in range(subs):
            here = slice(sub * rhs, (sub + 1) * rhs)
            own = slice(index * rows + sub * rhs, index * rows + (sub + 1) * rhs)
            opp = slice((1 - index) * rows + sub * rhs, (1 - index) * rows + (sub + 1) * rhs)
            total = with_self[own] + with_opp[opp] + base_x[here]
            value = (viscosity[sub] * total).astype(jnp.bfloat16)
            out[sub] = value
            to[partner[sub, face]] = value


def high_low(value):
    high = value.astype(jnp.bfloat16).astype(jnp.float32)
    return high, value - high


def coarse_rows(partials, owners, rows):
    subs = owners.shape[0]
    width = partials.shape[1]
    rhs = width // subs
    entries = jnp.zeros((2 * CORNERS, subs * LANES), jnp.float32)
    source = lax.broadcasted_iota(jnp.int32, (width, subs * LANES), 0)
    target = lax.broadcasted_iota(jnp.int32, (width, subs * LANES), 1)
    spread = (source // rhs) * LANES + (source % rhs) * COMPS
    for comp in range(COMPS):
        part = partials[comp * CORNERS : (comp + 1) * CORNERS]
        stacked = jnp.concatenate(high_low(part), axis=0).astype(jnp.bfloat16)
        place = (target == spread + comp).astype(jnp.float32).astype(jnp.bfloat16)
        entries += product(stacked, place)
    entries = entries[:CORNERS] + entries[CORNERS:]
    total = jnp.zeros((rows, LANES), jnp.float32)
    numbers = lax.broadcasted_iota(jnp.int32, (rows, CORNERS), 0)
    for sub in range(subs):
        onehot = (numbers == owners[sub : sub + 1, :]).astype(jnp.float32).astype(jnp.bfloat16)
        for term in high_low(entries[:, sub * LANES : (sub + 1) * LANES]):
            total += product(onehot, term.astype(jnp.bfloat16))
    return total


def rest_kernel(
    partner, viscosity, owners, base_y, base_z, cross_y, pair_x, cross_block, to_xa, to_xb,
    corner_map, ya, yb, to_ya, to_yb, local_z, dense,
):
    subs, rhs, size = to_xa.shape
    rows = subs * rhs
    from_x = product(pair_x[...], cross_block[...])
    from_xy = from_x + cross_y[...]
    places = [ya, yb, local_z.at[0], local_z.at[1]]
    for index, out in enumerate(places):
        base, cross = (base_y[index], from_x) if index < 2 else (base_z[index - 2], from_xy)
        for sub in range(subs):
            here = slice(sub * rhs, (sub + 1) * rhs)
            value = (viscosity[sub] * (base[here] + cross[here])).astype(jnp.bfloat16)
            out[sub] = value
            if index < 2:
                (to_ya, to_yb)[index][partner[sub, y_faces()[index]]] = value

    partials = jnp.zeros((COMPS * CORNERS, rows), jnp.float32)
    faces = (*x_faces(), *y_faces(), 4, 5)
    for index, (face, local) in enumerate(zip(faces, (to_xa, to_xb, *places))):
        order = [partner[sub, face] if index < 2 else sub for sub in range(subs)]
        partials += lax.dot_general(
            corner_map[face],
            jnp.concatenate([local[slot] for slot in order], axis=0),
            (((1,), (1,)), ((), ())),
            preferred_element_type=jnp.float32,
        )
    total = coarse_rows(partials, owners[...], dense.shape[0] * COARSE_DEV)
    dense[...] = total.reshape(dense.shape)


def apply_z_kernel(dense, local_z, applied, held, sems):
    del dense
    subs = local_z.shape[1]
    copies = []
    for sub in range(subs):
        up = local_z[0, sub].astype(jnp.float32)
        down = local_z[1, sub].astype(jnp.float32)
        if sub + 1 < subs:
            up = up - local_z[1, sub + 1].astype(jnp.float32)
        if sub > 0:
            down = down - local_z[0, sub - 1].astype(jnp.float32)
        held[sub, 0] = up
        held[sub, 1] = down
        copies.append(
            pltpu.make_async_copy(held.at[sub], applied.at[sub, pl.ds(4, 2)], sems.at[sub])
        )
        copies[-1].start()
    for copy in copies:
        copy.wait()


def apply_faces(faces, axis, local, got, held, applied, sems):
    copies = []
    for trade in range(2):
        for sub in range(held.shape[1]):
            other = got[trade][sub].astype(jnp.float32)
            if trade == 1:
                other = other * inner(axis)
            held[trade, sub] = local[trade][sub].astype(jnp.float32) - other
            copies.append(
                pltpu.make_async_copy(
                    held.at[trade, sub], applied.at[sub, faces[trade]], sems.at[trade, sub]
                )
            )
            copies[-1].start()
    return copies


def apply_y_kernel(applied_in, ya, yb, rya, ryb, applied, held, sems):
    del applied_in
    for copy in apply_faces(y_faces(), "sy", (ya, yb), (rya, ryb), held, applied, sems):
        copy.wait()


def apply_x_kernel(
    applied_in, xa, xb, rxa, rxb, parts, applied, coarse, held, sems, sums, sum_sem
):
    del applied_in
    total = parts[0]
    for source in range(1, parts.shape[0]):
        total = total + parts[source]
    sums[...] = total[:, : sums.shape[1]]
    copies = [pltpu.make_async_copy(sums, coarse, sum_sem)]
    copies[0].start()
    copies += apply_faces(x_faces(), "sx", (xa, xb), (rxa, rxb), held, applied, sems)
    for copy in copies:
        copy.wait()


def body(
    traces, viscosity, partner, corner_owner, self_block, opposite_block, cross_block, corner_map
):
    values = in_hbm(traces[0, 0])
    slots, visc, owners = partner[0, 0], viscosity[0, 0], corner_owner[0, 0]
    subs, _, rhs, size = values.shape
    count = lax.axis_size("sy")
    rows = subs * rhs
    face_shape = (subs, rhs, size)
    block_shape = (size, size)
    map_shape = (6, CORNERS * COMPS, size)
    bf16, f32 = jnp.bfloat16, jnp.float32

    xa, xb, ya, yb = pl.pallas_call(
        send_kernel,
        in_specs=[HBM],
        out_specs=[VMEM] * 4,
        out_shape=[in_vmem(face_shape, bf16)] * 4,
        scratch_shapes=[pltpu.SemaphoreType.DMA((4,))],
        compiler_params=params(8),
    )(values)
    rxa = first_swap(xa, "sx")
    rxb = second_swap(xb, "sx")
    rya = first_swap(ya, "sy")
    ryb = second_swap(yb, "sy")
    held_traces, self_v, opposite_v, cross_v, map_v, base_z, cross_z = pl.pallas_call(
        fetch_kernel,
        in_specs=[VMEM] * 3 + [HBM] * 5,
        out_specs=[VMEM] * 7,
        out_shape=[in_vmem(values.shape, bf16)]
        + [in_vmem(block_shape, bf16)] * 3
        + [in_vmem(map_shape, bf16), in_vmem((2, rows, size), f32), in_vmem((rows, size), f32)],
        scratch_shapes=[
            pltpu.VMEM(map_shape, bf16),
            pltpu.VMEM((2,) + face_shape, bf16),
            pltpu.SemaphoreType.DMA((11,)),
        ],
        compiler_params=params(12),
        cost_estimate=LONG,
    )(
        xa,
        xb,
        ya,
        values,
        *map(in_hbm, (self_block, opposite_block, cross_block)),
        in_hbm(jnp.transpose(corner_map, (1, 0, 2))),
    )
    base_y, cross_y, base_x = pl.pallas_call(
        y_kernel,
        in_specs=[SMEM] + [VMEM] * 7,
        out_specs=[VMEM] * 3,
        out_shape=[in_vmem((2, rows, size), f32)] + [in_vmem((rows, size), f32)] * 2,
        scratch_shapes=[pltpu.VMEM((2,) + face_shape, bf16)],
        compiler_params=params(12),
    )(slots, held_traces, rya, ryb, self_v, opposite_v, cross_v, cross_z)
    xa, xb, to_xa, to_xb, pair_x = pl.pallas_call(
        x_kernel,
        in_specs=[SMEM] * 2 + [VMEM] * 6,
        out_specs=[VMEM] * 5,
        out_shape=[in_vmem(face_shape, bf16)] * 4 + [in_vmem((rows, size), bf16)],
        scratch_shapes=[pltpu.VMEM((2,) + face_shape, bf16)],
        compiler_params=params(12),
    )(slots, visc, held_traces, rxa, rxb, self_v, opposite_v, base_x)
    rxb = second_swap(to_xb, "sx")
    rxa = first_swap(to_xa, "sx")

    ya, yb, to_ya, to_yb, local_z, dense = pl.pallas_call(
        rest_kernel,
        in_specs=[SMEM] * 2 + [VMEM] * 9,
        out_specs=[VMEM] * 6,
        out_shape=[in_vmem(face_shape, bf16)] * 4
        + [in_vmem((2,) + face_shape, bf16), in_vmem((count, COARSE_DEV, LANES), f32)],
        compiler_params=params(12),
    )(slots, visc, owners, base_y, base_z, cross_y, pair_x, cross_v, to_xa, to_xb, map_v)
    parts = lax.all_to_all(dense, "sy", 0, 0, tiled=True)
    rya = first_swap(to_ya, "sy")
    ryb = second_swap(to_yb, "sy")
    applied = pl.pallas_call(
        apply_z_kernel,
        in_specs=[VMEM] * 2,
        out_specs=HBM,
        out_shape=jax.ShapeDtypeStruct(values.shape, f32),
        scratch_shapes=[
            pltpu.VMEM((subs, 2, rhs, size), f32),
            pltpu.SemaphoreType.DMA((subs,)),
        ],
        compiler_params=params(8),
        cost_estimate=LONG,
    )(dense, local_z)
    out_shape = jax.ShapeDtypeStruct(values.shape, f32)
    scratch = [pltpu.VMEM((2,) + face_shape, f32), pltpu.SemaphoreType.DMA((2, subs))]
    applied = pl.pallas_call(
        apply_y_kernel,
        in_specs=[HBM] + [VMEM] * 4,
        out_specs=HBM,
        out_shape=out_shape,
        input_output_aliases={0: 0},
        scratch_shapes=scratch,
        compiler_params=params(8),
        cost_estimate=LONG,
    )(applied, ya, yb, rya, ryb)
    applied, coarse = pl.pallas_call(
        apply_x_kernel,
        in_specs=[HBM] + [VMEM] * 5,
        out_specs=[HBM, HBM],
        out_shape=[out_shape, jax.ShapeDtypeStruct((COARSE_DEV, rhs * COMPS), f32)],
        input_output_aliases={0: 0},
        scratch_shapes=scratch
        + [pltpu.VMEM((COARSE_DEV, rhs * COMPS), f32), pltpu.SemaphoreType.DMA],
        compiler_params=params(8),
    )(applied, xa, xb, rxa, rxb, parts)
    return applied[None, None], coarse.T


def solution(mesh):
    return jax.shard_map(
        body,
        mesh=mesh,
        in_specs=(
            P("sx", "sy", None, None, None, None),
            P("sx", "sy", None),
            P("sx", "sy", None, None),
            P("sx", "sy", None, None),
            P(),
            P(),
            P(),
            P(),
        ),
        out_specs=(P("sx", "sy", None, None, None, None), P(None, ("sx", "sy"))),
        check_vma=False,
    )
```

```python
import jax
import jax.numpy as jnp
from jax import lax
from jax.experimental import pallas as pl
from jax.experimental.pallas import tpu as pltpu
from jax.sharding import PartitionSpec as P

CORNERS = 8
COMPS = 3
COARSE_DEV = 8
LANES = 128

VMEM = pl.BlockSpec(memory_space=pltpu.VMEM)
SMEM = pl.BlockSpec(memory_space=pltpu.SMEM)
HBM = pl.BlockSpec(memory_space=pltpu.HBM)
ANY = pl.BlockSpec(memory_space=pl.ANY)


def in_vmem(shape, dtype):
    return pltpu.VMEM(shape, dtype)


def in_hbm(value):
    return pltpu.with_memory_space_constraint(value, pltpu.HBM)


def params(mib):
    return pltpu.CompilerParams(vmem_limit_bytes=mib * 1024 * 1024)


LONG = pl.CostEstimate(flops=20 * 10**9, bytes_accessed=0, transcendentals=0)


def odd(axis):
    return lax.rem(lax.axis_index(axis), 2)


def first_swap(value, axis):
    return lax.ppermute(value, axis, [(i, i ^ 1) for i in range(lax.axis_size(axis))])


def second_swap(value, axis):
    rows, cols = lax.axis_size("sx"), lax.axis_size("sy")
    pairs = []
    for i in range(rows):
        for j in range(cols):
            if axis == "sx":
                k = i - 1 if i % 2 == 0 else i + 1
                target = (k, j) if 0 <= k < rows else (i, j ^ 1)
            else:
                k = j - 1 if j % 2 == 0 else j + 1
                target = (i, k) if 0 <= k < cols else (i ^ 2, j)
            pairs.append((i * cols + j, target[0] * cols + target[1]))
    return lax.ppermute(value, ("sx", "sy"), pairs)


def inner(axis):
    me = lax.axis_index(axis)
    return ((me > 0) & (me < lax.axis_size(axis) - 1)).astype(jnp.float32)


def x_faces():
    return odd("sx"), 1 - odd("sx")


def y_faces():
    return 2 + odd("sy"), 3 - odd("sy")


def send_kernel(traces, xa, xb, ya, yb, sems):
    faces = (*x_faces(), *y_faces())
    copies = [
        pltpu.make_async_copy(traces.at[:, face], out, sems.at[index])
        for index, (face, out) in enumerate(zip(faces, (xa, xb, ya, yb)))
    ]
    for copy in copies:
        copy.start()
    for copy in copies:
        copy.wait()


def product(left, right):
    return jnp.dot(left, right, preferred_element_type=jnp.float32)


def trade_jumps(jumps, traces, partner, axis, faces, received):
    for trade, (face, got) in enumerate(zip(faces, received)):
        for sub in range(traces.shape[0]):
            other = got[partner[sub, face]].astype(jnp.float32)
            if trade == 1:
                other = other * inner(axis)
            own = traces[sub, face].astype(jnp.float32)
            jumps[trade, sub] = (own - other).astype(jnp.bfloat16)


def flat_face(jumps, index):
    _, subs, rhs, size = jumps.shape
    return jumps[index].reshape(subs * rhs, size)


def pair_sum(jumps, first):
    up = flat_face(jumps, first).astype(jnp.float32)
    return (up + flat_face(jumps, first + 1).astype(jnp.float32)).astype(jnp.bfloat16)


def fetch_kernel(
    xa, xb, ya, traces, self_block, opposite_block, cross_block, corner_map,
    traces_out, self_out, opposite_out, cross_out, map_out, base_z, cross_z,
    map_in, jumps, sems,
):
    del xa, xb, ya
    subs, _, rhs, size = traces.shape
    rows = subs * rhs
    copies = [
        pltpu.make_async_copy(traces, traces_out, sems.at[0]),
        pltpu.make_async_copy(corner_map, map_in, sems.at[1]),
    ]
    for source, target in (
        (self_block, self_out), (opposite_block, opposite_out), (cross_block, cross_out)
    ):
        for part in range(3):
            third = pl.ds(part * (size // 3), size // 3)
            copies.append(
                pltpu.make_async_copy(source.at[third], target.at[third], sems.at[len(copies)])
            )
    for copy in copies:
        copy.start()

    copies[0].wait()
    for sub in range(subs):
        up = traces_out[sub, 4].astype(jnp.float32)
        down = traces_out[sub, 5].astype(jnp.float32)
        if sub + 1 < subs:
            up = up - traces_out[sub + 1, 5].astype(jnp.float32)
        if sub > 0:
            down = down - traces_out[sub - 1, 4].astype(jnp.float32)
        jumps[0, sub] = up.astype(jnp.bfloat16)
        jumps[1, sub] = down.astype(jnp.bfloat16)
    copies[1].wait()
    width = CORNERS * COMPS
    row = lax.broadcasted_iota(jnp.int32, (width, width), 0)
    col = lax.broadcasted_iota(jnp.int32, (width, width), 1)
    order = (col == (row % CORNERS) * COMPS + row // CORNERS).astype(jnp.float32)
    order = order.astype(jnp.bfloat16)
    for face in range(6):
        map_out[face] = product(order, map_in[face]).astype(jnp.bfloat16)
    flat = jumps[...].reshape(2 * rows, size)
    for copy in copies[2:5]:
        copy.wait()
    with_self = product(flat, self_out[...])
    for copy in copies[5:8]:
        copy.wait()
    with_opp = product(flat, opposite_out[...])
    base_z[0] = with_self[:rows] + with_opp[rows:]
    base_z[1] = with_self[rows:] + with_opp[:rows]
    for copy in copies[8:]:
        copy.wait()
    cross_z[...] = product(pair_sum(jumps, 0), cross_out[...])


def y_kernel(
    partner, traces, rya, ryb, self_block, opposite_block, cross_block, cross_z,
    base_y, cross_y, base_x, jumps,
):
    subs, _, rhs, size = traces.shape
    rows = subs * rhs
    trade_jumps(jumps, traces, partner, "sy", y_faces(), (rya, ryb))
    from_y = product(pair_sum(jumps, 0), cross_block[...])
    cross_y[...] = from_y
    base_x[...] = from_y + cross_z[...]
    flat = jumps[...].reshape(2 * rows, size)
    with_self = product(flat, self_block[...])
    with_opp = product(flat, opposite_block[...])
    base_y[0] = with_self[:rows] + with_opp[rows:] + cross_z[...]
    base_y[1] = with_self[rows:] + with_opp[:rows] + cross_z[...]


def x_kernel(
    partner, viscosity, traces, rxa, rxb, self_block, opposite_block, base_x,
    xa, xb, to_xa, to_xb, pair_x, jumps,
):
    subs, _, rhs, size = traces.shape
    rows = subs * rhs
    trade_jumps(jumps, traces, partner, "sx", x_faces(), (rxa, rxb))
    flat = jumps[...].reshape(2 * rows, size)
    with_self = product(flat, self_block[...])
    with_opp = product(flat, opposite_block[...])
    pair_x[...] = pair_sum(jumps, 0)
    for index, (face, out, to) in enumerate(zip(x_faces(), (xa, xb), (to_xa, to_xb))):
        for sub in range(subs):
            here = slice(sub * rhs, (sub + 1) * rhs)
            own = slice(index * rows + sub * rhs, index * rows + (sub + 1) * rhs)
            opp = slice((1 - index) * rows + sub * rhs, (1 - index) * rows + (sub + 1) * rhs)
            total = with_self[own] + with_opp[opp] + base_x[here]
            value = (viscosity[sub] * total).astype(jnp.bfloat16)
            out[sub] = value
            to[partner[sub, face]] = value


def high_low(value):
    high = value.astype(jnp.bfloat16).astype(jnp.float32)
    return high, value - high


def coarse_rows(partials, owners, rows):
    subs = owners.shape[0]
    width = partials.shape[1]
    rhs = width // subs
    entries = jnp.zeros((2 * CORNERS, subs * LANES), jnp.float32)
    source = lax.broadcasted_iota(jnp.int32, (width, subs * LANES), 0)
    target = lax.broadcasted_iota(jnp.int32, (width, subs * LANES), 1)
    spread = (source // rhs) * LANES + (source % rhs) * COMPS
    for comp in range(COMPS):
        part = partials[comp * CORNERS : (comp + 1) * CORNERS]
        stacked = jnp.concatenate(high_low(part), axis=0).astype(jnp.bfloat16)
        place = (target == spread + comp).astype(jnp.float32).astype(jnp.bfloat16)
        entries += product(stacked, place)
    entries = entries[:CORNERS] + entries[CORNERS:]
    total = jnp.zeros((rows, LANES), jnp.float32)
    numbers = lax.broadcasted_iota(jnp.int32, (rows, CORNERS), 0)
    for sub in range(subs):
        onehot = (numbers == owners[sub : sub + 1, :]).astype(jnp.float32).astype(jnp.bfloat16)
        for term in high_low(entries[:, sub * LANES : (sub + 1) * LANES]):
            total += product(onehot, term.astype(jnp.bfloat16))
    return total


def rest_kernel(
    partner, viscosity, base_y, base_z, cross_y, pair_x, cross_block, to_xa, to_xb,
    ya, yb, to_ya, to_yb, local_z,
):
    del to_xa, to_xb
    subs, rhs, _ = ya.shape
    from_x = product(pair_x[...], cross_block[...])
    from_xy = from_x + cross_y[...]
    for index, out in enumerate((ya, yb, local_z.at[0], local_z.at[1])):
        base, cross = (base_y[index], from_x) if index < 2 else (base_z[index - 2], from_xy)
        for sub in range(subs):
            here = slice(sub * rhs, (sub + 1) * rhs)
            value = (viscosity[sub] * (base[here] + cross[here])).astype(jnp.bfloat16)
            out[sub] = value
            if index < 2:
                (to_ya, to_yb)[index][partner[sub, y_faces()[index]]] = value


def coarse_kernel(partner, owners, corner_map, to_xa, to_xb, to_ya, to_yb, local_z, dense):
    subs, rhs, _ = to_xa.shape
    partials = jnp.zeros((COMPS * CORNERS, subs * rhs), jnp.float32)
    faces = (*x_faces(), *y_faces(), 4, 5)
    places = (to_xa, to_xb, to_ya, to_yb, local_z.at[0], local_z.at[1])
    for index, (face, local) in enumerate(zip(faces, places)):
        order = [partner[sub, face] if index < 4 else sub for sub in range(subs)]
        partials += lax.dot_general(
            corner_map[face],
            jnp.concatenate([local[slot] for slot in order], axis=0),
            (((1,), (1,)), ((), ())),
            preferred_element_type=jnp.float32,
        )
    total = coarse_rows(partials, owners[...], dense.shape[0] * COARSE_DEV)
    dense[...] = total.reshape(dense.shape)


def apply_kernel(
    local_z, ya, yb, rya, ryb, xa, xb, rxa, rxb, parts, applied, coarse, held, sums, sems, sum_sem
):
    total = parts[0]
    for source in range(1, parts.shape[0]):
        total = total + parts[source]
    sums[...] = total[:, : sums.shape[1]]
    copies = [pltpu.make_async_copy(sums, coarse, sum_sem)]
    copies[0].start()

    def write(index, sub, face, value):
        held[index, sub] = value
        copies.append(
            pltpu.make_async_copy(held.at[index, sub], applied.at[sub, face], sems.at[index, sub])
        )
        copies[-1].start()

    subs = held.shape[1]
    for sub in range(subs):
        up = local_z[0, sub].astype(jnp.float32)
        down = local_z[1, sub].astype(jnp.float32)
        if sub + 1 < subs:
            up = up - local_z[1, sub + 1].astype(jnp.float32)
        if sub > 0:
            down = down - local_z[0, sub - 1].astype(jnp.float32)
        write(4, sub, 4, up)
        write(5, sub, 5, down)
    trades = zip((*y_faces(), *x_faces()), (ya, yb, xa, xb), (rya, ryb, rxa, rxb))
    for index, (face, local, got) in enumerate(trades):
        for sub in range(subs):
            other = got[sub].astype(jnp.float32)
            if index == 1:
                other = other * inner("sy")
            if index == 3:
                other = other * inner("sx")
            write(index, sub, face, local[sub].astype(jnp.float32) - other)
    for copy in copies:
        copy.wait()


def body(
    traces, viscosity, partner, corner_owner, self_block, opposite_block, cross_block, corner_map
):
    values = in_hbm(traces[0, 0])
    slots, visc, owners = partner[0, 0], viscosity[0, 0], corner_owner[0, 0]
    subs, _, rhs, size = values.shape
    count = lax.axis_size("sy")
    rows = subs * rhs
    face_shape = (subs, rhs, size)
    block_shape = (size, size)
    map_shape = (6, CORNERS * COMPS, size)
    bf16, f32 = jnp.bfloat16, jnp.float32

    xa, xb, ya, yb = pl.pallas_call(
        send_kernel,
        in_specs=[HBM],
        out_specs=[VMEM] * 4,
        out_shape=[in_vmem(face_shape, bf16)] * 4,
        scratch_shapes=[pltpu.SemaphoreType.DMA((4,))],
        compiler_params=params(8),
    )(values)
    rxa = first_swap(xa, "sx")
    rxb = second_swap(xb, "sx")
    rya = first_swap(ya, "sy")
    ryb = second_swap(yb, "sy")
    held_traces, self_v, opposite_v, cross_v, map_v, base_z, cross_z = pl.pallas_call(
        fetch_kernel,
        in_specs=[VMEM] * 3 + [HBM] * 5,
        out_specs=[VMEM] * 7,
        out_shape=[in_vmem(values.shape, bf16)]
        + [in_vmem(block_shape, bf16)] * 3
        + [in_vmem(map_shape, bf16), in_vmem((2, rows, size), f32), in_vmem((rows, size), f32)],
        scratch_shapes=[
            pltpu.VMEM(map_shape, bf16),
            pltpu.VMEM((2,) + face_shape, bf16),
            pltpu.SemaphoreType.DMA((11,)),
        ],
        compiler_params=params(12),
        cost_estimate=LONG,
    )(
        xa,
        xb,
        ya,
        values,
        *map(in_hbm, (self_block, opposite_block, cross_block)),
        in_hbm(jnp.transpose(corner_map, (1, 0, 2))),
    )
    base_y, cross_y, base_x = pl.pallas_call(
        y_kernel,
        in_specs=[SMEM] + [VMEM] * 7,
        out_specs=[VMEM] * 3,
        out_shape=[in_vmem((2, rows, size), f32)] + [in_vmem((rows, size), f32)] * 2,
        scratch_shapes=[pltpu.VMEM((2,) + face_shape, bf16)],
        compiler_params=params(12),
    )(slots, held_traces, rya, ryb, self_v, opposite_v, cross_v, cross_z)
    xa, xb, to_xa, to_xb, pair_x = pl.pallas_call(
        x_kernel,
        in_specs=[SMEM] * 2 + [VMEM] * 6,
        out_specs=[VMEM] * 5,
        out_shape=[in_vmem(face_shape, bf16)] * 4 + [in_vmem((rows, size), bf16)],
        scratch_shapes=[pltpu.VMEM((2,) + face_shape, bf16)],
        compiler_params=params(12),
    )(slots, visc, held_traces, rxa, rxb, self_v, opposite_v, base_x)
    rxb = second_swap(to_xb, "sx")
    rxa = first_swap(to_xa, "sx")

    ya, yb, to_ya, to_yb, local_z = pl.pallas_call(
        rest_kernel,
        in_specs=[SMEM] * 2 + [VMEM] * 7,
        out_specs=[VMEM] * 5,
        out_shape=[in_vmem(face_shape, bf16)] * 4 + [in_vmem((2,) + face_shape, bf16)],
        compiler_params=params(8),
    )(slots, visc, base_y, base_z, cross_y, pair_x, cross_v, to_xa, to_xb)
    rya = first_swap(to_ya, "sy")
    ryb = second_swap(to_yb, "sy")
    dense = pl.pallas_call(
        coarse_kernel,
        in_specs=[SMEM] + [VMEM] * 7,
        out_specs=VMEM,
        out_shape=in_vmem((count, COARSE_DEV, LANES), f32),
        compiler_params=params(8),
    )(slots, owners, map_v, to_xa, to_xb, to_ya, to_yb, local_z)
    parts = lax.all_to_all(dense, "sy", 0, 0, tiled=True)
    applied, coarse = pl.pallas_call(
        apply_kernel,
        in_specs=[VMEM] * 10,
        out_specs=[HBM] * 2,
        out_shape=[
            jax.ShapeDtypeStruct(values.shape, f32),
            jax.ShapeDtypeStruct((COARSE_DEV, rhs * COMPS), f32),
        ],
        scratch_shapes=[
            pltpu.VMEM((6,) + face_shape, f32),
            pltpu.VMEM((COARSE_DEV, rhs * COMPS), f32),
            pltpu.SemaphoreType.DMA((6, subs)),
            pltpu.SemaphoreType.DMA,
        ],
        compiler_params=params(12),
    )(local_z, ya, yb, rya, ryb, xa, xb, rxa, rxb, parts)
    return applied[None, None], coarse.T


def solution(mesh):
    return jax.shard_map(
        body,
        mesh=mesh,
        in_specs=(
            P("sx", "sy", None, None, None, None),
            P("sx", "sy", None),
            P("sx", "sy", None, None),
            P("sx", "sy", None, None),
            P(),
            P(),
            P(),
            P(),
        ),
        out_specs=(P("sx", "sy", None, None, None, None), P(None, ("sx", "sy"))),
        check_vma=False,
    )
```

```python
import jax
import jax.numpy as jnp
from jax import lax
from jax.experimental import pallas as pl
from jax.experimental.pallas import tpu as pltpu
from jax.sharding import PartitionSpec as P

CORNERS = 8
COMPS = 3
COARSE_DEV = 8
LANES = 128

VMEM = pl.BlockSpec(memory_space=pltpu.VMEM)
SMEM = pl.BlockSpec(memory_space=pltpu.SMEM)
HBM = pl.BlockSpec(memory_space=pltpu.HBM)
ANY = pl.BlockSpec(memory_space=pl.ANY)


def in_vmem(shape, dtype):
    return pltpu.VMEM(shape, dtype)


def in_hbm(value):
    return pltpu.with_memory_space_constraint(value, pltpu.HBM)


def params(mib):
    return pltpu.CompilerParams(vmem_limit_bytes=mib * 1024 * 1024)


LONG = pl.CostEstimate(flops=20 * 10**9, bytes_accessed=0, transcendentals=0)


def odd(axis):
    return lax.rem(lax.axis_index(axis), 2)


def first_swap(value, axis):
    return lax.ppermute(value, axis, [(i, i ^ 1) for i in range(lax.axis_size(axis))])


def second_swap(value, axis):
    rows, cols = lax.axis_size("sx"), lax.axis_size("sy")
    pairs = []
    for i in range(rows):
        for j in range(cols):
            if axis == "sx":
                k = i - 1 if i % 2 == 0 else i + 1
                target = (k, j) if 0 <= k < rows else (i, j ^ 1)
            else:
                k = j - 1 if j % 2 == 0 else j + 1
                target = (i, k) if 0 <= k < cols else (i ^ 2, j)
            pairs.append((i * cols + j, target[0] * cols + target[1]))
    return lax.ppermute(value, ("sx", "sy"), pairs)


def inner(axis):
    me = lax.axis_index(axis)
    return ((me > 0) & (me < lax.axis_size(axis) - 1)).astype(jnp.float32)


def x_faces():
    return odd("sx"), 1 - odd("sx")


def y_faces():
    return 2 + odd("sy"), 3 - odd("sy")


def send_kernel(traces, xa, xb, ya, yb, sems):
    faces = (*x_faces(), *y_faces())
    copies = [
        pltpu.make_async_copy(traces.at[:, face], out, sems.at[index])
        for index, (face, out) in enumerate(zip(faces, (xa, xb, ya, yb)))
    ]
    for copy in copies:
        copy.start()
    for copy in copies:
        copy.wait()


def product(left, right):
    return jnp.dot(left, right, preferred_element_type=jnp.float32)


def trade_jumps(jumps, traces, partner, axis, faces, received):
    for trade, (face, got) in enumerate(zip(faces, received)):
        for sub in range(traces.shape[0]):
            other = got[partner[sub, face]].astype(jnp.float32)
            if trade == 1:
                other = other * inner(axis)
            own = traces[sub, face].astype(jnp.float32)
            jumps[trade, sub] = (own - other).astype(jnp.bfloat16)


def flat_face(jumps, index):
    _, subs, rhs, size = jumps.shape
    return jumps[index].reshape(subs * rhs, size)


def pair_sum(jumps, first):
    up = flat_face(jumps, first).astype(jnp.float32)
    return (up + flat_face(jumps, first + 1).astype(jnp.float32)).astype(jnp.bfloat16)


def z_kernel(
    xa, xb, ya, traces, self_block, opposite_block, cross_block, corner_map,
    map_out, base_z, cross_z, jumps,
):
    del xa, xb, ya
    subs, _, rhs, size = traces.shape
    rows = subs * rhs
    for sub in range(subs):
        up = traces[sub, 4].astype(jnp.float32)
        down = traces[sub, 5].astype(jnp.float32)
        if sub + 1 < subs:
            up = up - traces[sub + 1, 5].astype(jnp.float32)
        if sub > 0:
            down = down - traces[sub - 1, 4].astype(jnp.float32)
        jumps[0, sub] = up.astype(jnp.bfloat16)
        jumps[1, sub] = down.astype(jnp.bfloat16)
    width = CORNERS * COMPS
    row = lax.broadcasted_iota(jnp.int32, (width, width), 0)
    col = lax.broadcasted_iota(jnp.int32, (width, width), 1)
    order = (col == (row % CORNERS) * COMPS + row // CORNERS).astype(jnp.float32)
    order = order.astype(jnp.bfloat16)
    for face in range(6):
        map_out[face] = product(order, corner_map[face]).astype(jnp.bfloat16)
    flat = jumps[...].reshape(2 * rows, size)
    with_self = product(flat, self_block[...])
    with_opp = product(flat, opposite_block[...])
    base_z[0] = with_self[:rows] + with_opp[rows:]
    base_z[1] = with_self[rows:] + with_opp[:rows]
    cross_z[...] = product(pair_sum(jumps, 0), cross_block[...])


def y_kernel(
    partner, traces, rya, ryb, self_block, opposite_block, cross_block, cross_z,
    base_y, cross_y, base_x, jumps,
):
    subs, _, rhs, size = traces.shape
    rows = subs * rhs
    trade_jumps(jumps, traces, partner, "sy", y_faces(), (rya, ryb))
    from_y = product(pair_sum(jumps, 0), cross_block[...])
    cross_y[...] = from_y
    base_x[...] = from_y + cross_z[...]
    flat = jumps[...].reshape(2 * rows, size)
    with_self = product(flat, self_block[...])
    with_opp = product(flat, opposite_block[...])
    base_y[0] = with_self[:rows] + with_opp[rows:] + cross_z[...]
    base_y[1] = with_self[rows:] + with_opp[:rows] + cross_z[...]


def high_low(value):
    high = value.astype(jnp.bfloat16).astype(jnp.float32)
    return high, value - high


def coarse_rows(partials, owners, rows):
    subs = owners.shape[0]
    width = partials.shape[1]
    rhs = width // subs
    entries = jnp.zeros((2 * CORNERS, subs * LANES), jnp.float32)
    source = lax.broadcasted_iota(jnp.int32, (width, subs * LANES), 0)
    target = lax.broadcasted_iota(jnp.int32, (width, subs * LANES), 1)
    spread = (source // rhs) * LANES + (source % rhs) * COMPS
    for comp in range(COMPS):
        part = partials[comp * CORNERS : (comp + 1) * CORNERS]
        stacked = jnp.concatenate(high_low(part), axis=0).astype(jnp.bfloat16)
        place = (target == spread + comp).astype(jnp.float32).astype(jnp.bfloat16)
        entries += product(stacked, place)
    entries = entries[:CORNERS] + entries[CORNERS:]
    total = jnp.zeros((rows, LANES), jnp.float32)
    numbers = lax.broadcasted_iota(jnp.int32, (rows, CORNERS), 0)
    for sub in range(subs):
        onehot = (numbers == owners[sub : sub + 1, :]).astype(jnp.float32).astype(jnp.bfloat16)
        for term in high_low(entries[:, sub * LANES : (sub + 1) * LANES]):
            total += product(onehot, term.astype(jnp.bfloat16))
    return total


def local_kernel(
    partner, viscosity, traces, rxa, rxb, self_block, opposite_block, cross_block,
    base_x, base_y, base_z, cross_y, owners, corner_map,
    xa, xb, ya, yb, local_z, to_xa, to_xb, to_ya, to_yb, dense, jumps,
):
    subs, _, rhs, size = traces.shape
    rows = subs * rhs
    trade_jumps(jumps, traces, partner, "sx", x_faces(), (rxa, rxb))
    flat = jumps[...].reshape(2 * rows, size)
    with_self = product(flat, self_block[...])
    with_opp = product(flat, opposite_block[...])
    from_x = product(pair_sum(jumps, 0), cross_block[...])
    from_xy = from_x + cross_y[...]
    totals = (
        with_self[:rows] + with_opp[rows:] + base_x[...],
        with_self[rows:] + with_opp[:rows] + base_x[...],
        base_y[0] + from_x,
        base_y[1] + from_x,
        base_z[0] + from_xy,
        base_z[1] + from_xy,
    )
    faces = (*x_faces(), *y_faces(), 4, 5)
    outs = (xa, xb, ya, yb, local_z.at[0], local_z.at[1])
    sent = (to_xa, to_xb, to_ya, to_yb)
    partials = jnp.zeros((COMPS * CORNERS, rows), jnp.float32)
    for index, (face, total, out) in enumerate(zip(faces, totals, outs)):
        for sub in range(subs):
            here = slice(sub * rhs, (sub + 1) * rhs)
            value = (viscosity[sub] * total[here]).astype(jnp.bfloat16)
            out[sub] = value
            if index < 4:
                sent[index][partner[sub, face]] = value
        partials += lax.dot_general(
            corner_map[face],
            out[...].reshape(rows, size),
            (((1,), (1,)), ((), ())),
            preferred_element_type=jnp.float32,
        )
    total = coarse_rows(partials, owners[...], dense.shape[0] * COARSE_DEV)
    dense[...] = total.reshape(dense.shape)


def apply_z_kernel(to_xa, to_xb, to_ya, to_yb, local_z, applied, held, sems):
    del to_xa, to_xb, to_ya, to_yb
    subs = local_z.shape[1]
    copies = []
    for sub in range(subs):
        up = local_z[0, sub].astype(jnp.float32)
        down = local_z[1, sub].astype(jnp.float32)
        if sub + 1 < subs:
            up = up - local_z[1, sub + 1].astype(jnp.float32)
        if sub > 0:
            down = down - local_z[0, sub - 1].astype(jnp.float32)
        held[sub, 0] = up
        held[sub, 1] = down
        copies.append(
            pltpu.make_async_copy(held.at[sub], applied.at[sub, pl.ds(4, 2)], sems.at[sub])
        )
        copies[-1].start()
    for copy in copies:
        copy.wait()


def apply_kernel(
    applied_in, ya, yb, rya, ryb, xa, xb, rxa, rxb, parts, applied, coarse, held, sums, sems, sum_sem
):
    del applied_in
    total = parts[0]
    for source in range(1, parts.shape[0]):
        total = total + parts[source]
    sums[...] = total[:, : sums.shape[1]]
    copies = [pltpu.make_async_copy(sums, coarse, sum_sem)]
    copies[0].start()
    trades = zip((*y_faces(), *x_faces()), (ya, yb, xa, xb), (rya, ryb, rxa, rxb))
    for index, (face, local, got) in enumerate(trades):
        for sub in range(held.shape[1]):
            other = got[sub].astype(jnp.float32)
            if index == 1:
                other = other * inner("sy")
            if index == 3:
                other = other * inner("sx")
            held[index, sub] = local[sub].astype(jnp.float32) - other
            copies.append(
                pltpu.make_async_copy(
                    held.at[index, sub], applied.at[sub, face], sems.at[index, sub]
                )
            )
            copies[-1].start()
    for copy in copies:
        copy.wait()


def body(
    traces, viscosity, partner, corner_owner, self_block, opposite_block, cross_block, corner_map
):
    values = traces[0, 0]
    slots, visc, owners = partner[0, 0], viscosity[0, 0], corner_owner[0, 0]
    subs, _, rhs, size = values.shape
    count = lax.axis_size("sy")
    rows = subs * rhs
    face_shape = (subs, rhs, size)
    map_shape = (6, CORNERS * COMPS, size)
    bf16, f32 = jnp.bfloat16, jnp.float32

    xa, xb, ya, yb = pl.pallas_call(
        send_kernel,
        in_specs=[HBM],
        out_specs=[VMEM] * 4,
        out_shape=[in_vmem(face_shape, bf16)] * 4,
        scratch_shapes=[pltpu.SemaphoreType.DMA((4,))],
        compiler_params=params(8),
        cost_estimate=LONG,
    )(in_hbm(values))
    rxa = first_swap(xa, "sx")
    rxb = second_swap(xb, "sx")
    rya = first_swap(ya, "sy")
    ryb = second_swap(yb, "sy")
    map_v, base_z, cross_z = pl.pallas_call(
        z_kernel,
        in_specs=[VMEM] * 8,
        out_specs=[VMEM] * 3,
        out_shape=[in_vmem(map_shape, bf16), in_vmem((2, rows, size), f32)]
        + [in_vmem((rows, size), f32)],
        scratch_shapes=[pltpu.VMEM((2,) + face_shape, bf16)],
        compiler_params=params(12),
        cost_estimate=LONG,
    )(
        xa, xb, ya, values, self_block, opposite_block, cross_block,
        jnp.transpose(corner_map, (1, 0, 2)),
    )
    base_y, cross_y, base_x = pl.pallas_call(
        y_kernel,
        in_specs=[SMEM] + [VMEM] * 7,
        out_specs=[VMEM] * 3,
        out_shape=[in_vmem((2, rows, size), f32)] + [in_vmem((rows, size), f32)] * 2,
        scratch_shapes=[pltpu.VMEM((2,) + face_shape, bf16)],
        compiler_params=params(12),
    )(slots, values, rya, ryb, self_block, opposite_block, cross_block, cross_z)
    xa, xb, ya, yb, local_z, to_xa, to_xb, to_ya, to_yb, dense = pl.pallas_call(
        local_kernel,
        in_specs=[SMEM] * 2 + [VMEM] * 12,
        out_specs=[VMEM] * 10,
        out_shape=[in_vmem(face_shape, bf16)] * 4
        + [in_vmem((2,) + face_shape, bf16)]
        + [in_vmem(face_shape, bf16)] * 4
        + [in_vmem((count, COARSE_DEV, LANES), f32)],
        scratch_shapes=[pltpu.VMEM((2,) + face_shape, bf16)],
        compiler_params=params(16),
    )(
        slots, visc, values, rxa, rxb, self_block, opposite_block, cross_block,
        base_x, base_y, base_z, cross_y, owners, map_v,
    )
    parts = lax.all_to_all(dense, "sy", 0, 0, tiled=True)
    rxa = first_swap(to_xa, "sx")
    rxb = second_swap(to_xb, "sx")
    rya = first_swap(to_ya, "sy")
    ryb = second_swap(to_yb, "sy")
    out_shape = jax.ShapeDtypeStruct(values.shape, f32)
    applied = pl.pallas_call(
        apply_z_kernel,
        in_specs=[VMEM] * 5,
        out_specs=HBM,
        out_shape=out_shape,
        scratch_shapes=[
            pltpu.VMEM((subs, 2, rhs, size), f32),
            pltpu.SemaphoreType.DMA((subs,)),
        ],
        compiler_params=params(8),
        cost_estimate=LONG,
    )(to_xa, to_xb, to_ya, to_yb, local_z)
    applied, coarse = pl.pallas_call(
        apply_kernel,
        in_specs=[HBM] + [VMEM] * 9,
        out_specs=[HBM] * 2,
        out_shape=[out_shape, jax.ShapeDtypeStruct((COARSE_DEV, rhs * COMPS), f32)],
        input_output_aliases={0: 0},
        scratch_shapes=[
            pltpu.VMEM((4,) + face_shape, f32),
            pltpu.VMEM((COARSE_DEV, rhs * COMPS), f32),
            pltpu.SemaphoreType.DMA((4, subs)),
            pltpu.SemaphoreType.DMA,
        ],
        compiler_params=params(12),
    )(applied, ya, yb, rya, ryb, xa, xb, rxa, rxb, parts)
    return applied[None, None], coarse.T


def solution(mesh):
    return jax.shard_map(
        body,
        mesh=mesh,
        in_specs=(
            P("sx", "sy", None, None, None, None),
            P("sx", "sy", None),
            P("sx", "sy", None, None),
            P("sx", "sy", None, None),
            P(),
            P(),
            P(),
            P(),
        ),
        out_specs=(P("sx", "sy", None, None, None, None), P(None, ("sx", "sy"))),
        check_vma=False,
    )
```

```python
import jax
import jax.numpy as jnp
from jax import lax
from jax.experimental import pallas as pl
from jax.experimental.pallas import tpu as pltpu
from jax.sharding import PartitionSpec as P

CORNERS = 8
COMPS = 3
COARSE_DEV = 8
LANES = 128

VMEM = pl.BlockSpec(memory_space=pltpu.VMEM)
SMEM = pl.BlockSpec(memory_space=pltpu.SMEM)
HBM = pl.BlockSpec(memory_space=pltpu.HBM)
ANY = pl.BlockSpec(memory_space=pl.ANY)


def in_vmem(shape, dtype):
    return pltpu.VMEM(shape, dtype)


def in_hbm(value):
    return pltpu.with_memory_space_constraint(value, pltpu.HBM)


def params(mib):
    return pltpu.CompilerParams(vmem_limit_bytes=mib * 1024 * 1024)


LONG = pl.CostEstimate(flops=20 * 10**9, bytes_accessed=0, transcendentals=0)


def odd(axis):
    return lax.rem(lax.axis_index(axis), 2)


def first_swap(value, axis):
    return lax.ppermute(value, axis, [(i, i ^ 1) for i in range(lax.axis_size(axis))])


def second_swap(value, axis):
    rows, cols = lax.axis_size("sx"), lax.axis_size("sy")
    pairs = []
    for i in range(rows):
        for j in range(cols):
            if axis == "sx":
                k = i - 1 if i % 2 == 0 else i + 1
                target = (k, j) if 0 <= k < rows else (i, j ^ 1)
            else:
                k = j - 1 if j % 2 == 0 else j + 1
                target = (i, k) if 0 <= k < cols else (i ^ 2, j)
            pairs.append((i * cols + j, target[0] * cols + target[1]))
    return lax.ppermute(value, ("sx", "sy"), pairs)


def inner(axis):
    me = lax.axis_index(axis)
    return ((me > 0) & (me < lax.axis_size(axis) - 1)).astype(jnp.float32)


def x_faces():
    return odd("sx"), 1 - odd("sx")


def y_faces():
    return 2 + odd("sy"), 3 - odd("sy")


def send_kernel(traces, xb, yb, xa, ya, sems):
    faces = (*x_faces(), *y_faces())
    copies = [
        pltpu.make_async_copy(traces.at[:, face], out, sems.at[index])
        for index, (face, out) in enumerate(zip(faces, (xa, xb, ya, yb)))
    ]
    for copy in copies:
        copy.start()
    for copy in copies:
        copy.wait()


def product(left, right):
    return jnp.dot(left, right, preferred_element_type=jnp.float32)


def trade_jumps(jumps, traces, partner, axis, faces, received):
    for trade, (face, got) in enumerate(zip(faces, received)):
        for sub in range(traces.shape[0]):
            other = got[partner[sub, face]].astype(jnp.float32)
            if trade == 1:
                other = other * inner(axis)
            own = traces[sub, face].astype(jnp.float32)
            jumps[trade, sub] = (own - other).astype(jnp.bfloat16)


def flat_face(jumps, index):
    _, subs, rhs, size = jumps.shape
    return jumps[index].reshape(subs * rhs, size)


def pair_sum(jumps, first):
    up = flat_face(jumps, first).astype(jnp.float32)
    return (up + flat_face(jumps, first + 1).astype(jnp.float32)).astype(jnp.bfloat16)


def z_kernel(
    yb, xa, ya, traces, self_block, opposite_block, cross_block, corner_map,
    map_out, base_z, cross_z, jumps,
):
    del xa, yb, ya
    subs, _, rhs, size = traces.shape
    rows = subs * rhs
    for sub in range(subs):
        up = traces[sub, 4].astype(jnp.float32)
        down = traces[sub, 5].astype(jnp.float32)
        if sub + 1 < subs:
            up = up - traces[sub + 1, 5].astype(jnp.float32)
        if sub > 0:
            down = down - traces[sub - 1, 4].astype(jnp.float32)
        jumps[0, sub] = up.astype(jnp.bfloat16)
        jumps[1, sub] = down.astype(jnp.bfloat16)
    width = CORNERS * COMPS
    row = lax.broadcasted_iota(jnp.int32, (width, width), 0)
    col = lax.broadcasted_iota(jnp.int32, (width, width), 1)
    order = (col == (row % CORNERS) * COMPS + row // CORNERS).astype(jnp.float32)
    order = order.astype(jnp.bfloat16)
    for face in range(6):
        map_out[face] = product(order, corner_map[face]).astype(jnp.bfloat16)
    flat = jumps[...].reshape(2 * rows, size)
    with_self = product(flat, self_block[...])
    with_opp = product(flat, opposite_block[...])
    base_z[0] = with_self[:rows] + with_opp[rows:]
    base_z[1] = with_self[rows:] + with_opp[:rows]
    cross_z[...] = product(pair_sum(jumps, 0), cross_block[...])


def y_kernel(
    partner, traces, rya, ryb, self_block, opposite_block, cross_block, cross_z,
    base_y, cross_y, base_x, jumps,
):
    subs, _, rhs, size = traces.shape
    rows = subs * rhs
    trade_jumps(jumps, traces, partner, "sy", y_faces(), (rya, ryb))
    from_y = product(pair_sum(jumps, 0), cross_block[...])
    cross_y[...] = from_y
    base_x[...] = from_y + cross_z[...]
    flat = jumps[...].reshape(2 * rows, size)
    with_self = product(flat, self_block[...])
    with_opp = product(flat, opposite_block[...])
    base_y[0] = with_self[:rows] + with_opp[rows:] + cross_z[...]
    base_y[1] = with_self[rows:] + with_opp[:rows] + cross_z[...]


def x_kernel(
    partner, viscosity, traces, rxa, rxb, self_block, opposite_block, base_x,
    xa, xb, to_xa, to_xb, pair_x, jumps,
):
    subs, _, rhs, size = traces.shape
    rows = subs * rhs
    trade_jumps(jumps, traces, partner, "sx", x_faces(), (rxa, rxb))
    flat = jumps[...].reshape(2 * rows, size)
    with_self = product(flat, self_block[...])
    with_opp = product(flat, opposite_block[...])
    pair_x[...] = pair_sum(jumps, 0)
    for index, (face, out, to) in enumerate(zip(x_faces(), (xa, xb), (to_xa, to_xb))):
        for sub in range(subs):
            here = slice(sub * rhs, (sub + 1) * rhs)
            own = slice(index * rows + sub * rhs, index * rows + (sub + 1) * rhs)
            opp = slice((1 - index) * rows + sub * rhs, (1 - index) * rows + (sub + 1) * rhs)
            total = with_self[own] + with_opp[opp] + base_x[here]
            value = (viscosity[sub] * total).astype(jnp.bfloat16)
            out[sub] = value
            to[partner[sub, face]] = value


def high_low(value):
    high = value.astype(jnp.bfloat16).astype(jnp.float32)
    return high, value - high


def coarse_rows(partials, owners, rows):
    subs = owners.shape[0]
    width = partials.shape[1]
    rhs = width // subs
    entries = jnp.zeros((2 * CORNERS, subs * LANES), jnp.float32)
    source = lax.broadcasted_iota(jnp.int32, (width, subs * LANES), 0)
    target = lax.broadcasted_iota(jnp.int32, (width, subs * LANES), 1)
    spread = (source // rhs) * LANES + (source % rhs) * COMPS
    for comp in range(COMPS):
        part = partials[comp * CORNERS : (comp + 1) * CORNERS]
        stacked = jnp.concatenate(high_low(part), axis=0).astype(jnp.bfloat16)
        place = (target == spread + comp).astype(jnp.float32).astype(jnp.bfloat16)
        entries += product(stacked, place)
    entries = entries[:CORNERS] + entries[CORNERS:]
    total = jnp.zeros((rows, LANES), jnp.float32)
    numbers = lax.broadcasted_iota(jnp.int32, (rows, CORNERS), 0)
    for sub in range(subs):
        onehot = (numbers == owners[sub : sub + 1, :]).astype(jnp.float32).astype(jnp.bfloat16)
        for term in high_low(entries[:, sub * LANES : (sub + 1) * LANES]):
            total += product(onehot, term.astype(jnp.bfloat16))
    return total


def rest_kernel(
    partner, viscosity, base_y, base_z, cross_y, pair_x, cross_block, to_xa, to_xb,
    ya, yb, to_ya, to_yb, local_z,
):
    del to_xa, to_xb
    subs, rhs, _ = ya.shape
    from_x = product(pair_x[...], cross_block[...])
    from_xy = from_x + cross_y[...]
    for index, out in enumerate((ya, yb, local_z.at[0], local_z.at[1])):
        base, cross = (base_y[index], from_x) if index < 2 else (base_z[index - 2], from_xy)
        for sub in range(subs):
            here = slice(sub * rhs, (sub + 1) * rhs)
            value = (viscosity[sub] * (base[here] + cross[here])).astype(jnp.bfloat16)
            out[sub] = value
            if index < 2:
                (to_ya, to_yb)[index][partner[sub, y_faces()[index]]] = value


def coarse_kernel(partner, owners, corner_map, xa, xb, to_ya, to_yb, local_z, dense):
    subs, rhs, _ = xa.shape
    partials = jnp.zeros((COMPS * CORNERS, subs * rhs), jnp.float32)
    faces = (*x_faces(), *y_faces(), 4, 5)
    places = (xa, xb, to_ya, to_yb, local_z.at[0], local_z.at[1])
    for index, (face, local) in enumerate(zip(faces, places)):
        order = [partner[sub, face] if index in (2, 3) else sub for sub in range(subs)]
        partials += lax.dot_general(
            corner_map[face],
            jnp.concatenate([local[slot] for slot in order], axis=0),
            (((1,), (1,)), ((), ())),
            preferred_element_type=jnp.float32,
        )
    total = coarse_rows(partials, owners[...], dense.shape[0] * COARSE_DEV)
    dense[...] = total.reshape(dense.shape)


def apply_z_kernel(dense, local_z, applied, held, sems):
    del dense
    subs = local_z.shape[1]
    copies = []
    for sub in range(subs):
        up = local_z[0, sub].astype(jnp.float32)
        down = local_z[1, sub].astype(jnp.float32)
        if sub + 1 < subs:
            up = up - local_z[1, sub + 1].astype(jnp.float32)
        if sub > 0:
            down = down - local_z[0, sub - 1].astype(jnp.float32)
        held[sub, 0] = up
        held[sub, 1] = down
        copies.append(
            pltpu.make_async_copy(held.at[sub], applied.at[sub, pl.ds(4, 2)], sems.at[sub])
        )
        copies[-1].start()
    for copy in copies:
        copy.wait()


def apply_kernel(
    applied_in, ya, yb, rya, ryb, xa, xb, rxa, rxb, parts, applied, coarse, held, sums, sems, sum_sem
):
    del applied_in
    total = parts[0]
    for source in range(1, parts.shape[0]):
        total = total + parts[source]
    sums[...] = total[:, : sums.shape[1]]
    copies = [pltpu.make_async_copy(sums, coarse, sum_sem)]
    copies[0].start()
    trades = zip((*y_faces(), *x_faces()), (ya, yb, xa, xb), (rya, ryb, rxa, rxb))
    for index, (face, local, got) in enumerate(trades):
        for sub in range(held.shape[1]):
            other = got[sub].astype(jnp.float32)
            if index == 1:
                other = other * inner("sy")
            if index == 3:
                other = other * inner("sx")
            held[index, sub] = local[sub].astype(jnp.float32) - other
            copies.append(
                pltpu.make_async_copy(
                    held.at[index, sub], applied.at[sub, face], sems.at[index, sub]
                )
            )
            copies[-1].start()
    for copy in copies:
        copy.wait()


def body(
    traces, viscosity, partner, corner_owner, self_block, opposite_block, cross_block, corner_map
):
    values = traces[0, 0]
    slots, visc, owners = partner[0, 0], viscosity[0, 0], corner_owner[0, 0]
    subs, _, rhs, size = values.shape
    count = lax.axis_size("sy")
    rows = subs * rhs
    face_shape = (subs, rhs, size)
    map_shape = (6, CORNERS * COMPS, size)
    bf16, f32 = jnp.bfloat16, jnp.float32

    xb, yb, xa, ya = pl.pallas_call(
        send_kernel,
        in_specs=[HBM],
        out_specs=[VMEM] * 4,
        out_shape=[in_vmem(face_shape, bf16)] * 4,
        scratch_shapes=[pltpu.SemaphoreType.DMA((4,))],
        compiler_params=params(8),
        cost_estimate=LONG,
    )(in_hbm(values))
    rxb = second_swap(xb, "sx")
    ryb = second_swap(yb, "sy")
    rxa = first_swap(xa, "sx")
    rya = first_swap(ya, "sy")
    map_v, base_z, cross_z = pl.pallas_call(
        z_kernel,
        in_specs=[VMEM] * 8,
        out_specs=[VMEM] * 3,
        out_shape=[in_vmem(map_shape, bf16), in_vmem((2, rows, size), f32)]
        + [in_vmem((rows, size), f32)],
        scratch_shapes=[pltpu.VMEM((2,) + face_shape, bf16)],
        compiler_params=params(12),
        cost_estimate=LONG,
    )(
        yb, xa, ya, values, self_block, opposite_block, cross_block,
        jnp.transpose(corner_map, (1, 0, 2)),
    )
    base_y, cross_y, base_x = pl.pallas_call(
        y_kernel,
        in_specs=[SMEM] + [VMEM] * 7,
        out_specs=[VMEM] * 3,
        out_shape=[in_vmem((2, rows, size), f32)] + [in_vmem((rows, size), f32)] * 2,
        scratch_shapes=[pltpu.VMEM((2,) + face_shape, bf16)],
        compiler_params=params(12),
    )(slots, values, rya, ryb, self_block, opposite_block, cross_block, cross_z)
    xa, xb, to_xa, to_xb, pair_x = pl.pallas_call(
        x_kernel,
        in_specs=[SMEM] * 2 + [VMEM] * 6,
        out_specs=[VMEM] * 5,
        out_shape=[in_vmem(face_shape, bf16)] * 4 + [in_vmem((rows, size), bf16)],
        scratch_shapes=[pltpu.VMEM((2,) + face_shape, bf16)],
        compiler_params=params(12),
    )(slots, visc, values, rxa, rxb, self_block, opposite_block, base_x)
    rxb = second_swap(to_xb, "sx")
    rxa = first_swap(to_xa, "sx")
    ya, yb, to_ya, to_yb, local_z = pl.pallas_call(
        rest_kernel,
        in_specs=[SMEM] * 2 + [VMEM] * 7,
        out_specs=[VMEM] * 5,
        out_shape=[in_vmem(face_shape, bf16)] * 4 + [in_vmem((2,) + face_shape, bf16)],
        compiler_params=params(8),
    )(slots, visc, base_y, base_z, cross_y, pair_x, cross_block, to_xa, to_xb)
    ryb = second_swap(to_yb, "sy")
    rya = first_swap(to_ya, "sy")
    dense = pl.pallas_call(
        coarse_kernel,
        in_specs=[SMEM] + [VMEM] * 7,
        out_specs=VMEM,
        out_shape=in_vmem((count, COARSE_DEV, LANES), f32),
        compiler_params=params(8),
    )(slots, owners, map_v, xa, xb, to_ya, to_yb, local_z)
    parts = lax.all_to_all(dense, "sy", 0, 0, tiled=True)
    out_shape = jax.ShapeDtypeStruct(values.shape, f32)
    applied = pl.pallas_call(
        apply_z_kernel,
        in_specs=[ANY, VMEM],
        out_specs=HBM,
        out_shape=out_shape,
        scratch_shapes=[
            pltpu.VMEM((subs, 2, rhs, size), f32),
            pltpu.SemaphoreType.DMA((subs,)),
        ],
        compiler_params=params(8),
        cost_estimate=LONG,
    )(dense, local_z)
    applied, coarse = pl.pallas_call(
        apply_kernel,
        in_specs=[HBM] + [VMEM] * 9,
        out_specs=[HBM] * 2,
        out_shape=[out_shape, jax.ShapeDtypeStruct((COARSE_DEV, rhs * COMPS), f32)],
        input_output_aliases={0: 0},
        scratch_shapes=[
            pltpu.VMEM((4,) + face_shape, f32),
            pltpu.VMEM((COARSE_DEV, rhs * COMPS), f32),
            pltpu.SemaphoreType.DMA((4, subs)),
            pltpu.SemaphoreType.DMA,
        ],
        compiler_params=params(12),
    )(applied, ya, yb, rya, ryb, xa, xb, rxa, rxb, parts)
    return applied[None, None], coarse.T


def solution(mesh):
    return jax.shard_map(
        body,
        mesh=mesh,
        in_specs=(
            P("sx", "sy", None, None, None, None),
            P("sx", "sy", None),
            P("sx", "sy", None, None),
            P("sx", "sy", None, None),
            P(),
            P(),
            P(),
            P(),
        ),
        out_specs=(P("sx", "sy", None, None, None, None), P(None, ("sx", "sy"))),
        check_vma=False,
    )
```

```python
import jax
import jax.numpy as jnp
from jax import lax
from jax.experimental import pallas as pl
from jax.experimental.pallas import tpu as pltpu
from jax.sharding import PartitionSpec as P

CORNERS = 8
COMPS = 3
COARSE_DEV = 8
LANES = 128

VMEM = pl.BlockSpec(memory_space=pltpu.VMEM)
SMEM = pl.BlockSpec(memory_space=pltpu.SMEM)
HBM = pl.BlockSpec(memory_space=pltpu.HBM)
ANY = pl.BlockSpec(memory_space=pl.ANY)


def in_vmem(shape, dtype):
    return pltpu.VMEM(shape, dtype)


def in_hbm(value):
    return pltpu.with_memory_space_constraint(value, pltpu.HBM)


def params(mib):
    return pltpu.CompilerParams(vmem_limit_bytes=mib * 1024 * 1024)


LONG = pl.CostEstimate(flops=20 * 10**9, bytes_accessed=0, transcendentals=0)


def odd(axis):
    return lax.rem(lax.axis_index(axis), 2)


def first_swap(value, axis):
    return lax.ppermute(value, axis, [(i, i ^ 1) for i in range(lax.axis_size(axis))])


def second_swap(value, axis):
    rows, cols = lax.axis_size("sx"), lax.axis_size("sy")
    pairs = []
    for i in range(rows):
        for j in range(cols):
            if axis == "sx":
                k = i - 1 if i % 2 == 0 else i + 1
                target = (k, j) if 0 <= k < rows else (i, j ^ 1)
            else:
                k = j - 1 if j % 2 == 0 else j + 1
                target = (i, k) if 0 <= k < cols else (i ^ 2, j)
            pairs.append((i * cols + j, target[0] * cols + target[1]))
    return lax.ppermute(value, ("sx", "sy"), pairs)


def cross_swap(value, axis, bits):
    return lax.ppermute(value, axis, [(i, i ^ bits) for i in range(lax.axis_size(axis))])


def inner(axis):
    me = lax.axis_index(axis)
    return ((me > 0) & (me < lax.axis_size(axis) - 1)).astype(jnp.float32)


def x_faces():
    return odd("sx"), 1 - odd("sx")


def y_faces():
    return 2 + odd("sy"), 3 - odd("sy")


def send_kernel(traces, xb, yb, xa, ya, sems):
    faces = (*x_faces(), *y_faces())
    copies = [
        pltpu.make_async_copy(traces.at[:, face], out, sems.at[index])
        for index, (face, out) in enumerate(zip(faces, (xa, xb, ya, yb)))
    ]
    for copy in copies:
        copy.start()
    for copy in copies:
        copy.wait()


def product(left, right):
    return jnp.dot(left, right, preferred_element_type=jnp.float32)


def trade_jumps(jumps, traces, partner, axis, faces, received):
    for trade, (face, got) in enumerate(zip(faces, received)):
        for sub in range(traces.shape[0]):
            other = got[partner[sub, face]].astype(jnp.float32)
            if trade == 1:
                other = other * inner(axis)
            own = traces[sub, face].astype(jnp.float32)
            jumps[trade, sub] = (own - other).astype(jnp.bfloat16)


def flat_face(jumps, index):
    _, subs, rhs, size = jumps.shape
    return jumps[index].reshape(subs * rhs, size)


def pair_sum(jumps, first):
    up = flat_face(jumps, first).astype(jnp.float32)
    return (up + flat_face(jumps, first + 1).astype(jnp.float32)).astype(jnp.bfloat16)


def z_kernel(
    yb, xa, ya, traces, self_block, opposite_block, cross_block, corner_map,
    map_out, base_z, cross_z, jumps,
):
    del xa, yb, ya
    subs, _, rhs, size = traces.shape
    rows = subs * rhs
    for sub in range(subs):
        up = traces[sub, 4].astype(jnp.float32)
        down = traces[sub, 5].astype(jnp.float32)
        if sub + 1 < subs:
            up = up - traces[sub + 1, 5].astype(jnp.float32)
        if sub > 0:
            down = down - traces[sub - 1, 4].astype(jnp.float32)
        jumps[0, sub] = up.astype(jnp.bfloat16)
        jumps[1, sub] = down.astype(jnp.bfloat16)
    width = CORNERS * COMPS
    row = lax.broadcasted_iota(jnp.int32, (width, width), 0)
    col = lax.broadcasted_iota(jnp.int32, (width, width), 1)
    order = (col == (row % CORNERS) * COMPS + row // CORNERS).astype(jnp.float32)
    order = order.astype(jnp.bfloat16)
    for face in range(6):
        map_out[face] = product(order, corner_map[face]).astype(jnp.bfloat16)
    flat = jumps[...].reshape(2 * rows, size)
    with_self = product(flat, self_block[...])
    with_opp = product(flat, opposite_block[...])
    base_z[0] = with_self[:rows] + with_opp[rows:]
    base_z[1] = with_self[rows:] + with_opp[:rows]
    cross_z[...] = product(pair_sum(jumps, 0), cross_block[...])


def y_kernel(
    partner, traces, rya, ryb, self_block, opposite_block, cross_block, cross_z,
    base_y, cross_y, base_x, jumps,
):
    subs, _, rhs, size = traces.shape
    rows = subs * rhs
    trade_jumps(jumps, traces, partner, "sy", y_faces(), (rya, ryb))
    from_y = product(pair_sum(jumps, 0), cross_block[...])
    cross_y[...] = from_y
    base_x[...] = from_y + cross_z[...]
    flat = jumps[...].reshape(2 * rows, size)
    with_self = product(flat, self_block[...])
    with_opp = product(flat, opposite_block[...])
    base_y[0] = with_self[:rows] + with_opp[rows:] + cross_z[...]
    base_y[1] = with_self[rows:] + with_opp[:rows] + cross_z[...]


def high_low(value):
    high = value.astype(jnp.bfloat16).astype(jnp.float32)
    return high, value - high


def coarse_rows(partials, owners, rows):
    subs = owners.shape[0]
    width = partials.shape[1]
    rhs = width // subs
    entries = jnp.zeros((2 * CORNERS, subs * LANES), jnp.float32)
    source = lax.broadcasted_iota(jnp.int32, (width, subs * LANES), 0)
    target = lax.broadcasted_iota(jnp.int32, (width, subs * LANES), 1)
    spread = (source // rhs) * LANES + (source % rhs) * COMPS
    for comp in range(COMPS):
        part = partials[comp * CORNERS : (comp + 1) * CORNERS]
        stacked = jnp.concatenate(high_low(part), axis=0).astype(jnp.bfloat16)
        place = (target == spread + comp).astype(jnp.float32).astype(jnp.bfloat16)
        entries += product(stacked, place)
    entries = entries[:CORNERS] + entries[CORNERS:]
    total = jnp.zeros((rows, LANES), jnp.float32)
    numbers = lax.broadcasted_iota(jnp.int32, (rows, CORNERS), 0)
    for sub in range(subs):
        onehot = (numbers == owners[sub : sub + 1, :]).astype(jnp.float32).astype(jnp.bfloat16)
        for term in high_low(entries[:, sub * LANES : (sub + 1) * LANES]):
            total += product(onehot, term.astype(jnp.bfloat16))
    return total


def local_kernel(
    partner, viscosity, traces, rxa, rxb, self_block, opposite_block, cross_block,
    base_x, base_y, base_z, cross_y, owners, corner_map,
    xa, xb, ya, yb, local_z, to_xa, to_xb, to_ya, to_yb, kept, jumps, dense,
):
    subs, _, rhs, size = traces.shape
    rows = subs * rhs
    trade_jumps(jumps, traces, partner, "sx", x_faces(), (rxa, rxb))
    flat = jumps[...].reshape(2 * rows, size)
    with_self = product(flat, self_block[...])
    with_opp = product(flat, opposite_block[...])
    from_x = product(pair_sum(jumps, 0), cross_block[...])
    from_xy = from_x + cross_y[...]
    totals = (
        with_self[:rows] + with_opp[rows:] + base_x[...],
        with_self[rows:] + with_opp[:rows] + base_x[...],
        base_y[0] + from_x,
        base_y[1] + from_x,
        base_z[0] + from_xy,
        base_z[1] + from_xy,
    )
    faces = (*x_faces(), *y_faces(), 4, 5)
    outs = (xa, xb, ya, yb, local_z.at[0], local_z.at[1])
    sent = (to_xa, to_xb, to_ya, to_yb)
    partials = jnp.zeros((COMPS * CORNERS, rows), jnp.float32)
    for index, (face, total, out) in enumerate(zip(faces, totals, outs)):
        for sub in range(subs):
            here = slice(sub * rhs, (sub + 1) * rhs)
            value = (viscosity[sub] * total[here]).astype(jnp.bfloat16)
            out[sub] = value
            if index < 4:
                sent[index][partner[sub, face]] = value
        partials += lax.dot_general(
            corner_map[face],
            out[...].reshape(rows, size),
            (((1,), (1,)), ((), ())),
            preferred_element_type=jnp.float32,
        )
    dense[...] = coarse_rows(partials, owners[...], dense.shape[0])
    me = lax.axis_index("sy")

    def block(bits):
        start = pl.multiple_of((me ^ bits) * COARSE_DEV, COARSE_DEV)
        return dense[pl.ds(start, COARSE_DEV), :]

    half, per_row = kept.shape[0], size // LANES
    for index in range((to_ya.shape[0] - subs) * per_row):
        lanes = slice(index % per_row * LANES, (index % per_row + 1) * LANES)
        both = jnp.zeros((2 * COARSE_DEV, LANES), jnp.float32)
        if index < half:
            kept[index] = block(2 * index)
            both = jnp.concatenate(high_low(block(2 * index + 1)), axis=0)
        to_ya[subs + index // per_row, :, lanes] = both.astype(jnp.bfloat16)


def first_add_kernel(subs, kept, got, keep, give):
    half, per_row = kept.shape[0], got.shape[2] // LANES
    for index in range(half):
        lanes = slice(index % per_row * LANES, (index % per_row + 1) * LANES)
        both = got[subs + index // per_row, :, lanes].astype(jnp.float32)
        total = kept[index] + both[:COARSE_DEV] + both[COARSE_DEV:]
        out = keep if index < half // 2 else give
        out[index % (half // 2)] = total


def next_add_kernel(after, kept, got, keep, give):
    del after
    half = kept.shape[0]
    total = kept[...] + got[...]
    keep[...] = total[: half // 2]
    give[...] = total[half // 2 :]


def last_add_kernel(kept, got, coarse, total, sem):
    total[...] = (kept[0] + got[0])[:, : total.shape[1]]
    copy = pltpu.make_async_copy(total, coarse, sem)
    copy.start()
    copy.wait()


def apply_z_kernel(to_yb, local_z, applied, held, sems):
    del to_yb
    subs = local_z.shape[1]
    copies = []
    for sub in range(subs):
        up = local_z[0, sub].astype(jnp.float32)
        down = local_z[1, sub].astype(jnp.float32)
        if sub + 1 < subs:
            up = up - local_z[1, sub + 1].astype(jnp.float32)
        if sub > 0:
            down = down - local_z[0, sub - 1].astype(jnp.float32)
        held[sub, 0] = up
        held[sub, 1] = down
        copies.append(
            pltpu.make_async_copy(held.at[sub], applied.at[sub, pl.ds(4, 2)], sems.at[sub])
        )
        copies[-1].start()
    for copy in copies:
        copy.wait()


def apply_kernel(applied_in, ya, yb, rya, ryb, xa, xb, rxa, rxb, applied, held, sems):
    del applied_in
    copies = []
    trades = zip((*y_faces(), *x_faces()), (ya, yb, xa, xb), (rya, ryb, rxa, rxb))
    for index, (face, local, got) in enumerate(trades):
        for sub in range(held.shape[1]):
            other = got[sub].astype(jnp.float32)
            if index == 1:
                other = other * inner("sy")
            if index == 3:
                other = other * inner("sx")
            held[index, sub] = local[sub].astype(jnp.float32) - other
            copies.append(
                pltpu.make_async_copy(
                    held.at[index, sub], applied.at[sub, face], sems.at[index, sub]
                )
            )
            copies[-1].start()
    for copy in copies:
        copy.wait()


def body(
    traces, viscosity, partner, corner_owner, self_block, opposite_block, cross_block, corner_map
):
    values = traces[0, 0]
    slots, visc, owners = partner[0, 0], viscosity[0, 0], corner_owner[0, 0]
    subs, _, rhs, size = values.shape
    count = lax.axis_size("sy")
    rows = subs * rhs
    face_shape = (subs, rhs, size)
    map_shape = (6, CORNERS * COMPS, size)
    bf16, f32 = jnp.bfloat16, jnp.float32

    xb, yb, xa, ya = pl.pallas_call(
        send_kernel,
        in_specs=[HBM],
        out_specs=[VMEM] * 4,
        out_shape=[in_vmem(face_shape, bf16)] * 4,
        scratch_shapes=[pltpu.SemaphoreType.DMA((4,))],
        compiler_params=params(8),
        cost_estimate=LONG,
    )(in_hbm(values))
    rxb = second_swap(xb, "sx")
    ryb = second_swap(yb, "sy")
    rxa = first_swap(xa, "sx")
    rya = first_swap(ya, "sy")
    map_v, base_z, cross_z = pl.pallas_call(
        z_kernel,
        in_specs=[VMEM] * 8,
        out_specs=[VMEM] * 3,
        out_shape=[in_vmem(map_shape, bf16), in_vmem((2, rows, size), f32)]
        + [in_vmem((rows, size), f32)],
        scratch_shapes=[pltpu.VMEM((2,) + face_shape, bf16)],
        compiler_params=params(12),
        cost_estimate=LONG,
    )(
        yb, xa, ya, values, self_block, opposite_block, cross_block,
        jnp.transpose(corner_map, (1, 0, 2)),
    )
    base_y, cross_y, base_x = pl.pallas_call(
        y_kernel,
        in_specs=[SMEM] + [VMEM] * 7,
        out_specs=[VMEM] * 3,
        out_shape=[in_vmem((2, rows, size), f32)] + [in_vmem((rows, size), f32)] * 2,
        scratch_shapes=[pltpu.VMEM((2,) + face_shape, bf16)],
        compiler_params=params(12),
    )(slots, values, rya, ryb, self_block, opposite_block, cross_block, cross_z)
    half, per_row = count // 2, size // LANES
    long_shape = (subs + -(-half // per_row), rhs, size)

    def blocks(number):
        return in_vmem((number, COARSE_DEV, LANES), f32)

    xa, xb, ya, yb, local_z, to_xa, to_xb, to_ya, to_yb, kept = pl.pallas_call(
        local_kernel,
        in_specs=[SMEM] * 2 + [VMEM] * 12,
        out_specs=[VMEM] * 10,
        out_shape=[in_vmem(face_shape, bf16)] * 4
        + [in_vmem((2,) + face_shape, bf16)]
        + [in_vmem(face_shape, bf16)] * 2
        + [in_vmem(long_shape, bf16), in_vmem(face_shape, bf16), blocks(half)],
        scratch_shapes=[
            pltpu.VMEM((2,) + face_shape, bf16),
            pltpu.VMEM((COARSE_DEV * count, LANES), f32),
        ],
        compiler_params=params(16),
    )(
        slots, visc, values, rxa, rxb, self_block, opposite_block, cross_block,
        base_x, base_y, base_z, cross_y, owners, map_v,
    )
    rya = first_swap(to_ya, "sy")
    rxb = second_swap(to_xb, "sx")
    rxa = first_swap(to_xa, "sx")
    half //= 2
    kept, give = pl.pallas_call(
        lambda *refs: first_add_kernel(subs, *refs),
        in_specs=[VMEM] * 2,
        out_specs=[VMEM] * 2,
        out_shape=[blocks(half)] * 2,
        compiler_params=params(4),
    )(kept, rya)
    got = cross_swap(give, "sy", 2 * half)
    ryb = second_swap(to_yb, "sy")
    out_shape = jax.ShapeDtypeStruct(values.shape, f32)
    applied = pl.pallas_call(
        apply_z_kernel,
        in_specs=[VMEM] * 2,
        out_specs=HBM,
        out_shape=out_shape,
        scratch_shapes=[
            pltpu.VMEM((subs, 2, rhs, size), f32),
            pltpu.SemaphoreType.DMA((subs,)),
        ],
        compiler_params=params(8),
        cost_estimate=LONG,
    )(to_yb, local_z)
    while half > 1:
        half //= 2
        kept, give = pl.pallas_call(
            next_add_kernel,
            in_specs=[HBM] + [VMEM] * 2,
            out_specs=[VMEM] * 2,
            out_shape=[blocks(half)] * 2,
            compiler_params=params(4),
        )(in_hbm(applied), kept, got)
        got = cross_swap(give, "sy", 2 * half)
    applied = pl.pallas_call(
        apply_kernel,
        in_specs=[HBM] + [VMEM] * 8,
        out_specs=HBM,
        out_shape=out_shape,
        input_output_aliases={0: 0},
        scratch_shapes=[pltpu.VMEM((4,) + face_shape, f32), pltpu.SemaphoreType.DMA((4, subs))],
        compiler_params=params(12),
        cost_estimate=LONG,
    )(applied, ya, yb, rya, ryb, xa, xb, rxa, rxb)
    coarse = pl.pallas_call(
        last_add_kernel,
        in_specs=[VMEM] * 2,
        out_specs=HBM,
        out_shape=jax.ShapeDtypeStruct((COARSE_DEV, rhs * COMPS), f32),
        scratch_shapes=[pltpu.VMEM((COARSE_DEV, rhs * COMPS), f32), pltpu.SemaphoreType.DMA],
        compiler_params=params(4),
    )(kept, got)
    return applied[None, None], coarse.T


def solution(mesh):
    return jax.shard_map(
        body,
        mesh=mesh,
        in_specs=(
            P("sx", "sy", None, None, None, None),
            P("sx", "sy", None),
            P("sx", "sy", None, None),
            P("sx", "sy", None, None),
            P(),
            P(),
            P(),
            P(),
        ),
        out_specs=(P("sx", "sy", None, None, None, None), P(None, ("sx", "sy"))),
        check_vma=False,
    )
```

```python
import jax
import jax.numpy as jnp
from jax import lax
from jax.experimental import pallas as pl
from jax.experimental.pallas import tpu as pltpu
from jax.sharding import PartitionSpec as P

CORNERS = 8
COMPS = 3
COARSE_DEV = 8
LANES = 128

VMEM = pl.BlockSpec(memory_space=pltpu.VMEM)
SMEM = pl.BlockSpec(memory_space=pltpu.SMEM)
HBM = pl.BlockSpec(memory_space=pltpu.HBM)
ANY = pl.BlockSpec(memory_space=pl.ANY)


def in_vmem(shape, dtype):
    return pltpu.VMEM(shape, dtype)


def in_hbm(value):
    return pltpu.with_memory_space_constraint(value, pltpu.HBM)


def params(mib):
    return pltpu.CompilerParams(vmem_limit_bytes=mib * 1024 * 1024)


LONG = pl.CostEstimate(flops=20 * 10**9, bytes_accessed=0, transcendentals=0)


def odd(axis):
    return lax.rem(lax.axis_index(axis), 2)


def first_swap(value, axis):
    return lax.ppermute(value, axis, [(i, i ^ 1) for i in range(lax.axis_size(axis))])


def second_swap(value, axis):
    rows, cols = lax.axis_size("sx"), lax.axis_size("sy")
    pairs = []
    for i in range(rows):
        for j in range(cols):
            if axis == "sx":
                k = i - 1 if i % 2 == 0 else i + 1
                target = (k, j) if 0 <= k < rows else (i, j ^ 1)
            else:
                k = j - 1 if j % 2 == 0 else j + 1
                target = (i, k) if 0 <= k < cols else (i ^ 2, j)
            pairs.append((i * cols + j, target[0] * cols + target[1]))
    return lax.ppermute(value, ("sx", "sy"), pairs)


def cross_swap(value, axis, bits):
    return lax.ppermute(value, axis, [(i, i ^ bits) for i in range(lax.axis_size(axis))])


def inner(axis):
    me = lax.axis_index(axis)
    return ((me > 0) & (me < lax.axis_size(axis) - 1)).astype(jnp.float32)


def x_faces():
    return odd("sx"), 1 - odd("sx")


def y_faces():
    return 2 + odd("sy"), 3 - odd("sy")


def send_kernel(traces, xb, yb, xa, ya, sems):
    faces = (*x_faces(), *y_faces())
    copies = [
        pltpu.make_async_copy(traces.at[:, face], out, sems.at[index])
        for index, (face, out) in enumerate(zip(faces, (xa, xb, ya, yb)))
    ]
    for copy in copies:
        copy.start()
    for copy in copies:
        copy.wait()


def product(left, right):
    return jnp.dot(left, right, preferred_element_type=jnp.float32)


def trade_jumps(jumps, traces, partner, axis, faces, received):
    for trade, (face, got) in enumerate(zip(faces, received)):
        for sub in range(traces.shape[0]):
            other = got[partner[sub, face]].astype(jnp.float32)
            if trade == 1:
                other = other * inner(axis)
            own = traces[sub, face].astype(jnp.float32)
            jumps[trade, sub] = (own - other).astype(jnp.bfloat16)


def flat_face(jumps, index):
    _, subs, rhs, size = jumps.shape
    return jumps[index].reshape(subs * rhs, size)


def pair_sum(jumps, first):
    up = flat_face(jumps, first).astype(jnp.float32)
    return (up + flat_face(jumps, first + 1).astype(jnp.float32)).astype(jnp.bfloat16)


def z_kernel(
    yb, xa, ya, traces, self_block, opposite_block, cross_block, corner_map,
    map_out, base_z, cross_z, jumps,
):
    del xa, yb, ya
    subs, _, rhs, size = traces.shape
    rows = subs * rhs
    for sub in range(subs):
        up = traces[sub, 4].astype(jnp.float32)
        down = traces[sub, 5].astype(jnp.float32)
        if sub + 1 < subs:
            up = up - traces[sub + 1, 5].astype(jnp.float32)
        if sub > 0:
            down = down - traces[sub - 1, 4].astype(jnp.float32)
        jumps[0, sub] = up.astype(jnp.bfloat16)
        jumps[1, sub] = down.astype(jnp.bfloat16)
    width = CORNERS * COMPS
    row = lax.broadcasted_iota(jnp.int32, (width, width), 0)
    col = lax.broadcasted_iota(jnp.int32, (width, width), 1)
    order = (col == (row % CORNERS) * COMPS + row // CORNERS).astype(jnp.float32)
    order = order.astype(jnp.bfloat16)
    for face in range(6):
        map_out[face] = product(order, corner_map[face]).astype(jnp.bfloat16)
    flat = jumps[...].reshape(2 * rows, size)
    with_self = product(flat, self_block[...])
    with_opp = product(flat, opposite_block[...])
    base_z[0] = with_self[:rows] + with_opp[rows:]
    base_z[1] = with_self[rows:] + with_opp[:rows]
    cross_z[...] = product(pair_sum(jumps, 0), cross_block[...])


def y_kernel(
    partner, traces, ryb, rya, rxb, self_block, opposite_block, cross_block, cross_z,
    base_y, cross_y, base_x, jumps,
):
    del rxb
    subs, _, rhs, size = traces.shape
    rows = subs * rhs
    trade_jumps(jumps, traces, partner, "sy", y_faces(), (rya, ryb))
    from_y = product(pair_sum(jumps, 0), cross_block[...])
    cross_y[...] = from_y
    base_x[...] = from_y + cross_z[...]
    flat = jumps[...].reshape(2 * rows, size)
    with_self = product(flat, self_block[...])
    with_opp = product(flat, opposite_block[...])
    base_y[0] = with_self[:rows] + with_opp[rows:] + cross_z[...]
    base_y[1] = with_self[rows:] + with_opp[:rows] + cross_z[...]


def high_low(value):
    high = value.astype(jnp.bfloat16).astype(jnp.float32)
    return high, value - high


def coarse_rows(partials, owners, rows):
    subs = owners.shape[0]
    width = partials.shape[1]
    rhs = width // subs
    entries = jnp.zeros((2 * CORNERS, subs * LANES), jnp.float32)
    source = lax.broadcasted_iota(jnp.int32, (width, subs * LANES), 0)
    target = lax.broadcasted_iota(jnp.int32, (width, subs * LANES), 1)
    spread = (source // rhs) * LANES + (source % rhs) * COMPS
    for comp in range(COMPS):
        part = partials[comp * CORNERS : (comp + 1) * CORNERS]
        stacked = jnp.concatenate(high_low(part), axis=0).astype(jnp.bfloat16)
        place = (target == spread + comp).astype(jnp.float32).astype(jnp.bfloat16)
        entries += product(stacked, place)
    entries = entries[:CORNERS] + entries[CORNERS:]
    total = jnp.zeros((rows, LANES), jnp.float32)
    numbers = lax.broadcasted_iota(jnp.int32, (rows, CORNERS), 0)
    for sub in range(subs):
        onehot = (numbers == owners[sub : sub + 1, :]).astype(jnp.float32).astype(jnp.bfloat16)
        for term in high_low(entries[:, sub * LANES : (sub + 1) * LANES]):
            total += product(onehot, term.astype(jnp.bfloat16))
    return total


def local_kernel(
    partner, viscosity, traces, rxa, rxb, self_block, opposite_block, cross_block,
    base_x, base_y, base_z, cross_y, owners, corner_map,
    xa, xb, ya, yb, local_z, to_xa, to_xb, to_ya, to_yb, kept, jumps, dense,
):
    subs, _, rhs, size = traces.shape
    rows = subs * rhs
    trade_jumps(jumps, traces, partner, "sx", x_faces(), (rxa, rxb))
    flat = jumps[...].reshape(2 * rows, size)
    with_self = product(flat, self_block[...])
    with_opp = product(flat, opposite_block[...])
    from_x = product(pair_sum(jumps, 0), cross_block[...])
    from_xy = from_x + cross_y[...]
    totals = (
        with_self[:rows] + with_opp[rows:] + base_x[...],
        with_self[rows:] + with_opp[:rows] + base_x[...],
        base_y[0] + from_x,
        base_y[1] + from_x,
        base_z[0] + from_xy,
        base_z[1] + from_xy,
    )
    faces = (*x_faces(), *y_faces(), 4, 5)
    outs = (xa, xb, ya, yb, local_z.at[0], local_z.at[1])
    sent = (to_xa, to_xb, to_ya, to_yb)
    partials = jnp.zeros((COMPS * CORNERS, rows), jnp.float32)
    for index, (face, total, out) in enumerate(zip(faces, totals, outs)):
        for sub in range(subs):
            here = slice(sub * rhs, (sub + 1) * rhs)
            value = (viscosity[sub] * total[here]).astype(jnp.bfloat16)
            out[sub] = value
            if index < 4:
                sent[index][partner[sub, face]] = value
        partials += lax.dot_general(
            corner_map[face],
            out[...].reshape(rows, size),
            (((1,), (1,)), ((), ())),
            preferred_element_type=jnp.float32,
        )
    dense[...] = coarse_rows(partials, owners[...], dense.shape[0])
    me = lax.axis_index("sy")

    def block(bits):
        start = pl.multiple_of((me ^ bits) * COARSE_DEV, COARSE_DEV)
        return dense[pl.ds(start, COARSE_DEV), :]

    half, per_row = kept.shape[0], size // LANES
    for index in range((to_ya.shape[0] - subs) * per_row):
        lanes = slice(index % per_row * LANES, (index % per_row + 1) * LANES)
        both = jnp.zeros((2 * COARSE_DEV, LANES), jnp.float32)
        if index < half:
            kept[index] = block(2 * index)
            both = jnp.concatenate(high_low(block(2 * index + 1)), axis=0)
        to_ya[subs + index // per_row, :, lanes] = both.astype(jnp.bfloat16)


def first_add_kernel(subs, kept, got, keep, give):
    half, per_row = kept.shape[0], got.shape[2] // LANES
    for index in range(half):
        lanes = slice(index % per_row * LANES, (index % per_row + 1) * LANES)
        both = got[subs + index // per_row, :, lanes].astype(jnp.float32)
        total = kept[index] + both[:COARSE_DEV] + both[COARSE_DEV:]
        out = keep if index < half // 2 else give
        out[index % (half // 2)] = total


def next_add_kernel(after, kept, got, keep, give):
    del after
    half = kept.shape[0]
    total = kept[...] + got[...]
    keep[...] = total[: half // 2]
    give[...] = total[half // 2 :]


def last_add_kernel(kept, got, coarse, total, sem):
    total[...] = (kept[0] + got[0])[:, : total.shape[1]]
    copy = pltpu.make_async_copy(total, coarse, sem)
    copy.start()
    copy.wait()


def apply_z_kernel(to_yb, local_z, applied, held, sems):
    del to_yb
    subs = local_z.shape[1]
    copies = []
    for sub in range(subs):
        up = local_z[0, sub].astype(jnp.float32)
        down = local_z[1, sub].astype(jnp.float32)
        if sub + 1 < subs:
            up = up - local_z[1, sub + 1].astype(jnp.float32)
        if sub > 0:
            down = down - local_z[0, sub - 1].astype(jnp.float32)
        held[sub, 0] = up
        held[sub, 1] = down
        copies.append(
            pltpu.make_async_copy(held.at[sub], applied.at[sub, pl.ds(4, 2)], sems.at[sub])
        )
        copies[-1].start()
    for copy in copies:
        copy.wait()


def apply_kernel(applied_in, rxb, ryb, rxa, rya, ya, yb, xa, xb, applied, held, sems):
    del applied_in
    copies = []
    trades = zip((*y_faces(), *x_faces()), (ya, yb, xa, xb), (rya, ryb, rxa, rxb))
    for index, (face, local, got) in enumerate(trades):
        for sub in range(held.shape[1]):
            other = got[sub].astype(jnp.float32)
            if index == 1:
                other = other * inner("sy")
            if index == 3:
                other = other * inner("sx")
            held[index, sub] = local[sub].astype(jnp.float32) - other
            copies.append(
                pltpu.make_async_copy(
                    held.at[index, sub], applied.at[sub, face], sems.at[index, sub]
                )
            )
            copies[-1].start()
    for copy in copies:
        copy.wait()


def body(
    traces, viscosity, partner, corner_owner, self_block, opposite_block, cross_block, corner_map
):
    values = traces[0, 0]
    slots, visc, owners = partner[0, 0], viscosity[0, 0], corner_owner[0, 0]
    subs, _, rhs, size = values.shape
    count = lax.axis_size("sy")
    rows = subs * rhs
    face_shape = (subs, rhs, size)
    map_shape = (6, CORNERS * COMPS, size)
    bf16, f32 = jnp.bfloat16, jnp.float32

    xb, yb, xa, ya = pl.pallas_call(
        send_kernel,
        in_specs=[HBM],
        out_specs=[VMEM] * 4,
        out_shape=[in_vmem(face_shape, bf16)] * 4,
        scratch_shapes=[pltpu.SemaphoreType.DMA((4,))],
        compiler_params=params(8),
        cost_estimate=LONG,
    )(in_hbm(values))
    rxb = second_swap(xb, "sx")
    ryb = second_swap(yb, "sy")
    rxa = first_swap(xa, "sx")
    rya = first_swap(ya, "sy")
    map_v, base_z, cross_z = pl.pallas_call(
        z_kernel,
        in_specs=[VMEM] * 8,
        out_specs=[VMEM] * 3,
        out_shape=[in_vmem(map_shape, bf16), in_vmem((2, rows, size), f32)]
        + [in_vmem((rows, size), f32)],
        scratch_shapes=[pltpu.VMEM((2,) + face_shape, bf16)],
        compiler_params=params(12),
        cost_estimate=LONG,
    )(
        yb, xa, ya, values, self_block, opposite_block, cross_block,
        jnp.transpose(corner_map, (1, 0, 2)),
    )
    base_y, cross_y, base_x = pl.pallas_call(
        y_kernel,
        in_specs=[SMEM] + [VMEM] * 8,
        out_specs=[VMEM] * 3,
        out_shape=[in_vmem((2, rows, size), f32)] + [in_vmem((rows, size), f32)] * 2,
        scratch_shapes=[pltpu.VMEM((2,) + face_shape, bf16)],
        compiler_params=params(12),
    )(slots, values, ryb, rya, rxb, self_block, opposite_block, cross_block, cross_z)
    half, per_row = count // 2, size // LANES
    long_shape = (subs + -(-half // per_row), rhs, size)

    def blocks(number):
        return in_vmem((number, COARSE_DEV, LANES), f32)

    xa, xb, ya, yb, local_z, to_xa, to_xb, to_ya, to_yb, kept = pl.pallas_call(
        local_kernel,
        in_specs=[SMEM] * 2 + [VMEM] * 12,
        out_specs=[VMEM] * 10,
        out_shape=[in_vmem(face_shape, bf16)] * 4
        + [in_vmem((2,) + face_shape, bf16)]
        + [in_vmem(face_shape, bf16)] * 2
        + [in_vmem(long_shape, bf16), in_vmem(face_shape, bf16), blocks(half)],
        scratch_shapes=[
            pltpu.VMEM((2,) + face_shape, bf16),
            pltpu.VMEM((COARSE_DEV * count, LANES), f32),
        ],
        compiler_params=params(16),
    )(
        slots, visc, values, rxa, rxb, self_block, opposite_block, cross_block,
        base_x, base_y, base_z, cross_y, owners, map_v,
    )
    rya = first_swap(to_ya, "sy")
    rxb = second_swap(to_xb, "sx")
    rxa = first_swap(to_xa, "sx")
    half //= 2
    kept, give = pl.pallas_call(
        lambda *refs: first_add_kernel(subs, *refs),
        in_specs=[VMEM] * 2,
        out_specs=[VMEM] * 2,
        out_shape=[blocks(half)] * 2,
        compiler_params=params(4),
    )(kept, rya)
    got = cross_swap(give, "sy", 2 * half)
    ryb = second_swap(to_yb, "sy")
    out_shape = jax.ShapeDtypeStruct(values.shape, f32)
    applied = pl.pallas_call(
        apply_z_kernel,
        in_specs=[VMEM] * 2,
        out_specs=HBM,
        out_shape=out_shape,
        scratch_shapes=[
            pltpu.VMEM((subs, 2, rhs, size), f32),
            pltpu.SemaphoreType.DMA((subs,)),
        ],
        compiler_params=params(8),
        cost_estimate=LONG,
    )(to_yb, local_z)
    while half > 1:
        half //= 2
        kept, give = pl.pallas_call(
            next_add_kernel,
            in_specs=[HBM] + [VMEM] * 2,
            out_specs=[VMEM] * 2,
            out_shape=[blocks(half)] * 2,
            compiler_params=params(4),
        )(in_hbm(applied), kept, got)
        got = cross_swap(give, "sy", 2 * half)
    applied = pl.pallas_call(
        apply_kernel,
        in_specs=[HBM] + [VMEM] * 8,
        out_specs=HBM,
        out_shape=out_shape,
        input_output_aliases={0: 0},
        scratch_shapes=[pltpu.VMEM((4,) + face_shape, f32), pltpu.SemaphoreType.DMA((4, subs))],
        compiler_params=params(12),
        cost_estimate=LONG,
    )(applied, rxb, ryb, rxa, rya, ya, yb, xa, xb)
    coarse = pl.pallas_call(
        last_add_kernel,
        in_specs=[VMEM] * 2,
        out_specs=HBM,
        out_shape=jax.ShapeDtypeStruct((COARSE_DEV, rhs * COMPS), f32),
        scratch_shapes=[pltpu.VMEM((COARSE_DEV, rhs * COMPS), f32), pltpu.SemaphoreType.DMA],
        compiler_params=params(4),
    )(kept, got)
    return applied[None, None], coarse.T


def solution(mesh):
    return jax.shard_map(
        body,
        mesh=mesh,
        in_specs=(
            P("sx", "sy", None, None, None, None),
            P("sx", "sy", None),
            P("sx", "sy", None, None),
            P("sx", "sy", None, None),
            P(),
            P(),
            P(),
            P(),
        ),
        out_specs=(P("sx", "sy", None, None, None, None), P(None, ("sx", "sy"))),
        check_vma=False,
    )
```

```python
import jax
import jax.numpy as jnp
from jax import lax
from jax.experimental import pallas as pl
from jax.experimental.pallas import tpu as pltpu
from jax.sharding import PartitionSpec as P

CORNERS = 8
COMPS = 3
COARSE_DEV = 8
LANES = 128

VMEM = pl.BlockSpec(memory_space=pltpu.VMEM)
SMEM = pl.BlockSpec(memory_space=pltpu.SMEM)
HBM = pl.BlockSpec(memory_space=pltpu.HBM)
ANY = pl.BlockSpec(memory_space=pl.ANY)


def in_vmem(shape, dtype):
    return pltpu.VMEM(shape, dtype)


def in_hbm(value):
    return pltpu.with_memory_space_constraint(value, pltpu.HBM)


def params(mib):
    return pltpu.CompilerParams(vmem_limit_bytes=mib * 1024 * 1024)


LONG = pl.CostEstimate(flops=20 * 10**9, bytes_accessed=0, transcendentals=0)


def odd(axis):
    return lax.rem(lax.axis_index(axis), 2)


def first_swap(value, axis):
    return lax.ppermute(value, axis, [(i, i ^ 1) for i in range(lax.axis_size(axis))])


def second_swap(value, axis):
    rows, cols = lax.axis_size("sx"), lax.axis_size("sy")
    pairs = []
    for i in range(rows):
        for j in range(cols):
            if axis == "sx":
                k = i - 1 if i % 2 == 0 else i + 1
                target = (k, j) if 0 <= k < rows else (i, j ^ 1)
            else:
                k = j - 1 if j % 2 == 0 else j + 1
                target = (i, k) if 0 <= k < cols else (i ^ 2, j)
            pairs.append((i * cols + j, target[0] * cols + target[1]))
    return lax.ppermute(value, ("sx", "sy"), pairs)


def cross_swap(value, axis, bits):
    return lax.ppermute(value, axis, [(i, i ^ bits) for i in range(lax.axis_size(axis))])


def inner(axis):
    me = lax.axis_index(axis)
    return ((me > 0) & (me < lax.axis_size(axis) - 1)).astype(jnp.float32)


def x_faces():
    return odd("sx"), 1 - odd("sx")


def y_faces():
    return 2 + odd("sy"), 3 - odd("sy")


def send_kernel(traces, xb, yb, xa, ya, sems):
    faces = (*x_faces(), *y_faces())
    copies = [
        pltpu.make_async_copy(traces.at[:, face], out, sems.at[index])
        for index, (face, out) in enumerate(zip(faces, (xa, xb, ya, yb)))
    ]
    for copy in copies:
        copy.start()
    for copy in copies:
        copy.wait()


def product(left, right):
    return jnp.dot(left, right, preferred_element_type=jnp.float32)


def trade_jumps(jumps, traces, partner, axis, faces, received):
    for trade, (face, got) in enumerate(zip(faces, received)):
        for sub in range(traces.shape[0]):
            other = got[partner[sub, face]].astype(jnp.float32)
            if trade == 1:
                other = other * inner(axis)
            own = traces[sub, face].astype(jnp.float32)
            jumps[trade, sub] = (own - other).astype(jnp.bfloat16)


def flat_face(jumps, index):
    _, subs, rhs, size = jumps.shape
    return jumps[index].reshape(subs * rhs, size)


def pair_sum(jumps, first):
    up = flat_face(jumps, first).astype(jnp.float32)
    return (up + flat_face(jumps, first + 1).astype(jnp.float32)).astype(jnp.bfloat16)


def z_kernel(
    yb, xa, ya, traces, self_block, opposite_block, cross_block, corner_map,
    map_out, base_z, cross_z, jumps,
):
    del xa, yb, ya
    subs, _, rhs, size = traces.shape
    rows = subs * rhs
    for sub in range(subs):
        up = traces[sub, 4].astype(jnp.float32)
        down = traces[sub, 5].astype(jnp.float32)
        if sub + 1 < subs:
            up = up - traces[sub + 1, 5].astype(jnp.float32)
        if sub > 0:
            down = down - traces[sub - 1, 4].astype(jnp.float32)
        jumps[0, sub] = up.astype(jnp.bfloat16)
        jumps[1, sub] = down.astype(jnp.bfloat16)
    width = CORNERS * COMPS
    row = lax.broadcasted_iota(jnp.int32, (width, width), 0)
    col = lax.broadcasted_iota(jnp.int32, (width, width), 1)
    order = (col == (row % CORNERS) * COMPS + row // CORNERS).astype(jnp.float32)
    order = order.astype(jnp.bfloat16)
    for face in range(6):
        map_out[face] = product(order, corner_map[face]).astype(jnp.bfloat16)
    flat = jumps[...].reshape(2 * rows, size)
    with_self = product(flat, self_block[...])
    with_opp = product(flat, opposite_block[...])
    base_z[0] = with_self[:rows] + with_opp[rows:]
    base_z[1] = with_self[rows:] + with_opp[:rows]
    cross_z[...] = product(pair_sum(jumps, 0), cross_block[...])


def y_kernel(
    partner, traces, ryb, rya, rxb, self_block, opposite_block, cross_block, cross_z,
    base_y, cross_y, base_x, jumps,
):
    del rxb
    subs, _, rhs, size = traces.shape
    rows = subs * rhs
    trade_jumps(jumps, traces, partner, "sy", y_faces(), (rya, ryb))
    from_y = product(pair_sum(jumps, 0), cross_block[...])
    cross_y[...] = from_y
    base_x[...] = from_y + cross_z[...]
    flat = jumps[...].reshape(2 * rows, size)
    with_self = product(flat, self_block[...])
    with_opp = product(flat, opposite_block[...])
    base_y[0] = with_self[:rows] + with_opp[rows:] + cross_z[...]
    base_y[1] = with_self[rows:] + with_opp[:rows] + cross_z[...]


def high_low(value):
    high = value.astype(jnp.bfloat16).astype(jnp.float32)
    return high, value - high


def coarse_rows(partials, owners, rows):
    subs = owners.shape[0]
    width = partials.shape[1]
    rhs = width // subs
    entries = jnp.zeros((2 * CORNERS, subs * LANES), jnp.float32)
    source = lax.broadcasted_iota(jnp.int32, (width, subs * LANES), 0)
    target = lax.broadcasted_iota(jnp.int32, (width, subs * LANES), 1)
    spread = (source // rhs) * LANES + (source % rhs) * COMPS
    for comp in range(COMPS):
        part = partials[comp * CORNERS : (comp + 1) * CORNERS]
        stacked = jnp.concatenate(high_low(part), axis=0).astype(jnp.bfloat16)
        place = (target == spread + comp).astype(jnp.float32).astype(jnp.bfloat16)
        entries += product(stacked, place)
    entries = entries[:CORNERS] + entries[CORNERS:]
    total = jnp.zeros((rows, LANES), jnp.float32)
    numbers = lax.broadcasted_iota(jnp.int32, (rows, CORNERS), 0)
    for sub in range(subs):
        onehot = (numbers == owners[sub : sub + 1, :]).astype(jnp.float32).astype(jnp.bfloat16)
        for term in high_low(entries[:, sub * LANES : (sub + 1) * LANES]):
            total += product(onehot, term.astype(jnp.bfloat16))
    return total


def local_kernel(
    partner, viscosity, traces, rxa, rxb, self_block, opposite_block, cross_block,
    base_x, base_y, base_z, cross_y, owners, corner_map,
    xa, xb, ya, yb, local_z, to_xa, to_xb, to_ya, to_yb, kept, jumps, dense,
):
    subs, _, rhs, size = traces.shape
    rows = subs * rhs
    trade_jumps(jumps, traces, partner, "sx", x_faces(), (rxa, rxb))
    flat = jumps[...].reshape(2 * rows, size)
    with_self = product(flat, self_block[...])
    with_opp = product(flat, opposite_block[...])
    from_x = product(pair_sum(jumps, 0), cross_block[...])
    from_xy = from_x + cross_y[...]
    totals = (
        with_self[:rows] + with_opp[rows:] + base_x[...],
        with_self[rows:] + with_opp[:rows] + base_x[...],
        base_y[0] + from_x,
        base_y[1] + from_x,
        base_z[0] + from_xy,
        base_z[1] + from_xy,
    )
    faces = (*x_faces(), *y_faces(), 4, 5)
    outs = (xa, xb, ya, yb, local_z.at[0], local_z.at[1])
    sent = (to_xa, to_xb, to_ya, to_yb)
    partials = jnp.zeros((COMPS * CORNERS, rows), jnp.float32)
    for index, (face, total, out) in enumerate(zip(faces, totals, outs)):
        for sub in range(subs):
            here = slice(sub * rhs, (sub + 1) * rhs)
            value = (viscosity[sub] * total[here]).astype(jnp.bfloat16)
            out[sub] = value
            if index < 4:
                sent[index][partner[sub, face]] = value
        partials += lax.dot_general(
            corner_map[face],
            out[...].reshape(rows, size),
            (((1,), (1,)), ((), ())),
            preferred_element_type=jnp.float32,
        )
    dense[...] = coarse_rows(partials, owners[...], dense.shape[0])
    me = lax.axis_index("sy")

    def block(bits):
        start = pl.multiple_of((me ^ bits) * COARSE_DEV, COARSE_DEV)
        return dense[pl.ds(start, COARSE_DEV), :]

    half, per_row = kept.shape[0], size // LANES
    for index in range((to_ya.shape[0] - subs) * per_row):
        lanes = slice(index % per_row * LANES, (index % per_row + 1) * LANES)
        both = jnp.zeros((2 * COARSE_DEV, LANES), jnp.float32)
        if index < half:
            kept[index] = block(2 * index)
            both = jnp.concatenate(high_low(block(2 * index + 1)), axis=0)
        to_ya[subs + index // per_row, :, lanes] = both.astype(jnp.bfloat16)


def first_add_kernel(subs, kept, got, *outs):
    per_row = got.shape[2] // LANES
    for index in range(kept.shape[0]):
        lanes = slice(index % per_row * LANES, (index % per_row + 1) * LANES)
        both = got[subs + index // per_row, :, lanes].astype(jnp.float32)
        total = kept[index] + both[:COARSE_DEV] + both[COARSE_DEV:]
        outs[index % 4][index // 4] = total


def last_add_kernel(*refs):
    *terms, coarse, total, sem = refs
    value = terms[0][0]
    for term in terms[1:]:
        value = value + term[0]
    total[...] = value[:, : total.shape[1]]
    copy = pltpu.make_async_copy(total, coarse, sem)
    copy.start()
    copy.wait()


def apply_kernel(rxb, ryb, rxa, rya, local_z, ya, yb, xa, xb, applied, held, sems):
    subs = held.shape[1]
    copies = []

    def write(index, sub, face, value):
        held[index, sub] = value
        copies.append(
            pltpu.make_async_copy(held.at[index, sub], applied.at[sub, face], sems.at[index, sub])
        )
        copies[-1].start()

    trades = zip((*y_faces(), *x_faces()), (ya, yb, xa, xb), (rya, ryb, rxa, rxb))
    for index, (face, local, got) in enumerate(trades):
        for sub in range(subs):
            other = got[sub].astype(jnp.float32)
            if index == 1:
                other = other * inner("sy")
            if index == 3:
                other = other * inner("sx")
            write(index, sub, face, local[sub].astype(jnp.float32) - other)
    for sub in range(subs):
        up = local_z[0, sub].astype(jnp.float32)
        down = local_z[1, sub].astype(jnp.float32)
        if sub + 1 < subs:
            up = up - local_z[1, sub + 1].astype(jnp.float32)
        if sub > 0:
            down = down - local_z[0, sub - 1].astype(jnp.float32)
        write(4, sub, 4, up)
        write(5, sub, 5, down)
    for copy in copies:
        copy.wait()


def body(
    traces, viscosity, partner, corner_owner, self_block, opposite_block, cross_block, corner_map
):
    values = traces[0, 0]
    slots, visc, owners = partner[0, 0], viscosity[0, 0], corner_owner[0, 0]
    subs, _, rhs, size = values.shape
    count = lax.axis_size("sy")
    rows = subs * rhs
    face_shape = (subs, rhs, size)
    map_shape = (6, CORNERS * COMPS, size)
    bf16, f32 = jnp.bfloat16, jnp.float32

    xb, yb, xa, ya = pl.pallas_call(
        send_kernel,
        in_specs=[HBM],
        out_specs=[VMEM] * 4,
        out_shape=[in_vmem(face_shape, bf16)] * 4,
        scratch_shapes=[pltpu.SemaphoreType.DMA((4,))],
        compiler_params=params(8),
        cost_estimate=LONG,
    )(in_hbm(values))
    rxb = second_swap(xb, "sx")
    ryb = second_swap(yb, "sy")
    rxa = first_swap(xa, "sx")
    rya = first_swap(ya, "sy")
    map_v, base_z, cross_z = pl.pallas_call(
        z_kernel,
        in_specs=[VMEM] * 8,
        out_specs=[VMEM] * 3,
        out_shape=[in_vmem(map_shape, bf16), in_vmem((2, rows, size), f32)]
        + [in_vmem((rows, size), f32)],
        scratch_shapes=[pltpu.VMEM((2,) + face_shape, bf16)],
        compiler_params=params(12),
        cost_estimate=LONG,
    )(
        yb, xa, ya, values, self_block, opposite_block, cross_block,
        jnp.transpose(corner_map, (1, 0, 2)),
    )
    base_y, cross_y, base_x = pl.pallas_call(
        y_kernel,
        in_specs=[SMEM] + [VMEM] * 8,
        out_specs=[VMEM] * 3,
        out_shape=[in_vmem((2, rows, size), f32)] + [in_vmem((rows, size), f32)] * 2,
        scratch_shapes=[pltpu.VMEM((2,) + face_shape, bf16)],
        compiler_params=params(12),
    )(slots, values, ryb, rya, rxb, self_block, opposite_block, cross_block, cross_z)
    half, per_row = count // 2, size // LANES
    long_shape = (subs + -(-half // per_row), rhs, size)

    def blocks(number):
        return in_vmem((number, COARSE_DEV, LANES), f32)

    xa, xb, ya, yb, local_z, to_xa, to_xb, to_ya, to_yb, kept = pl.pallas_call(
        local_kernel,
        in_specs=[SMEM] * 2 + [VMEM] * 12,
        out_specs=[VMEM] * 10,
        out_shape=[in_vmem(face_shape, bf16)] * 4
        + [in_vmem((2,) + face_shape, bf16)]
        + [in_vmem(face_shape, bf16)] * 2
        + [in_vmem(long_shape, bf16), in_vmem(face_shape, bf16), blocks(half)],
        scratch_shapes=[
            pltpu.VMEM((2,) + face_shape, bf16),
            pltpu.VMEM((COARSE_DEV * count, LANES), f32),
        ],
        compiler_params=params(16),
    )(
        slots, visc, values, rxa, rxb, self_block, opposite_block, cross_block,
        base_x, base_y, base_z, cross_y, owners, map_v,
    )
    rya = first_swap(to_ya, "sy")
    rxb = second_swap(to_xb, "sx")
    rxa = first_swap(to_xa, "sx")
    ryb = second_swap(to_yb, "sy")
    parts = pl.pallas_call(
        lambda *refs: first_add_kernel(subs, *refs),
        in_specs=[VMEM] * 2,
        out_specs=[VMEM] * 4,
        out_shape=[blocks(half // 4)] * 4,
        compiler_params=params(4),
    )(kept, rya)
    terms = [parts[0]] + [cross_swap(parts[k], "sy", 2 * k) for k in (3, 2, 1)]
    base_bits = 8
    while base_bits < count:
        total = sum(terms[1:], terms[0])
        width = min(4, count // base_bits)
        terms = [total[0::width]] + [
            cross_swap(total[k::width], "sy", base_bits * k) for k in range(1, width)
        ]
        base_bits *= width
    applied = pl.pallas_call(
        apply_kernel,
        in_specs=[VMEM] * 9,
        out_specs=HBM,
        out_shape=jax.ShapeDtypeStruct(values.shape, f32),
        scratch_shapes=[pltpu.VMEM((6,) + face_shape, f32), pltpu.SemaphoreType.DMA((6, subs))],
        compiler_params=params(12),
        cost_estimate=LONG,
    )(rxb, ryb, rxa, rya, local_z, ya, yb, xa, xb)
    coarse = pl.pallas_call(
        last_add_kernel,
        in_specs=[VMEM] * len(terms),
        out_specs=HBM,
        out_shape=jax.ShapeDtypeStruct((COARSE_DEV, rhs * COMPS), f32),
        scratch_shapes=[pltpu.VMEM((COARSE_DEV, rhs * COMPS), f32), pltpu.SemaphoreType.DMA],
        compiler_params=params(4),
    )(*terms)
    return applied[None, None], coarse.T


def solution(mesh):
    return jax.shard_map(
        body,
        mesh=mesh,
        in_specs=(
            P("sx", "sy", None, None, None, None),
            P("sx", "sy", None),
            P("sx", "sy", None, None),
            P("sx", "sy", None, None),
            P(),
            P(),
            P(),
            P(),
        ),
        out_specs=(P("sx", "sy", None, None, None, None), P(None, ("sx", "sy"))),
        check_vma=False,
    )
```

```python
import jax
import jax.numpy as jnp
from jax import lax
from jax.experimental import pallas as pl
from jax.experimental.pallas import tpu as pltpu
from jax.sharding import PartitionSpec as P

CORNERS = 8
COMPS = 3
COARSE_DEV = 8
LANES = 128

VMEM = pl.BlockSpec(memory_space=pltpu.VMEM)
SMEM = pl.BlockSpec(memory_space=pltpu.SMEM)
HBM = pl.BlockSpec(memory_space=pltpu.HBM)
ANY = pl.BlockSpec(memory_space=pl.ANY)


def in_vmem(shape, dtype):
    return pltpu.VMEM(shape, dtype)


def in_hbm(value):
    return pltpu.with_memory_space_constraint(value, pltpu.HBM)


def params(mib):
    return pltpu.CompilerParams(vmem_limit_bytes=mib * 1024 * 1024)


LONG = pl.CostEstimate(flops=20 * 10**9, bytes_accessed=0, transcendentals=0)


def odd(axis):
    return lax.rem(lax.axis_index(axis), 2)


def first_swap(value, axis):
    return lax.ppermute(value, axis, [(i, i ^ 1) for i in range(lax.axis_size(axis))])


def second_swap(value, axis):
    rows, cols = lax.axis_size("sx"), lax.axis_size("sy")
    pairs = []
    for i in range(rows):
        for j in range(cols):
            if axis == "sx":
                k = i - 1 if i % 2 == 0 else i + 1
                target = (k, j) if 0 <= k < rows else (i, j ^ 1)
            else:
                k = j - 1 if j % 2 == 0 else j + 1
                target = (i, k) if 0 <= k < cols else (i ^ 2, j)
            pairs.append((i * cols + j, target[0] * cols + target[1]))
    return lax.ppermute(value, ("sx", "sy"), pairs)


def cross_swap(value, axis, bits):
    return lax.ppermute(value, axis, [(i, i ^ bits) for i in range(lax.axis_size(axis))])


def inner(axis):
    me = lax.axis_index(axis)
    return ((me > 0) & (me < lax.axis_size(axis) - 1)).astype(jnp.float32)


def x_faces():
    return odd("sx"), 1 - odd("sx")


def y_faces():
    return 2 + odd("sy"), 3 - odd("sy")


def send_kernel(traces, xb, yb, xa, ya, sems):
    faces = (*x_faces(), *y_faces())
    copies = [
        pltpu.make_async_copy(traces.at[:, face], out, sems.at[index])
        for index, (face, out) in enumerate(zip(faces, (xa, xb, ya, yb)))
    ]
    for copy in copies:
        copy.start()
    for copy in copies:
        copy.wait()


def product(left, right):
    return jnp.dot(left, right, preferred_element_type=jnp.float32)


def trade_jumps(jumps, traces, partner, axis, faces, received):
    for trade, (face, got) in enumerate(zip(faces, received)):
        for sub in range(traces.shape[0]):
            other = got[partner[sub, face]].astype(jnp.float32)
            if trade == 1:
                other = other * inner(axis)
            own = traces[sub, face].astype(jnp.float32)
            jumps[trade, sub] = (own - other).astype(jnp.bfloat16)


def flat_face(jumps, index):
    _, subs, rhs, size = jumps.shape
    return jumps[index].reshape(subs * rhs, size)


def pair_sum(jumps, first):
    up = flat_face(jumps, first).astype(jnp.float32)
    return (up + flat_face(jumps, first + 1).astype(jnp.float32)).astype(jnp.bfloat16)


def z_kernel(
    yb, xa, ya, traces, self_block, opposite_block, cross_block, corner_map,
    map_out, base_z, cross_z, jumps,
):
    del xa, yb, ya
    subs, _, rhs, size = traces.shape
    rows = subs * rhs
    for sub in range(subs):
        up = traces[sub, 4].astype(jnp.float32)
        down = traces[sub, 5].astype(jnp.float32)
        if sub + 1 < subs:
            up = up - traces[sub + 1, 5].astype(jnp.float32)
        if sub > 0:
            down = down - traces[sub - 1, 4].astype(jnp.float32)
        jumps[0, sub] = up.astype(jnp.bfloat16)
        jumps[1, sub] = down.astype(jnp.bfloat16)
    width = CORNERS * COMPS
    row = lax.broadcasted_iota(jnp.int32, (width, width), 0)
    col = lax.broadcasted_iota(jnp.int32, (width, width), 1)
    order = (col == (row % CORNERS) * COMPS + row // CORNERS).astype(jnp.float32)
    order = order.astype(jnp.bfloat16)
    for face in range(6):
        map_out[face] = product(order, corner_map[face]).astype(jnp.bfloat16)
    flat = jumps[...].reshape(2 * rows, size)
    with_self = product(flat, self_block[...])
    with_opp = product(flat, opposite_block[...])
    base_z[0] = with_self[:rows] + with_opp[rows:]
    base_z[1] = with_self[rows:] + with_opp[:rows]
    cross_z[...] = product(pair_sum(jumps, 0), cross_block[...])


def y_kernel(
    partner, traces, ryb, rya, rxb, self_block, opposite_block, cross_block, cross_z,
    base_y, cross_y, base_x, jumps,
):
    del rxb
    subs, _, rhs, size = traces.shape
    rows = subs * rhs
    trade_jumps(jumps, traces, partner, "sy", y_faces(), (rya, ryb))
    from_y = product(pair_sum(jumps, 0), cross_block[...])
    cross_y[...] = from_y
    base_x[...] = from_y + cross_z[...]
    flat = jumps[...].reshape(2 * rows, size)
    with_self = product(flat, self_block[...])
    with_opp = product(flat, opposite_block[...])
    base_y[0] = with_self[:rows] + with_opp[rows:] + cross_z[...]
    base_y[1] = with_self[rows:] + with_opp[:rows] + cross_z[...]


def high_low(value):
    high = value.astype(jnp.bfloat16).astype(jnp.float32)
    return high, value - high


def coarse_rows(partials, owners, rows):
    subs = owners.shape[0]
    width = partials.shape[1]
    rhs = width // subs
    entries = jnp.zeros((2 * CORNERS, subs * LANES), jnp.float32)
    source = lax.broadcasted_iota(jnp.int32, (width, subs * LANES), 0)
    target = lax.broadcasted_iota(jnp.int32, (width, subs * LANES), 1)
    spread = (source // rhs) * LANES + (source % rhs) * COMPS
    for comp in range(COMPS):
        part = partials[comp * CORNERS : (comp + 1) * CORNERS]
        stacked = jnp.concatenate(high_low(part), axis=0).astype(jnp.bfloat16)
        place = (target == spread + comp).astype(jnp.float32).astype(jnp.bfloat16)
        entries += product(stacked, place)
    entries = entries[:CORNERS] + entries[CORNERS:]
    total = jnp.zeros((rows, LANES), jnp.float32)
    numbers = lax.broadcasted_iota(jnp.int32, (rows, CORNERS), 0)
    for sub in range(subs):
        onehot = (numbers == owners[sub : sub + 1, :]).astype(jnp.float32).astype(jnp.bfloat16)
        for term in high_low(entries[:, sub * LANES : (sub + 1) * LANES]):
            total += product(onehot, term.astype(jnp.bfloat16))
    return total


def local_kernel(
    partner, viscosity, traces, rxa, rxb, self_block, opposite_block, cross_block,
    base_x, base_y, base_z, cross_y, owners, corner_map,
    xa, xb, ya, yb, local_z, to_xa, to_xb, to_ya, to_yb, kept, jumps, dense,
):
    subs, _, rhs, size = traces.shape
    rows = subs * rhs
    trade_jumps(jumps, traces, partner, "sx", x_faces(), (rxa, rxb))
    flat = jumps[...].reshape(2 * rows, size)
    with_self = product(flat, self_block[...])
    with_opp = product(flat, opposite_block[...])
    from_x = product(pair_sum(jumps, 0), cross_block[...])
    from_xy = from_x + cross_y[...]
    totals = (
        with_self[:rows] + with_opp[rows:] + base_x[...],
        with_self[rows:] + with_opp[:rows] + base_x[...],
        base_y[0] + from_x,
        base_y[1] + from_x,
        base_z[0] + from_xy,
        base_z[1] + from_xy,
    )
    faces = (*x_faces(), *y_faces(), 4, 5)
    outs = (xa, xb, ya, yb, local_z.at[0], local_z.at[1])
    sent = (to_xa, to_xb, to_ya, to_yb)
    partials = jnp.zeros((COMPS * CORNERS, rows), jnp.float32)
    for index, (face, total, out) in enumerate(zip(faces, totals, outs)):
        for sub in range(subs):
            here = slice(sub * rhs, (sub + 1) * rhs)
            value = (viscosity[sub] * total[here]).astype(jnp.bfloat16)
            out[sub] = value
            if index < 4:
                sent[index][partner[sub, face]] = value
        partials += lax.dot_general(
            corner_map[face],
            out[...].reshape(rows, size),
            (((1,), (1,)), ((), ())),
            preferred_element_type=jnp.float32,
        )
    dense[...] = coarse_rows(partials, owners[...], dense.shape[0])
    me = lax.axis_index("sy")

    def block(bits):
        start = pl.multiple_of((me ^ bits) * COARSE_DEV, COARSE_DEV)
        return dense[pl.ds(start, COARSE_DEV), :]

    half, per_row = kept.shape[0], size // LANES
    for index in range((to_ya.shape[0] - subs) * per_row):
        lanes = slice(index % per_row * LANES, (index % per_row + 1) * LANES)
        both = jnp.zeros((2 * COARSE_DEV, LANES), jnp.float32)
        if index < half:
            kept[index] = block(2 * index)
            both = jnp.concatenate(high_low(block(2 * index + 1)), axis=0)
        to_ya[subs + index // per_row, :, lanes] = both.astype(jnp.bfloat16)


def first_add_kernel(subs, after, kept, got, *refs):
    del after
    keep, give = refs[3:5]
    half, per_row = kept.shape[0], got.shape[2] // LANES
    for index in range(half):
        lanes = slice(index % per_row * LANES, (index % per_row + 1) * LANES)
        both = got[subs + index // per_row, :, lanes].astype(jnp.float32)
        total = kept[index] + both[:COARSE_DEV] + both[COARSE_DEV:]
        out = keep if index < half // 2 else give
        out[index % (half // 2)] = total


def next_add_kernel(after, kept, got, keep, give):
    del after
    half = kept.shape[0]
    total = kept[...] + got[...]
    keep[...] = total[: half // 2]
    give[...] = total[half // 2 :]


def last_add_kernel(after, kept, got, coarse, total, sem):
    del after
    total[...] = (kept[0] + got[0])[:, : total.shape[1]]
    copy = pltpu.make_async_copy(total, coarse, sem)
    copy.start()
    copy.wait()


def apply_z_kernel(local_z, applied, held, sems):
    subs = local_z.shape[1]
    copies = []
    for sub in range(subs):
        up = local_z[0, sub].astype(jnp.float32)
        down = local_z[1, sub].astype(jnp.float32)
        if sub + 1 < subs:
            up = up - local_z[1, sub + 1].astype(jnp.float32)
        if sub > 0:
            down = down - local_z[0, sub - 1].astype(jnp.float32)
        held[sub, 0] = up
        held[sub, 1] = down
        copies.append(
            pltpu.make_async_copy(held.at[sub], applied.at[sub, pl.ds(4, 2)], sems.at[sub])
        )
        copies[-1].start()
    for copy in copies:
        copy.wait()


def apply_kernel(applied_in, rxb, ryb, rxa, rya, ya, yb, xa, xb, applied, held, sems):
    del applied_in
    copies = []
    trades = zip((*y_faces(), *x_faces()), (ya, yb, xa, xb), (rya, ryb, rxa, rxb))
    for index, (face, local, got) in enumerate(trades):
        for sub in range(held.shape[1]):
            other = got[sub].astype(jnp.float32)
            if index == 1:
                other = other * inner("sy")
            if index == 3:
                other = other * inner("sx")
            held[index, sub] = local[sub].astype(jnp.float32) - other
            copies.append(
                pltpu.make_async_copy(
                    held.at[index, sub], applied.at[sub, face], sems.at[index, sub]
                )
            )
            copies[-1].start()
    for copy in copies:
        copy.wait()


def body(
    traces, viscosity, partner, corner_owner, self_block, opposite_block, cross_block, corner_map
):
    values = traces[0, 0]
    slots, visc, owners = partner[0, 0], viscosity[0, 0], corner_owner[0, 0]
    subs, _, rhs, size = values.shape
    count = lax.axis_size("sy")
    rows = subs * rhs
    face_shape = (subs, rhs, size)
    map_shape = (6, CORNERS * COMPS, size)
    bf16, f32 = jnp.bfloat16, jnp.float32

    xb, yb, xa, ya = pl.pallas_call(
        send_kernel,
        in_specs=[HBM],
        out_specs=[VMEM] * 4,
        out_shape=[in_vmem(face_shape, bf16)] * 4,
        scratch_shapes=[pltpu.SemaphoreType.DMA((4,))],
        compiler_params=params(8),
        cost_estimate=LONG,
    )(in_hbm(values))
    rxb = second_swap(xb, "sx")
    ryb = second_swap(yb, "sy")
    rxa = first_swap(xa, "sx")
    rya = first_swap(ya, "sy")
    map_v, base_z, cross_z = pl.pallas_call(
        z_kernel,
        in_specs=[VMEM] * 8,
        out_specs=[VMEM] * 3,
        out_shape=[in_vmem(map_shape, bf16), in_vmem((2, rows, size), f32)]
        + [in_vmem((rows, size), f32)],
        scratch_shapes=[pltpu.VMEM((2,) + face_shape, bf16)],
        compiler_params=params(12),
        cost_estimate=LONG,
    )(
        yb, xa, ya, values, self_block, opposite_block, cross_block,
        jnp.transpose(corner_map, (1, 0, 2)),
    )
    base_y, cross_y, base_x = pl.pallas_call(
        y_kernel,
        in_specs=[SMEM] + [VMEM] * 8,
        out_specs=[VMEM] * 3,
        out_shape=[in_vmem((2, rows, size), f32)] + [in_vmem((rows, size), f32)] * 2,
        scratch_shapes=[pltpu.VMEM((2,) + face_shape, bf16)],
        compiler_params=params(12),
    )(slots, values, ryb, rya, rxb, self_block, opposite_block, cross_block, cross_z)
    half, per_row = count // 2, size // LANES
    long_shape = (subs + -(-half // per_row), rhs, size)

    def blocks(number):
        return in_vmem((number, COARSE_DEV, LANES), f32)

    xa, xb, ya, yb, local_z, to_xa, to_xb, to_ya, to_yb, kept = pl.pallas_call(
        local_kernel,
        in_specs=[SMEM] * 2 + [VMEM] * 12,
        out_specs=[VMEM] * 10,
        out_shape=[in_vmem(face_shape, bf16)] * 4
        + [in_vmem((2,) + face_shape, bf16)]
        + [in_vmem(face_shape, bf16)] * 2
        + [in_vmem(long_shape, bf16), in_vmem(face_shape, bf16), blocks(half)],
        scratch_shapes=[
            pltpu.VMEM((2,) + face_shape, bf16),
            pltpu.VMEM((COARSE_DEV * count, LANES), f32),
        ],
        compiler_params=params(16),
    )(
        slots, visc, values, rxa, rxb, self_block, opposite_block, cross_block,
        base_x, base_y, base_z, cross_y, owners, map_v,
    )
    rya = first_swap(to_ya, "sy")
    out_shape = jax.ShapeDtypeStruct(values.shape, f32)
    applied = pl.pallas_call(
        apply_z_kernel,
        in_specs=[VMEM],
        out_specs=HBM,
        out_shape=out_shape,
        scratch_shapes=[
            pltpu.VMEM((subs, 2, rhs, size), f32),
            pltpu.SemaphoreType.DMA((subs,)),
        ],
        compiler_params=params(8),
        cost_estimate=LONG,
    )(local_z)
    half //= 2
    kept, give, to_xa, to_xb, to_yb = pl.pallas_call(
        lambda *refs: first_add_kernel(subs, *refs),
        in_specs=[HBM] + [VMEM] * 5,
        out_specs=[VMEM] * 5,
        out_shape=[blocks(half)] * 2 + [in_vmem(face_shape, bf16)] * 3,
        input_output_aliases={3: 2, 4: 3, 5: 4},
        compiler_params=params(4),
    )(in_hbm(applied), kept, rya, to_xa, to_xb, to_yb)
    got = cross_swap(give, "sy", 2 * half)
    rxb = second_swap(to_xb, "sx")
    ryb = second_swap(to_yb, "sy")
    rxa = first_swap(to_xa, "sx")
    while half > 1:
        half //= 2
        kept, give = pl.pallas_call(
            next_add_kernel,
            in_specs=[HBM] + [VMEM] * 2,
            out_specs=[VMEM] * 2,
            out_shape=[blocks(half)] * 2,
            compiler_params=params(4),
            cost_estimate=LONG,
        )(in_hbm(applied), kept, got)
        got = cross_swap(give, "sy", 2 * half)
    applied = pl.pallas_call(
        apply_kernel,
        in_specs=[HBM] + [VMEM] * 8,
        out_specs=HBM,
        out_shape=out_shape,
        input_output_aliases={0: 0},
        scratch_shapes=[pltpu.VMEM((4,) + face_shape, f32), pltpu.SemaphoreType.DMA((4, subs))],
        compiler_params=params(12),
        cost_estimate=LONG,
    )(applied, rxb, ryb, rxa, rya, ya, yb, xa, xb)
    coarse = pl.pallas_call(
        last_add_kernel,
        in_specs=[HBM] + [VMEM] * 2,
        out_specs=HBM,
        out_shape=jax.ShapeDtypeStruct((COARSE_DEV, rhs * COMPS), f32),
        scratch_shapes=[pltpu.VMEM((COARSE_DEV, rhs * COMPS), f32), pltpu.SemaphoreType.DMA],
        compiler_params=params(4),
    )(in_hbm(applied), kept, got)
    return applied[None, None], coarse.T


def solution(mesh):
    return jax.shard_map(
        body,
        mesh=mesh,
        in_specs=(
            P("sx", "sy", None, None, None, None),
            P("sx", "sy", None),
            P("sx", "sy", None, None),
            P("sx", "sy", None, None),
            P(),
            P(),
            P(),
            P(),
        ),
        out_specs=(P("sx", "sy", None, None, None, None), P(None, ("sx", "sy"))),
        check_vma=False,
    )
```

```python
import jax
import jax.numpy as jnp
from jax import lax
from jax.experimental import pallas as pl
from jax.experimental.pallas import tpu as pltpu
from jax.sharding import PartitionSpec as P

CORNERS = 8
COMPS = 3
COARSE_DEV = 8
LANES = 128

VMEM = pl.BlockSpec(memory_space=pltpu.VMEM)
SMEM = pl.BlockSpec(memory_space=pltpu.SMEM)
HBM = pl.BlockSpec(memory_space=pltpu.HBM)
ANY = pl.BlockSpec(memory_space=pl.ANY)


def in_vmem(shape, dtype):
    return pltpu.VMEM(shape, dtype)


def in_hbm(value):
    return pltpu.with_memory_space_constraint(value, pltpu.HBM)


def params(mib):
    return pltpu.CompilerParams(vmem_limit_bytes=mib * 1024 * 1024)


LONG = pl.CostEstimate(flops=20 * 10**9, bytes_accessed=0, transcendentals=0)


def odd(axis):
    return lax.rem(lax.axis_index(axis), 2)


def first_swap(value, axis):
    return lax.ppermute(value, axis, [(i, i ^ 1) for i in range(lax.axis_size(axis))])


def second_swap(value, axis):
    rows, cols = lax.axis_size("sx"), lax.axis_size("sy")
    pairs = []
    for i in range(rows):
        for j in range(cols):
            if axis == "sx":
                k = i - 1 if i % 2 == 0 else i + 1
                target = (k, j) if 0 <= k < rows else (i, j ^ 1)
            else:
                k = j - 1 if j % 2 == 0 else j + 1
                target = (i, k) if 0 <= k < cols else (i ^ 2, j)
            pairs.append((i * cols + j, target[0] * cols + target[1]))
    return lax.ppermute(value, ("sx", "sy"), pairs)


def cross_swap(value, axis, bits):
    return lax.ppermute(value, axis, [(i, i ^ bits) for i in range(lax.axis_size(axis))])


def inner(axis):
    me = lax.axis_index(axis)
    return ((me > 0) & (me < lax.axis_size(axis) - 1)).astype(jnp.float32)


def x_faces():
    return odd("sx"), 1 - odd("sx")


def y_faces():
    return 2 + odd("sy"), 3 - odd("sy")


def send_kernel(traces, xb, yb, xa, ya, sems):
    faces = (*x_faces(), *y_faces())
    copies = [
        pltpu.make_async_copy(traces.at[:, face], out, sems.at[index])
        for index, (face, out) in enumerate(zip(faces, (xa, xb, ya, yb)))
    ]
    for copy in copies:
        copy.start()
    for copy in copies:
        copy.wait()


def product(left, right):
    return jnp.dot(left, right, preferred_element_type=jnp.float32)


def trade_jumps(jumps, traces, partner, axis, faces, received):
    for trade, (face, got) in enumerate(zip(faces, received)):
        for sub in range(traces.shape[0]):
            other = got[partner[sub, face]].astype(jnp.float32)
            if trade == 1:
                other = other * inner(axis)
            own = traces[sub, face].astype(jnp.float32)
            jumps[trade, sub] = (own - other).astype(jnp.bfloat16)


def flat_face(jumps, index):
    _, subs, rhs, size = jumps.shape
    return jumps[index].reshape(subs * rhs, size)


def pair_sum(jumps, first):
    up = flat_face(jumps, first).astype(jnp.float32)
    return (up + flat_face(jumps, first + 1).astype(jnp.float32)).astype(jnp.bfloat16)


def z_kernel(
    xa, traces, self_block, opposite_block, cross_block, corner_map,
    map_out, base_z, cross_z, jumps,
):
    del xa
    subs, _, rhs, size = traces.shape
    rows = subs * rhs
    for sub in range(subs):
        up = traces[sub, 4].astype(jnp.float32)
        down = traces[sub, 5].astype(jnp.float32)
        if sub + 1 < subs:
            up = up - traces[sub + 1, 5].astype(jnp.float32)
        if sub > 0:
            down = down - traces[sub - 1, 4].astype(jnp.float32)
        jumps[0, sub] = up.astype(jnp.bfloat16)
        jumps[1, sub] = down.astype(jnp.bfloat16)
    width = CORNERS * COMPS
    row = lax.broadcasted_iota(jnp.int32, (width, LANES), 0)
    col = lax.broadcasted_iota(jnp.int32, (width, LANES), 1)
    place = (col % CORNERS) * COMPS + col // CORNERS
    order = ((row == place) & (col < width)).astype(jnp.float32).astype(jnp.bfloat16)
    for face in range(6):
        moved = lax.dot_general(
            corner_map[face], order, (((0,), (0,)), ((), ())), preferred_element_type=jnp.float32
        )
        map_out[face] = moved.astype(jnp.bfloat16)
    flat = jumps[...].reshape(2 * rows, size)
    with_self = product(flat, self_block[...])
    with_opp = product(flat, opposite_block[...])
    base_z[0] = with_self[:rows] + with_opp[rows:]
    base_z[1] = with_self[rows:] + with_opp[:rows]
    cross_z[...] = product(pair_sum(jumps, 0), cross_block[...])


def y_kernel(
    partner, traces, ryb, rya, rxb, self_block, opposite_block, cross_block, cross_z,
    base_y, cross_y, base_x, jumps,
):
    del rxb
    subs, _, rhs, size = traces.shape
    rows = subs * rhs
    trade_jumps(jumps, traces, partner, "sy", y_faces(), (rya, ryb))
    from_y = product(pair_sum(jumps, 0), cross_block[...])
    cross_y[...] = from_y
    base_x[...] = from_y + cross_z[...]
    flat = jumps[...].reshape(2 * rows, size)
    with_self = product(flat, self_block[...])
    with_opp = product(flat, opposite_block[...])
    base_y[0] = with_self[:rows] + with_opp[rows:] + cross_z[...]
    base_y[1] = with_self[rows:] + with_opp[:rows] + cross_z[...]


def high_low(value):
    high = value.astype(jnp.bfloat16).astype(jnp.float32)
    return high, value - high


def coarse_rows(partials, owners, rows):
    subs = owners.shape[0]
    width = partials.shape[1]
    rhs = width // subs
    entries = jnp.zeros((2 * CORNERS, subs * LANES), jnp.float32)
    source = lax.broadcasted_iota(jnp.int32, (width, subs * LANES), 0)
    target = lax.broadcasted_iota(jnp.int32, (width, subs * LANES), 1)
    spread = (source // rhs) * LANES + (source % rhs) * COMPS
    for comp in range(COMPS):
        part = partials[comp * CORNERS : (comp + 1) * CORNERS]
        stacked = jnp.concatenate(high_low(part), axis=0).astype(jnp.bfloat16)
        place = (target == spread + comp).astype(jnp.float32).astype(jnp.bfloat16)
        entries += product(stacked, place)
    entries = entries[:CORNERS] + entries[CORNERS:]
    total = jnp.zeros((rows, LANES), jnp.float32)
    numbers = lax.broadcasted_iota(jnp.int32, (rows, CORNERS), 0)
    for sub in range(subs):
        onehot = (numbers == owners[sub : sub + 1, :]).astype(jnp.float32).astype(jnp.bfloat16)
        for term in high_low(entries[:, sub * LANES : (sub + 1) * LANES]):
            total += product(onehot, term.astype(jnp.bfloat16))
    return total


def local_kernel(
    partner, viscosity, traces, rxa, rxb, self_block, opposite_block, cross_block,
    base_x, base_y, base_z, cross_y, owners, corner_map,
    xa, xb, ya, yb, local_z, to_xa, to_xb, to_ya, to_yb, kept, jumps, dense,
):
    subs, _, rhs, size = traces.shape
    rows = subs * rhs
    trade_jumps(jumps, traces, partner, "sx", x_faces(), (rxa, rxb))
    flat = jumps[...].reshape(2 * rows, size)
    with_self = product(flat, self_block[...])
    with_opp = product(flat, opposite_block[...])
    from_x = product(pair_sum(jumps, 0), cross_block[...])
    from_xy = from_x + cross_y[...]
    totals = (
        with_self[:rows] + with_opp[rows:] + base_x[...],
        with_self[rows:] + with_opp[:rows] + base_x[...],
        base_y[0] + from_x,
        base_y[1] + from_x,
        base_z[0] + from_xy,
        base_z[1] + from_xy,
    )
    faces = (*x_faces(), *y_faces(), 4, 5)
    outs = (xa, xb, ya, yb, local_z.at[0], local_z.at[1])
    sent = (to_xa, to_xb, to_ya, to_yb)
    partials = jnp.zeros((rows, LANES), jnp.float32)
    for index, (face, total, out) in enumerate(zip(faces, totals, outs)):
        for sub in range(subs):
            here = slice(sub * rhs, (sub + 1) * rhs)
            value = (viscosity[sub] * total[here]).astype(jnp.bfloat16)
            out[sub] = value
            if index < 4:
                sent[index][partner[sub, face]] = value
        partials += product(out[...].reshape(rows, size), corner_map[face])
    partials = partials.T
    dense[...] = coarse_rows(partials, owners[...], dense.shape[0])
    me = lax.axis_index("sy")

    def block(bits):
        start = pl.multiple_of((me ^ bits) * COARSE_DEV, COARSE_DEV)
        return dense[pl.ds(start, COARSE_DEV), :]

    half, per_row = kept.shape[0], size // LANES
    for index in range((to_ya.shape[0] - subs) * per_row):
        lanes = slice(index % per_row * LANES, (index % per_row + 1) * LANES)
        both = jnp.zeros((2 * COARSE_DEV, LANES), jnp.float32)
        if index < half:
            kept[index] = block(2 * index)
            both = jnp.concatenate(high_low(block(2 * index + 1)), axis=0)
        to_ya[subs + index // per_row, :, lanes] = both.astype(jnp.bfloat16)


def first_add_kernel(subs, kept, got, keep, give):
    half, per_row = kept.shape[0], got.shape[2] // LANES
    for index in range(half):
        lanes = slice(index % per_row * LANES, (index % per_row + 1) * LANES)
        both = got[subs + index // per_row, :, lanes].astype(jnp.float32)
        total = kept[index] + both[:COARSE_DEV] + both[COARSE_DEV:]
        out = keep if index < half // 2 else give
        out[index % (half // 2)] = total


def next_add_kernel(after, kept, got, keep, give):
    del after
    half = kept.shape[0]
    total = kept[...] + got[...]
    keep[...] = total[: half // 2]
    give[...] = total[half // 2 :]


def last_add_kernel(kept, got, coarse, total, sem):
    total[...] = (kept[0] + got[0])[:, : total.shape[1]]
    copy = pltpu.make_async_copy(total, coarse, sem)
    copy.start()
    copy.wait()


def apply_z_kernel(to_yb, local_z, applied, held, sems):
    del to_yb
    subs = local_z.shape[1]
    copies = []
    for sub in range(subs):
        up = local_z[0, sub].astype(jnp.float32)
        down = local_z[1, sub].astype(jnp.float32)
        if sub + 1 < subs:
            up = up - local_z[1, sub + 1].astype(jnp.float32)
        if sub > 0:
            down = down - local_z[0, sub - 1].astype(jnp.float32)
        held[sub, 0] = up
        held[sub, 1] = down
        copies.append(
            pltpu.make_async_copy(held.at[sub], applied.at[sub, pl.ds(4, 2)], sems.at[sub])
        )
        copies[-1].start()
    for copy in copies:
        copy.wait()


def apply_kernel(applied_in, rxa, ryb, rxb, rya, ya, yb, xa, xb, applied, held, sems):
    del applied_in
    copies = []
    trades = zip((*y_faces(), *x_faces()), (ya, yb, xa, xb), (rya, ryb, rxa, rxb))
    for index, (face, local, got) in enumerate(trades):
        for sub in range(held.shape[1]):
            other = got[sub].astype(jnp.float32)
            if index == 1:
                other = other * inner("sy")
            if index == 3:
                other = other * inner("sx")
            held[index, sub] = local[sub].astype(jnp.float32) - other
            copies.append(
                pltpu.make_async_copy(
                    held.at[index, sub], applied.at[sub, face], sems.at[index, sub]
                )
            )
            copies[-1].start()
    for copy in copies:
        copy.wait()


def body(
    traces, viscosity, partner, corner_owner, self_block, opposite_block, cross_block, corner_map
):
    values = traces[0, 0]
    slots, visc, owners = partner[0, 0], viscosity[0, 0], corner_owner[0, 0]
    subs, _, rhs, size = values.shape
    count = lax.axis_size("sy")
    rows = subs * rhs
    face_shape = (subs, rhs, size)
    bf16, f32 = jnp.bfloat16, jnp.float32

    xb, yb, xa, ya = pl.pallas_call(
        send_kernel,
        in_specs=[HBM],
        out_specs=[VMEM] * 4,
        out_shape=[in_vmem(face_shape, bf16)] * 4,
        scratch_shapes=[pltpu.SemaphoreType.DMA((4,))],
        compiler_params=params(8),
        cost_estimate=LONG,
    )(in_hbm(values))
    rxb = second_swap(xb, "sx")
    ryb = second_swap(yb, "sy")
    rxa = first_swap(xa, "sx")
    rya = first_swap(ya, "sy")
    map_v, base_z, cross_z = pl.pallas_call(
        z_kernel,
        in_specs=[VMEM] * 6,
        out_specs=[VMEM] * 3,
        out_shape=[in_vmem((6, size, LANES), bf16), in_vmem((2, rows, size), f32)]
        + [in_vmem((rows, size), f32)],
        scratch_shapes=[pltpu.VMEM((2,) + face_shape, bf16)],
        compiler_params=params(12),
        cost_estimate=LONG,
    )(
        xa, values, self_block, opposite_block, cross_block,
        jnp.transpose(corner_map, (1, 0, 2)),
    )
    base_y, cross_y, base_x = pl.pallas_call(
        y_kernel,
        in_specs=[SMEM] + [VMEM] * 8,
        out_specs=[VMEM] * 3,
        out_shape=[in_vmem((2, rows, size), f32)] + [in_vmem((rows, size), f32)] * 2,
        scratch_shapes=[pltpu.VMEM((2,) + face_shape, bf16)],
        compiler_params=params(12),
    )(slots, values, ryb, rya, rxb, self_block, opposite_block, cross_block, cross_z)
    half, per_row = count // 2, size // LANES
    long_shape = (subs + -(-half // per_row), rhs, size)

    def blocks(number):
        return in_vmem((number, COARSE_DEV, LANES), f32)

    xa, xb, ya, yb, local_z, to_xa, to_xb, to_ya, to_yb, kept = pl.pallas_call(
        local_kernel,
        in_specs=[SMEM] * 2 + [VMEM] * 12,
        out_specs=[VMEM] * 10,
        out_shape=[in_vmem(face_shape, bf16)] * 4
        + [in_vmem((2,) + face_shape, bf16)]
        + [in_vmem(face_shape, bf16)] * 2
        + [in_vmem(long_shape, bf16), in_vmem(face_shape, bf16), blocks(half)],
        scratch_shapes=[
            pltpu.VMEM((2,) + face_shape, bf16),
            pltpu.VMEM((COARSE_DEV * count, LANES), f32),
        ],
        compiler_params=params(16),
    )(
        slots, visc, values, rxa, rxb, self_block, opposite_block, cross_block,
        base_x, base_y, base_z, cross_y, owners, map_v,
    )
    rya = first_swap(to_ya, "sy")
    rxb = second_swap(to_xb, "sx")
    rxa = first_swap(to_xa, "sx")
    half //= 2
    kept, give = pl.pallas_call(
        lambda *refs: first_add_kernel(subs, *refs),
        in_specs=[VMEM] * 2,
        out_specs=[VMEM] * 2,
        out_shape=[blocks(half)] * 2,
        compiler_params=params(4),
    )(kept, rya)
    got = cross_swap(give, "sy", 2 * half)
    ryb = second_swap(to_yb, "sy")
    out_shape = jax.ShapeDtypeStruct(values.shape, f32)
    applied = pl.pallas_call(
        apply_z_kernel,
        in_specs=[VMEM] * 2,
        out_specs=HBM,
        out_shape=out_shape,
        scratch_shapes=[
            pltpu.VMEM((subs, 2, rhs, size), f32),
            pltpu.SemaphoreType.DMA((subs,)),
        ],
        compiler_params=params(8),
        cost_estimate=LONG,
    )(to_yb, local_z)
    while half > 1:
        half //= 2
        kept, give = pl.pallas_call(
            next_add_kernel,
            in_specs=[HBM] + [VMEM] * 2,
            out_specs=[VMEM] * 2,
            out_shape=[blocks(half)] * 2,
            compiler_params=params(4),
        )(in_hbm(applied), kept, got)
        got = cross_swap(give, "sy", 2 * half)
    applied = pl.pallas_call(
        apply_kernel,
        in_specs=[HBM] + [VMEM] * 8,
        out_specs=HBM,
        out_shape=out_shape,
        input_output_aliases={0: 0},
        scratch_shapes=[pltpu.VMEM((4,) + face_shape, f32), pltpu.SemaphoreType.DMA((4, subs))],
        compiler_params=params(12),
        cost_estimate=LONG,
    )(applied, rxa, ryb, rxb, rya, ya, yb, xa, xb)
    coarse = pl.pallas_call(
        last_add_kernel,
        in_specs=[VMEM] * 2,
        out_specs=HBM,
        out_shape=jax.ShapeDtypeStruct((COARSE_DEV, rhs * COMPS), f32),
        scratch_shapes=[pltpu.VMEM((COARSE_DEV, rhs * COMPS), f32), pltpu.SemaphoreType.DMA],
        compiler_params=params(4),
    )(kept, got)
    return applied[None, None], coarse.T


def solution(mesh):
    return jax.shard_map(
        body,
        mesh=mesh,
        in_specs=(
            P("sx", "sy", None, None, None, None),
            P("sx", "sy", None),
            P("sx", "sy", None, None),
            P("sx", "sy", None, None),
            P(),
            P(),
            P(),
            P(),
        ),
        out_specs=(P("sx", "sy", None, None, None, None), P(None, ("sx", "sy"))),
        check_vma=False,
    )
```

```python
import jax
import jax.numpy as jnp
from jax import lax
from jax.experimental import pallas as pl
from jax.experimental.pallas import tpu as pltpu
from jax.sharding import PartitionSpec as P

CORNERS = 8
COMPS = 3
COARSE_DEV = 8
LANES = 128

VMEM = pl.BlockSpec(memory_space=pltpu.VMEM)
SMEM = pl.BlockSpec(memory_space=pltpu.SMEM)
HBM = pl.BlockSpec(memory_space=pltpu.HBM)
ANY = pl.BlockSpec(memory_space=pl.ANY)


def in_vmem(shape, dtype):
    return pltpu.VMEM(shape, dtype)


def in_hbm(value):
    return pltpu.with_memory_space_constraint(value, pltpu.HBM)


def params(mib):
    return pltpu.CompilerParams(vmem_limit_bytes=mib * 1024 * 1024)


LONG = pl.CostEstimate(flops=20 * 10**9, bytes_accessed=0, transcendentals=0)


def odd(axis):
    return lax.rem(lax.axis_index(axis), 2)


def first_swap(value, axis):
    return lax.ppermute(value, axis, [(i, i ^ 1) for i in range(lax.axis_size(axis))])


def second_swap(value, axis):
    rows, cols = lax.axis_size("sx"), lax.axis_size("sy")
    pairs = []
    for i in range(rows):
        for j in range(cols):
            if axis == "sx":
                k = i - 1 if i % 2 == 0 else i + 1
                target = (k, j) if 0 <= k < rows else (i, j ^ 1)
            else:
                k = j - 1 if j % 2 == 0 else j + 1
                target = (i, k) if 0 <= k < cols else (i ^ 2, j)
            pairs.append((i * cols + j, target[0] * cols + target[1]))
    return lax.ppermute(value, ("sx", "sy"), pairs)


def cross_swap(value, axis, bits):
    return lax.ppermute(value, axis, [(i, i ^ bits) for i in range(lax.axis_size(axis))])


def inner(axis):
    me = lax.axis_index(axis)
    return ((me > 0) & (me < lax.axis_size(axis) - 1)).astype(jnp.float32)


def x_faces():
    return odd("sx"), 1 - odd("sx")


def y_faces():
    return 2 + odd("sy"), 3 - odd("sy")


def send_kernel(traces, xb, yb, xa, ya, sems):
    faces = (*x_faces(), *y_faces())
    copies = [
        pltpu.make_async_copy(traces.at[:, face], out, sems.at[index])
        for index, (face, out) in enumerate(zip(faces, (xa, xb, ya, yb)))
    ]
    for copy in copies:
        copy.start()
    for copy in copies:
        copy.wait()


def product(left, right):
    return jnp.dot(left, right, preferred_element_type=jnp.float32)


def trade_jumps(jumps, traces, partner, axis, faces, received):
    for trade, (face, got) in enumerate(zip(faces, received)):
        for sub in range(traces.shape[0]):
            other = got[partner[sub, face]].astype(jnp.float32)
            if trade == 1:
                other = other * inner(axis)
            own = traces[sub, face].astype(jnp.float32)
            jumps[trade, sub] = (own - other).astype(jnp.bfloat16)


def flat_face(jumps, index):
    _, subs, rhs, size = jumps.shape
    return jumps[index].reshape(subs * rhs, size)


def pair_sum(jumps, first):
    up = flat_face(jumps, first).astype(jnp.float32)
    return (up + flat_face(jumps, first + 1).astype(jnp.float32)).astype(jnp.bfloat16)


def z_kernel(
    xa, owners, traces, self_block, opposite_block, cross_block, corner_map,
    map_out, spread, onehot, base_z, cross_z, jumps,
):
    del xa
    subs, _, rhs, size = traces.shape
    rows = subs * rhs
    for sub in range(subs):
        up = traces[sub, 4].astype(jnp.float32)
        down = traces[sub, 5].astype(jnp.float32)
        if sub + 1 < subs:
            up = up - traces[sub + 1, 5].astype(jnp.float32)
        if sub > 0:
            down = down - traces[sub - 1, 4].astype(jnp.float32)
        jumps[0, sub] = up.astype(jnp.bfloat16)
        jumps[1, sub] = down.astype(jnp.bfloat16)
    width = CORNERS * COMPS
    row = lax.broadcasted_iota(jnp.int32, (width, LANES), 0)
    col = lax.broadcasted_iota(jnp.int32, (width, LANES), 1)
    place = (col % CORNERS) * COMPS + col // CORNERS
    order = ((row == place) & (col < width)).astype(jnp.float32).astype(jnp.bfloat16)
    for face in range(6):
        moved = lax.dot_general(
            corner_map[face], order, (((0,), (0,)), ((), ())), preferred_element_type=jnp.float32
        )
        map_out[face] = moved.astype(jnp.bfloat16)
    source = lax.broadcasted_iota(jnp.int32, (rows, subs * LANES), 0)
    target = lax.broadcasted_iota(jnp.int32, (rows, subs * LANES), 1)
    lane = (source // rhs) * LANES + (source % rhs) * COMPS
    for comp in range(COMPS):
        spread[comp] = (target == lane + comp).astype(jnp.float32).astype(jnp.bfloat16)
    numbers = lax.broadcasted_iota(jnp.int32, onehot.shape, 0)
    onehot[...] = (numbers == owners[...]).astype(jnp.float32).astype(jnp.bfloat16)
    flat = jumps[...].reshape(2 * rows, size)
    with_self = product(flat, self_block[...])
    with_opp = product(flat, opposite_block[...])
    base_z[0] = with_self[:rows] + with_opp[rows:]
    base_z[1] = with_self[rows:] + with_opp[:rows]
    cross_z[...] = product(pair_sum(jumps, 0), cross_block[...])


def y_kernel(
    partner, traces, ryb, rya, rxb, self_block, opposite_block, cross_block, cross_z,
    base_y, cross_y, base_x, jumps,
):
    del rxb
    subs, _, rhs, size = traces.shape
    rows = subs * rhs
    trade_jumps(jumps, traces, partner, "sy", y_faces(), (rya, ryb))
    from_y = product(pair_sum(jumps, 0), cross_block[...])
    cross_y[...] = from_y
    base_x[...] = from_y + cross_z[...]
    flat = jumps[...].reshape(2 * rows, size)
    with_self = product(flat, self_block[...])
    with_opp = product(flat, opposite_block[...])
    base_y[0] = with_self[:rows] + with_opp[rows:] + cross_z[...]
    base_y[1] = with_self[rows:] + with_opp[:rows] + cross_z[...]


def high_low(value):
    high = value.astype(jnp.bfloat16).astype(jnp.float32)
    return high, value - high


def coarse_rows(partials, spread, onehot):
    subs = onehot.shape[1] // (2 * CORNERS)
    entries = jnp.zeros((2 * CORNERS, subs * LANES), jnp.float32)
    for comp in range(COMPS):
        part = partials[comp * CORNERS : (comp + 1) * CORNERS]
        stacked = jnp.concatenate(high_low(part), axis=0).astype(jnp.bfloat16)
        entries += product(stacked, spread[comp])
    entries = entries[:CORNERS] + entries[CORNERS:]
    by_sub = [entries[:, sub * LANES : (sub + 1) * LANES] for sub in range(subs)]
    both = jnp.concatenate(high_low(jnp.concatenate(by_sub, axis=0)), axis=0)
    return product(onehot[...], both.astype(jnp.bfloat16))


def local_kernel(
    partner, viscosity, traces, rxa, rxb, self_block, opposite_block, cross_block,
    base_x, base_y, base_z, cross_y, spread, onehot, corner_map,
    xa, xb, ya, yb, local_z, to_xa, to_xb, to_ya, to_yb, kept, jumps, dense,
):
    subs, _, rhs, size = traces.shape
    rows = subs * rhs
    trade_jumps(jumps, traces, partner, "sx", x_faces(), (rxa, rxb))
    flat = jumps[...].reshape(2 * rows, size)
    with_self = product(flat, self_block[...])
    with_opp = product(flat, opposite_block[...])
    from_x = product(pair_sum(jumps, 0), cross_block[...])
    from_xy = from_x + cross_y[...]
    totals = (
        with_self[:rows] + with_opp[rows:] + base_x[...],
        with_self[rows:] + with_opp[:rows] + base_x[...],
        base_y[0] + from_x,
        base_y[1] + from_x,
        base_z[0] + from_xy,
        base_z[1] + from_xy,
    )
    faces = (*x_faces(), *y_faces(), 4, 5)
    outs = (xa, xb, ya, yb, local_z.at[0], local_z.at[1])
    sent = (to_xa, to_xb, to_ya, to_yb)
    partials = jnp.zeros((rows, LANES), jnp.float32)
    for index, (face, total, out) in enumerate(zip(faces, totals, outs)):
        for sub in range(subs):
            here = slice(sub * rhs, (sub + 1) * rhs)
            value = (viscosity[sub] * total[here]).astype(jnp.bfloat16)
            out[sub] = value
            if index < 4:
                sent[index][partner[sub, face]] = value
        partials += product(out[...].reshape(rows, size), corner_map[face])
    partials = partials.T
    dense[...] = coarse_rows(partials, spread, onehot)
    me = lax.axis_index("sy")

    def block(bits):
        start = pl.multiple_of((me ^ bits) * COARSE_DEV, COARSE_DEV)
        return dense[pl.ds(start, COARSE_DEV), :]

    half, per_row = kept.shape[0], size // LANES
    for index in range((to_ya.shape[0] - subs) * per_row):
        lanes = slice(index % per_row * LANES, (index % per_row + 1) * LANES)
        both = jnp.zeros((2 * COARSE_DEV, LANES), jnp.float32)
        if index < half:
            kept[index] = block(2 * index)
            both = jnp.concatenate(high_low(block(2 * index + 1)), axis=0)
        to_ya[subs + index // per_row, :, lanes] = both.astype(jnp.bfloat16)


def first_add_kernel(subs, kept, got, keep, give):
    half, per_row = kept.shape[0], got.shape[2] // LANES
    for index in range(half):
        lanes = slice(index % per_row * LANES, (index % per_row + 1) * LANES)
        both = got[subs + index // per_row, :, lanes].astype(jnp.float32)
        total = kept[index] + both[:COARSE_DEV] + both[COARSE_DEV:]
        out = keep if index < half // 2 else give
        out[index % (half // 2)] = total


def next_add_kernel(after, kept, got, keep, give):
    del after
    half = kept.shape[0]
    total = kept[...] + got[...]
    keep[...] = total[: half // 2]
    give[...] = total[half // 2 :]


def last_add_kernel(kept, got, coarse, total, sem):
    total[...] = (kept[0] + got[0])[:, : total.shape[1]]
    copy = pltpu.make_async_copy(total, coarse, sem)
    copy.start()
    copy.wait()


def apply_z_kernel(to_yb, local_z, applied, held, sems):
    del to_yb
    subs = local_z.shape[1]
    copies = []
    for sub in range(subs):
        up = local_z[0, sub].astype(jnp.float32)
        down = local_z[1, sub].astype(jnp.float32)
        if sub + 1 < subs:
            up = up - local_z[1, sub + 1].astype(jnp.float32)
        if sub > 0:
            down = down - local_z[0, sub - 1].astype(jnp.float32)
        held[sub, 0] = up
        held[sub, 1] = down
        copies.append(
            pltpu.make_async_copy(held.at[sub], applied.at[sub, pl.ds(4, 2)], sems.at[sub])
        )
        copies[-1].start()
    for copy in copies:
        copy.wait()


def apply_kernel(applied_in, rxa, ryb, rxb, rya, ya, yb, xa, xb, applied, held, sems):
    del applied_in
    copies = []
    trades = zip((*y_faces(), *x_faces()), (ya, yb, xa, xb), (rya, ryb, rxa, rxb))
    for index, (face, local, got) in enumerate(trades):
        for sub in range(held.shape[1]):
            other = got[sub].astype(jnp.float32)
            if index == 1:
                other = other * inner("sy")
            if index == 3:
                other = other * inner("sx")
            held[index, sub] = local[sub].astype(jnp.float32) - other
            copies.append(
                pltpu.make_async_copy(
                    held.at[index, sub], applied.at[sub, face], sems.at[index, sub]
                )
            )
            copies[-1].start()
    for copy in copies:
        copy.wait()


def body(
    traces, viscosity, partner, corner_owner, self_block, opposite_block, cross_block, corner_map
):
    values = traces[0, 0]
    slots, visc, owners = partner[0, 0], viscosity[0, 0], corner_owner[0, 0]
    subs, _, rhs, size = values.shape
    count = lax.axis_size("sy")
    rows = subs * rhs
    face_shape = (subs, rhs, size)
    bf16, f32 = jnp.bfloat16, jnp.float32

    xb, yb, xa, ya = pl.pallas_call(
        send_kernel,
        in_specs=[HBM],
        out_specs=[VMEM] * 4,
        out_shape=[in_vmem(face_shape, bf16)] * 4,
        scratch_shapes=[pltpu.SemaphoreType.DMA((4,))],
        compiler_params=params(8),
        cost_estimate=LONG,
    )(in_hbm(values))
    rxb = second_swap(xb, "sx")
    ryb = second_swap(yb, "sy")
    rxa = first_swap(xa, "sx")
    rya = first_swap(ya, "sy")
    owner_row = jnp.tile(owners.reshape(1, -1), (1, 2))
    map_v, spread, onehot, base_z, cross_z = pl.pallas_call(
        z_kernel,
        in_specs=[VMEM] * 7,
        out_specs=[VMEM] * 5,
        out_shape=[in_vmem((6, size, LANES), bf16), in_vmem((COMPS, rows, subs * LANES), bf16)]
        + [in_vmem((COARSE_DEV * count, 2 * subs * CORNERS), bf16), in_vmem((2, rows, size), f32)]
        + [in_vmem((rows, size), f32)],
        scratch_shapes=[pltpu.VMEM((2,) + face_shape, bf16)],
        compiler_params=params(12),
        cost_estimate=LONG,
    )(
        xa, owner_row, values, self_block, opposite_block, cross_block,
        jnp.transpose(corner_map, (1, 0, 2)),
    )
    base_y, cross_y, base_x = pl.pallas_call(
        y_kernel,
        in_specs=[SMEM] + [VMEM] * 8,
        out_specs=[VMEM] * 3,
        out_shape=[in_vmem((2, rows, size), f32)] + [in_vmem((rows, size), f32)] * 2,
        scratch_shapes=[pltpu.VMEM((2,) + face_shape, bf16)],
        compiler_params=params(12),
    )(slots, values, ryb, rya, rxb, self_block, opposite_block, cross_block, cross_z)
    half, per_row = count // 2, size // LANES
    long_shape = (subs + -(-half // per_row), rhs, size)

    def blocks(number):
        return in_vmem((number, COARSE_DEV, LANES), f32)

    xa, xb, ya, yb, local_z, to_xa, to_xb, to_ya, to_yb, kept = pl.pallas_call(
        local_kernel,
        in_specs=[SMEM] * 2 + [VMEM] * 13,
        out_specs=[VMEM] * 10,
        out_shape=[in_vmem(face_shape, bf16)] * 4
        + [in_vmem((2,) + face_shape, bf16)]
        + [in_vmem(face_shape, bf16)] * 2
        + [in_vmem(long_shape, bf16), in_vmem(face_shape, bf16), blocks(half)],
        scratch_shapes=[
            pltpu.VMEM((2,) + face_shape, bf16),
            pltpu.VMEM((COARSE_DEV * count, LANES), f32),
        ],
        compiler_params=params(16),
    )(
        slots, visc, values, rxa, rxb, self_block, opposite_block, cross_block,
        base_x, base_y, base_z, cross_y, spread, onehot, map_v,
    )
    rya = first_swap(to_ya, "sy")
    rxb = second_swap(to_xb, "sx")
    rxa = first_swap(to_xa, "sx")
    half //= 2
    kept, give = pl.pallas_call(
        lambda *refs: first_add_kernel(subs, *refs),
        in_specs=[VMEM] * 2,
        out_specs=[VMEM] * 2,
        out_shape=[blocks(half)] * 2,
        compiler_params=params(4),
    )(kept, rya)
    got = cross_swap(give, "sy", 2 * half)
    ryb = second_swap(to_yb, "sy")
    out_shape = jax.ShapeDtypeStruct(values.shape, f32)
    applied = pl.pallas_call(
        apply_z_kernel,
        in_specs=[VMEM] * 2,
        out_specs=HBM,
        out_shape=out_shape,
        scratch_shapes=[
            pltpu.VMEM((subs, 2, rhs, size), f32),
            pltpu.SemaphoreType.DMA((subs,)),
        ],
        compiler_params=params(8),
        cost_estimate=LONG,
    )(to_yb, local_z)
    while half > 1:
        half //= 2
        kept, give = pl.pallas_call(
            next_add_kernel,
            in_specs=[HBM] + [VMEM] * 2,
            out_specs=[VMEM] * 2,
            out_shape=[blocks(half)] * 2,
            compiler_params=params(4),
        )(in_hbm(applied), kept, got)
        got = cross_swap(give, "sy", 2 * half)
    applied = pl.pallas_call(
        apply_kernel,
        in_specs=[HBM] + [VMEM] * 8,
        out_specs=HBM,
        out_shape=out_shape,
        input_output_aliases={0: 0},
        scratch_shapes=[pltpu.VMEM((4,) + face_shape, f32), pltpu.SemaphoreType.DMA((4, subs))],
        compiler_params=params(12),
        cost_estimate=LONG,
    )(applied, rxa, ryb, rxb, rya, ya, yb, xa, xb)
    coarse = pl.pallas_call(
        last_add_kernel,
        in_specs=[VMEM] * 2,
        out_specs=HBM,
        out_shape=jax.ShapeDtypeStruct((COARSE_DEV, rhs * COMPS), f32),
        scratch_shapes=[pltpu.VMEM((COARSE_DEV, rhs * COMPS), f32), pltpu.SemaphoreType.DMA],
        compiler_params=params(4),
    )(kept, got)
    return applied[None, None], coarse.T


def solution(mesh):
    return jax.shard_map(
        body,
        mesh=mesh,
        in_specs=(
            P("sx", "sy", None, None, None, None),
            P("sx", "sy", None),
            P("sx", "sy", None, None),
            P("sx", "sy", None, None),
            P(),
            P(),
            P(),
            P(),
        ),
        out_specs=(P("sx", "sy", None, None, None, None), P(None, ("sx", "sy"))),
        check_vma=False,
    )
```

```python
import jax
import jax.numpy as jnp
from jax import lax
from jax.experimental import pallas as pl
from jax.experimental.pallas import tpu as pltpu
from jax.sharding import PartitionSpec as P

CORNERS = 8
COMPS = 3
COARSE_DEV = 8
LANES = 128

VMEM = pl.BlockSpec(memory_space=pltpu.VMEM)
SMEM = pl.BlockSpec(memory_space=pltpu.SMEM)
HBM = pl.BlockSpec(memory_space=pltpu.HBM)
ANY = pl.BlockSpec(memory_space=pl.ANY)


def in_vmem(shape, dtype):
    return pltpu.VMEM(shape, dtype)


def in_hbm(value):
    return pltpu.with_memory_space_constraint(value, pltpu.HBM)


def params(mib):
    return pltpu.CompilerParams(vmem_limit_bytes=mib * 1024 * 1024)


LONG = pl.CostEstimate(flops=20 * 10**9, bytes_accessed=0, transcendentals=0)


def odd(axis):
    return lax.rem(lax.axis_index(axis), 2)


def first_swap(value, axis):
    return lax.ppermute(value, axis, [(i, i ^ 1) for i in range(lax.axis_size(axis))])


def second_swap(value, axis):
    rows, cols = lax.axis_size("sx"), lax.axis_size("sy")
    pairs = []
    for i in range(rows):
        for j in range(cols):
            if axis == "sx":
                k = i - 1 if i % 2 == 0 else i + 1
                target = (k, j) if 0 <= k < rows else (i, j ^ 1)
            else:
                k = j - 1 if j % 2 == 0 else j + 1
                target = (i, k) if 0 <= k < cols else (i ^ 2, j)
            pairs.append((i * cols + j, target[0] * cols + target[1]))
    return lax.ppermute(value, ("sx", "sy"), pairs)


def cross_swap(value, axis, bits):
    return lax.ppermute(value, axis, [(i, i ^ bits) for i in range(lax.axis_size(axis))])


def inner(axis):
    me = lax.axis_index(axis)
    return ((me > 0) & (me < lax.axis_size(axis) - 1)).astype(jnp.float32)


def x_faces():
    return odd("sx"), 1 - odd("sx")


def y_faces():
    return 2 + odd("sy"), 3 - odd("sy")


def send_kernel(traces, xb, yb, xa, ya, sems):
    faces = (*x_faces(), *y_faces())
    copies = [
        pltpu.make_async_copy(traces.at[:, face], out, sems.at[index])
        for index, (face, out) in enumerate(zip(faces, (xa, xb, ya, yb)))
    ]
    for copy in copies:
        copy.start()
    for copy in copies:
        copy.wait()


def product(left, right):
    return jnp.dot(left, right, preferred_element_type=jnp.float32)


def trade_jumps(jumps, traces, partner, axis, faces, received):
    for trade, (face, got) in enumerate(zip(faces, received)):
        for sub in range(traces.shape[0]):
            other = got[partner[sub, face]].astype(jnp.float32)
            if trade == 1:
                other = other * inner(axis)
            own = traces[sub, face].astype(jnp.float32)
            jumps[trade, sub] = (own - other).astype(jnp.bfloat16)


def flat_face(jumps, index):
    _, subs, rhs, size = jumps.shape
    return jumps[index].reshape(subs * rhs, size)


def pair_sum(jumps, first):
    up = flat_face(jumps, first).astype(jnp.float32)
    return (up + flat_face(jumps, first + 1).astype(jnp.float32)).astype(jnp.bfloat16)


def z_kernel(
    xa, traces, self_block, opposite_block, cross_block, corner_map,
    map_out, spread, base_z, cross_z, jumps,
):
    del xa
    subs, _, rhs, size = traces.shape
    rows = subs * rhs
    for sub in range(subs):
        up = traces[sub, 4].astype(jnp.float32)
        down = traces[sub, 5].astype(jnp.float32)
        if sub + 1 < subs:
            up = up - traces[sub + 1, 5].astype(jnp.float32)
        if sub > 0:
            down = down - traces[sub - 1, 4].astype(jnp.float32)
        jumps[0, sub] = up.astype(jnp.bfloat16)
        jumps[1, sub] = down.astype(jnp.bfloat16)
    width = CORNERS * COMPS
    row = lax.broadcasted_iota(jnp.int32, (width, LANES), 0)
    col = lax.broadcasted_iota(jnp.int32, (width, LANES), 1)
    place = (col % CORNERS) * COMPS + col // CORNERS
    order = ((row == place) & (col < width)).astype(jnp.float32).astype(jnp.bfloat16)
    for face in range(6):
        moved = lax.dot_general(
            corner_map[face], order, (((0,), (0,)), ((), ())), preferred_element_type=jnp.float32
        )
        map_out[face] = moved.astype(jnp.bfloat16)
    source = lax.broadcasted_iota(jnp.int32, (rows, subs * LANES), 0)
    target = lax.broadcasted_iota(jnp.int32, (rows, subs * LANES), 1)
    lane = (source // rhs) * LANES + (source % rhs) * COMPS
    for comp in range(COMPS):
        spread[comp] = (target == lane + comp).astype(jnp.float32).astype(jnp.bfloat16)
    flat = jumps[...].reshape(2 * rows, size)
    with_self = product(flat, self_block[...])
    with_opp = product(flat, opposite_block[...])
    base_z[0] = with_self[:rows] + with_opp[rows:]
    base_z[1] = with_self[rows:] + with_opp[:rows]
    cross_z[...] = product(pair_sum(jumps, 0), cross_block[...])


def y_kernel(
    partner, traces, ryb, rya, rxb, self_block, opposite_block, cross_block, cross_z, owners,
    base_y, cross_y, base_x, onehot, jumps,
):
    del rxb
    numbers = lax.broadcasted_iota(jnp.int32, (onehot.shape[0], CORNERS), 0)
    parts = [
        (numbers == owners[sub : sub + 1, :]).astype(jnp.float32) for sub in range(owners.shape[0])
    ]
    onehot[...] = jnp.concatenate(parts * 2, axis=1).astype(jnp.bfloat16)
    subs, _, rhs, size = traces.shape
    rows = subs * rhs
    trade_jumps(jumps, traces, partner, "sy", y_faces(), (rya, ryb))
    from_y = product(pair_sum(jumps, 0), cross_block[...])
    cross_y[...] = from_y
    base_x[...] = from_y + cross_z[...]
    flat = jumps[...].reshape(2 * rows, size)
    with_self = product(flat, self_block[...])
    with_opp = product(flat, opposite_block[...])
    base_y[0] = with_self[:rows] + with_opp[rows:] + cross_z[...]
    base_y[1] = with_self[rows:] + with_opp[:rows] + cross_z[...]


def high_low(value):
    high = value.astype(jnp.bfloat16).astype(jnp.float32)
    return high, value - high


def coarse_rows(partials, spread, onehot):
    subs = onehot.shape[1] // (2 * CORNERS)
    entries = jnp.zeros((2 * CORNERS, subs * LANES), jnp.float32)
    for comp in range(COMPS):
        part = partials[comp * CORNERS : (comp + 1) * CORNERS]
        stacked = jnp.concatenate(high_low(part), axis=0).astype(jnp.bfloat16)
        entries += product(stacked, spread[comp])
    entries = entries[:CORNERS] + entries[CORNERS:]
    by_sub = [entries[:, sub * LANES : (sub + 1) * LANES] for sub in range(subs)]
    both = jnp.concatenate(high_low(jnp.concatenate(by_sub, axis=0)), axis=0)
    return product(onehot[...], both.astype(jnp.bfloat16))


def local_kernel(
    partner, viscosity, traces, rxa, rxb, self_block, opposite_block, cross_block,
    base_x, base_y, base_z, cross_y, spread, onehot, corner_map,
    xa, xb, ya, yb, local_z, to_xa, to_xb, to_ya, to_yb, kept, jumps, dense,
):
    subs, _, rhs, size = traces.shape
    rows = subs * rhs
    trade_jumps(jumps, traces, partner, "sx", x_faces(), (rxa, rxb))
    flat = jumps[...].reshape(2 * rows, size)
    with_self = product(flat, self_block[...])
    with_opp = product(flat, opposite_block[...])
    from_x = product(pair_sum(jumps, 0), cross_block[...])
    from_xy = from_x + cross_y[...]
    totals = (
        with_self[:rows] + with_opp[rows:] + base_x[...],
        with_self[rows:] + with_opp[:rows] + base_x[...],
        base_y[0] + from_x,
        base_y[1] + from_x,
        base_z[0] + from_xy,
        base_z[1] + from_xy,
    )
    faces = (*x_faces(), *y_faces(), 4, 5)
    outs = (xa, xb, ya, yb, local_z.at[0], local_z.at[1])
    sent = (to_xa, to_xb, to_ya, to_yb)
    partials = jnp.zeros((rows, LANES), jnp.float32)
    for index, (face, total, out) in enumerate(zip(faces, totals, outs)):
        for sub in range(subs):
            here = slice(sub * rhs, (sub + 1) * rhs)
            value = (viscosity[sub] * total[here]).astype(jnp.bfloat16)
            out[sub] = value
            if index < 4:
                sent[index][partner[sub, face]] = value
        partials += product(out[...].reshape(rows, size), corner_map[face])
    partials = partials.T
    dense[...] = coarse_rows(partials, spread, onehot)
    me = lax.axis_index("sy")

    def block(bits):
        start = pl.multiple_of((me ^ bits) * COARSE_DEV, COARSE_DEV)
        return dense[pl.ds(start, COARSE_DEV), :]

    half, per_row = kept.shape[0], size // LANES
    for index in range((to_ya.shape[0] - subs) * per_row):
        lanes = slice(index % per_row * LANES, (index % per_row + 1) * LANES)
        both = jnp.zeros((2 * COARSE_DEV, LANES), jnp.float32)
        if index < half:
            kept[index] = block(2 * index)
            both = jnp.concatenate(high_low(block(2 * index + 1)), axis=0)
        to_ya[subs + index // per_row, :, lanes] = both.astype(jnp.bfloat16)


def first_add_kernel(subs, kept, got, keep, give):
    half, per_row = kept.shape[0], got.shape[2] // LANES
    for index in range(half):
        lanes = slice(index % per_row * LANES, (index % per_row + 1) * LANES)
        both = got[subs + index // per_row, :, lanes].astype(jnp.float32)
        total = kept[index] + both[:COARSE_DEV] + both[COARSE_DEV:]
        out = keep if index < half // 2 else give
        out[index % (half // 2)] = total


def next_add_kernel(after, kept, got, keep, give):
    del after
    half = kept.shape[0]
    total = kept[...] + got[...]
    keep[...] = total[: half // 2]
    give[...] = total[half // 2 :]


def last_add_kernel(kept, got, coarse, total, sem):
    total[...] = (kept[0] + got[0])[:, : total.shape[1]]
    copy = pltpu.make_async_copy(total, coarse, sem)
    copy.start()
    copy.wait()


def apply_z_kernel(to_yb, local_z, applied, held, sems):
    del to_yb
    subs = local_z.shape[1]
    copies = []
    for sub in range(subs):
        up = local_z[0, sub].astype(jnp.float32)
        down = local_z[1, sub].astype(jnp.float32)
        if sub + 1 < subs:
            up = up - local_z[1, sub + 1].astype(jnp.float32)
        if sub > 0:
            down = down - local_z[0, sub - 1].astype(jnp.float32)
        held[sub, 0] = up
        held[sub, 1] = down
        copies.append(
            pltpu.make_async_copy(held.at[sub], applied.at[sub, pl.ds(4, 2)], sems.at[sub])
        )
        copies[-1].start()
    for copy in copies:
        copy.wait()


def apply_kernel(applied_in, rxa, ryb, rxb, rya, ya, yb, xa, xb, applied, held, sems):
    del applied_in
    copies = []
    trades = zip((*y_faces(), *x_faces()), (ya, yb, xa, xb), (rya, ryb, rxa, rxb))
    for index, (face, local, got) in enumerate(trades):
        for sub in range(held.shape[1]):
            other = got[sub].astype(jnp.float32)
            if index == 1:
                other = other * inner("sy")
            if index == 3:
                other = other * inner("sx")
            held[index, sub] = local[sub].astype(jnp.float32) - other
            copies.append(
                pltpu.make_async_copy(
                    held.at[index, sub], applied.at[sub, face], sems.at[index, sub]
                )
            )
            copies[-1].start()
    for copy in copies:
        copy.wait()


def body(
    traces, viscosity, partner, corner_owner, self_block, opposite_block, cross_block, corner_map
):
    values = traces[0, 0]
    slots, visc, owners = partner[0, 0], viscosity[0, 0], corner_owner[0, 0]
    subs, _, rhs, size = values.shape
    count = lax.axis_size("sy")
    rows = subs * rhs
    face_shape = (subs, rhs, size)
    bf16, f32 = jnp.bfloat16, jnp.float32

    xb, yb, xa, ya = pl.pallas_call(
        send_kernel,
        in_specs=[HBM],
        out_specs=[VMEM] * 4,
        out_shape=[in_vmem(face_shape, bf16)] * 4,
        scratch_shapes=[pltpu.SemaphoreType.DMA((4,))],
        compiler_params=params(8),
        cost_estimate=LONG,
    )(in_hbm(values))
    rxb = second_swap(xb, "sx")
    ryb = second_swap(yb, "sy")
    rxa = first_swap(xa, "sx")
    rya = first_swap(ya, "sy")
    map_v, spread, base_z, cross_z = pl.pallas_call(
        z_kernel,
        in_specs=[VMEM] * 6,
        out_specs=[VMEM] * 4,
        out_shape=[in_vmem((6, size, LANES), bf16), in_vmem((COMPS, rows, subs * LANES), bf16)]
        + [in_vmem((2, rows, size), f32)]
        + [in_vmem((rows, size), f32)],
        scratch_shapes=[pltpu.VMEM((2,) + face_shape, bf16)],
        compiler_params=params(12),
        cost_estimate=LONG,
    )(
        xa, values, self_block, opposite_block, cross_block,
        jnp.transpose(corner_map, (1, 0, 2)),
    )
    base_y, cross_y, base_x, onehot = pl.pallas_call(
        y_kernel,
        in_specs=[SMEM] + [VMEM] * 9,
        out_specs=[VMEM] * 4,
        out_shape=[in_vmem((2, rows, size), f32)] + [in_vmem((rows, size), f32)] * 2
        + [in_vmem((COARSE_DEV * count, 2 * subs * CORNERS), bf16)],
        scratch_shapes=[pltpu.VMEM((2,) + face_shape, bf16)],
        compiler_params=params(12),
    )(slots, values, ryb, rya, rxb, self_block, opposite_block, cross_block, cross_z, owners)
    half, per_row = count // 2, size // LANES
    long_shape = (subs + -(-half // per_row), rhs, size)

    def blocks(number):
        return in_vmem((number, COARSE_DEV, LANES), f32)

    xa, xb, ya, yb, local_z, to_xa, to_xb, to_ya, to_yb, kept = pl.pallas_call(
        local_kernel,
        in_specs=[SMEM] * 2 + [VMEM] * 13,
        out_specs=[VMEM] * 10,
        out_shape=[in_vmem(face_shape, bf16)] * 4
        + [in_vmem((2,) + face_shape, bf16)]
        + [in_vmem(face_shape, bf16)] * 2
        + [in_vmem(long_shape, bf16), in_vmem(face_shape, bf16), blocks(half)],
        scratch_shapes=[
            pltpu.VMEM((2,) + face_shape, bf16),
            pltpu.VMEM((COARSE_DEV * count, LANES), f32),
        ],
        compiler_params=params(16),
    )(
        slots, visc, values, rxa, rxb, self_block, opposite_block, cross_block,
        base_x, base_y, base_z, cross_y, spread, onehot, map_v,
    )
    rya = first_swap(to_ya, "sy")
    rxb = second_swap(to_xb, "sx")
    rxa = first_swap(to_xa, "sx")
    half //= 2
    kept, give = pl.pallas_call(
        lambda *refs: first_add_kernel(subs, *refs),
        in_specs=[VMEM] * 2,
        out_specs=[VMEM] * 2,
        out_shape=[blocks(half)] * 2,
        compiler_params=params(4),
    )(kept, rya)
    got = cross_swap(give, "sy", 2 * half)
    ryb = second_swap(to_yb, "sy")
    out_shape = jax.ShapeDtypeStruct(values.shape, f32)
    applied = pl.pallas_call(
        apply_z_kernel,
        in_specs=[VMEM] * 2,
        out_specs=HBM,
        out_shape=out_shape,
        scratch_shapes=[
            pltpu.VMEM((subs, 2, rhs, size), f32),
            pltpu.SemaphoreType.DMA((subs,)),
        ],
        compiler_params=params(8),
        cost_estimate=LONG,
    )(to_yb, local_z)
    while half > 1:
        half //= 2
        kept, give = pl.pallas_call(
            next_add_kernel,
            in_specs=[HBM] + [VMEM] * 2,
            out_specs=[VMEM] * 2,
            out_shape=[blocks(half)] * 2,
            compiler_params=params(4),
        )(in_hbm(applied), kept, got)
        got = cross_swap(give, "sy", 2 * half)
    applied = pl.pallas_call(
        apply_kernel,
        in_specs=[HBM] + [VMEM] * 8,
        out_specs=HBM,
        out_shape=out_shape,
        input_output_aliases={0: 0},
        scratch_shapes=[pltpu.VMEM((4,) + face_shape, f32), pltpu.SemaphoreType.DMA((4, subs))],
        compiler_params=params(12),
        cost_estimate=LONG,
    )(applied, rxa, ryb, rxb, rya, ya, yb, xa, xb)
    coarse = pl.pallas_call(
        last_add_kernel,
        in_specs=[VMEM] * 2,
        out_specs=HBM,
        out_shape=jax.ShapeDtypeStruct((COARSE_DEV, rhs * COMPS), f32),
        scratch_shapes=[pltpu.VMEM((COARSE_DEV, rhs * COMPS), f32), pltpu.SemaphoreType.DMA],
        compiler_params=params(4),
    )(kept, got)
    return applied[None, None], coarse.T


def solution(mesh):
    return jax.shard_map(
        body,
        mesh=mesh,
        in_specs=(
            P("sx", "sy", None, None, None, None),
            P("sx", "sy", None),
            P("sx", "sy", None, None),
            P("sx", "sy", None, None),
            P(),
            P(),
            P(),
            P(),
        ),
        out_specs=(P("sx", "sy", None, None, None, None), P(None, ("sx", "sy"))),
        check_vma=False,
    )
```

```python
import jax
import jax.numpy as jnp
from jax import lax
from jax.experimental import pallas as pl
from jax.experimental.pallas import tpu as pltpu
from jax.sharding import PartitionSpec as P

CORNERS = 8
COMPS = 3
COARSE_DEV = 8
LANES = 128

VMEM = pl.BlockSpec(memory_space=pltpu.VMEM)
SMEM = pl.BlockSpec(memory_space=pltpu.SMEM)
HBM = pl.BlockSpec(memory_space=pltpu.HBM)
ANY = pl.BlockSpec(memory_space=pl.ANY)


def in_vmem(shape, dtype):
    return pltpu.VMEM(shape, dtype)


def in_hbm(value):
    return pltpu.with_memory_space_constraint(value, pltpu.HBM)


def params(mib):
    return pltpu.CompilerParams(vmem_limit_bytes=mib * 1024 * 1024)


LONG = pl.CostEstimate(flops=20 * 10**9, bytes_accessed=0, transcendentals=0)


def odd(axis):
    return lax.rem(lax.axis_index(axis), 2)


def first_swap(value, axis):
    return lax.ppermute(value, axis, [(i, i ^ 1) for i in range(lax.axis_size(axis))])


def second_swap(value, axis):
    rows, cols = lax.axis_size("sx"), lax.axis_size("sy")
    pairs = []
    for i in range(rows):
        for j in range(cols):
            if axis == "sx":
                k = i - 1 if i % 2 == 0 else i + 1
                target = (k, j) if 0 <= k < rows else (i, j ^ 1)
            else:
                k = j - 1 if j % 2 == 0 else j + 1
                target = (i, k) if 0 <= k < cols else (i ^ 2, j)
            pairs.append((i * cols + j, target[0] * cols + target[1]))
    return lax.ppermute(value, ("sx", "sy"), pairs)


def cross_swap(value, axis, bits):
    return lax.ppermute(value, axis, [(i, i ^ bits) for i in range(lax.axis_size(axis))])


def inner(axis):
    me = lax.axis_index(axis)
    return ((me > 0) & (me < lax.axis_size(axis) - 1)).astype(jnp.float32)


def x_faces():
    return odd("sx"), 1 - odd("sx")


def y_faces():
    return 2 + odd("sy"), 3 - odd("sy")


def send_kernel(traces, xb, yb, xa, ya, sems):
    faces = (*x_faces(), *y_faces())
    copies = [
        pltpu.make_async_copy(traces.at[:, face], out, sems.at[index])
        for index, (face, out) in enumerate(zip(faces, (xa, xb, ya, yb)))
    ]
    for copy in copies:
        copy.start()
    for copy in copies:
        copy.wait()


def product(left, right):
    return jnp.dot(left, right, preferred_element_type=jnp.float32)


def trade_jumps(jumps, traces, partner, axis, faces, received):
    for trade, (face, got) in enumerate(zip(faces, received)):
        for sub in range(traces.shape[0]):
            other = got[partner[sub, face]].astype(jnp.float32)
            if trade == 1:
                other = other * inner(axis)
            own = traces[sub, face].astype(jnp.float32)
            jumps[trade, sub] = (own - other).astype(jnp.bfloat16)


def flat_face(jumps, index):
    _, subs, rhs, size = jumps.shape
    return jumps[index].reshape(subs * rhs, size)


def pair_sum(jumps, first):
    up = flat_face(jumps, first).astype(jnp.float32)
    return (up + flat_face(jumps, first + 1).astype(jnp.float32)).astype(jnp.bfloat16)


def z_kernel(
    xa, traces, self_block, opposite_block, cross_block, corner_map,
    map_out, spread, base_z, cross_z, jumps,
):
    del xa
    subs, _, rhs, size = traces.shape
    rows = subs * rhs
    for sub in range(subs):
        up = traces[sub, 4].astype(jnp.float32)
        down = traces[sub, 5].astype(jnp.float32)
        if sub + 1 < subs:
            up = up - traces[sub + 1, 5].astype(jnp.float32)
        if sub > 0:
            down = down - traces[sub - 1, 4].astype(jnp.float32)
        jumps[0, sub] = up.astype(jnp.bfloat16)
        jumps[1, sub] = down.astype(jnp.bfloat16)
    width = CORNERS * COMPS
    row = lax.broadcasted_iota(jnp.int32, (width, LANES), 0)
    col = lax.broadcasted_iota(jnp.int32, (width, LANES), 1)
    place = (col % CORNERS) * COMPS + col // CORNERS
    order = ((row == place) & (col < width)).astype(jnp.float32).astype(jnp.bfloat16)
    for face in range(6):
        moved = lax.dot_general(
            corner_map[face], order, (((0,), (0,)), ((), ())), preferred_element_type=jnp.float32
        )
        map_out[face] = moved.astype(jnp.bfloat16)
    source = lax.broadcasted_iota(jnp.int32, (rows, subs * LANES), 0)
    target = lax.broadcasted_iota(jnp.int32, (rows, subs * LANES), 1)
    lane = (source // rhs) * LANES + (source % rhs) * COMPS
    for comp in range(COMPS):
        spread[comp] = (target == lane + comp).astype(jnp.float32).astype(jnp.bfloat16)
    flat = jumps[...].reshape(2 * rows, size)
    with_self = product(flat, self_block[...])
    with_opp = product(flat, opposite_block[...])
    base_z[0] = with_self[:rows] + with_opp[rows:]
    base_z[1] = with_self[rows:] + with_opp[:rows]
    cross_z[...] = product(pair_sum(jumps, 0), cross_block[...])


def y_kernel(
    partner, traces, ryb, rya, rxb, self_block, opposite_block, cross_block, cross_z, owners,
    base_y, cross_y, base_x, onehot, jumps,
):
    del rxb
    numbers = lax.broadcasted_iota(jnp.int32, (onehot.shape[0], CORNERS), 0)
    parts = [
        (numbers == owners[sub : sub + 1, :]).astype(jnp.float32) for sub in range(owners.shape[0])
    ]
    onehot[...] = jnp.concatenate(parts * 2, axis=1).astype(jnp.bfloat16)
    subs, _, rhs, size = traces.shape
    rows = subs * rhs
    trade_jumps(jumps, traces, partner, "sy", y_faces(), (rya, ryb))
    from_y = product(pair_sum(jumps, 0), cross_block[...])
    cross_y[...] = from_y
    base_x[...] = from_y + cross_z[...]
    flat = jumps[...].reshape(2 * rows, size)
    with_self = product(flat, self_block[...])
    with_opp = product(flat, opposite_block[...])
    base_y[0] = with_self[:rows] + with_opp[rows:] + cross_z[...]
    base_y[1] = with_self[rows:] + with_opp[:rows] + cross_z[...]


def high_low(value):
    high = value.astype(jnp.bfloat16).astype(jnp.float32)
    return high, value - high


def coarse_rows(partials, spread, onehot):
    subs = onehot.shape[1] // (2 * CORNERS)
    entries = jnp.zeros((2 * CORNERS, subs * LANES), jnp.float32)
    for comp in range(COMPS):
        part = partials[comp * CORNERS : (comp + 1) * CORNERS]
        stacked = jnp.concatenate(high_low(part), axis=0).astype(jnp.bfloat16)
        entries += product(stacked, spread[comp])
    entries = entries[:CORNERS] + entries[CORNERS:]
    by_sub = [entries[:, sub * LANES : (sub + 1) * LANES] for sub in range(subs)]
    both = jnp.concatenate(high_low(jnp.concatenate(by_sub, axis=0)), axis=0)
    return product(onehot[...], both.astype(jnp.bfloat16))


def local_kernel(
    partner, viscosity, traces, rxa, rxb, self_block, opposite_block, cross_block,
    base_x, base_y, base_z, cross_y, spread, onehot, corner_map,
    xa, xb, ya, yb, local_z, to_xa, to_xb, to_ya, to_yb, kept, jumps, dense,
):
    subs, _, rhs, size = traces.shape
    rows = subs * rhs
    trade_jumps(jumps, traces, partner, "sx", x_faces(), (rxa, rxb))
    flat = jumps[...].reshape(2 * rows, size)
    with_self = product(flat, self_block[...])
    with_opp = product(flat, opposite_block[...])
    from_x = product(pair_sum(jumps, 0), cross_block[...])
    from_xy = from_x + cross_y[...]
    totals = (
        with_self[:rows] + with_opp[rows:] + base_x[...],
        with_self[rows:] + with_opp[:rows] + base_x[...],
        base_y[0] + from_x,
        base_y[1] + from_x,
        base_z[0] + from_xy,
        base_z[1] + from_xy,
    )
    faces = (*x_faces(), *y_faces(), 4, 5)
    outs = (xa, xb, ya, yb, local_z.at[0], local_z.at[1])
    sent = (to_xa, to_xb, to_ya, to_yb)
    partials = jnp.zeros((rows, LANES), jnp.float32)
    for index, (face, total, out) in enumerate(zip(faces, totals, outs)):
        for sub in range(subs):
            here = slice(sub * rhs, (sub + 1) * rhs)
            value = (viscosity[sub] * total[here]).astype(jnp.bfloat16)
            out[sub] = value
            if index < 4:
                sent[index][partner[sub, face]] = value
        partials += product(out[...].reshape(rows, size), corner_map[face])
    partials = partials.T
    dense[...] = coarse_rows(partials, spread, onehot)
    me = lax.axis_index("sy")

    def block(bits):
        start = pl.multiple_of((me ^ bits) * COARSE_DEV, COARSE_DEV)
        return dense[pl.ds(start, COARSE_DEV), :]

    half, per_row = kept.shape[0], size // LANES
    for index in range((to_ya.shape[0] - subs) * per_row):
        lanes = slice(index % per_row * LANES, (index % per_row + 1) * LANES)
        both = jnp.zeros((2 * COARSE_DEV, LANES), jnp.float32)
        if index < half:
            kept[index] = block(2 * index)
            both = jnp.concatenate(high_low(block(2 * index + 1)), axis=0)
        to_ya[subs + index // per_row, :, lanes] = both.astype(jnp.bfloat16)


def first_add_kernel(subs, kept, got, *refs):
    keep, give = refs[2:4]
    half, per_row = kept.shape[0], got.shape[2] // LANES
    for index in range(half):
        lanes = slice(index % per_row * LANES, (index % per_row + 1) * LANES)
        both = got[subs + index // per_row, :, lanes].astype(jnp.float32)
        total = kept[index] + both[:COARSE_DEV] + both[COARSE_DEV:]
        out = keep if index < half // 2 else give
        out[index % (half // 2)] = total


def next_add_kernel(after, rxb, kept, got, keep, give):
    del after, rxb
    half = kept.shape[0]
    total = kept[...] + got[...]
    keep[...] = total[: half // 2]
    give[...] = total[half // 2 :]


def last_add_kernel(after, kept, got, coarse, total, sem):
    del after
    total[...] = (kept[0] + got[0])[:, : total.shape[1]]
    copy = pltpu.make_async_copy(total, coarse, sem)
    copy.start()
    copy.wait()


def apply_z_kernel(kept, local_z, applied, held, sems):
    del kept
    subs = local_z.shape[1]
    copies = []
    for sub in range(subs):
        up = local_z[0, sub].astype(jnp.float32)
        down = local_z[1, sub].astype(jnp.float32)
        if sub + 1 < subs:
            up = up - local_z[1, sub + 1].astype(jnp.float32)
        if sub > 0:
            down = down - local_z[0, sub - 1].astype(jnp.float32)
        held[sub, 0] = up
        held[sub, 1] = down
        copies.append(
            pltpu.make_async_copy(held.at[sub], applied.at[sub, pl.ds(4, 2)], sems.at[sub])
        )
        copies[-1].start()
    for copy in copies:
        copy.wait()


def apply_kernel(applied_in, rxb, rxa, ryb, rya, ya, yb, xa, xb, applied, held, sems):
    del applied_in
    copies = []
    trades = zip((*y_faces(), *x_faces()), (ya, yb, xa, xb), (rya, ryb, rxa, rxb))
    for index, (face, local, got) in enumerate(trades):
        for sub in range(held.shape[1]):
            other = got[sub].astype(jnp.float32)
            if index == 1:
                other = other * inner("sy")
            if index == 3:
                other = other * inner("sx")
            held[index, sub] = local[sub].astype(jnp.float32) - other
            copies.append(
                pltpu.make_async_copy(
                    held.at[index, sub], applied.at[sub, face], sems.at[index, sub]
                )
            )
            copies[-1].start()
    for copy in copies:
        copy.wait()


def body(
    traces, viscosity, partner, corner_owner, self_block, opposite_block, cross_block, corner_map
):
    values = traces[0, 0]
    slots, visc, owners = partner[0, 0], viscosity[0, 0], corner_owner[0, 0]
    subs, _, rhs, size = values.shape
    count = lax.axis_size("sy")
    rows = subs * rhs
    face_shape = (subs, rhs, size)
    bf16, f32 = jnp.bfloat16, jnp.float32

    xb, yb, xa, ya = pl.pallas_call(
        send_kernel,
        in_specs=[HBM],
        out_specs=[VMEM] * 4,
        out_shape=[in_vmem(face_shape, bf16)] * 4,
        scratch_shapes=[pltpu.SemaphoreType.DMA((4,))],
        compiler_params=params(8),
        cost_estimate=LONG,
    )(in_hbm(values))
    rxb = second_swap(xb, "sx")
    ryb = second_swap(yb, "sy")
    rxa = first_swap(xa, "sx")
    rya = first_swap(ya, "sy")
    map_v, spread, base_z, cross_z = pl.pallas_call(
        z_kernel,
        in_specs=[VMEM] * 6,
        out_specs=[VMEM] * 4,
        out_shape=[in_vmem((6, size, LANES), bf16), in_vmem((COMPS, rows, subs * LANES), bf16)]
        + [in_vmem((2, rows, size), f32)]
        + [in_vmem((rows, size), f32)],
        scratch_shapes=[pltpu.VMEM((2,) + face_shape, bf16)],
        compiler_params=params(12),
        cost_estimate=LONG,
    )(
        xa, values, self_block, opposite_block, cross_block,
        jnp.transpose(corner_map, (1, 0, 2)),
    )
    base_y, cross_y, base_x, onehot = pl.pallas_call(
        y_kernel,
        in_specs=[SMEM] + [VMEM] * 9,
        out_specs=[VMEM] * 4,
        out_shape=[in_vmem((2, rows, size), f32)] + [in_vmem((rows, size), f32)] * 2
        + [in_vmem((COARSE_DEV * count, 2 * subs * CORNERS), bf16)],
        scratch_shapes=[pltpu.VMEM((2,) + face_shape, bf16)],
        compiler_params=params(12),
    )(slots, values, ryb, rya, rxb, self_block, opposite_block, cross_block, cross_z, owners)
    half, per_row = count // 2, size // LANES
    long_shape = (subs + -(-half // per_row), rhs, size)

    def blocks(number):
        return in_vmem((number, COARSE_DEV, LANES), f32)

    xa, xb, ya, yb, local_z, to_xa, to_xb, to_ya, to_yb, kept = pl.pallas_call(
        local_kernel,
        in_specs=[SMEM] * 2 + [VMEM] * 13,
        out_specs=[VMEM] * 10,
        out_shape=[in_vmem(face_shape, bf16)] * 4
        + [in_vmem((2,) + face_shape, bf16)]
        + [in_vmem(face_shape, bf16)] * 2
        + [in_vmem(long_shape, bf16), in_vmem(face_shape, bf16), blocks(half)],
        scratch_shapes=[
            pltpu.VMEM((2,) + face_shape, bf16),
            pltpu.VMEM((COARSE_DEV * count, LANES), f32),
        ],
        compiler_params=params(16),
    )(
        slots, visc, values, rxa, rxb, self_block, opposite_block, cross_block,
        base_x, base_y, base_z, cross_y, spread, onehot, map_v,
    )
    rya = first_swap(to_ya, "sy")
    rxb = second_swap(to_xb, "sx")
    out_shape = jax.ShapeDtypeStruct(values.shape, f32)
    half //= 2
    kept, give, to_xa, to_yb = pl.pallas_call(
        lambda *refs: first_add_kernel(subs, *refs),
        in_specs=[VMEM] * 4,
        out_specs=[VMEM] * 4,
        out_shape=[blocks(half)] * 2 + [in_vmem(face_shape, bf16)] * 2,
        input_output_aliases={2: 2, 3: 3},
        compiler_params=params(4),
    )(kept, rya, to_xa, to_yb)
    got = cross_swap(give, "sy", 2 * half)
    applied = pl.pallas_call(
        apply_z_kernel,
        in_specs=[VMEM] * 2,
        out_specs=HBM,
        out_shape=out_shape,
        scratch_shapes=[
            pltpu.VMEM((subs, 2, rhs, size), f32),
            pltpu.SemaphoreType.DMA((subs,)),
        ],
        compiler_params=params(8),
        cost_estimate=LONG,
    )(kept, local_z)
    ryb = second_swap(to_yb, "sy")
    rxa = first_swap(to_xa, "sx")
    while half > 1:
        half //= 2
        kept, give = pl.pallas_call(
            next_add_kernel,
            in_specs=[HBM] + [VMEM] * 3,
            out_specs=[VMEM] * 2,
            out_shape=[blocks(half)] * 2,
            compiler_params=params(4),
            cost_estimate=LONG,
        )(in_hbm(applied), rxb, kept, got)
        got = cross_swap(give, "sy", 2 * half)
    applied = pl.pallas_call(
        apply_kernel,
        in_specs=[HBM] + [VMEM] * 8,
        out_specs=HBM,
        out_shape=out_shape,
        input_output_aliases={0: 0},
        scratch_shapes=[pltpu.VMEM((4,) + face_shape, f32), pltpu.SemaphoreType.DMA((4, subs))],
        compiler_params=params(12),
        cost_estimate=LONG,
    )(applied, rxb, rxa, ryb, rya, ya, yb, xa, xb)
    coarse = pl.pallas_call(
        last_add_kernel,
        in_specs=[HBM] + [VMEM] * 2,
        out_specs=HBM,
        out_shape=jax.ShapeDtypeStruct((COARSE_DEV, rhs * COMPS), f32),
        scratch_shapes=[pltpu.VMEM((COARSE_DEV, rhs * COMPS), f32), pltpu.SemaphoreType.DMA],
        compiler_params=params(4),
    )(in_hbm(applied), kept, got)
    return applied[None, None], coarse.T


def solution(mesh):
    return jax.shard_map(
        body,
        mesh=mesh,
        in_specs=(
            P("sx", "sy", None, None, None, None),
            P("sx", "sy", None),
            P("sx", "sy", None, None),
            P("sx", "sy", None, None),
            P(),
            P(),
            P(),
            P(),
        ),
        out_specs=(P("sx", "sy", None, None, None, None), P(None, ("sx", "sy"))),
        check_vma=False,
    )
```

```python
import jax
import jax.numpy as jnp
from jax import lax
from jax.experimental import pallas as pl
from jax.experimental.pallas import tpu as pltpu
from jax.sharding import PartitionSpec as P

CORNERS = 8
COMPS = 3
COARSE_DEV = 8
LANES = 128

VMEM = pl.BlockSpec(memory_space=pltpu.VMEM)
SMEM = pl.BlockSpec(memory_space=pltpu.SMEM)
HBM = pl.BlockSpec(memory_space=pltpu.HBM)
ANY = pl.BlockSpec(memory_space=pl.ANY)


def in_vmem(shape, dtype):
    return pltpu.VMEM(shape, dtype)


def in_hbm(value):
    return pltpu.with_memory_space_constraint(value, pltpu.HBM)


def params(mib):
    return pltpu.CompilerParams(vmem_limit_bytes=mib * 1024 * 1024)


LONG = pl.CostEstimate(flops=20 * 10**9, bytes_accessed=0, transcendentals=0)


def odd(axis):
    return lax.rem(lax.axis_index(axis), 2)


def first_swap(value, axis):
    return lax.ppermute(value, axis, [(i, i ^ 1) for i in range(lax.axis_size(axis))])


def second_swap(value, axis):
    rows, cols = lax.axis_size("sx"), lax.axis_size("sy")
    pairs = []
    for i in range(rows):
        for j in range(cols):
            if axis == "sx":
                k = i - 1 if i % 2 == 0 else i + 1
                target = (k, j) if 0 <= k < rows else (i, j ^ 1)
            else:
                k = j - 1 if j % 2 == 0 else j + 1
                target = (i, k) if 0 <= k < cols else (i ^ 2, j)
            pairs.append((i * cols + j, target[0] * cols + target[1]))
    return lax.ppermute(value, ("sx", "sy"), pairs)


def cross_swap(value, axis, bits):
    return lax.ppermute(value, axis, [(i, i ^ bits) for i in range(lax.axis_size(axis))])


def inner(axis):
    me = lax.axis_index(axis)
    return ((me > 0) & (me < lax.axis_size(axis) - 1)).astype(jnp.float32)


def x_faces():
    return odd("sx"), 1 - odd("sx")


def y_faces():
    return 2 + odd("sy"), 3 - odd("sy")


def send_kernel(traces, xb, yb, xa, ya, sems):
    faces = (*x_faces(), *y_faces())
    copies = [
        pltpu.make_async_copy(traces.at[:, face], out, sems.at[index])
        for index, (face, out) in enumerate(zip(faces, (xa, xb, ya, yb)))
    ]
    for copy in copies:
        copy.start()
    for copy in copies:
        copy.wait()


def product(left, right):
    return jnp.dot(left, right, preferred_element_type=jnp.float32)


def trade_jumps(jumps, traces, partner, axis, faces, received):
    for trade, (face, got) in enumerate(zip(faces, received)):
        for sub in range(traces.shape[0]):
            other = got[partner[sub, face]].astype(jnp.float32)
            if trade == 1:
                other = other * inner(axis)
            own = traces[sub, face].astype(jnp.float32)
            jumps[trade, sub] = (own - other).astype(jnp.bfloat16)


def flat_face(jumps, index):
    _, subs, rhs, size = jumps.shape
    return jumps[index].reshape(subs * rhs, size)


def pair_sum(jumps, first):
    up = flat_face(jumps, first).astype(jnp.float32)
    return (up + flat_face(jumps, first + 1).astype(jnp.float32)).astype(jnp.bfloat16)


def z_kernel(
    xa, traces, self_block, opposite_block, cross_block, corner_map,
    map_out, spread, base_z, cross_z, jumps,
):
    del xa
    subs, _, rhs, size = traces.shape
    rows = subs * rhs
    for sub in range(subs):
        up = traces[sub, 4].astype(jnp.float32)
        down = traces[sub, 5].astype(jnp.float32)
        if sub + 1 < subs:
            up = up - traces[sub + 1, 5].astype(jnp.float32)
        if sub > 0:
            down = down - traces[sub - 1, 4].astype(jnp.float32)
        jumps[0, sub] = up.astype(jnp.bfloat16)
        jumps[1, sub] = down.astype(jnp.bfloat16)
    width = CORNERS * COMPS
    row = lax.broadcasted_iota(jnp.int32, (width, LANES), 0)
    col = lax.broadcasted_iota(jnp.int32, (width, LANES), 1)
    place = (col % CORNERS) * COMPS + col // CORNERS
    order = ((row == place) & (col < width)).astype(jnp.float32).astype(jnp.bfloat16)
    for face in range(6):
        moved = lax.dot_general(
            corner_map[face], order, (((0,), (0,)), ((), ())), preferred_element_type=jnp.float32
        )
        map_out[face] = moved.astype(jnp.bfloat16)
    source = lax.broadcasted_iota(jnp.int32, (rows, subs * LANES), 0)
    target = lax.broadcasted_iota(jnp.int32, (rows, subs * LANES), 1)
    lane = (source // rhs) * LANES + (source % rhs) * COMPS
    for comp in range(COMPS):
        spread[comp] = (target == lane + comp).astype(jnp.float32).astype(jnp.bfloat16)
    flat = jumps[...].reshape(2 * rows, size)
    with_self = product(flat, self_block[...])
    with_opp = product(flat, opposite_block[...])
    base_z[0] = with_self[:rows] + with_opp[rows:]
    base_z[1] = with_self[rows:] + with_opp[:rows]
    cross_z[...] = product(pair_sum(jumps, 0), cross_block[...])


def y_kernel(
    partner, traces, ryb, rya, rxb, self_block, opposite_block, cross_block, cross_z, owners,
    base_y, cross_y, base_x, onehot, jumps,
):
    del rxb
    numbers = lax.broadcasted_iota(jnp.int32, (onehot.shape[0], CORNERS), 0)
    parts = [
        (numbers == owners[sub : sub + 1, :]).astype(jnp.float32) for sub in range(owners.shape[0])
    ]
    onehot[...] = jnp.concatenate(parts * 2, axis=1).astype(jnp.bfloat16)
    subs, _, rhs, size = traces.shape
    rows = subs * rhs
    trade_jumps(jumps, traces, partner, "sy", y_faces(), (rya, ryb))
    from_y = product(pair_sum(jumps, 0), cross_block[...])
    cross_y[...] = from_y
    base_x[...] = from_y + cross_z[...]
    flat = jumps[...].reshape(2 * rows, size)
    with_self = product(flat, self_block[...])
    with_opp = product(flat, opposite_block[...])
    base_y[0] = with_self[:rows] + with_opp[rows:] + cross_z[...]
    base_y[1] = with_self[rows:] + with_opp[:rows] + cross_z[...]


def high_low(value):
    high = value.astype(jnp.bfloat16).astype(jnp.float32)
    return high, value - high


def coarse_rows(partials, spread, onehot):
    subs = onehot.shape[1] // (2 * CORNERS)
    entries = jnp.zeros((2 * CORNERS, subs * LANES), jnp.float32)
    for comp in range(COMPS):
        part = partials[comp * CORNERS : (comp + 1) * CORNERS]
        stacked = jnp.concatenate(high_low(part), axis=0).astype(jnp.bfloat16)
        entries += product(stacked, spread[comp])
    entries = entries[:CORNERS] + entries[CORNERS:]
    by_sub = [entries[:, sub * LANES : (sub + 1) * LANES] for sub in range(subs)]
    both = jnp.concatenate(high_low(jnp.concatenate(by_sub, axis=0)), axis=0)
    return product(onehot[...], both.astype(jnp.bfloat16))


def local_kernel(
    partner, viscosity, traces, rxa, rxb, self_block, opposite_block, cross_block,
    base_x, base_y, base_z, cross_y, spread, onehot, corner_map,
    xa, xb, ya, yb, local_z, to_xa, to_xb, to_ya, to_yb, kept, give, jumps, dense,
):
    subs, _, rhs, size = traces.shape
    rows = subs * rhs
    trade_jumps(jumps, traces, partner, "sx", x_faces(), (rxa, rxb))
    flat = jumps[...].reshape(2 * rows, size)
    with_self = product(flat, self_block[...])
    with_opp = product(flat, opposite_block[...])
    from_x = product(pair_sum(jumps, 0), cross_block[...])
    from_xy = from_x + cross_y[...]
    totals = (
        with_self[:rows] + with_opp[rows:] + base_x[...],
        with_self[rows:] + with_opp[:rows] + base_x[...],
        base_y[0] + from_x,
        base_y[1] + from_x,
        base_z[0] + from_xy,
        base_z[1] + from_xy,
    )
    faces = (*x_faces(), *y_faces(), 4, 5)
    outs = (xa, xb, ya, yb, local_z.at[0], local_z.at[1])
    sent = (to_xa, to_xb, to_ya, to_yb)
    partials = jnp.zeros((rows, LANES), jnp.float32)
    for index, (face, total, out) in enumerate(zip(faces, totals, outs)):
        for sub in range(subs):
            here = slice(sub * rhs, (sub + 1) * rhs)
            value = (viscosity[sub] * total[here]).astype(jnp.bfloat16)
            out[sub] = value
            if index < 4:
                sent[index][partner[sub, face]] = value
        partials += product(out[...].reshape(rows, size), corner_map[face])
    partials = partials.T
    dense[...] = coarse_rows(partials, spread, onehot)
    me = lax.axis_index("sy")

    def block(bits):
        start = pl.multiple_of((me ^ bits) * COARSE_DEV, COARSE_DEV)
        return dense[pl.ds(start, COARSE_DEV), :]

    for index in range(kept.shape[0]):
        kept[index] = block(2 * index)
        give[index] = block(2 * index + 1)


def first_add_kernel(kept, got, *refs):
    keep, give = refs[3:5]
    half = kept.shape[0]
    total = kept[...] + got[...]
    keep[...] = total[: half // 2]
    give[...] = total[half // 2 :]


def next_add_kernel(after, rxb, kept, got, keep, give):
    del after, rxb
    half = kept.shape[0]
    total = kept[...] + got[...]
    keep[...] = total[: half // 2]
    give[...] = total[half // 2 :]


def last_add_kernel(after, kept, got, coarse, total, sem):
    del after
    total[...] = (kept[0] + got[0])[:, : total.shape[1]]
    copy = pltpu.make_async_copy(total, coarse, sem)
    copy.start()
    copy.wait()


def apply_z_kernel(kept, local_z, applied, held, sems):
    del kept
    subs = local_z.shape[1]
    copies = []
    for sub in range(subs):
        up = local_z[0, sub].astype(jnp.float32)
        down = local_z[1, sub].astype(jnp.float32)
        if sub + 1 < subs:
            up = up - local_z[1, sub + 1].astype(jnp.float32)
        if sub > 0:
            down = down - local_z[0, sub - 1].astype(jnp.float32)
        held[sub, 0] = up
        held[sub, 1] = down
        copies.append(
            pltpu.make_async_copy(held.at[sub], applied.at[sub, pl.ds(4, 2)], sems.at[sub])
        )
        copies[-1].start()
    for copy in copies:
        copy.wait()


def apply_kernel(applied_in, rxb, rxa, ryb, rya, ya, yb, xa, xb, applied, held, sems):
    del applied_in
    copies = []
    trades = zip((*y_faces(), *x_faces()), (ya, yb, xa, xb), (rya, ryb, rxa, rxb))
    for index, (face, local, got) in enumerate(trades):
        for sub in range(held.shape[1]):
            other = got[sub].astype(jnp.float32)
            if index == 1:
                other = other * inner("sy")
            if index == 3:
                other = other * inner("sx")
            held[index, sub] = local[sub].astype(jnp.float32) - other
            copies.append(
                pltpu.make_async_copy(
                    held.at[index, sub], applied.at[sub, face], sems.at[index, sub]
                )
            )
            copies[-1].start()
    for copy in copies:
        copy.wait()


def body(
    traces, viscosity, partner, corner_owner, self_block, opposite_block, cross_block, corner_map
):
    values = traces[0, 0]
    slots, visc, owners = partner[0, 0], viscosity[0, 0], corner_owner[0, 0]
    subs, _, rhs, size = values.shape
    count = lax.axis_size("sy")
    rows = subs * rhs
    face_shape = (subs, rhs, size)
    bf16, f32 = jnp.bfloat16, jnp.float32

    xb, yb, xa, ya = pl.pallas_call(
        send_kernel,
        in_specs=[HBM],
        out_specs=[VMEM] * 4,
        out_shape=[in_vmem(face_shape, bf16)] * 4,
        scratch_shapes=[pltpu.SemaphoreType.DMA((4,))],
        compiler_params=params(8),
        cost_estimate=LONG,
    )(in_hbm(values))
    rxb = second_swap(xb, "sx")
    ryb = second_swap(yb, "sy")
    rxa = first_swap(xa, "sx")
    rya = first_swap(ya, "sy")
    map_v, spread, base_z, cross_z = pl.pallas_call(
        z_kernel,
        in_specs=[VMEM] * 6,
        out_specs=[VMEM] * 4,
        out_shape=[in_vmem((6, size, LANES), bf16), in_vmem((COMPS, rows, subs * LANES), bf16)]
        + [in_vmem((2, rows, size), f32)]
        + [in_vmem((rows, size), f32)],
        scratch_shapes=[pltpu.VMEM((2,) + face_shape, bf16)],
        compiler_params=params(12),
        cost_estimate=LONG,
    )(
        xa, values, self_block, opposite_block, cross_block,
        jnp.transpose(corner_map, (1, 0, 2)),
    )
    base_y, cross_y, base_x, onehot = pl.pallas_call(
        y_kernel,
        in_specs=[SMEM] + [VMEM] * 9,
        out_specs=[VMEM] * 4,
        out_shape=[in_vmem((2, rows, size), f32)] + [in_vmem((rows, size), f32)] * 2
        + [in_vmem((COARSE_DEV * count, 2 * subs * CORNERS), bf16)],
        scratch_shapes=[pltpu.VMEM((2,) + face_shape, bf16)],
        compiler_params=params(12),
    )(slots, values, ryb, rya, rxb, self_block, opposite_block, cross_block, cross_z, owners)
    half = count // 2

    def blocks(number):
        return in_vmem((number, COARSE_DEV, LANES), f32)

    xa, xb, ya, yb, local_z, to_xa, to_xb, to_ya, to_yb, kept, give = pl.pallas_call(
        local_kernel,
        in_specs=[SMEM] * 2 + [VMEM] * 13,
        out_specs=[VMEM] * 11,
        out_shape=[in_vmem(face_shape, bf16)] * 4
        + [in_vmem((2,) + face_shape, bf16)]
        + [in_vmem(face_shape, bf16)] * 4
        + [blocks(half)] * 2,
        scratch_shapes=[
            pltpu.VMEM((2,) + face_shape, bf16),
            pltpu.VMEM((COARSE_DEV * count, LANES), f32),
        ],
        compiler_params=params(16),
    )(
        slots, visc, values, rxa, rxb, self_block, opposite_block, cross_block,
        base_x, base_y, base_z, cross_y, spread, onehot, map_v,
    )
    got = cross_swap(give, "sy", 1)
    rxb = second_swap(to_xb, "sx")
    out_shape = jax.ShapeDtypeStruct(values.shape, f32)
    half //= 2
    kept, give, to_xa, to_yb, to_ya = pl.pallas_call(
        first_add_kernel,
        in_specs=[VMEM] * 5,
        out_specs=[VMEM] * 5,
        out_shape=[blocks(half)] * 2 + [in_vmem(face_shape, bf16)] * 3,
        input_output_aliases={2: 2, 3: 3, 4: 4},
        compiler_params=params(4),
    )(kept, got, to_xa, to_yb, to_ya)
    got = cross_swap(give, "sy", 2 * half)
    applied = pl.pallas_call(
        apply_z_kernel,
        in_specs=[VMEM] * 2,
        out_specs=HBM,
        out_shape=out_shape,
        scratch_shapes=[
            pltpu.VMEM((subs, 2, rhs, size), f32),
            pltpu.SemaphoreType.DMA((subs,)),
        ],
        compiler_params=params(8),
        cost_estimate=LONG,
    )(kept, local_z)
    ryb = second_swap(to_yb, "sy")
    rxa = first_swap(to_xa, "sx")
    rya = first_swap(to_ya, "sy")
    while half > 1:
        half //= 2
        kept, give = pl.pallas_call(
            next_add_kernel,
            in_specs=[HBM] + [VMEM] * 3,
            out_specs=[VMEM] * 2,
            out_shape=[blocks(half)] * 2,
            compiler_params=params(4),
            cost_estimate=LONG,
        )(in_hbm(applied), rxb, kept, got)
        got = cross_swap(give, "sy", 2 * half)
    applied = pl.pallas_call(
        apply_kernel,
        in_specs=[HBM] + [VMEM] * 8,
        out_specs=HBM,
        out_shape=out_shape,
        input_output_aliases={0: 0},
        scratch_shapes=[pltpu.VMEM((4,) + face_shape, f32), pltpu.SemaphoreType.DMA((4, subs))],
        compiler_params=params(12),
        cost_estimate=LONG,
    )(applied, rxb, rxa, ryb, rya, ya, yb, xa, xb)
    coarse = pl.pallas_call(
        last_add_kernel,
        in_specs=[HBM] + [VMEM] * 2,
        out_specs=HBM,
        out_shape=jax.ShapeDtypeStruct((COARSE_DEV, rhs * COMPS), f32),
        scratch_shapes=[pltpu.VMEM((COARSE_DEV, rhs * COMPS), f32), pltpu.SemaphoreType.DMA],
        compiler_params=params(4),
    )(in_hbm(applied), kept, got)
    return applied[None, None], coarse.T


def solution(mesh):
    return jax.shard_map(
        body,
        mesh=mesh,
        in_specs=(
            P("sx", "sy", None, None, None, None),
            P("sx", "sy", None),
            P("sx", "sy", None, None),
            P("sx", "sy", None, None),
            P(),
            P(),
            P(),
            P(),
        ),
        out_specs=(P("sx", "sy", None, None, None, None), P(None, ("sx", "sy"))),
        check_vma=False,
    )
```

```python
import jax
import jax.numpy as jnp
from jax import lax
from jax.experimental import pallas as pl
from jax.experimental.pallas import tpu as pltpu
from jax.sharding import PartitionSpec as P

CORNERS = 8
COMPS = 3
COARSE_DEV = 8
LANES = 128

VMEM = pl.BlockSpec(memory_space=pltpu.VMEM)
SMEM = pl.BlockSpec(memory_space=pltpu.SMEM)
HBM = pl.BlockSpec(memory_space=pltpu.HBM)
ANY = pl.BlockSpec(memory_space=pl.ANY)


def in_vmem(shape, dtype):
    return pltpu.VMEM(shape, dtype)


def in_hbm(value):
    return pltpu.with_memory_space_constraint(value, pltpu.HBM)


def params(mib):
    return pltpu.CompilerParams(vmem_limit_bytes=mib * 1024 * 1024)


LONG = pl.CostEstimate(flops=20 * 10**9, bytes_accessed=0, transcendentals=0)


def odd(axis):
    return lax.rem(lax.axis_index(axis), 2)


def first_swap(value, axis):
    return lax.ppermute(value, axis, [(i, i ^ 1) for i in range(lax.axis_size(axis))])


def second_swap(value, axis):
    rows, cols = lax.axis_size("sx"), lax.axis_size("sy")
    pairs = []
    for i in range(rows):
        for j in range(cols):
            if axis == "sx":
                k = i - 1 if i % 2 == 0 else i + 1
                target = (k, j) if 0 <= k < rows else (i, j ^ 1)
            else:
                k = j - 1 if j % 2 == 0 else j + 1
                target = (i, k) if 0 <= k < cols else (i ^ 2, j)
            pairs.append((i * cols + j, target[0] * cols + target[1]))
    return lax.ppermute(value, ("sx", "sy"), pairs)


def cross_swap(value, axis, bits):
    return lax.ppermute(value, axis, [(i, i ^ bits) for i in range(lax.axis_size(axis))])


def inner(axis):
    me = lax.axis_index(axis)
    return ((me > 0) & (me < lax.axis_size(axis) - 1)).astype(jnp.float32)


def x_faces():
    return odd("sx"), 1 - odd("sx")


def y_faces():
    return 2 + odd("sy"), 3 - odd("sy")


def send_kernel(traces, xb, yb, xa, ya, sems):
    faces = (*x_faces(), *y_faces())
    copies = [
        pltpu.make_async_copy(traces.at[:, face], out, sems.at[index])
        for index, (face, out) in enumerate(zip(faces, (xa, xb, ya, yb)))
    ]
    for copy in copies:
        copy.start()
    for copy in copies:
        copy.wait()


def product(left, right):
    return jnp.dot(left, right, preferred_element_type=jnp.float32)


def trade_jumps(jumps, traces, partner, axis, faces, received):
    for trade, (face, got) in enumerate(zip(faces, received)):
        for sub in range(traces.shape[0]):
            other = got[partner[sub, face]].astype(jnp.float32)
            if trade == 1:
                other = other * inner(axis)
            own = traces[sub, face].astype(jnp.float32)
            jumps[trade, sub] = (own - other).astype(jnp.bfloat16)


def flat_face(jumps, index):
    _, subs, rhs, size = jumps.shape
    return jumps[index].reshape(subs * rhs, size)


def pair_sum(jumps, first):
    up = flat_face(jumps, first).astype(jnp.float32)
    return (up + flat_face(jumps, first + 1).astype(jnp.float32)).astype(jnp.bfloat16)


def z_kernel(
    xa, traces, self_block, opposite_block, cross_block, corner_map,
    map_out, spread, base_z, cross_z, jumps,
):
    del xa
    subs, _, rhs, size = traces.shape
    rows = subs * rhs
    for sub in range(subs):
        up = traces[sub, 4].astype(jnp.float32)
        down = traces[sub, 5].astype(jnp.float32)
        if sub + 1 < subs:
            up = up - traces[sub + 1, 5].astype(jnp.float32)
        if sub > 0:
            down = down - traces[sub - 1, 4].astype(jnp.float32)
        jumps[0, sub] = up.astype(jnp.bfloat16)
        jumps[1, sub] = down.astype(jnp.bfloat16)
    width = CORNERS * COMPS
    row = lax.broadcasted_iota(jnp.int32, (width, LANES), 0)
    col = lax.broadcasted_iota(jnp.int32, (width, LANES), 1)
    place = (col % CORNERS) * COMPS + col // CORNERS
    order = ((row == place) & (col < width)).astype(jnp.float32).astype(jnp.bfloat16)
    for face in range(6):
        moved = lax.dot_general(
            corner_map[face], order, (((0,), (0,)), ((), ())), preferred_element_type=jnp.float32
        )
        map_out[face] = moved.astype(jnp.bfloat16)
    source = lax.broadcasted_iota(jnp.int32, (rows, subs * LANES), 0)
    target = lax.broadcasted_iota(jnp.int32, (rows, subs * LANES), 1)
    lane = (source // rhs) * LANES + (source % rhs) * COMPS
    for comp in range(COMPS):
        spread[comp] = (target == lane + comp).astype(jnp.float32).astype(jnp.bfloat16)
    flat = jumps[...].reshape(2 * rows, size)
    with_self = product(flat, self_block[...])
    with_opp = product(flat, opposite_block[...])
    base_z[0] = with_self[:rows] + with_opp[rows:]
    base_z[1] = with_self[rows:] + with_opp[:rows]
    cross_z[...] = product(pair_sum(jumps, 0), cross_block[...])


def y_kernel(
    partner, traces, ryb, rya, rxb, self_block, opposite_block, cross_block, cross_z, owners,
    base_y, cross_y, base_x, onehot, jumps,
):
    del rxb
    numbers = lax.broadcasted_iota(jnp.int32, (onehot.shape[0], CORNERS), 0)
    parts = [
        (numbers == owners[sub : sub + 1, :]).astype(jnp.float32) for sub in range(owners.shape[0])
    ]
    onehot[...] = jnp.concatenate(parts * 2, axis=1).astype(jnp.bfloat16)
    subs, _, rhs, size = traces.shape
    rows = subs * rhs
    trade_jumps(jumps, traces, partner, "sy", y_faces(), (rya, ryb))
    from_y = product(pair_sum(jumps, 0), cross_block[...])
    cross_y[...] = from_y
    base_x[...] = from_y + cross_z[...]
    flat = jumps[...].reshape(2 * rows, size)
    with_self = product(flat, self_block[...])
    with_opp = product(flat, opposite_block[...])
    base_y[0] = with_self[:rows] + with_opp[rows:] + cross_z[...]
    base_y[1] = with_self[rows:] + with_opp[:rows] + cross_z[...]


def high_low(value):
    high = value.astype(jnp.bfloat16).astype(jnp.float32)
    return high, value - high


def coarse_rows(partials, spread, onehot):
    subs = onehot.shape[1] // (2 * CORNERS)
    entries = jnp.zeros((2 * CORNERS, subs * LANES), jnp.float32)
    for comp in range(COMPS):
        part = partials[comp * CORNERS : (comp + 1) * CORNERS]
        stacked = jnp.concatenate(high_low(part), axis=0).astype(jnp.bfloat16)
        entries += product(stacked, spread[comp])
    entries = entries[:CORNERS] + entries[CORNERS:]
    by_sub = [entries[:, sub * LANES : (sub + 1) * LANES] for sub in range(subs)]
    both = jnp.concatenate(high_low(jnp.concatenate(by_sub, axis=0)), axis=0)
    return product(onehot[...], both.astype(jnp.bfloat16))


def local_kernel(
    partner, viscosity, traces, rxa, rxb, self_block, opposite_block, cross_block,
    base_x, base_y, base_z, cross_y, spread, onehot, corner_map,
    xa, xb, ya, yb, local_z, to_xa, to_xb, to_ya, to_yb, kept, jumps, dense,
):
    subs, _, rhs, size = traces.shape
    rows = subs * rhs
    trade_jumps(jumps, traces, partner, "sx", x_faces(), (rxa, rxb))
    flat = jumps[...].reshape(2 * rows, size)
    with_self = product(flat, self_block[...])
    with_opp = product(flat, opposite_block[...])
    from_x = product(pair_sum(jumps, 0), cross_block[...])
    from_xy = from_x + cross_y[...]
    totals = (
        with_self[:rows] + with_opp[rows:] + base_x[...],
        with_self[rows:] + with_opp[:rows] + base_x[...],
        base_y[0] + from_x,
        base_y[1] + from_x,
        base_z[0] + from_xy,
        base_z[1] + from_xy,
    )
    faces = (*x_faces(), *y_faces(), 4, 5)
    outs = (xa, xb, ya, yb, local_z.at[0], local_z.at[1])
    sent = (to_xa, to_xb, to_ya, to_yb)
    partials = jnp.zeros((rows, LANES), jnp.float32)
    for index, (face, total, out) in enumerate(zip(faces, totals, outs)):
        for sub in range(subs):
            here = slice(sub * rhs, (sub + 1) * rhs)
            value = (viscosity[sub] * total[here]).astype(jnp.bfloat16)
            out[sub] = value
            if index < 4:
                sent[index][partner[sub, face]] = value
        partials += product(out[...].reshape(rows, size), corner_map[face])
    partials = partials.T
    dense[...] = coarse_rows(partials, spread, onehot)
    me = lax.axis_index("sy")

    def block(bits):
        start = pl.multiple_of((me ^ bits) * COARSE_DEV, COARSE_DEV)
        return dense[pl.ds(start, COARSE_DEV), :]

    half, per_row = kept.shape[0], size // LANES
    for index in range((to_ya.shape[0] - subs) * per_row):
        lanes = slice(index % per_row * LANES, (index % per_row + 1) * LANES)
        both = jnp.zeros((2 * COARSE_DEV, LANES), jnp.float32)
        if index < half:
            kept[index] = block(2 * index)
            both = jnp.concatenate(high_low(block(2 * index + 1)), axis=0)
        to_ya[subs + index // per_row, :, lanes] = both.astype(jnp.bfloat16)


def first_add_kernel(subs, kept, got, *refs):
    keep, give = refs[2:4]
    half, per_row = kept.shape[0], got.shape[2] // LANES
    for index in range(half):
        lanes = slice(index % per_row * LANES, (index % per_row + 1) * LANES)
        both = got[subs + index // per_row, :, lanes].astype(jnp.float32)
        total = kept[index] + both[:COARSE_DEV] + both[COARSE_DEV:]
        out = keep if index % 2 == 0 else give
        out[index // 2] = total


def next_add_kernel(after, rxb, kept, got, keep, give):
    del after, rxb
    for index in range(kept.shape[0]):
        out = keep if index % 2 == 0 else give
        out[index // 2] = kept[index] + got[index]


def last_add_kernel(after, kept, got, coarse, total, sem):
    del after
    total[...] = (kept[0] + got[0])[:, : total.shape[1]]
    copy = pltpu.make_async_copy(total, coarse, sem)
    copy.start()
    copy.wait()


def apply_z_kernel(kept, local_z, applied, held, sems):
    del kept
    subs = local_z.shape[1]
    copies = []
    for sub in range(subs):
        up = local_z[0, sub].astype(jnp.float32)
        down = local_z[1, sub].astype(jnp.float32)
        if sub + 1 < subs:
            up = up - local_z[1, sub + 1].astype(jnp.float32)
        if sub > 0:
            down = down - local_z[0, sub - 1].astype(jnp.float32)
        held[sub, 0] = up
        held[sub, 1] = down
        copies.append(
            pltpu.make_async_copy(held.at[sub], applied.at[sub, pl.ds(4, 2)], sems.at[sub])
        )
        copies[-1].start()
    for copy in copies:
        copy.wait()


def apply_kernel(applied_in, rxb, rxa, ryb, rya, ya, yb, xa, xb, applied, held, sems):
    del applied_in
    copies = []
    trades = zip((*y_faces(), *x_faces()), (ya, yb, xa, xb), (rya, ryb, rxa, rxb))
    for index, (face, local, got) in enumerate(trades):
        for sub in range(held.shape[1]):
            other = got[sub].astype(jnp.float32)
            if index == 1:
                other = other * inner("sy")
            if index == 3:
                other = other * inner("sx")
            held[index, sub] = local[sub].astype(jnp.float32) - other
            copies.append(
                pltpu.make_async_copy(
                    held.at[index, sub], applied.at[sub, face], sems.at[index, sub]
                )
            )
            copies[-1].start()
    for copy in copies:
        copy.wait()


def body(
    traces, viscosity, partner, corner_owner, self_block, opposite_block, cross_block, corner_map
):
    values = traces[0, 0]
    slots, visc, owners = partner[0, 0], viscosity[0, 0], corner_owner[0, 0]
    subs, _, rhs, size = values.shape
    count = lax.axis_size("sy")
    rows = subs * rhs
    face_shape = (subs, rhs, size)
    bf16, f32 = jnp.bfloat16, jnp.float32

    xb, yb, xa, ya = pl.pallas_call(
        send_kernel,
        in_specs=[HBM],
        out_specs=[VMEM] * 4,
        out_shape=[in_vmem(face_shape, bf16)] * 4,
        scratch_shapes=[pltpu.SemaphoreType.DMA((4,))],
        compiler_params=params(8),
        cost_estimate=LONG,
    )(in_hbm(values))
    rxb = second_swap(xb, "sx")
    ryb = second_swap(yb, "sy")
    rxa = first_swap(xa, "sx")
    rya = first_swap(ya, "sy")
    map_v, spread, base_z, cross_z = pl.pallas_call(
        z_kernel,
        in_specs=[VMEM] * 6,
        out_specs=[VMEM] * 4,
        out_shape=[in_vmem((6, size, LANES), bf16), in_vmem((COMPS, rows, subs * LANES), bf16)]
        + [in_vmem((2, rows, size), f32)]
        + [in_vmem((rows, size), f32)],
        scratch_shapes=[pltpu.VMEM((2,) + face_shape, bf16)],
        compiler_params=params(12),
        cost_estimate=LONG,
    )(
        xa, values, self_block, opposite_block, cross_block,
        jnp.transpose(corner_map, (1, 0, 2)),
    )
    base_y, cross_y, base_x, onehot = pl.pallas_call(
        y_kernel,
        in_specs=[SMEM] + [VMEM] * 9,
        out_specs=[VMEM] * 4,
        out_shape=[in_vmem((2, rows, size), f32)] + [in_vmem((rows, size), f32)] * 2
        + [in_vmem((COARSE_DEV * count, 2 * subs * CORNERS), bf16)],
        scratch_shapes=[pltpu.VMEM((2,) + face_shape, bf16)],
        compiler_params=params(12),
    )(slots, values, ryb, rya, rxb, self_block, opposite_block, cross_block, cross_z, owners)
    half, per_row = count // 2, size // LANES
    long_shape = (subs + -(-half // per_row), rhs, size)

    def blocks(number):
        return in_vmem((number, COARSE_DEV, LANES), f32)

    xa, xb, ya, yb, local_z, to_xa, to_xb, to_ya, to_yb, kept = pl.pallas_call(
        local_kernel,
        in_specs=[SMEM] * 2 + [VMEM] * 13,
        out_specs=[VMEM] * 10,
        out_shape=[in_vmem(face_shape, bf16)] * 4
        + [in_vmem((2,) + face_shape, bf16)]
        + [in_vmem(face_shape, bf16)] * 2
        + [in_vmem(long_shape, bf16), in_vmem(face_shape, bf16), blocks(half)],
        scratch_shapes=[
            pltpu.VMEM((2,) + face_shape, bf16),
            pltpu.VMEM((COARSE_DEV * count, LANES), f32),
        ],
        compiler_params=params(16),
    )(
        slots, visc, values, rxa, rxb, self_block, opposite_block, cross_block,
        base_x, base_y, base_z, cross_y, spread, onehot, map_v,
    )
    rya = first_swap(to_ya, "sy")
    rxb = second_swap(to_xb, "sx")
    out_shape = jax.ShapeDtypeStruct(values.shape, f32)
    half //= 2
    bits = 2
    kept, give, to_xa, to_yb = pl.pallas_call(
        lambda *refs: first_add_kernel(subs, *refs),
        in_specs=[VMEM] * 4,
        out_specs=[VMEM] * 4,
        out_shape=[blocks(half)] * 2 + [in_vmem(face_shape, bf16)] * 2,
        input_output_aliases={2: 2, 3: 3},
        compiler_params=params(4),
    )(kept, rya, to_xa, to_yb)
    got = cross_swap(give, "sy", bits)
    applied = pl.pallas_call(
        apply_z_kernel,
        in_specs=[VMEM] * 2,
        out_specs=HBM,
        out_shape=out_shape,
        scratch_shapes=[
            pltpu.VMEM((subs, 2, rhs, size), f32),
            pltpu.SemaphoreType.DMA((subs,)),
        ],
        compiler_params=params(8),
        cost_estimate=LONG,
    )(kept, local_z)
    ryb = second_swap(to_yb, "sy")
    rxa = first_swap(to_xa, "sx")
    while half > 1:
        half //= 2
        bits *= 2
        kept, give = pl.pallas_call(
            next_add_kernel,
            in_specs=[HBM] + [VMEM] * 3,
            out_specs=[VMEM] * 2,
            out_shape=[blocks(half)] * 2,
            compiler_params=params(4),
            cost_estimate=LONG,
        )(in_hbm(applied), rxb, kept, got)
        got = cross_swap(give, "sy", bits)
    applied = pl.pallas_call(
        apply_kernel,
        in_specs=[HBM] + [VMEM] * 8,
        out_specs=HBM,
        out_shape=out_shape,
        input_output_aliases={0: 0},
        scratch_shapes=[pltpu.VMEM((4,) + face_shape, f32), pltpu.SemaphoreType.DMA((4, subs))],
        compiler_params=params(12),
        cost_estimate=LONG,
    )(applied, rxb, rxa, ryb, rya, ya, yb, xa, xb)
    coarse = pl.pallas_call(
        last_add_kernel,
        in_specs=[HBM] + [VMEM] * 2,
        out_specs=HBM,
        out_shape=jax.ShapeDtypeStruct((COARSE_DEV, rhs * COMPS), f32),
        scratch_shapes=[pltpu.VMEM((COARSE_DEV, rhs * COMPS), f32), pltpu.SemaphoreType.DMA],
        compiler_params=params(4),
    )(in_hbm(applied), kept, got)
    return applied[None, None], coarse.T


def solution(mesh):
    return jax.shard_map(
        body,
        mesh=mesh,
        in_specs=(
            P("sx", "sy", None, None, None, None),
            P("sx", "sy", None),
            P("sx", "sy", None, None),
            P("sx", "sy", None, None),
            P(),
            P(),
            P(),
            P(),
        ),
        out_specs=(P("sx", "sy", None, None, None, None), P(None, ("sx", "sy"))),
        check_vma=False,
    )
```

```python
import jax
import jax.numpy as jnp
from jax import lax
from jax.experimental import pallas as pl
from jax.experimental.pallas import tpu as pltpu
from jax.sharding import PartitionSpec as P

CORNERS = 8
COMPS = 3
COARSE_DEV = 8
LANES = 128

VMEM = pl.BlockSpec(memory_space=pltpu.VMEM)
SMEM = pl.BlockSpec(memory_space=pltpu.SMEM)
HBM = pl.BlockSpec(memory_space=pltpu.HBM)
ANY = pl.BlockSpec(memory_space=pl.ANY)


def in_vmem(shape, dtype):
    return pltpu.VMEM(shape, dtype)


def in_hbm(value):
    return pltpu.with_memory_space_constraint(value, pltpu.HBM)


def params(mib):
    return pltpu.CompilerParams(vmem_limit_bytes=mib * 1024 * 1024)


LONG = pl.CostEstimate(flops=20 * 10**9, bytes_accessed=0, transcendentals=0)


def odd(axis):
    return lax.rem(lax.axis_index(axis), 2)


def first_swap(value, axis):
    return lax.ppermute(value, axis, [(i, i ^ 1) for i in range(lax.axis_size(axis))])


def second_swap(value, axis):
    rows, cols = lax.axis_size("sx"), lax.axis_size("sy")
    pairs = []
    for i in range(rows):
        for j in range(cols):
            if axis == "sx":
                k = i - 1 if i % 2 == 0 else i + 1
                target = (k, j) if 0 <= k < rows else (i, j ^ 1)
            else:
                k = j - 1 if j % 2 == 0 else j + 1
                target = (i, k) if 0 <= k < cols else (i ^ 2, j)
            pairs.append((i * cols + j, target[0] * cols + target[1]))
    return lax.ppermute(value, ("sx", "sy"), pairs)


def cross_swap(value, axis, bits):
    return lax.ppermute(value, axis, [(i, i ^ bits) for i in range(lax.axis_size(axis))])


def inner(axis):
    me = lax.axis_index(axis)
    return ((me > 0) & (me < lax.axis_size(axis) - 1)).astype(jnp.float32)


def x_faces():
    return odd("sx"), 1 - odd("sx")


def y_faces():
    return 2 + odd("sy"), 3 - odd("sy")


def send_kernel(traces, xb, yb, xa, ya, sems):
    faces = (*x_faces(), *y_faces())
    copies = [
        pltpu.make_async_copy(traces.at[:, face], out, sems.at[index])
        for index, (face, out) in enumerate(zip(faces, (xa, xb, ya, yb)))
    ]
    for copy in copies:
        copy.start()
    for copy in copies:
        copy.wait()


def product(left, right):
    return jnp.dot(left, right, preferred_element_type=jnp.float32)


def trade_jumps(jumps, traces, partner, axis, faces, received):
    for trade, (face, got) in enumerate(zip(faces, received)):
        for sub in range(traces.shape[0]):
            other = got[partner[sub, face]].astype(jnp.float32)
            if trade == 1:
                other = other * inner(axis)
            own = traces[sub, face].astype(jnp.float32)
            jumps[trade, sub] = (own - other).astype(jnp.bfloat16)


def flat_face(jumps, index):
    _, subs, rhs, size = jumps.shape
    return jumps[index].reshape(subs * rhs, size)


def pair_sum(jumps, first):
    up = flat_face(jumps, first).astype(jnp.float32)
    return (up + flat_face(jumps, first + 1).astype(jnp.float32)).astype(jnp.bfloat16)


def z_kernel(
    xa, traces, self_block, opposite_block, cross_block, corner_map,
    map_out, spread, base_z, cross_z, jumps,
):
    del xa
    subs, _, rhs, size = traces.shape
    rows = subs * rhs
    for sub in range(subs):
        up = traces[sub, 4].astype(jnp.float32)
        down = traces[sub, 5].astype(jnp.float32)
        if sub + 1 < subs:
            up = up - traces[sub + 1, 5].astype(jnp.float32)
        if sub > 0:
            down = down - traces[sub - 1, 4].astype(jnp.float32)
        jumps[0, sub] = up.astype(jnp.bfloat16)
        jumps[1, sub] = down.astype(jnp.bfloat16)
    width = CORNERS * COMPS
    row = lax.broadcasted_iota(jnp.int32, (width, LANES), 0)
    col = lax.broadcasted_iota(jnp.int32, (width, LANES), 1)
    place = (col % CORNERS) * COMPS + col // CORNERS
    order = ((row == place) & (col < width)).astype(jnp.float32).astype(jnp.bfloat16)
    for face in range(6):
        moved = lax.dot_general(
            corner_map[face], order, (((0,), (0,)), ((), ())), preferred_element_type=jnp.float32
        )
        map_out[face] = moved.astype(jnp.bfloat16)
    source = lax.broadcasted_iota(jnp.int32, (rows, subs * LANES), 0)
    target = lax.broadcasted_iota(jnp.int32, (rows, subs * LANES), 1)
    lane = (source // rhs) * LANES + (source % rhs) * COMPS
    for comp in range(COMPS):
        spread[comp] = (target == lane + comp).astype(jnp.float32).astype(jnp.bfloat16)
    flat = jumps[...].reshape(2 * rows, size)
    with_self = product(flat, self_block[...])
    with_opp = product(flat, opposite_block[...])
    base_z[0] = with_self[:rows] + with_opp[rows:]
    base_z[1] = with_self[rows:] + with_opp[:rows]
    cross_z[...] = product(pair_sum(jumps, 0), cross_block[...])


def y_kernel(
    partner, traces, ryb, rya, rxb, self_block, opposite_block, cross_block, cross_z, owners,
    base_y, cross_y, base_x, onehot, jumps,
):
    del rxb
    numbers = lax.broadcasted_iota(jnp.int32, (onehot.shape[0], CORNERS), 0)
    parts = [
        (numbers == owners[sub : sub + 1, :]).astype(jnp.float32) for sub in range(owners.shape[0])
    ]
    onehot[...] = jnp.concatenate(parts * 2, axis=1).astype(jnp.bfloat16)
    subs, _, rhs, size = traces.shape
    rows = subs * rhs
    trade_jumps(jumps, traces, partner, "sy", y_faces(), (rya, ryb))
    from_y = product(pair_sum(jumps, 0), cross_block[...])
    cross_y[...] = from_y
    base_x[...] = from_y + cross_z[...]
    flat = jumps[...].reshape(2 * rows, size)
    with_self = product(flat, self_block[...])
    with_opp = product(flat, opposite_block[...])
    base_y[0] = with_self[:rows] + with_opp[rows:] + cross_z[...]
    base_y[1] = with_self[rows:] + with_opp[:rows] + cross_z[...]


def high_low(value):
    high = value.astype(jnp.bfloat16).astype(jnp.float32)
    return high, value - high


def coarse_rows(partials, spread, onehot):
    subs = onehot.shape[1] // (2 * CORNERS)
    entries = jnp.zeros((2 * CORNERS, subs * LANES), jnp.float32)
    for comp in range(COMPS):
        part = partials[comp * CORNERS : (comp + 1) * CORNERS]
        stacked = jnp.concatenate(high_low(part), axis=0).astype(jnp.bfloat16)
        entries += product(stacked, spread[comp])
    entries = entries[:CORNERS] + entries[CORNERS:]
    by_sub = [entries[:, sub * LANES : (sub + 1) * LANES] for sub in range(subs)]
    both = jnp.concatenate(high_low(jnp.concatenate(by_sub, axis=0)), axis=0)
    return product(onehot[...], both.astype(jnp.bfloat16))


def local_kernel(
    partner, viscosity, traces, rxa, rxb, self_block, opposite_block, cross_block,
    base_x, base_y, base_z, cross_y, spread, onehot, corner_map,
    xa, xb, ya, yb, local_z, to_xa, to_xb, to_ya, to_yb, kept, jumps, dense,
):
    subs, _, rhs, size = traces.shape
    rows = subs * rhs
    trade_jumps(jumps, traces, partner, "sx", x_faces(), (rxa, rxb))
    flat = jumps[...].reshape(2 * rows, size)
    with_self = product(flat, self_block[...])
    with_opp = product(flat, opposite_block[...])
    from_x = product(pair_sum(jumps, 0), cross_block[...])
    from_xy = from_x + cross_y[...]
    totals = (
        with_self[:rows] + with_opp[rows:] + base_x[...],
        with_self[rows:] + with_opp[:rows] + base_x[...],
        base_y[0] + from_x,
        base_y[1] + from_x,
        base_z[0] + from_xy,
        base_z[1] + from_xy,
    )
    faces = (*x_faces(), *y_faces(), 4, 5)
    outs = (xa, xb, ya, yb, local_z.at[0], local_z.at[1])
    sent = (to_xa, to_xb, to_ya, to_yb)
    partials = jnp.zeros((rows, LANES), jnp.float32)
    for index, (face, total, out) in enumerate(zip(faces, totals, outs)):
        for sub in range(subs):
            here = slice(sub * rhs, (sub + 1) * rhs)
            value = (viscosity[sub] * total[here]).astype(jnp.bfloat16)
            out[sub] = value
            if index < 4:
                sent[index][partner[sub, face]] = value
        partials += product(out[...].reshape(rows, size), corner_map[face])
    partials = partials.T
    dense[...] = coarse_rows(partials, spread, onehot)
    me = lax.axis_index("sy")

    def block(bits):
        start = pl.multiple_of((me ^ bits) * COARSE_DEV, COARSE_DEV)
        return dense[pl.ds(start, COARSE_DEV), :]

    half, per_row = kept.shape[0], size // LANES
    for index in range((to_ya.shape[0] - subs) * per_row):
        lanes = slice(index % per_row * LANES, (index % per_row + 1) * LANES)
        both = jnp.zeros((2 * COARSE_DEV, LANES), jnp.float32)
        if index < half:
            kept[index] = block(2 * index)
            both = jnp.concatenate(high_low(block(2 * index + 1)), axis=0)
        to_ya[subs + index // per_row, :, lanes] = both.astype(jnp.bfloat16)


def first_add_kernel(subs, kept, got, *refs):
    keep, give = refs[3:5]
    half, per_row = kept.shape[0], got.shape[2] // LANES
    for index in range(half):
        lanes = slice(index % per_row * LANES, (index % per_row + 1) * LANES)
        both = got[subs + index // per_row, :, lanes].astype(jnp.float32)
        total = kept[index] + both[:COARSE_DEV] + both[COARSE_DEV:]
        out = keep if index % 2 == 0 else give
        out[index // 2] = total


def next_add_kernel(after, kept, got, keep, give):
    del after
    for index in range(kept.shape[0]):
        out = keep if index % 2 == 0 else give
        out[index // 2] = kept[index] + got[index]


def last_add_kernel(after, kept, got, coarse, total, sem):
    del after
    total[...] = (kept[0] + got[0])[:, : total.shape[1]]
    copy = pltpu.make_async_copy(total, coarse, sem)
    copy.start()
    copy.wait()


def apply_z_kernel(kept, local_z, applied, held, sems):
    del kept
    subs = local_z.shape[1]
    copies = []
    for sub in range(subs):
        up = local_z[0, sub].astype(jnp.float32)
        down = local_z[1, sub].astype(jnp.float32)
        if sub + 1 < subs:
            up = up - local_z[1, sub + 1].astype(jnp.float32)
        if sub > 0:
            down = down - local_z[0, sub - 1].astype(jnp.float32)
        held[sub, 0] = up
        held[sub, 1] = down
        copies.append(
            pltpu.make_async_copy(held.at[sub], applied.at[sub, pl.ds(4, 2)], sems.at[sub])
        )
        copies[-1].start()
    for copy in copies:
        copy.wait()


def apply_kernel(applied_in, rxa, rxb, ryb, rya, ya, yb, xa, xb, applied, held, sems):
    del applied_in
    copies = []
    trades = zip((*y_faces(), *x_faces()), (ya, yb, xa, xb), (rya, ryb, rxa, rxb))
    for index, (face, local, got) in enumerate(trades):
        for sub in range(held.shape[1]):
            other = got[sub].astype(jnp.float32)
            if index == 1:
                other = other * inner("sy")
            if index == 3:
                other = other * inner("sx")
            held[index, sub] = local[sub].astype(jnp.float32) - other
            copies.append(
                pltpu.make_async_copy(
                    held.at[index, sub], applied.at[sub, face], sems.at[index, sub]
                )
            )
            copies[-1].start()
    for copy in copies:
        copy.wait()


def body(
    traces, viscosity, partner, corner_owner, self_block, opposite_block, cross_block, corner_map
):
    values = traces[0, 0]
    slots, visc, owners = partner[0, 0], viscosity[0, 0], corner_owner[0, 0]
    subs, _, rhs, size = values.shape
    count = lax.axis_size("sy")
    rows = subs * rhs
    face_shape = (subs, rhs, size)
    bf16, f32 = jnp.bfloat16, jnp.float32

    xb, yb, xa, ya = pl.pallas_call(
        send_kernel,
        in_specs=[HBM],
        out_specs=[VMEM] * 4,
        out_shape=[in_vmem(face_shape, bf16)] * 4,
        scratch_shapes=[pltpu.SemaphoreType.DMA((4,))],
        compiler_params=params(8),
        cost_estimate=LONG,
    )(in_hbm(values))
    rxb = second_swap(xb, "sx")
    ryb = second_swap(yb, "sy")
    rxa = first_swap(xa, "sx")
    rya = first_swap(ya, "sy")
    map_v, spread, base_z, cross_z = pl.pallas_call(
        z_kernel,
        in_specs=[VMEM] * 6,
        out_specs=[VMEM] * 4,
        out_shape=[in_vmem((6, size, LANES), bf16), in_vmem((COMPS, rows, subs * LANES), bf16)]
        + [in_vmem((2, rows, size), f32)]
        + [in_vmem((rows, size), f32)],
        scratch_shapes=[pltpu.VMEM((2,) + face_shape, bf16)],
        compiler_params=params(12),
        cost_estimate=LONG,
    )(
        xa, values, self_block, opposite_block, cross_block,
        jnp.transpose(corner_map, (1, 0, 2)),
    )
    base_y, cross_y, base_x, onehot = pl.pallas_call(
        y_kernel,
        in_specs=[SMEM] + [VMEM] * 9,
        out_specs=[VMEM] * 4,
        out_shape=[in_vmem((2, rows, size), f32)] + [in_vmem((rows, size), f32)] * 2
        + [in_vmem((COARSE_DEV * count, 2 * subs * CORNERS), bf16)],
        scratch_shapes=[pltpu.VMEM((2,) + face_shape, bf16)],
        compiler_params=params(12),
    )(slots, values, ryb, rya, rxb, self_block, opposite_block, cross_block, cross_z, owners)
    half, per_row = count // 2, size // LANES
    long_shape = (subs + -(-half // per_row), rhs, size)

    def blocks(number):
        return in_vmem((number, COARSE_DEV, LANES), f32)

    xa, xb, ya, yb, local_z, to_xa, to_xb, to_ya, to_yb, kept = pl.pallas_call(
        local_kernel,
        in_specs=[SMEM] * 2 + [VMEM] * 13,
        out_specs=[VMEM] * 10,
        out_shape=[in_vmem(face_shape, bf16)] * 4
        + [in_vmem((2,) + face_shape, bf16)]
        + [in_vmem(face_shape, bf16)] * 2
        + [in_vmem(long_shape, bf16), in_vmem(face_shape, bf16), blocks(half)],
        scratch_shapes=[
            pltpu.VMEM((2,) + face_shape, bf16),
            pltpu.VMEM((COARSE_DEV * count, LANES), f32),
        ],
        compiler_params=params(16),
    )(
        slots, visc, values, rxa, rxb, self_block, opposite_block, cross_block,
        base_x, base_y, base_z, cross_y, spread, onehot, map_v,
    )
    rya = first_swap(to_ya, "sy")
    out_shape = jax.ShapeDtypeStruct(values.shape, f32)
    half //= 2
    bits = 2
    kept, give, to_xa, to_xb, to_yb = pl.pallas_call(
        lambda *refs: first_add_kernel(subs, *refs),
        in_specs=[VMEM] * 5,
        out_specs=[VMEM] * 5,
        out_shape=[blocks(half)] * 2 + [in_vmem(face_shape, bf16)] * 3,
        input_output_aliases={2: 2, 3: 3, 4: 4},
        compiler_params=params(4),
    )(kept, rya, to_xa, to_xb, to_yb)
    got = cross_swap(give, "sy", bits)
    applied = pl.pallas_call(
        apply_z_kernel,
        in_specs=[VMEM] * 2,
        out_specs=HBM,
        out_shape=out_shape,
        scratch_shapes=[
            pltpu.VMEM((subs, 2, rhs, size), f32),
            pltpu.SemaphoreType.DMA((subs,)),
        ],
        compiler_params=params(8),
        cost_estimate=LONG,
    )(kept, local_z)
    rxa = first_swap(to_xa, "sx")
    rxb = second_swap(to_xb, "sx")
    ryb = second_swap(to_yb, "sy")
    while half > 1:
        half //= 2
        bits *= 2
        kept, give = pl.pallas_call(
            next_add_kernel,
            in_specs=[HBM] + [VMEM] * 2,
            out_specs=[VMEM] * 2,
            out_shape=[blocks(half)] * 2,
            compiler_params=params(4),
            cost_estimate=LONG,
        )(in_hbm(applied), kept, got)
        got = cross_swap(give, "sy", bits)
    applied = pl.pallas_call(
        apply_kernel,
        in_specs=[HBM] + [VMEM] * 8,
        out_specs=HBM,
        out_shape=out_shape,
        input_output_aliases={0: 0},
        scratch_shapes=[pltpu.VMEM((4,) + face_shape, f32), pltpu.SemaphoreType.DMA((4, subs))],
        compiler_params=params(12),
        cost_estimate=LONG,
    )(applied, rxa, rxb, ryb, rya, ya, yb, xa, xb)
    coarse = pl.pallas_call(
        last_add_kernel,
        in_specs=[HBM] + [VMEM] * 2,
        out_specs=HBM,
        out_shape=jax.ShapeDtypeStruct((COARSE_DEV, rhs * COMPS), f32),
        scratch_shapes=[pltpu.VMEM((COARSE_DEV, rhs * COMPS), f32), pltpu.SemaphoreType.DMA],
        compiler_params=params(4),
    )(in_hbm(applied), kept, got)
    return applied[None, None], coarse.T


def solution(mesh):
    return jax.shard_map(
        body,
        mesh=mesh,
        in_specs=(
            P("sx", "sy", None, None, None, None),
            P("sx", "sy", None),
            P("sx", "sy", None, None),
            P("sx", "sy", None, None),
            P(),
            P(),
            P(),
            P(),
        ),
        out_specs=(P("sx", "sy", None, None, None, None), P(None, ("sx", "sy"))),
        check_vma=False,
    )
```

```python
import jax
import jax.numpy as jnp
from jax import lax
from jax.experimental import pallas as pl
from jax.experimental.pallas import tpu as pltpu
from jax.sharding import PartitionSpec as P

CORNERS = 8
COMPS = 3
COARSE_DEV = 8
LANES = 128

VMEM = pl.BlockSpec(memory_space=pltpu.VMEM)
SMEM = pl.BlockSpec(memory_space=pltpu.SMEM)
HBM = pl.BlockSpec(memory_space=pltpu.HBM)
ANY = pl.BlockSpec(memory_space=pl.ANY)


def in_vmem(shape, dtype):
    return pltpu.VMEM(shape, dtype)


def in_hbm(value):
    return pltpu.with_memory_space_constraint(value, pltpu.HBM)


def params(mib):
    return pltpu.CompilerParams(vmem_limit_bytes=mib * 1024 * 1024)


LONG = pl.CostEstimate(flops=20 * 10**9, bytes_accessed=0, transcendentals=0)


def odd(axis):
    return lax.rem(lax.axis_index(axis), 2)


def first_swap(value, axis):
    return lax.ppermute(value, axis, [(i, i ^ 1) for i in range(lax.axis_size(axis))])


def second_swap(value, axis):
    rows, cols = lax.axis_size("sx"), lax.axis_size("sy")
    pairs = []
    for i in range(rows):
        for j in range(cols):
            if axis == "sx":
                k = i - 1 if i % 2 == 0 else i + 1
                target = (k, j) if 0 <= k < rows else (i, j ^ 1)
            else:
                k = j - 1 if j % 2 == 0 else j + 1
                target = (i, k) if 0 <= k < cols else (i ^ 2, j)
            pairs.append((i * cols + j, target[0] * cols + target[1]))
    return lax.ppermute(value, ("sx", "sy"), pairs)


def cross_swap(value, axis, bits):
    return lax.ppermute(value, axis, [(i, i ^ bits) for i in range(lax.axis_size(axis))])


def inner(axis):
    me = lax.axis_index(axis)
    return ((me > 0) & (me < lax.axis_size(axis) - 1)).astype(jnp.float32)


def x_faces():
    return odd("sx"), 1 - odd("sx")


def y_faces():
    return 2 + odd("sy"), 3 - odd("sy")


def send_kernel(traces, xb, yb, xa, ya, sems):
    faces = (*x_faces(), *y_faces())
    copies = [
        pltpu.make_async_copy(traces.at[:, face], out, sems.at[index])
        for index, (face, out) in enumerate(zip(faces, (xa, xb, ya, yb)))
    ]
    for copy in copies:
        copy.start()
    for copy in copies:
        copy.wait()


def product(left, right):
    return jnp.dot(left, right, preferred_element_type=jnp.float32)


def trade_jumps(jumps, traces, partner, axis, faces, received):
    for trade, (face, got) in enumerate(zip(faces, received)):
        for sub in range(traces.shape[0]):
            other = got[partner[sub, face]].astype(jnp.float32)
            if trade == 1:
                other = other * inner(axis)
            own = traces[sub, face].astype(jnp.float32)
            jumps[trade, sub] = (own - other).astype(jnp.bfloat16)


def flat_face(jumps, index):
    _, subs, rhs, size = jumps.shape
    return jumps[index].reshape(subs * rhs, size)


def pair_sum(jumps, first):
    up = flat_face(jumps, first).astype(jnp.float32)
    return (up + flat_face(jumps, first + 1).astype(jnp.float32)).astype(jnp.bfloat16)


def z_kernel(
    xa, traces, self_block, opposite_block, cross_block, corner_map,
    map_out, spread, base_z, cross_z, jumps,
):
    del xa
    subs, _, rhs, size = traces.shape
    rows = subs * rhs
    for sub in range(subs):
        up = traces[sub, 4].astype(jnp.float32)
        down = traces[sub, 5].astype(jnp.float32)
        if sub + 1 < subs:
            up = up - traces[sub + 1, 5].astype(jnp.float32)
        if sub > 0:
            down = down - traces[sub - 1, 4].astype(jnp.float32)
        jumps[0, sub] = up.astype(jnp.bfloat16)
        jumps[1, sub] = down.astype(jnp.bfloat16)
    width = CORNERS * COMPS
    row = lax.broadcasted_iota(jnp.int32, (width, LANES), 0)
    col = lax.broadcasted_iota(jnp.int32, (width, LANES), 1)
    place = (col % CORNERS) * COMPS + col // CORNERS
    order = ((row == place) & (col < width)).astype(jnp.float32).astype(jnp.bfloat16)
    for face in range(6):
        moved = lax.dot_general(
            corner_map[face], order, (((0,), (0,)), ((), ())), preferred_element_type=jnp.float32
        )
        map_out[face] = moved.astype(jnp.bfloat16)
    source = lax.broadcasted_iota(jnp.int32, (rows, subs * LANES), 0)
    target = lax.broadcasted_iota(jnp.int32, (rows, subs * LANES), 1)
    lane = (source // rhs) * LANES + (source % rhs) * COMPS
    for comp in range(COMPS):
        spread[comp] = (target == lane + comp).astype(jnp.float32).astype(jnp.bfloat16)
    flat = jumps[...].reshape(2 * rows, size)
    with_self = product(flat, self_block[...])
    with_opp = product(flat, opposite_block[...])
    base_z[0] = with_self[:rows] + with_opp[rows:]
    base_z[1] = with_self[rows:] + with_opp[:rows]
    cross_z[...] = product(pair_sum(jumps, 0), cross_block[...])


def y_kernel(
    partner, traces, ryb, rya, rxb, self_block, opposite_block, cross_block, cross_z, owners,
    base_y, cross_y, base_x, onehot, jumps,
):
    del rxb
    numbers = lax.broadcasted_iota(jnp.int32, (onehot.shape[0], CORNERS), 0)
    parts = [
        (numbers == owners[sub : sub + 1, :]).astype(jnp.float32) for sub in range(owners.shape[0])
    ]
    onehot[...] = jnp.concatenate(parts * 2, axis=1).astype(jnp.bfloat16)
    subs, _, rhs, size = traces.shape
    rows = subs * rhs
    trade_jumps(jumps, traces, partner, "sy", y_faces(), (rya, ryb))
    from_y = product(pair_sum(jumps, 0), cross_block[...])
    cross_y[...] = from_y
    base_x[...] = from_y + cross_z[...]
    flat = jumps[...].reshape(2 * rows, size)
    with_self = product(flat, self_block[...])
    with_opp = product(flat, opposite_block[...])
    base_y[0] = with_self[:rows] + with_opp[rows:] + cross_z[...]
    base_y[1] = with_self[rows:] + with_opp[:rows] + cross_z[...]


def high_low(value):
    high = value.astype(jnp.bfloat16).astype(jnp.float32)
    return high, value - high


def coarse_rows(partials, spread, onehot):
    subs = onehot.shape[1] // (2 * CORNERS)
    entries = jnp.zeros((2 * CORNERS, subs * LANES), jnp.float32)
    for comp in range(COMPS):
        part = partials[comp * CORNERS : (comp + 1) * CORNERS]
        stacked = jnp.concatenate(high_low(part), axis=0).astype(jnp.bfloat16)
        entries += product(stacked, spread[comp])
    entries = entries[:CORNERS] + entries[CORNERS:]
    by_sub = [entries[:, sub * LANES : (sub + 1) * LANES] for sub in range(subs)]
    both = jnp.concatenate(high_low(jnp.concatenate(by_sub, axis=0)), axis=0)
    return product(onehot[...], both.astype(jnp.bfloat16))


def local_kernel(
    partner, viscosity, traces, rxa, rxb, self_block, opposite_block, cross_block,
    base_x, base_y, base_z, cross_y, spread, onehot, corner_map,
    xa, xb, ya, yb, local_z, to_xa, to_xb, to_ya, to_yb, kept, jumps, dense,
):
    subs, _, rhs, size = traces.shape
    rows = subs * rhs
    trade_jumps(jumps, traces, partner, "sx", x_faces(), (rxa, rxb))
    flat = jumps[...].reshape(2 * rows, size)
    with_self = product(flat, self_block[...])
    with_opp = product(flat, opposite_block[...])
    from_x = product(pair_sum(jumps, 0), cross_block[...])
    from_xy = from_x + cross_y[...]
    totals = (
        with_self[:rows] + with_opp[rows:] + base_x[...],
        with_self[rows:] + with_opp[:rows] + base_x[...],
        base_y[0] + from_x,
        base_y[1] + from_x,
        base_z[0] + from_xy,
        base_z[1] + from_xy,
    )
    faces = (*x_faces(), *y_faces(), 4, 5)
    outs = (xa, xb, ya, yb, local_z.at[0], local_z.at[1])
    sent = (to_xa, to_xb, to_ya, to_yb)
    partials = jnp.zeros((rows, LANES), jnp.float32)
    for index, (face, total, out) in enumerate(zip(faces, totals, outs)):
        for sub in range(subs):
            here = slice(sub * rhs, (sub + 1) * rhs)
            value = (viscosity[:, sub : sub + 1] * total[here]).astype(jnp.bfloat16)
            out[sub] = value
            if index < 4:
                sent[index][partner[sub, face]] = value
        partials += product(out[...].reshape(rows, size), corner_map[face])
    partials = partials.T
    dense[...] = coarse_rows(partials, spread, onehot)
    me = lax.axis_index("sy")

    def block(bits):
        start = pl.multiple_of((me ^ bits) * COARSE_DEV, COARSE_DEV)
        return dense[pl.ds(start, COARSE_DEV), :]

    half, per_row = kept.shape[0], size // LANES
    for index in range((to_ya.shape[0] - subs) * per_row):
        lanes = slice(index % per_row * LANES, (index % per_row + 1) * LANES)
        both = jnp.zeros((2 * COARSE_DEV, LANES), jnp.float32)
        if index < half:
            kept[index] = block(2 * index)
            both = jnp.concatenate(high_low(block(2 * index + 1)), axis=0)
        to_ya[subs + index // per_row, :, lanes] = both.astype(jnp.bfloat16)


def first_add_kernel(subs, kept, got, *refs):
    keep, give = refs[2:4]
    half, per_row = kept.shape[0], got.shape[2] // LANES
    for index in range(half):
        lanes = slice(index % per_row * LANES, (index % per_row + 1) * LANES)
        both = got[subs + index // per_row, :, lanes].astype(jnp.float32)
        total = kept[index] + both[:COARSE_DEV] + both[COARSE_DEV:]
        out = keep if index % 2 == 0 else give
        out[index // 2] = total


def next_add_kernel(after, rxb, kept, got, keep, give):
    del after, rxb
    for index in range(kept.shape[0]):
        out = keep if index % 2 == 0 else give
        out[index // 2] = kept[index] + got[index]


def last_add_kernel(after, kept, got, coarse, total, sem):
    del after
    total[...] = (kept[0] + got[0])[:, : total.shape[1]]
    copy = pltpu.make_async_copy(total, coarse, sem)
    copy.start()
    copy.wait()


def apply_z_kernel(kept, local_z, applied, held, sems):
    del kept
    subs = local_z.shape[1]
    copies = []
    for sub in range(subs):
        up = local_z[0, sub].astype(jnp.float32)
        down = local_z[1, sub].astype(jnp.float32)
        if sub + 1 < subs:
            up = up - local_z[1, sub + 1].astype(jnp.float32)
        if sub > 0:
            down = down - local_z[0, sub - 1].astype(jnp.float32)
        held[sub, 0] = up
        held[sub, 1] = down
        copies.append(
            pltpu.make_async_copy(held.at[sub], applied.at[sub, pl.ds(4, 2)], sems.at[sub])
        )
        copies[-1].start()
    for copy in copies:
        copy.wait()


def apply_kernel(applied_in, rxb, rxa, ryb, rya, ya, yb, xa, xb, applied, held, sems):
    del applied_in
    copies = []
    trades = zip((*y_faces(), *x_faces()), (ya, yb, xa, xb), (rya, ryb, rxa, rxb))
    for index, (face, local, got) in enumerate(trades):
        for sub in range(held.shape[1]):
            other = got[sub].astype(jnp.float32)
            if index == 1:
                other = other * inner("sy")
            if index == 3:
                other = other * inner("sx")
            held[index, sub] = local[sub].astype(jnp.float32) - other
            copies.append(
                pltpu.make_async_copy(
                    held.at[index, sub], applied.at[sub, face], sems.at[index, sub]
                )
            )
            copies[-1].start()
    for copy in copies:
        copy.wait()


def body(
    traces, viscosity, partner, corner_owner, self_block, opposite_block, cross_block, corner_map
):
    values = traces[0, 0]
    slots, visc, owners = partner[0, 0], viscosity[0], corner_owner[0, 0]
    subs, _, rhs, size = values.shape
    count = lax.axis_size("sy")
    rows = subs * rhs
    face_shape = (subs, rhs, size)
    bf16, f32 = jnp.bfloat16, jnp.float32

    xb, yb, xa, ya = pl.pallas_call(
        send_kernel,
        in_specs=[HBM],
        out_specs=[VMEM] * 4,
        out_shape=[in_vmem(face_shape, bf16)] * 4,
        scratch_shapes=[pltpu.SemaphoreType.DMA((4,))],
        compiler_params=params(8),
        cost_estimate=LONG,
    )(in_hbm(values))
    rxb = second_swap(xb, "sx")
    ryb = second_swap(yb, "sy")
    rxa = first_swap(xa, "sx")
    rya = first_swap(ya, "sy")
    map_v, spread, base_z, cross_z = pl.pallas_call(
        z_kernel,
        in_specs=[VMEM] * 6,
        out_specs=[VMEM] * 4,
        out_shape=[in_vmem((6, size, LANES), bf16), in_vmem((COMPS, rows, subs * LANES), bf16)]
        + [in_vmem((2, rows, size), f32)]
        + [in_vmem((rows, size), f32)],
        scratch_shapes=[pltpu.VMEM((2,) + face_shape, bf16)],
        compiler_params=params(12),
        cost_estimate=LONG,
    )(
        xa, values, self_block, opposite_block, cross_block,
        jnp.transpose(corner_map, (1, 0, 2)),
    )
    base_y, cross_y, base_x, onehot = pl.pallas_call(
        y_kernel,
        in_specs=[SMEM] + [VMEM] * 9,
        out_specs=[VMEM] * 4,
        out_shape=[in_vmem((2, rows, size), f32)] + [in_vmem((rows, size), f32)] * 2
        + [in_vmem((COARSE_DEV * count, 2 * subs * CORNERS), bf16)],
        scratch_shapes=[pltpu.VMEM((2,) + face_shape, bf16)],
        compiler_params=params(12),
    )(slots, values, ryb, rya, rxb, self_block, opposite_block, cross_block, cross_z, owners)
    half, per_row = count // 2, size // LANES
    long_shape = (subs + -(-half // per_row), rhs, size)

    def blocks(number):
        return in_vmem((number, COARSE_DEV, LANES), f32)

    xa, xb, ya, yb, local_z, to_xa, to_xb, to_ya, to_yb, kept = pl.pallas_call(
        local_kernel,
        in_specs=[SMEM] + [VMEM] * 14,
        out_specs=[VMEM] * 10,
        out_shape=[in_vmem(face_shape, bf16)] * 4
        + [in_vmem((2,) + face_shape, bf16)]
        + [in_vmem(face_shape, bf16)] * 2
        + [in_vmem(long_shape, bf16), in_vmem(face_shape, bf16), blocks(half)],
        scratch_shapes=[
            pltpu.VMEM((2,) + face_shape, bf16),
            pltpu.VMEM((COARSE_DEV * count, LANES), f32),
        ],
        compiler_params=params(16),
    )(
        slots, visc, values, rxa, rxb, self_block, opposite_block, cross_block,
        base_x, base_y, base_z, cross_y, spread, onehot, map_v,
    )
    rya = first_swap(to_ya, "sy")
    rxb = second_swap(to_xb, "sx")
    out_shape = jax.ShapeDtypeStruct(values.shape, f32)
    half //= 2
    bits = 2
    kept, give, to_xa, to_yb = pl.pallas_call(
        lambda *refs: first_add_kernel(subs, *refs),
        in_specs=[VMEM] * 4,
        out_specs=[VMEM] * 4,
        out_shape=[blocks(half)] * 2 + [in_vmem(face_shape, bf16)] * 2,
        input_output_aliases={2: 2, 3: 3},
        compiler_params=params(4),
    )(kept, rya, to_xa, to_yb)
    got = cross_swap(give, "sy", bits)
    applied = pl.pallas_call(
        apply_z_kernel,
        in_specs=[VMEM] * 2,
        out_specs=HBM,
        out_shape=out_shape,
        scratch_shapes=[
            pltpu.VMEM((subs, 2, rhs, size), f32),
            pltpu.SemaphoreType.DMA((subs,)),
        ],
        compiler_params=params(8),
        cost_estimate=LONG,
    )(kept, local_z)
    ryb = second_swap(to_yb, "sy")
    rxa = first_swap(to_xa, "sx")
    while half > 1:
        half //= 2
        bits *= 2
        kept, give = pl.pallas_call(
            next_add_kernel,
            in_specs=[HBM] + [VMEM] * 3,
            out_specs=[VMEM] * 2,
            out_shape=[blocks(half)] * 2,
            compiler_params=params(4),
            cost_estimate=LONG,
        )(in_hbm(applied), rxb, kept, got)
        got = cross_swap(give, "sy", bits)
    applied = pl.pallas_call(
        apply_kernel,
        in_specs=[HBM] + [VMEM] * 8,
        out_specs=HBM,
        out_shape=out_shape,
        input_output_aliases={0: 0},
        scratch_shapes=[pltpu.VMEM((4,) + face_shape, f32), pltpu.SemaphoreType.DMA((4, subs))],
        compiler_params=params(12),
        cost_estimate=LONG,
    )(applied, rxb, rxa, ryb, rya, ya, yb, xa, xb)
    coarse = pl.pallas_call(
        last_add_kernel,
        in_specs=[HBM] + [VMEM] * 2,
        out_specs=HBM,
        out_shape=jax.ShapeDtypeStruct((COARSE_DEV, rhs * COMPS), f32),
        scratch_shapes=[pltpu.VMEM((COARSE_DEV, rhs * COMPS), f32), pltpu.SemaphoreType.DMA],
        compiler_params=params(4),
    )(in_hbm(applied), kept, got)
    return applied[None, None], coarse.T


def solution(mesh):
    return jax.shard_map(
        body,
        mesh=mesh,
        in_specs=(
            P("sx", "sy", None, None, None, None),
            P("sx", "sy", None),
            P("sx", "sy", None, None),
            P("sx", "sy", None, None),
            P(),
            P(),
            P(),
            P(),
        ),
        out_specs=(P("sx", "sy", None, None, None, None), P(None, ("sx", "sy"))),
        check_vma=False,
    )
```

```python
import jax
import jax.numpy as jnp
from jax import lax
from jax.experimental import pallas as pl
from jax.experimental.pallas import tpu as pltpu
from jax.sharding import PartitionSpec as P

CORNERS = 8
COMPS = 3
COARSE_DEV = 8
LANES = 128

VMEM = pl.BlockSpec(memory_space=pltpu.VMEM)
SMEM = pl.BlockSpec(memory_space=pltpu.SMEM)
HBM = pl.BlockSpec(memory_space=pltpu.HBM)
ANY = pl.BlockSpec(memory_space=pl.ANY)


def in_vmem(shape, dtype):
    return pltpu.VMEM(shape, dtype)


def in_hbm(value):
    return pltpu.with_memory_space_constraint(value, pltpu.HBM)


def params(mib):
    return pltpu.CompilerParams(vmem_limit_bytes=mib * 1024 * 1024)


LONG = pl.CostEstimate(flops=20 * 10**9, bytes_accessed=0, transcendentals=0)


def odd(axis):
    return lax.rem(lax.axis_index(axis), 2)


def first_swap(value, axis):
    return lax.ppermute(value, axis, [(i, i ^ 1) for i in range(lax.axis_size(axis))])


def second_swap(value, axis):
    rows, cols = lax.axis_size("sx"), lax.axis_size("sy")
    pairs = []
    for i in range(rows):
        for j in range(cols):
            if axis == "sx":
                k = i - 1 if i % 2 == 0 else i + 1
                target = (k, j) if 0 <= k < rows else (i, j ^ 1)
            else:
                k = j - 1 if j % 2 == 0 else j + 1
                target = (i, k) if 0 <= k < cols else (i ^ 2, j)
            pairs.append((i * cols + j, target[0] * cols + target[1]))
    return lax.ppermute(value, ("sx", "sy"), pairs)


def cross_swap(value, axis, bits):
    return lax.ppermute(value, axis, [(i, i ^ bits) for i in range(lax.axis_size(axis))])


def inner(axis):
    me = lax.axis_index(axis)
    return ((me > 0) & (me < lax.axis_size(axis) - 1)).astype(jnp.float32)


def x_faces():
    return odd("sx"), 1 - odd("sx")


def y_faces():
    return 2 + odd("sy"), 3 - odd("sy")


def send_kernel(traces, xb, yb, xa, ya, sems):
    faces = (*x_faces(), *y_faces())
    copies = [
        pltpu.make_async_copy(traces.at[:, face], out, sems.at[index])
        for index, (face, out) in enumerate(zip(faces, (xa, xb, ya, yb)))
    ]
    for copy in copies:
        copy.start()
    for copy in copies:
        copy.wait()


def product(left, right):
    return jnp.dot(left, right, preferred_element_type=jnp.float32)


def trade_jumps(jumps, traces, partner, axis, faces, received):
    for trade, (face, got) in enumerate(zip(faces, received)):
        for sub in range(traces.shape[0]):
            other = got[partner[sub, face]].astype(jnp.float32)
            if trade == 1:
                other = other * inner(axis)
            own = traces[sub, face].astype(jnp.float32)
            jumps[trade, sub] = (own - other).astype(jnp.bfloat16)


def flat_face(jumps, index):
    _, subs, rhs, size = jumps.shape
    return jumps[index].reshape(subs * rhs, size)


def pair_sum(jumps, first):
    up = flat_face(jumps, first).astype(jnp.float32)
    return (up + flat_face(jumps, first + 1).astype(jnp.float32)).astype(jnp.bfloat16)


def z_kernel(
    xa, traces, self_block, opposite_block, cross_block, corner_map,
    map_out, spread, base_z, cross_z, jumps,
):
    del xa
    subs, _, rhs, size = traces.shape
    rows = subs * rhs
    for sub in range(subs):
        up = traces[sub, 4].astype(jnp.float32)
        down = traces[sub, 5].astype(jnp.float32)
        if sub + 1 < subs:
            up = up - traces[sub + 1, 5].astype(jnp.float32)
        if sub > 0:
            down = down - traces[sub - 1, 4].astype(jnp.float32)
        jumps[0, sub] = up.astype(jnp.bfloat16)
        jumps[1, sub] = down.astype(jnp.bfloat16)
    width = CORNERS * COMPS
    row = lax.broadcasted_iota(jnp.int32, (width, LANES), 0)
    col = lax.broadcasted_iota(jnp.int32, (width, LANES), 1)
    place = (col % CORNERS) * COMPS + col // CORNERS
    order = ((row == place) & (col < width)).astype(jnp.float32).astype(jnp.bfloat16)
    for face in range(6):
        moved = lax.dot_general(
            corner_map[face], order, (((0,), (0,)), ((), ())), preferred_element_type=jnp.float32
        )
        map_out[face] = moved.astype(jnp.bfloat16)
    source = lax.broadcasted_iota(jnp.int32, (rows, subs * LANES), 0)
    target = lax.broadcasted_iota(jnp.int32, (rows, subs * LANES), 1)
    lane = (source // rhs) * LANES + (source % rhs) * COMPS
    for comp in range(COMPS):
        spread[comp] = (target == lane + comp).astype(jnp.float32).astype(jnp.bfloat16)
    flat = jumps[...].reshape(2 * rows, size)
    with_self = product(flat, self_block[...])
    with_opp = product(flat, opposite_block[...])
    base_z[0] = with_self[:rows] + with_opp[rows:]
    base_z[1] = with_self[rows:] + with_opp[:rows]
    cross_z[...] = product(pair_sum(jumps, 0), cross_block[...])


def y_kernel(
    partner, traces, rxb, ryb, rya, self_block, opposite_block, cross_block, cross_z, owners,
    base_y, cross_y, base_x, jump_xb, onehot, jumps,
):
    numbers = lax.broadcasted_iota(jnp.int32, (onehot.shape[0], CORNERS), 0)
    parts = [
        (numbers == owners[sub : sub + 1, :]).astype(jnp.float32) for sub in range(owners.shape[0])
    ]
    onehot[...] = jnp.concatenate(parts * 2, axis=1).astype(jnp.bfloat16)
    subs, _, rhs, size = traces.shape
    rows = subs * rhs
    trade_jumps(jumps, traces, partner, "sy", y_faces(), (rya, ryb))
    from_y = product(pair_sum(jumps, 0), cross_block[...])
    cross_y[...] = from_y
    face = x_faces()[1]
    for sub in range(subs):
        other = rxb[partner[sub, face]].astype(jnp.float32) * inner("sx")
        own = traces[sub, face].astype(jnp.float32)
        jumps[2, sub] = (own - other).astype(jnp.bfloat16)
    jump_xb[...] = jumps[2]
    flat = jumps[...].reshape(3 * rows, size)
    with_self = product(flat, self_block[...])
    with_opp = product(flat, opposite_block[...])
    base_y[0] = with_self[:rows] + with_opp[rows : 2 * rows] + cross_z[...]
    base_y[1] = with_self[rows : 2 * rows] + with_opp[:rows] + cross_z[...]
    base_x[0] = from_y + cross_z[...] + with_opp[2 * rows :]
    base_x[1] = from_y + cross_z[...] + with_self[2 * rows :]


def high_low(value):
    high = value.astype(jnp.bfloat16).astype(jnp.float32)
    return high, value - high


def coarse_rows(partials, spread, onehot):
    subs = onehot.shape[1] // (2 * CORNERS)
    entries = jnp.zeros((2 * CORNERS, subs * LANES), jnp.float32)
    for comp in range(COMPS):
        part = partials[comp * CORNERS : (comp + 1) * CORNERS]
        stacked = jnp.concatenate(high_low(part), axis=0).astype(jnp.bfloat16)
        entries += product(stacked, spread[comp])
    entries = entries[:CORNERS] + entries[CORNERS:]
    by_sub = [entries[:, sub * LANES : (sub + 1) * LANES] for sub in range(subs)]
    both = jnp.concatenate(high_low(jnp.concatenate(by_sub, axis=0)), axis=0)
    return product(onehot[...], both.astype(jnp.bfloat16))


def local_kernel(
    partner, viscosity, traces, rxa, jump_xb, self_block, opposite_block, cross_block,
    base_x, base_y, base_z, cross_y, spread, onehot, corner_map,
    xa, xb, ya, yb, local_z, to_xa, to_xb, to_ya, to_yb, kept, jumps, dense,
):
    subs, _, rhs, size = traces.shape
    rows = subs * rhs
    face = x_faces()[0]
    for sub in range(subs):
        other = rxa[partner[sub, face]].astype(jnp.float32)
        own = traces[sub, face].astype(jnp.float32)
        jumps[0, sub] = (own - other).astype(jnp.bfloat16)
    jumps[1] = jump_xb[...]
    flat = flat_face(jumps, 0)
    with_self = product(flat, self_block[...])
    with_opp = product(flat, opposite_block[...])
    from_x = product(pair_sum(jumps, 0), cross_block[...])
    from_xy = from_x + cross_y[...]
    totals = (
        with_self + base_x[0],
        with_opp + base_x[1],
        base_y[0] + from_x,
        base_y[1] + from_x,
        base_z[0] + from_xy,
        base_z[1] + from_xy,
    )
    faces = (*x_faces(), *y_faces(), 4, 5)
    outs = (xa, xb, ya, yb, local_z.at[0], local_z.at[1])
    sent = (to_xa, to_xb, to_ya, to_yb)
    partials = jnp.zeros((rows, LANES), jnp.float32)
    for index, (face, total, out) in enumerate(zip(faces, totals, outs)):
        for sub in range(subs):
            here = slice(sub * rhs, (sub + 1) * rhs)
            value = (viscosity[sub] * total[here]).astype(jnp.bfloat16)
            out[sub] = value
            if index < 4:
                sent[index][partner[sub, face]] = value
        partials += product(out[...].reshape(rows, size), corner_map[face])
    partials = partials.T
    dense[...] = coarse_rows(partials, spread, onehot)
    me = lax.axis_index("sy")

    def block(bits):
        start = pl.multiple_of((me ^ bits) * COARSE_DEV, COARSE_DEV)
        return dense[pl.ds(start, COARSE_DEV), :]

    half, per_row = kept.shape[0], size // LANES
    for index in range((to_ya.shape[0] - subs) * per_row):
        lanes = slice(index % per_row * LANES, (index % per_row + 1) * LANES)
        both = jnp.zeros((2 * COARSE_DEV, LANES), jnp.float32)
        if index < half:
            kept[index] = block(2 * index)
            both = jnp.concatenate(high_low(block(2 * index + 1)), axis=0)
        to_ya[subs + index // per_row, :, lanes] = both.astype(jnp.bfloat16)


def first_add_kernel(subs, kept, got, *refs):
    keep, give = refs[2:4]
    half, per_row = kept.shape[0], got.shape[2] // LANES
    for index in range(half):
        lanes = slice(index % per_row * LANES, (index % per_row + 1) * LANES)
        both = got[subs + index // per_row, :, lanes].astype(jnp.float32)
        total = kept[index] + both[:COARSE_DEV] + both[COARSE_DEV:]
        out = keep if index % 2 == 0 else give
        out[index // 2] = total


def next_add_kernel(after, rxb, kept, got, keep, give):
    del after, rxb
    for index in range(kept.shape[0]):
        out = keep if index % 2 == 0 else give
        out[index // 2] = kept[index] + got[index]


def last_add_kernel(after, kept, got, coarse, total, sem):
    del after
    total[...] = (kept[0] + got[0])[:, : total.shape[1]]
    copy = pltpu.make_async_copy(total, coarse, sem)
    copy.start()
    copy.wait()


def apply_z_kernel(kept, local_z, applied, held, sems):
    del kept
    subs = local_z.shape[1]
    copies = []
    for sub in range(subs):
        up = local_z[0, sub].astype(jnp.float32)
        down = local_z[1, sub].astype(jnp.float32)
        if sub + 1 < subs:
            up = up - local_z[1, sub + 1].astype(jnp.float32)
        if sub > 0:
            down = down - local_z[0, sub - 1].astype(jnp.float32)
        held[sub, 0] = up
        held[sub, 1] = down
        copies.append(
            pltpu.make_async_copy(held.at[sub], applied.at[sub, pl.ds(4, 2)], sems.at[sub])
        )
        copies[-1].start()
    for copy in copies:
        copy.wait()


def apply_kernel(applied_in, rxb, rxa, ryb, rya, ya, yb, xa, xb, applied, held, sems):
    del applied_in
    copies = []
    trades = zip((*y_faces(), *x_faces()), (ya, yb, xa, xb), (rya, ryb, rxa, rxb))
    for index, (face, local, got) in enumerate(trades):
        for sub in range(held.shape[1]):
            other = got[sub].astype(jnp.float32)
            if index == 1:
                other = other * inner("sy")
            if index == 3:
                other = other * inner("sx")
            held[index, sub] = local[sub].astype(jnp.float32) - other
            copies.append(
                pltpu.make_async_copy(
                    held.at[index, sub], applied.at[sub, face], sems.at[index, sub]
                )
            )
            copies[-1].start()
    for copy in copies:
        copy.wait()


def body(
    traces, viscosity, partner, corner_owner, self_block, opposite_block, cross_block, corner_map
):
    values = traces[0, 0]
    slots, visc, owners = partner[0, 0], viscosity[0, 0], corner_owner[0, 0]
    subs, _, rhs, size = values.shape
    count = lax.axis_size("sy")
    rows = subs * rhs
    face_shape = (subs, rhs, size)
    bf16, f32 = jnp.bfloat16, jnp.float32

    xb, yb, xa, ya = pl.pallas_call(
        send_kernel,
        in_specs=[HBM],
        out_specs=[VMEM] * 4,
        out_shape=[in_vmem(face_shape, bf16)] * 4,
        scratch_shapes=[pltpu.SemaphoreType.DMA((4,))],
        compiler_params=params(8),
        cost_estimate=LONG,
    )(in_hbm(values))
    rxb = second_swap(xb, "sx")
    ryb = second_swap(yb, "sy")
    rxa = first_swap(xa, "sx")
    rya = first_swap(ya, "sy")
    map_v, spread, base_z, cross_z = pl.pallas_call(
        z_kernel,
        in_specs=[VMEM] * 6,
        out_specs=[VMEM] * 4,
        out_shape=[in_vmem((6, size, LANES), bf16), in_vmem((COMPS, rows, subs * LANES), bf16)]
        + [in_vmem((2, rows, size), f32)]
        + [in_vmem((rows, size), f32)],
        scratch_shapes=[pltpu.VMEM((2,) + face_shape, bf16)],
        compiler_params=params(12),
        cost_estimate=LONG,
    )(
        xa, values, self_block, opposite_block, cross_block,
        jnp.transpose(corner_map, (1, 0, 2)),
    )
    base_y, cross_y, base_x, jump_xb, onehot = pl.pallas_call(
        y_kernel,
        in_specs=[SMEM] + [VMEM] * 9,
        out_specs=[VMEM] * 5,
        out_shape=[in_vmem((2, rows, size), f32), in_vmem((rows, size), f32)]
        + [in_vmem((2, rows, size), f32), in_vmem(face_shape, bf16)]
        + [in_vmem((COARSE_DEV * count, 2 * subs * CORNERS), bf16)],
        scratch_shapes=[pltpu.VMEM((3,) + face_shape, bf16)],
        compiler_params=params(12),
    )(slots, values, rxb, ryb, rya, self_block, opposite_block, cross_block, cross_z, owners)
    half, per_row = count // 2, size // LANES
    long_shape = (subs + -(-half // per_row), rhs, size)

    def blocks(number):
        return in_vmem((number, COARSE_DEV, LANES), f32)

    xa, xb, ya, yb, local_z, to_xa, to_xb, to_ya, to_yb, kept = pl.pallas_call(
        local_kernel,
        in_specs=[SMEM] * 2 + [VMEM] * 13,
        out_specs=[VMEM] * 10,
        out_shape=[in_vmem(face_shape, bf16)] * 4
        + [in_vmem((2,) + face_shape, bf16)]
        + [in_vmem(face_shape, bf16)] * 2
        + [in_vmem(long_shape, bf16), in_vmem(face_shape, bf16), blocks(half)],
        scratch_shapes=[
            pltpu.VMEM((2,) + face_shape, bf16),
            pltpu.VMEM((COARSE_DEV * count, LANES), f32),
        ],
        compiler_params=params(16),
    )(
        slots, visc, values, rxa, jump_xb, self_block, opposite_block, cross_block,
        base_x, base_y, base_z, cross_y, spread, onehot, map_v,
    )
    rya = first_swap(to_ya, "sy")
    rxb = second_swap(to_xb, "sx")
    out_shape = jax.ShapeDtypeStruct(values.shape, f32)
    half //= 2
    bits = 2
    kept, give, to_xa, to_yb = pl.pallas_call(
        lambda *refs: first_add_kernel(subs, *refs),
        in_specs=[VMEM] * 4,
        out_specs=[VMEM] * 4,
        out_shape=[blocks(half)] * 2 + [in_vmem(face_shape, bf16)] * 2,
        input_output_aliases={2: 2, 3: 3},
        compiler_params=params(4),
    )(kept, rya, to_xa, to_yb)
    got = cross_swap(give, "sy", bits)
    applied = pl.pallas_call(
        apply_z_kernel,
        in_specs=[VMEM] * 2,
        out_specs=HBM,
        out_shape=out_shape,
        scratch_shapes=[
            pltpu.VMEM((subs, 2, rhs, size), f32),
            pltpu.SemaphoreType.DMA((subs,)),
        ],
        compiler_params=params(8),
        cost_estimate=LONG,
    )(kept, local_z)
    ryb = second_swap(to_yb, "sy")
    rxa = first_swap(to_xa, "sx")
    while half > 1:
        half //= 2
        bits *= 2
        kept, give = pl.pallas_call(
            next_add_kernel,
            in_specs=[HBM] + [VMEM] * 3,
            out_specs=[VMEM] * 2,
            out_shape=[blocks(half)] * 2,
            compiler_params=params(4),
            cost_estimate=LONG,
        )(in_hbm(applied), rxb, kept, got)
        got = cross_swap(give, "sy", bits)
    applied = pl.pallas_call(
        apply_kernel,
        in_specs=[HBM] + [VMEM] * 8,
        out_specs=HBM,
        out_shape=out_shape,
        input_output_aliases={0: 0},
        scratch_shapes=[pltpu.VMEM((4,) + face_shape, f32), pltpu.SemaphoreType.DMA((4, subs))],
        compiler_params=params(12),
        cost_estimate=LONG,
    )(applied, rxb, rxa, ryb, rya, ya, yb, xa, xb)
    coarse = pl.pallas_call(
        last_add_kernel,
        in_specs=[HBM] + [VMEM] * 2,
        out_specs=HBM,
        out_shape=jax.ShapeDtypeStruct((COARSE_DEV, rhs * COMPS), f32),
        scratch_shapes=[pltpu.VMEM((COARSE_DEV, rhs * COMPS), f32), pltpu.SemaphoreType.DMA],
        compiler_params=params(4),
    )(in_hbm(applied), kept, got)
    return applied[None, None], coarse.T


def solution(mesh):
    return jax.shard_map(
        body,
        mesh=mesh,
        in_specs=(
            P("sx", "sy", None, None, None, None),
            P("sx", "sy", None),
            P("sx", "sy", None, None),
            P("sx", "sy", None, None),
            P(),
            P(),
            P(),
            P(),
        ),
        out_specs=(P("sx", "sy", None, None, None, None), P(None, ("sx", "sy"))),
        check_vma=False,
    )
```

```python
import jax
import jax.numpy as jnp
from jax import lax
from jax.experimental import pallas as pl
from jax.experimental.pallas import tpu as pltpu
from jax.sharding import PartitionSpec as P

CORNERS = 8
COMPS = 3
COARSE_DEV = 8
LANES = 128

VMEM = pl.BlockSpec(memory_space=pltpu.VMEM)
SMEM = pl.BlockSpec(memory_space=pltpu.SMEM)
HBM = pl.BlockSpec(memory_space=pltpu.HBM)
ANY = pl.BlockSpec(memory_space=pl.ANY)


def in_vmem(shape, dtype):
    return pltpu.VMEM(shape, dtype)


def in_hbm(value):
    return pltpu.with_memory_space_constraint(value, pltpu.HBM)


def params(mib):
    return pltpu.CompilerParams(vmem_limit_bytes=mib * 1024 * 1024)


LONG = pl.CostEstimate(flops=20 * 10**9, bytes_accessed=0, transcendentals=0)


def odd(axis):
    return lax.rem(lax.axis_index(axis), 2)


def first_swap(value, axis):
    return lax.ppermute(value, axis, [(i, i ^ 1) for i in range(lax.axis_size(axis))])


def second_swap(value, axis):
    rows, cols = lax.axis_size("sx"), lax.axis_size("sy")
    pairs = []
    for i in range(rows):
        for j in range(cols):
            if axis == "sx":
                k = i - 1 if i % 2 == 0 else i + 1
                target = (k, j) if 0 <= k < rows else (i, j ^ 1)
            else:
                k = j - 1 if j % 2 == 0 else j + 1
                target = (i, k) if 0 <= k < cols else (i ^ 2, j)
            pairs.append((i * cols + j, target[0] * cols + target[1]))
    return lax.ppermute(value, ("sx", "sy"), pairs)


def cross_swap(value, axis, bits):
    return lax.ppermute(value, axis, [(i, i ^ bits) for i in range(lax.axis_size(axis))])


def inner(axis):
    me = lax.axis_index(axis)
    return ((me > 0) & (me < lax.axis_size(axis) - 1)).astype(jnp.float32)


def x_faces():
    return odd("sx"), 1 - odd("sx")


def y_faces():
    return 2 + odd("sy"), 3 - odd("sy")


def send_kernel(traces, xb, yb, xa, ya, sems):
    faces = (*x_faces(), *y_faces())
    copies = [
        pltpu.make_async_copy(traces.at[:, face], out, sems.at[index])
        for index, (face, out) in enumerate(zip(faces, (xa, xb, ya, yb)))
    ]
    for copy in copies:
        copy.start()
    for copy in copies:
        copy.wait()


def product(left, right):
    return jnp.dot(left, right, preferred_element_type=jnp.float32)


def trade_jumps(jumps, traces, partner, axis, faces, received):
    for trade, (face, got) in enumerate(zip(faces, received)):
        for sub in range(traces.shape[0]):
            other = got[partner[sub, face]].astype(jnp.float32)
            if trade == 1:
                other = other * inner(axis)
            own = traces[sub, face].astype(jnp.float32)
            jumps[trade, sub] = (own - other).astype(jnp.bfloat16)


def flat_face(jumps, index):
    _, subs, rhs, size = jumps.shape
    return jumps[index].reshape(subs * rhs, size)


def pair_sum(jumps, first):
    up = flat_face(jumps, first).astype(jnp.float32)
    return (up + flat_face(jumps, first + 1).astype(jnp.float32)).astype(jnp.bfloat16)


def z_kernel(
    xa, traces, self_block, opposite_block, cross_block, corner_map,
    map_out, spread, base_z, cross_z, jumps,
):
    del xa
    subs, _, rhs, size = traces.shape
    rows = subs * rhs
    for sub in range(subs):
        up = traces[sub, 4].astype(jnp.float32)
        down = traces[sub, 5].astype(jnp.float32)
        if sub + 1 < subs:
            up = up - traces[sub + 1, 5].astype(jnp.float32)
        if sub > 0:
            down = down - traces[sub - 1, 4].astype(jnp.float32)
        jumps[0, sub] = up.astype(jnp.bfloat16)
        jumps[1, sub] = down.astype(jnp.bfloat16)
    width = CORNERS * COMPS
    row = lax.broadcasted_iota(jnp.int32, (width, LANES), 0)
    col = lax.broadcasted_iota(jnp.int32, (width, LANES), 1)
    place = (col % CORNERS) * COMPS + col // CORNERS
    order = ((row == place) & (col < width)).astype(jnp.float32).astype(jnp.bfloat16)
    for face in range(6):
        moved = lax.dot_general(
            corner_map[face], order, (((0,), (0,)), ((), ())), preferred_element_type=jnp.float32
        )
        map_out[face] = moved.astype(jnp.bfloat16)
    source = lax.broadcasted_iota(jnp.int32, (rows, subs * LANES), 0)
    target = lax.broadcasted_iota(jnp.int32, (rows, subs * LANES), 1)
    lane = (source // rhs) * LANES + (source % rhs) * COMPS
    for comp in range(COMPS):
        spread[comp] = (target == lane + comp).astype(jnp.float32).astype(jnp.bfloat16)
    flat = jumps[...].reshape(2 * rows, size)
    with_self = product(flat, self_block[...])
    with_opp = product(flat, opposite_block[...])
    base_z[0] = with_self[:rows] + with_opp[rows:]
    base_z[1] = with_self[rows:] + with_opp[:rows]
    cross_z[...] = product(pair_sum(jumps, 0), cross_block[...])


def y_kernel(
    partner, traces, ryb, rya, rxb, self_block, opposite_block, cross_block, cross_z, owners,
    base_y, cross_y, base_x, onehot, jumps,
):
    del rxb
    numbers = lax.broadcasted_iota(jnp.int32, (onehot.shape[0], CORNERS), 0)
    parts = [
        (numbers == owners[sub : sub + 1, :]).astype(jnp.float32) for sub in range(owners.shape[0])
    ]
    onehot[...] = jnp.concatenate(parts * 2, axis=1).astype(jnp.bfloat16)
    subs, _, rhs, size = traces.shape
    rows = subs * rhs
    trade_jumps(jumps, traces, partner, "sy", y_faces(), (rya, ryb))
    from_y = product(pair_sum(jumps, 0), cross_block[...])
    cross_y[...] = from_y
    base_x[...] = from_y + cross_z[...]
    flat = jumps[...].reshape(2 * rows, size)
    with_self = product(flat, self_block[...])
    with_opp = product(flat, opposite_block[...])
    base_y[0] = with_self[:rows] + with_opp[rows:] + cross_z[...]
    base_y[1] = with_self[rows:] + with_opp[:rows] + cross_z[...]


def high_low(value):
    high = value.astype(jnp.bfloat16).astype(jnp.float32)
    return high, value - high


def coarse_rows(partials, spread, onehot):
    subs = onehot.shape[1] // (2 * CORNERS)
    entries = jnp.zeros((2 * CORNERS, subs * LANES), jnp.float32)
    for comp in range(COMPS):
        part = partials[comp * CORNERS : (comp + 1) * CORNERS]
        stacked = jnp.concatenate(high_low(part), axis=0).astype(jnp.bfloat16)
        entries += product(stacked, spread[comp])
    entries = entries[:CORNERS] + entries[CORNERS:]
    by_sub = [entries[:, sub * LANES : (sub + 1) * LANES] for sub in range(subs)]
    both = jnp.concatenate(high_low(jnp.concatenate(by_sub, axis=0)), axis=0)
    return product(onehot[...], both.astype(jnp.bfloat16))


def local_kernel(
    partner, viscosity, traces, rxa, rxb, self_block, opposite_block, cross_block,
    base_x, base_y, base_z, cross_y, spread, onehot, corner_map,
    xa, xb, ya, yb, local_z, to_xa, to_xb, to_ya, to_yb, kept, jumps, dense,
):
    subs, _, rhs, size = traces.shape
    rows = subs * rhs
    trade_jumps(jumps, traces, partner, "sx", x_faces(), (rxa, rxb))
    flat = jumps[...].reshape(2 * rows, size)
    with_self = product(flat, self_block[...])
    with_opp = product(flat, opposite_block[...])
    from_x = product(pair_sum(jumps, 0), cross_block[...])
    from_xy = from_x + cross_y[...]
    totals = (
        with_self[:rows] + with_opp[rows:] + base_x[...],
        with_self[rows:] + with_opp[:rows] + base_x[...],
        base_y[0] + from_x,
        base_y[1] + from_x,
        base_z[0] + from_xy,
        base_z[1] + from_xy,
    )
    faces = (*x_faces(), *y_faces(), 4, 5)
    outs = (xa, xb, ya, yb, local_z.at[0], local_z.at[1])
    sent = (to_xa, to_xb, to_ya, to_yb)
    partials = jnp.zeros((rows, LANES), jnp.float32)
    for index, (face, total, out) in enumerate(zip(faces, totals, outs)):
        for sub in range(subs):
            here = slice(sub * rhs, (sub + 1) * rhs)
            value = (viscosity[sub] * total[here]).astype(jnp.bfloat16)
            out[sub] = value
            if index < 4:
                sent[index][partner[sub, face]] = value
        partials += product(out[...].reshape(rows, size), corner_map[face])
    partials = partials.T
    dense[...] = coarse_rows(partials, spread, onehot)
    me = lax.axis_index("sy")

    def block(bits):
        start = pl.multiple_of((me ^ bits) * COARSE_DEV, COARSE_DEV)
        return dense[pl.ds(start, COARSE_DEV), :]

    half, per_row = kept.shape[0], size // LANES
    for index in range((to_ya.shape[0] - subs) * per_row):
        lanes = slice(index % per_row * LANES, (index % per_row + 1) * LANES)
        both = jnp.zeros((2 * COARSE_DEV, LANES), jnp.float32)
        if index < half:
            kept[index] = block(2 * index)
            both = jnp.concatenate(high_low(block(2 * index + 1)), axis=0)
        to_ya[subs + index // per_row, :, lanes] = both.astype(jnp.bfloat16)


def first_add_kernel(subs, kept, got, *refs):
    keep, give = refs[2:4]
    half, per_row = kept.shape[0], got.shape[2] // LANES
    for index in range(half):
        lanes = slice(index % per_row * LANES, (index % per_row + 1) * LANES)
        both = got[subs + index // per_row, :, lanes].astype(jnp.float32)
        total = kept[index] + both[:COARSE_DEV] + both[COARSE_DEV:]
        out = keep if index % 2 == 0 else give
        out[index // 2] = total


def next_add_kernel(after, rxb, kept, got, keep, give):
    del after, rxb
    for index in range(kept.shape[0]):
        out = keep if index % 2 == 0 else give
        out[index // 2] = kept[index] + got[index]


def last_add_kernel(after, kept, got, coarse, total, sem):
    del after
    total[...] = (kept[0] + got[0])[:, : total.shape[1]]
    copy = pltpu.make_async_copy(total, coarse, sem)
    copy.start()
    copy.wait()


def apply_z_kernel(kept, local_z, applied, held, sems):
    del kept
    subs = local_z.shape[1]
    copies = []
    for sub in range(subs):
        up = local_z[0, sub].astype(jnp.float32)
        down = local_z[1, sub].astype(jnp.float32)
        if sub + 1 < subs:
            up = up - local_z[1, sub + 1].astype(jnp.float32)
        if sub > 0:
            down = down - local_z[0, sub - 1].astype(jnp.float32)
        held[sub, 0] = up
        held[sub, 1] = down
        copies.append(
            pltpu.make_async_copy(held.at[sub], applied.at[sub, pl.ds(4, 2)], sems.at[sub])
        )
        copies[-1].start()
    for copy in copies:
        copy.wait()


def apply_kernel(applied_in, rxb, ryb, rxa, rya, ya, yb, xa, xb, applied, held, sems):
    del applied_in
    copies = []
    trades = zip((*y_faces(), *x_faces()), (ya, yb, xa, xb), (rya, ryb, rxa, rxb))
    for index, (face, local, got) in enumerate(trades):
        for sub in range(held.shape[1]):
            other = got[sub].astype(jnp.float32)
            if index == 1:
                other = other * inner("sy")
            if index == 3:
                other = other * inner("sx")
            held[index, sub] = local[sub].astype(jnp.float32) - other
            copies.append(
                pltpu.make_async_copy(
                    held.at[index, sub], applied.at[sub, face], sems.at[index, sub]
                )
            )
            copies[-1].start()
    for copy in copies:
        copy.wait()


def body(
    traces, viscosity, partner, corner_owner, self_block, opposite_block, cross_block, corner_map
):
    values = traces[0, 0]
    slots, visc, owners = partner[0, 0], viscosity[0, 0], corner_owner[0, 0]
    subs, _, rhs, size = values.shape
    count = lax.axis_size("sy")
    rows = subs * rhs
    face_shape = (subs, rhs, size)
    bf16, f32 = jnp.bfloat16, jnp.float32

    xb, yb, xa, ya = pl.pallas_call(
        send_kernel,
        in_specs=[HBM],
        out_specs=[VMEM] * 4,
        out_shape=[in_vmem(face_shape, bf16)] * 4,
        scratch_shapes=[pltpu.SemaphoreType.DMA((4,))],
        compiler_params=params(8),
        cost_estimate=LONG,
    )(in_hbm(values))
    rxb = second_swap(xb, "sx")
    ryb = second_swap(yb, "sy")
    rxa = first_swap(xa, "sx")
    rya = first_swap(ya, "sy")
    map_v, spread, base_z, cross_z = pl.pallas_call(
        z_kernel,
        in_specs=[VMEM] * 6,
        out_specs=[VMEM] * 4,
        out_shape=[in_vmem((6, size, LANES), bf16), in_vmem((COMPS, rows, subs * LANES), bf16)]
        + [in_vmem((2, rows, size), f32)]
        + [in_vmem((rows, size), f32)],
        scratch_shapes=[pltpu.VMEM((2,) + face_shape, bf16)],
        compiler_params=params(12),
        cost_estimate=LONG,
    )(
        xa, values, self_block, opposite_block, cross_block,
        jnp.transpose(corner_map, (1, 0, 2)),
    )
    base_y, cross_y, base_x, onehot = pl.pallas_call(
        y_kernel,
        in_specs=[SMEM] + [VMEM] * 9,
        out_specs=[VMEM] * 4,
        out_shape=[in_vmem((2, rows, size), f32)] + [in_vmem((rows, size), f32)] * 2
        + [in_vmem((COARSE_DEV * count, 2 * subs * CORNERS), bf16)],
        scratch_shapes=[pltpu.VMEM((2,) + face_shape, bf16)],
        compiler_params=params(12),
    )(slots, values, ryb, rya, rxb, self_block, opposite_block, cross_block, cross_z, owners)
    half, per_row = count // 2, size // LANES
    long_shape = (subs + -(-half // per_row), rhs, size)

    def blocks(number):
        return in_vmem((number, COARSE_DEV, LANES), f32)

    xa, xb, ya, yb, local_z, to_xa, to_xb, to_ya, to_yb, kept = pl.pallas_call(
        local_kernel,
        in_specs=[SMEM] * 2 + [VMEM] * 13,
        out_specs=[VMEM] * 10,
        out_shape=[in_vmem(face_shape, bf16)] * 4
        + [in_vmem((2,) + face_shape, bf16)]
        + [in_vmem(face_shape, bf16)] * 2
        + [in_vmem(long_shape, bf16), in_vmem(face_shape, bf16), blocks(half)],
        scratch_shapes=[
            pltpu.VMEM((2,) + face_shape, bf16),
            pltpu.VMEM((COARSE_DEV * count, LANES), f32),
        ],
        compiler_params=params(16),
    )(
        slots, visc, values, rxa, rxb, self_block, opposite_block, cross_block,
        base_x, base_y, base_z, cross_y, spread, onehot, map_v,
    )
    rya = first_swap(to_ya, "sy")
    rxb = second_swap(to_xb, "sx")
    out_shape = jax.ShapeDtypeStruct(values.shape, f32)
    half //= 2
    bits = 2
    kept, give, to_xa, to_yb = pl.pallas_call(
        lambda *refs: first_add_kernel(subs, *refs),
        in_specs=[VMEM] * 4,
        out_specs=[VMEM] * 4,
        out_shape=[blocks(half)] * 2 + [in_vmem(face_shape, bf16)] * 2,
        input_output_aliases={2: 2, 3: 3},
        compiler_params=params(4),
    )(kept, rya, to_xa, to_yb)
    got = cross_swap(give, "sy", bits)
    applied = pl.pallas_call(
        apply_z_kernel,
        in_specs=[VMEM] * 2,
        out_specs=HBM,
        out_shape=out_shape,
        scratch_shapes=[
            pltpu.VMEM((subs, 2, rhs, size), f32),
            pltpu.SemaphoreType.DMA((subs,)),
        ],
        compiler_params=params(8),
        cost_estimate=LONG,
    )(kept, local_z)
    ryb = second_swap(to_yb, "sy")
    rxa = first_swap(to_xa, "sx")
    while half > 1:
        half //= 2
        bits *= 2
        kept, give = pl.pallas_call(
            next_add_kernel,
            in_specs=[HBM] + [VMEM] * 3,
            out_specs=[VMEM] * 2,
            out_shape=[blocks(half)] * 2,
            compiler_params=params(4),
            cost_estimate=LONG,
        )(in_hbm(applied), rxb, kept, got)
        got = cross_swap(give, "sy", bits)
    applied = pl.pallas_call(
        apply_kernel,
        in_specs=[HBM] + [VMEM] * 8,
        out_specs=HBM,
        out_shape=out_shape,
        input_output_aliases={0: 0},
        scratch_shapes=[pltpu.VMEM((4,) + face_shape, f32), pltpu.SemaphoreType.DMA((4, subs))],
        compiler_params=params(12),
        cost_estimate=LONG,
    )(applied, rxb, ryb, rxa, rya, ya, yb, xa, xb)
    coarse = pl.pallas_call(
        last_add_kernel,
        in_specs=[HBM] + [VMEM] * 2,
        out_specs=HBM,
        out_shape=jax.ShapeDtypeStruct((COARSE_DEV, rhs * COMPS), f32),
        scratch_shapes=[pltpu.VMEM((COARSE_DEV, rhs * COMPS), f32), pltpu.SemaphoreType.DMA],
        compiler_params=params(4),
    )(in_hbm(applied), kept, got)
    return applied[None, None], coarse.T


def solution(mesh):
    return jax.shard_map(
        body,
        mesh=mesh,
        in_specs=(
            P("sx", "sy", None, None, None, None),
            P("sx", "sy", None),
            P("sx", "sy", None, None),
            P("sx", "sy", None, None),
            P(),
            P(),
            P(),
            P(),
        ),
        out_specs=(P("sx", "sy", None, None, None, None), P(None, ("sx", "sy"))),
        check_vma=False,
    )
```
